32 devices in a mesh: dp: 8 (over y, x, core), mp: 4 (over z).
Axes of the slice: x: 2, y: 2, z: 4, core: 2. Of those that a mesh axis runs over, the one named last changes fastest.
Arguments:
- block_input: bfloat16 [8192, 1024], P('dp'), may hold values from -6 to 6
- layer_one_input: bfloat16 [8192, 1024], P('dp', 'mp'), may hold values from -6 to 6
- segment_ids: int32 [8, 1024], P('dp'), may hold values from 0 to 7, never falling along the last dimension, each value on 1 to 512 neighbouring positions
- grad_output: bfloat16 [8192, 1024], P('dp'), may hold values from -6 to 6
- norm_one: float32 [1024], replicated, may hold values from 0.1 to 1.9
- w_query: bfloat16 [1024, 1024], P(None, 'mp'), may hold values from -0.1875 to 0.1875
- w_key: bfloat16 [1024, 1024], P(None, 'mp'), may hold values from -0.1875 to 0.1875
- w_value: bfloat16 [1024, 1024], P(None, 'mp'), may hold values from -0.1875 to 0.1875
- w_out: bfloat16 [1024, 1024], P('mp'), may hold values from -1.5 to 1.5
- norm_two: float32 [1024], replicated, may hold values from 0.1 to 1.9
- w_gate: bfloat16 [1024, 2816], P(None, 'mp'), may hold values from -0.1875 to 0.1875
- w_up: bfloat16 [1024, 2816], P(None, 'mp'), may hold values from -0.1875 to 0.1875
- w_down: bfloat16 [2816, 1024], P('mp'), may hold values from -0.109375 to 0.109375
- w_value_one: bfloat16 [1024, 1024], P('mp'), may hold values from -0.1875 to 0.1875
Outputs:
- output: bfloat16 [8192, 1024], P('dp')
- grad_input: float32 [8192, 1024], P('dp')
- grad_layer_one_input: float32 [8192, 1024], P('dp', 'mp')
- grad_norm_one: float32 [1024], replicated
- grad_query: float32 [1024, 1024], P(None, 'mp')
- grad_key: float32 [1024, 1024], P(None, 'mp')
- grad_value: float32 [1024, 1024], P(None, 'mp')
- grad_out_proj: float32 [1024, 1024], P('mp')
- grad_norm_two: float32 [1024], replicated
- grad_gate: float32 [1024, 2816], P(None, 'mp')
- grad_up: float32 [1024, 2816], P(None, 'mp')
- grad_down: float32 [2816, 1024], P('mp')
- grad_value_one: float32 [1024, 1024], P('mp')
The draws below stay inside these ranges and needn't reach their ends.
Inputs may be any that keep to these rules, and one draw needn't show every extreme that they name: `segment_ids`: non-decreasing along each sequence, each document 1 to 512 tokens, one of exactly 512 in every sequence.
All inputs are finite; a program needn't handle non-finite values.
Results may differ from the reference program's by a relative error of at most 0.012.
Values may be sent and summed in bfloat16 or wider, within the bound.
A program may use at most 128 MiB of HBM per device.

```python
import math
import jax
import jax.numpy as jnp
import numpy as np
from jax import lax

D = 1024
HEADS = 16
HD = 64
FF = 2816
TOK_DEV = 1024
SEQS = 8
TOKENS = 8192


def level_of(rng, extent, pieces, least, largest):
    factor_of = 1.0
    for axis_at, blocks in pieces:
        steps = jax.random.uniform(jax.random.fold_in(jax.random.fold_in(rng, 6), axis_at), (blocks,), jnp.float32, least / len(pieces), largest / len(pieces))
        factor_of = factor_of * jnp.repeat(jnp.exp(steps), extent[axis_at] // blocks).reshape((-1,) + (1,) * (len(extent) - 1 - axis_at))
    return factor_of


def split_up(count, total, most, slope):
    weights = [(1 << 20) // math.isqrt(grade ** slope) + 1 for grade in range(2, count + 1)]
    rest, counts = total - most - (count - 1), [1] * (count - 1)
    while rest > 0:
        free = [i for i in range(count - 1) if counts[i] < most]
        mass, remaining = sum([weights[i] for i in free]), rest
        for i in free:
            extra = min(most - counts[i], max(1, remaining * weights[i] // mass), rest)
            counts[i] = counts[i] + extra
            rest = rest - extra
    return np.array([most] + counts)


def uneven_parts(key, number_of, total, most, skew):
    if number_of == 2:
        one = jax.random.randint(key, (), max(1, total - most), min(most, total - 1) + 1)
        return jnp.stack([one, total - one])
    sizes = jnp.asarray(split_up(number_of, total, most, skew), jnp.int32)
    couples = (number_of - 1) // 2
    giver, taker = sizes[1:1 + 2 * couples:2], sizes[2:2 + 2 * couples:2]
    slack = jnp.minimum(giver - 1, most - taker)
    shifted = jax.random.randint(jax.random.fold_in(key, 1), (couples,), 0, 1 << 20) % (slack + 1)
    sizes = sizes.at[1:1 + 2 * couples:2].set(giver - shifted).at[2:2 + 2 * couples:2].set(taker + shifted)
    return sizes[jax.random.permutation(jax.random.fold_in(key, 2), number_of)]


def scatter_about(rng, dims, scale, reach, shards=(), kind=jnp.bfloat16):
    values = jax.random.normal(rng, dims, jnp.float32) * scale
    if len(shards) > 0:
        values = level_of(rng, dims, shards, -0.22, 0.18) * values
    return jnp.clip(values, min=-reach, max=reach).astype(kind)


def setup_inputs(seed: int = 0) -> dict:
    splits = jax.random.split(jax.random.key(seed), 15)
    block_input = scatter_about(splits[0], (TOKENS, D), 1.0, 6.0, ((0, 8),))
    layer_one_input = scatter_about(splits[1], (TOKENS, D), 1.0, 6.0, ((0, 8), (1, 4)))
    segment_ids = jax.vmap(lambda own: jnp.searchsorted(jnp.cumsum(uneven_parts(own, 8, TOK_DEV, TOK_DEV // 2, 0)), jnp.arange(TOK_DEV), side="right"))(jax.random.split(splits[2], SEQS)).reshape((SEQS, TOK_DEV)).astype(jnp.int32)
    grad_output = scatter_about(splits[3], (TOKENS, D), 1.0, 6.0, ((0, 8),))
    norm_one = jnp.clip(1.0 + 0.18 * jax.random.normal(splits[4], (D,), jnp.float32), 0.1, 1.9)
    w_query = scatter_about(splits[5], (D, D), D ** -0.5, 0.1875, ((1, 4),))
    w_key = scatter_about(splits[6], (D, D), D ** -0.5, 0.1875, ((1, 4),))
    w_value = scatter_about(splits[7], (D, D), D ** -0.5, 0.1875, ((1, 4),))
    w_out = scatter_about(splits[8], (D, D), (D // 64) ** -0.5, 1.5, ((0, 4),))
    norm_two = jnp.clip(1.0 + 0.18 * jax.random.normal(splits[9], (D,), jnp.float32), 0.1, 1.9)
    w_gate = scatter_about(splits[10], (D, FF), D ** -0.5, 0.1875, ((1, 4),))
    w_up = scatter_about(splits[11], (D, FF), D ** -0.5, 0.1875, ((1, 4),))
    w_down = scatter_about(splits[12], (FF, D), FF ** -0.5, 0.109375, ((0, 4),))
    w_value_one = scatter_about(splits[13], (D, D), D ** -0.5, 0.1875, ((0, 4),))
    return {"block_input": block_input, "layer_one_input": layer_one_input, "segment_ids": segment_ids, "grad_output": grad_output, "norm_one": norm_one, "w_query": w_query, "w_key": w_key, "w_value": w_value, "w_out": w_out, "norm_two": norm_two, "w_gate": w_gate, "w_up": w_up, "w_down": w_down, "w_value_one": w_value_one}


PRECISE = lax.Precision.HIGHEST
EPSILON = 1e-06

@jax.custom_vjp
def low(v):
    return lax.optimization_barrier(v.astype(jnp.bfloat16)).astype(jnp.float32)

@jax.custom_vjp
def low_back(v):
    return v

def low_keep(v):
    return (low(v), None)

def low_pass(kept, grad):
    return (grad,)

def back_keep(v):
    return (v, None)

def back_low(kept, grad):
    return (low(grad),)
low.defvjp(low_keep, low_pass)
low_back.defvjp(back_keep, back_low)

def mix_norm(activations, gain_vec):
    return activations * lax.rsqrt(lax.optimization_barrier(jnp.mean(activations * activations, axis=-1, keepdims=True)) + EPSILON) * gain_vec

def positions_of(segments):
    position = lax.broadcasted_iota(jnp.int32, segments.shape, 1)
    changed = (segments[:, 1:] != segments[:, :-1]).astype(jnp.int32)
    starts = jnp.concatenate([jnp.ones_like(segments[:, :1]), changed], axis=1)
    return position - lax.cummax(position * starts, axis=1)

def rope_tables(positions, width):
    half_width = width // 2
    rates = jnp.exp(jnp.arange(half_width, dtype=jnp.float32) * (-math.log(10000.0) / half_width))
    angles = positions.astype(jnp.float32)[:, None] * rates[None, :]
    return (jnp.cos(angles)[:, None, :], jnp.sin(angles)[:, None, :])

def rotate(tensor, cosine, sine_part, turn):
    half_width = tensor.shape[-1] // 2
    left_half = tensor[..., :half_width]
    right_half = tensor[..., half_width:]
    return jnp.concatenate([left_half * cosine - turn * right_half * sine_part, right_half * cosine + turn * left_half * sine_part], axis=-1)

def attend_block(queries, key_rows, values, seg_rows, seg_all, first_row):
    block_rows = queries.shape[0]
    scores = low_back(jnp.einsum('qhd,khd->hqk', queries, key_rows, precision=PRECISE) * HD ** (-0.5))
    row_index = first_row + lax.broadcasted_iota(jnp.int32, (block_rows, key_rows.shape[0]), 0)
    col_index = lax.broadcasted_iota(jnp.int32, (block_rows, key_rows.shape[0]), 1)
    allowed = (seg_rows[:, None] == seg_all[None, :]) & (col_index <= row_index)
    scores = jnp.where(allowed[None], scores, -1e+30)
    weights = low(jax.nn.softmax(scores, axis=-1))
    return jnp.einsum('hqk,khd->qhd', weights, values, precision=PRECISE)

def attend_sequence(packed):
    queries, key_rows, values, seg_all = packed
    row_count = queries.shape[0]
    block_rows = min(512, row_count)
    blocks = row_count // block_rows
    query_blocks = queries.reshape(blocks, block_rows, HEADS, HD)
    seg_blocks = seg_all.reshape(blocks, block_rows)
    first_rows = jnp.arange(blocks, dtype=jnp.int32) * block_rows

    def one_block(item):
        return attend_block(item[0], key_rows, values, item[1], seg_all, item[2])
    result = lax.map(jax.checkpoint(one_block), (query_blocks, seg_blocks, first_rows))
    return result.reshape(row_count, HEADS, HD)

def block_forward(inputs, first_inputs, gain_one, query_w, key_w, value_w, out_w, gain_two, gate_w, up_w, down_w, first_value_w, segments, cosine, sine_part):
    token_count = inputs.shape[0]
    seq_count = segments.shape[0]
    normed = low(mix_norm(inputs, gain_one))
    queries = low_back(jnp.dot(normed, query_w, precision=PRECISE)).reshape(token_count, HEADS, HD)
    key_rows = low_back(jnp.dot(normed, key_w, precision=PRECISE)).reshape(token_count, HEADS, HD)
    own_values = low_back(jnp.dot(normed, value_w, precision=PRECISE))
    first_values = low_back(jnp.dot(first_inputs, first_value_w, precision=PRECISE))
    mixed_values = low(0.5 * own_values + 0.5 * first_values).reshape(token_count, HEADS, HD)
    turned_q = low(rotate(queries, cosine, sine_part, 1.0))
    turned_k = low(rotate(key_rows, cosine, sine_part, 1.0))
    packed = (turned_q.reshape(seq_count, -1, HEADS, HD), turned_k.reshape(seq_count, -1, HEADS, HD), mixed_values.reshape(seq_count, -1, HEADS, HD), segments)
    attended = lax.map(jax.checkpoint(attend_sequence), packed)
    attended = low(low_back(attended.reshape(token_count, HEADS * HD)))
    residual = inputs + low_back(jnp.dot(attended, out_w, precision=PRECISE))
    normed_two = low(mix_norm(residual, gain_two))
    gate_pre = low_back(jnp.dot(normed_two, gate_w, precision=PRECISE))
    up_pre = low_back(jnp.dot(normed_two, up_w, precision=PRECISE))
    hidden = low(jax.nn.silu(gate_pre) * up_pre)
    return residual + low_back(jnp.dot(hidden, down_w, precision=PRECISE))

def reference(block_input, layer_one_input, segment_ids, grad_output, norm_one, w_query, w_key, w_value, w_out, norm_two, w_gate, w_up, w_down, w_value_one):
    positions = positions_of(segment_ids).reshape(-1)
    cosine, sine_part = rope_tables(positions, HD)

    def forward(inputs, first_inputs, gain_one, query_w, key_w, value_w, out_w, gain_two, gate_w, up_w, down_w, first_value_w):
        return block_forward(inputs, first_inputs, gain_one, query_w, key_w, value_w, out_w, gain_two, gate_w, up_w, down_w, first_value_w, segment_ids, cosine, sine_part)
    result, pullback = jax.vjp(forward, block_input.astype(jnp.float32), layer_one_input.astype(jnp.float32), norm_one.astype(jnp.float32), w_query.astype(jnp.float32), w_key.astype(jnp.float32), w_value.astype(jnp.float32), w_out.astype(jnp.float32), norm_two.astype(jnp.float32), w_gate.astype(jnp.float32), w_up.astype(jnp.float32), w_down.astype(jnp.float32), w_value_one.astype(jnp.float32))
    grads = pullback(grad_output.astype(jnp.float32))
    return (result.astype(jnp.bfloat16), grads[0], grads[1], grads[2], grads[3], grads[4], grads[5], grads[6], grads[7], grads[8], grads[9], grads[10], grads[11])
```

```python
import math

import jax
import jax.numpy as jnp
from jax import lax
from jax.sharding import PartitionSpec as P

HD = 64


EPSILON = 1e-06


def positions_of(segments):
    position = lax.broadcasted_iota(jnp.int32, segments.shape, 1)
    changed = (segments[:, 1:] != segments[:, :-1]).astype(jnp.int32)
    starts = jnp.concatenate([jnp.ones_like(segments[:, :1]), changed], axis=1)
    return position - lax.cummax(position * starts, axis=1)


def rope_tables(positions, width):
    half_width = width // 2
    rates = jnp.exp(jnp.arange(half_width, dtype=jnp.float32) * (-math.log(10000.0) / half_width))
    angles = positions.astype(jnp.float32)[:, None] * rates[None, :]
    return (jnp.cos(angles)[:, None, :], jnp.sin(angles)[:, None, :])


def rotate(tensor, cosine, sine_part, turn):
    half_width = tensor.shape[-1] // 2
    left_half = tensor[..., :half_width]
    right_half = tensor[..., half_width:]
    return jnp.concatenate(
        [
            left_half * cosine - turn * right_half * sine_part,
            right_half * cosine + turn * left_half * sine_part,
        ],
        axis=-1,
    )


def over_rows(left_side, right_side):
    return lax.dot_general(
        left_side, right_side, (((0,), (0,)), ((), ())), preferred_element_type=jnp.float32
    )


def against(left_side, right_side):
    return lax.dot_general(
        left_side, right_side, (((1,), (1,)), ((), ())), preferred_element_type=jnp.float32
    )


def norm_back(activations, scale_vec, gain_vec, grad_normed):
    grad_gain = jnp.sum(grad_normed * activations * scale_vec, axis=0)
    scaled = grad_normed * gain_vec
    inner = jnp.mean(scaled * activations, axis=-1, keepdims=True)
    return (grad_gain, scale_vec * scaled - activations * scale_vec * scale_vec * scale_vec * inner)


def masked_scores(q_block, key_rows, seg_block, seg_all, first_row, score_scale):
    block_rows = q_block.shape[0]
    scores = (
        jnp.einsum("qhd,khd->hqk", q_block, key_rows, preferred_element_type=jnp.float32)
        * score_scale
    )
    row_index = first_row + lax.broadcasted_iota(jnp.int32, (block_rows, key_rows.shape[0]), 0)
    col_index = lax.broadcasted_iota(jnp.int32, (block_rows, key_rows.shape[0]), 1)
    allowed = (seg_block[:, None] == seg_all[None, :]) & (col_index <= row_index)
    return jnp.where(allowed[None], scores, -1e30)


def attend_forward(queries, key_rows, values, seg_all, score_scale):
    row_count, head_count, width = queries.shape
    block_rows = min(512, row_count)

    def one_block(block_index):
        first_row = block_index * block_rows
        q_block = lax.dynamic_slice_in_dim(queries, first_row, block_rows, 0)
        seg_block = lax.dynamic_slice_in_dim(seg_all, first_row, block_rows, 0)
        scores = masked_scores(q_block, key_rows, seg_block, seg_all, first_row, score_scale)
        largest = jnp.max(scores, axis=-1, keepdims=True)
        raised = jnp.exp(scores - largest)
        summed = jnp.sum(raised, axis=-1, keepdims=True)
        weights = (raised / summed).astype(jnp.bfloat16)
        result = jnp.einsum("hqk,khd->qhd", weights, values, preferred_element_type=jnp.float32)
        return (result, (largest + jnp.log(summed))[..., 0])

    results, log_totals = lax.map(one_block, jnp.arange(row_count // block_rows, dtype=jnp.int32))
    return (results.reshape(row_count, head_count, width), log_totals)


def attend_backward(queries, key_rows, values, seg_all, log_totals, grad_attended, score_scale):
    row_count = queries.shape[0]
    block_rows = min(512, row_count)

    def one_block(carried, block_index):
        grad_keys, grad_values = carried
        first_row = block_index * block_rows
        q_block = lax.dynamic_slice_in_dim(queries, first_row, block_rows, 0)
        seg_block = lax.dynamic_slice_in_dim(seg_all, first_row, block_rows, 0)
        grad_block = lax.dynamic_slice_in_dim(grad_attended, first_row, block_rows, 0)
        scores = masked_scores(q_block, key_rows, seg_block, seg_all, first_row, score_scale)
        probs = jnp.exp(scores - log_totals[block_index][..., None])
        grad_probs = jnp.einsum(
            "qhd,khd->hqk", grad_block, values, preferred_element_type=jnp.float32
        )
        inner = jnp.sum(probs * grad_probs, axis=-1, keepdims=True)
        grad_scores = (probs * (grad_probs - inner)).astype(jnp.bfloat16)
        grad_query = (
            jnp.einsum("hqk,khd->qhd", grad_scores, key_rows, preferred_element_type=jnp.float32)
            * score_scale
        )
        grad_keys = (
            grad_keys
            + jnp.einsum("hqk,qhd->khd", grad_scores, q_block, preferred_element_type=jnp.float32)
            * score_scale
        )
        grad_values = grad_values + jnp.einsum(
            "hqk,qhd->khd",
            probs.astype(jnp.bfloat16),
            grad_block,
            preferred_element_type=jnp.float32,
        )
        return ((grad_keys, grad_values), grad_query)

    zero_rows = jnp.zeros(key_rows.shape, jnp.float32)
    (grad_keys, grad_values), grad_queries = lax.scan(
        one_block, (zero_rows, zero_rows), jnp.arange(row_count // block_rows, dtype=jnp.int32)
    )
    return (grad_queries.reshape(key_rows.shape), grad_keys, grad_values)


def on_device(
    block_input,
    layer_one_input,
    segment_ids,
    grad_output,
    norm_one,
    w_query,
    w_key,
    w_value,
    w_out,
    norm_two,
    w_gate,
    w_up,
    w_down,
    w_value_one,
):
    token_count = block_input.shape[0]
    head_count = w_query.shape[1] // HD
    score_scale = HD ** (-0.5)
    seg_all = segment_ids[0]
    cosine, sine_part = rope_tables(positions_of(segment_ids)[0], HD)
    share_rows = token_count // lax.axis_size("mp")
    share_start = lax.axis_index("mp") * share_rows
    inputs = block_input.astype(jnp.float32)
    scale_one = lax.rsqrt(jnp.mean(inputs * inputs, axis=-1, keepdims=True) + EPSILON)
    normed = (inputs * scale_one * norm_one).astype(jnp.bfloat16)
    queries = jnp.dot(normed, w_query, preferred_element_type=jnp.float32).reshape(
        token_count, head_count, HD
    )
    key_rows = jnp.dot(normed, w_key, preferred_element_type=jnp.float32).reshape(
        token_count, head_count, HD
    )
    own_values = jnp.dot(normed, w_value, preferred_element_type=jnp.float32)
    first_values = lax.psum_scatter(
        jnp.dot(layer_one_input, w_value_one, preferred_element_type=jnp.float32).astype(
            jnp.bfloat16
        ),
        "mp",
        scatter_dimension=1,
        tiled=True,
    ).astype(jnp.float32)
    mixed_values = (
        (0.5 * own_values + 0.5 * first_values)
        .astype(jnp.bfloat16)
        .reshape(token_count, head_count, HD)
    )
    turned_q = rotate(queries, cosine, sine_part, 1.0).astype(jnp.bfloat16)
    turned_k = rotate(key_rows, cosine, sine_part, 1.0).astype(jnp.bfloat16)
    attended, log_totals = attend_forward(turned_q, turned_k, mixed_values, seg_all, score_scale)
    attended = attended.reshape(token_count, head_count * HD).astype(jnp.bfloat16)
    branch_one = jnp.dot(attended, w_out, preferred_element_type=jnp.float32)
    inputs_here = lax.dynamic_slice_in_dim(inputs, share_start, share_rows, 0)
    scale_one_here = lax.dynamic_slice_in_dim(scale_one, share_start, share_rows, 0)
    grad_rows = lax.dynamic_slice_in_dim(grad_output, share_start, share_rows, 0).astype(
        jnp.float32
    )
    residual = inputs_here + lax.psum_scatter(
        branch_one.astype(jnp.bfloat16), "mp", scatter_dimension=0, tiled=True
    ).astype(jnp.float32)
    scale_two = lax.rsqrt(jnp.mean(residual * residual, axis=-1, keepdims=True) + EPSILON)
    normed_two = (residual * scale_two * norm_two).astype(jnp.bfloat16)
    normed_two = lax.all_gather(normed_two, "mp", axis=0, tiled=True)
    gate_pre = jnp.dot(normed_two, w_gate, preferred_element_type=jnp.float32)
    up_pre = jnp.dot(normed_two, w_up, preferred_element_type=jnp.float32)
    sigmoid_gate = jax.nn.sigmoid(gate_pre)
    silu_gate = gate_pre * sigmoid_gate
    hidden = (silu_gate * up_pre).astype(jnp.bfloat16)
    branch_two = jnp.dot(hidden, w_down, preferred_element_type=jnp.float32)
    output_share = (
        residual
        + lax.psum_scatter(
            branch_two.astype(jnp.bfloat16), "mp", scatter_dimension=0, tiled=True
        ).astype(jnp.float32)
    ).astype(jnp.bfloat16)
    output = lax.all_gather(output_share, "mp", axis=0, tiled=True)
    grad_down = over_rows(hidden, grad_output)
    grad_hidden = against(grad_output, w_down)
    grad_gate_pre = (
        grad_hidden * up_pre * sigmoid_gate * (1.0 + gate_pre * (1.0 - sigmoid_gate))
    ).astype(jnp.bfloat16)
    grad_up_pre = (grad_hidden * silu_gate).astype(jnp.bfloat16)
    grad_gate = over_rows(normed_two, grad_gate_pre)
    grad_up = over_rows(normed_two, grad_up_pre)
    back_two = against(grad_gate_pre, w_gate) + against(grad_up_pre, w_up)
    grad_normed_two = lax.psum_scatter(
        back_two.astype(jnp.bfloat16), "mp", scatter_dimension=0, tiled=True
    ).astype(jnp.float32)
    grad_norm_two, grad_through_two = norm_back(residual, scale_two, norm_two, grad_normed_two)
    grad_residual = grad_rows + grad_through_two
    residual_low = grad_residual.astype(jnp.bfloat16)
    residual_low = lax.all_gather(residual_low, "mp", axis=0, tiled=True)
    grad_out_proj = over_rows(attended, residual_low)
    grad_attended = (
        against(residual_low, w_out).astype(jnp.bfloat16).reshape(token_count, head_count, HD)
    )
    grad_turned_q, grad_turned_k, grad_mixed = attend_backward(
        turned_q, turned_k, mixed_values, seg_all, log_totals, grad_attended, score_scale
    )
    grad_value_part = (0.5 * grad_mixed).reshape(token_count, head_count * HD).astype(jnp.bfloat16)
    grad_first_full = lax.all_gather(grad_value_part, "mp", axis=1, tiled=True)
    grad_queries = (
        rotate(grad_turned_q, cosine, sine_part, -1.0)
        .reshape(token_count, head_count * HD)
        .astype(jnp.bfloat16)
    )
    grad_keys = (
        rotate(grad_turned_k, cosine, sine_part, -1.0)
        .reshape(token_count, head_count * HD)
        .astype(jnp.bfloat16)
    )
    grad_query = over_rows(normed, grad_queries)
    grad_key = over_rows(normed, grad_keys)
    grad_value = over_rows(normed, grad_value_part)
    back_one = (
        against(grad_queries, w_query)
        + against(grad_keys, w_key)
        + against(grad_value_part, w_value)
    )
    grad_normed = lax.psum_scatter(
        back_one.astype(jnp.bfloat16), "mp", scatter_dimension=0, tiled=True
    ).astype(jnp.float32)
    grad_norm_one, grad_through_one = norm_back(inputs_here, scale_one_here, norm_one, grad_normed)
    gain_rows = jnp.concatenate([grad_norm_one, grad_norm_two])[None, :]
    grad_input, gain_all = (
        lax.all_gather(
            (grad_residual + grad_through_one).astype(jnp.bfloat16), "mp", axis=0, tiled=True
        ).astype(jnp.float32),
        lax.all_gather(gain_rows, "mp", axis=0, tiled=True),
    )
    gain_total = jnp.sum(gain_all, axis=0)
    width = norm_one.shape[0]
    grad_norm_one = gain_total[:width]
    grad_norm_two = gain_total[width:]
    grad_value_one = over_rows(layer_one_input, grad_first_full)
    grad_layer_one_input = against(grad_first_full, w_value_one)
    grad_norm_one, grad_norm_two = lax.psum((grad_norm_one, grad_norm_two), "dp")
    summed = lax.psum(
        tuple(
            part.astype(jnp.bfloat16)
            for part in (
                grad_query,
                grad_key,
                grad_value,
                grad_out_proj,
                grad_value_one,
                grad_gate,
                grad_up,
                grad_down,
            )
        ),
        "dp",
    )
    (
        grad_query,
        grad_key,
        grad_value,
        grad_out_proj,
        grad_value_one,
        grad_gate,
        grad_up,
        grad_down,
    ) = tuple(part.astype(jnp.float32) for part in summed)
    return (
        output,
        grad_input,
        grad_layer_one_input,
        grad_norm_one,
        grad_query,
        grad_key,
        grad_value,
        grad_out_proj,
        grad_norm_two,
        grad_gate,
        grad_up,
        grad_down,
        grad_value_one,
    )


def solution(mesh):
    return jax.shard_map(
        on_device,
        mesh=mesh,
        in_specs=(
            P("dp", None),
            P("dp", "mp"),
            P("dp", None),
            P("dp", None),
            P(),
            P(None, "mp"),
            P(None, "mp"),
            P(None, "mp"),
            P("mp", None),
            P(),
            P(None, "mp"),
            P(None, "mp"),
            P("mp", None),
            P("mp", None),
        ),
        out_specs=(
            P("dp", None),
            P("dp", None),
            P("dp", "mp"),
            P(),
            P(None, "mp"),
            P(None, "mp"),
            P(None, "mp"),
            P("mp", None),
            P(),
            P(None, "mp"),
            P(None, "mp"),
            P("mp", None),
            P("mp", None),
        ),
        check_vma=False,
    )
```

```python
import functools
import math
from types import SimpleNamespace

import jax
import jax.numpy as jnp
from jax import lax
from jax.experimental import pallas as pl
from jax.experimental.pallas import tpu as pltpu
from jax.sharding import PartitionSpec as P

HD = 64


EPSILON = 1e-06
VMEM_LIMIT = 64 * 2**20 - 2**16


def positions_of(segments):
    position = lax.broadcasted_iota(jnp.int32, segments.shape, 1)
    changed = (segments[:, 1:] != segments[:, :-1]).astype(jnp.int32)
    starts = jnp.concatenate([jnp.ones_like(segments[:, :1]), changed], axis=1)
    return position - lax.cummax(position * starts, axis=1)


def rope_tables(positions, width):
    half_width = width // 2
    rates = jnp.exp(jnp.arange(half_width, dtype=jnp.float32) * (-math.log(10000.0) / half_width))
    angles = positions.astype(jnp.float32)[:, None] * rates[None, :]
    return (jnp.cos(angles)[:, None, :], jnp.sin(angles)[:, None, :])


def rotate(tensor, cosine, sine_part, turn):
    half_width = tensor.shape[-1] // 2
    left_half = tensor[..., :half_width]
    right_half = tensor[..., half_width:]
    return jnp.concatenate(
        [
            left_half * cosine - turn * right_half * sine_part,
            right_half * cosine + turn * left_half * sine_part,
        ],
        axis=-1,
    )


def over_rows(left_side, right_side):
    return lax.dot_general(
        left_side, right_side, (((0,), (0,)), ((), ())), preferred_element_type=jnp.float32
    )


def against(left_side, right_side):
    return lax.dot_general(
        left_side, right_side, (((1,), (1,)), ((), ())), preferred_element_type=jnp.float32
    )


def norm_back(activations, scale_vec, gain_vec, grad_normed):
    grad_gain = jnp.sum(grad_normed * activations * scale_vec, axis=0)
    scaled = grad_normed * gain_vec
    inner = jnp.mean(scaled * activations, axis=-1, keepdims=True)
    return (grad_gain, scale_vec * scaled - activations * scale_vec * scale_vec * scale_vec * inner)


def masked_scores(q_block, key_rows, seg_block, seg_all, first_row, score_scale):
    block_rows = q_block.shape[0]
    scores = (
        jnp.einsum("qhd,khd->hqk", q_block, key_rows, preferred_element_type=jnp.float32)
        * score_scale
    )
    row_index = first_row + lax.broadcasted_iota(jnp.int32, (block_rows, key_rows.shape[0]), 0)
    col_index = lax.broadcasted_iota(jnp.int32, (block_rows, key_rows.shape[0]), 1)
    allowed = (seg_block[:, None] == seg_all[None, :]) & (col_index <= row_index)
    return jnp.where(allowed[None], scores, -1e30)


def attend_forward(queries, key_rows, values, seg_all, score_scale):
    row_count, head_count, width = queries.shape
    block_rows = min(512, row_count)

    def one_block(block_index):
        first_row = block_index * block_rows
        q_block = lax.dynamic_slice_in_dim(queries, first_row, block_rows, 0)
        seg_block = lax.dynamic_slice_in_dim(seg_all, first_row, block_rows, 0)
        scores = masked_scores(q_block, key_rows, seg_block, seg_all, first_row, score_scale)
        largest = jnp.max(scores, axis=-1, keepdims=True)
        raised = jnp.exp(scores - largest)
        summed = jnp.sum(raised, axis=-1, keepdims=True)
        weights = (raised / summed).astype(jnp.bfloat16)
        result = jnp.einsum("hqk,khd->qhd", weights, values, preferred_element_type=jnp.float32)
        return (result, (largest + jnp.log(summed))[..., 0])

    results, log_totals = lax.map(one_block, jnp.arange(row_count // block_rows, dtype=jnp.int32))
    return (results.reshape(row_count, head_count, width), log_totals)


def attend_backward(queries, key_rows, values, seg_all, log_totals, grad_attended, score_scale):
    row_count = queries.shape[0]
    block_rows = min(512, row_count)

    def one_block(carried, block_index):
        grad_keys, grad_values = carried
        first_row = block_index * block_rows
        q_block = lax.dynamic_slice_in_dim(queries, first_row, block_rows, 0)
        seg_block = lax.dynamic_slice_in_dim(seg_all, first_row, block_rows, 0)
        grad_block = lax.dynamic_slice_in_dim(grad_attended, first_row, block_rows, 0)
        scores = masked_scores(q_block, key_rows, seg_block, seg_all, first_row, score_scale)
        probs = jnp.exp(scores - log_totals[block_index][..., None])
        grad_probs = jnp.einsum(
            "qhd,khd->hqk", grad_block, values, preferred_element_type=jnp.float32
        )
        inner = jnp.sum(probs * grad_probs, axis=-1, keepdims=True)
        grad_scores = (probs * (grad_probs - inner)).astype(jnp.bfloat16)
        grad_query = (
            jnp.einsum("hqk,khd->qhd", grad_scores, key_rows, preferred_element_type=jnp.float32)
            * score_scale
        )
        grad_keys = (
            grad_keys
            + jnp.einsum("hqk,qhd->khd", grad_scores, q_block, preferred_element_type=jnp.float32)
            * score_scale
        )
        grad_values = grad_values + jnp.einsum(
            "hqk,qhd->khd",
            probs.astype(jnp.bfloat16),
            grad_block,
            preferred_element_type=jnp.float32,
        )
        return ((grad_keys, grad_values), grad_query)

    zero_rows = jnp.zeros(key_rows.shape, jnp.float32)
    (grad_keys, grad_values), grad_queries = lax.scan(
        one_block, (zero_rows, zero_rows), jnp.arange(row_count // block_rows, dtype=jnp.int32)
    )
    return (grad_queries.reshape(key_rows.shape), grad_keys, grad_values)


def by_collectives(
    block_input,
    layer_one_input,
    segment_ids,
    grad_output,
    norm_one,
    w_query,
    w_key,
    w_value,
    w_out,
    norm_two,
    w_gate,
    w_up,
    w_down,
    w_value_one,
):
    token_count = block_input.shape[0]
    head_count = w_query.shape[1] // HD
    score_scale = HD ** (-0.5)
    seg_all = segment_ids[0]
    cosine, sine_part = rope_tables(positions_of(segment_ids)[0], HD)
    share_rows = token_count // lax.axis_size("mp")
    share_start = lax.axis_index("mp") * share_rows
    inputs = block_input.astype(jnp.float32)
    scale_one = lax.rsqrt(jnp.mean(inputs * inputs, axis=-1, keepdims=True) + EPSILON)
    normed = (inputs * scale_one * norm_one).astype(jnp.bfloat16)
    queries = jnp.dot(normed, w_query, preferred_element_type=jnp.float32).reshape(
        token_count, head_count, HD
    )
    key_rows = jnp.dot(normed, w_key, preferred_element_type=jnp.float32).reshape(
        token_count, head_count, HD
    )
    own_values = jnp.dot(normed, w_value, preferred_element_type=jnp.float32)
    first_values = lax.psum_scatter(
        jnp.dot(layer_one_input, w_value_one, preferred_element_type=jnp.float32).astype(
            jnp.bfloat16
        ),
        "mp",
        scatter_dimension=1,
        tiled=True,
    ).astype(jnp.float32)
    mixed_values = (
        (0.5 * own_values + 0.5 * first_values)
        .astype(jnp.bfloat16)
        .reshape(token_count, head_count, HD)
    )
    turned_q = rotate(queries, cosine, sine_part, 1.0).astype(jnp.bfloat16)
    turned_k = rotate(key_rows, cosine, sine_part, 1.0).astype(jnp.bfloat16)
    attended, log_totals = attend_forward(turned_q, turned_k, mixed_values, seg_all, score_scale)
    attended = attended.reshape(token_count, head_count * HD).astype(jnp.bfloat16)
    branch_one = jnp.dot(attended, w_out, preferred_element_type=jnp.float32)
    inputs_here = lax.dynamic_slice_in_dim(inputs, share_start, share_rows, 0)
    scale_one_here = lax.dynamic_slice_in_dim(scale_one, share_start, share_rows, 0)
    grad_rows = lax.dynamic_slice_in_dim(grad_output, share_start, share_rows, 0).astype(
        jnp.float32
    )
    residual = inputs_here + lax.psum_scatter(
        branch_one.astype(jnp.bfloat16), "mp", scatter_dimension=0, tiled=True
    ).astype(jnp.float32)
    scale_two = lax.rsqrt(jnp.mean(residual * residual, axis=-1, keepdims=True) + EPSILON)
    normed_two = (residual * scale_two * norm_two).astype(jnp.bfloat16)
    normed_two = lax.all_gather(normed_two, "mp", axis=0, tiled=True)
    gate_pre = jnp.dot(normed_two, w_gate, preferred_element_type=jnp.float32)
    up_pre = jnp.dot(normed_two, w_up, preferred_element_type=jnp.float32)
    sigmoid_gate = jax.nn.sigmoid(gate_pre)
    silu_gate = gate_pre * sigmoid_gate
    hidden = (silu_gate * up_pre).astype(jnp.bfloat16)
    branch_two = jnp.dot(hidden, w_down, preferred_element_type=jnp.float32)
    output_share = (
        residual
        + lax.psum_scatter(
            branch_two.astype(jnp.bfloat16), "mp", scatter_dimension=0, tiled=True
        ).astype(jnp.float32)
    ).astype(jnp.bfloat16)
    output = lax.all_gather(output_share, "mp", axis=0, tiled=True)
    grad_down = over_rows(hidden, grad_output)
    grad_hidden = against(grad_output, w_down)
    grad_gate_pre = (
        grad_hidden * up_pre * sigmoid_gate * (1.0 + gate_pre * (1.0 - sigmoid_gate))
    ).astype(jnp.bfloat16)
    grad_up_pre = (grad_hidden * silu_gate).astype(jnp.bfloat16)
    grad_gate = over_rows(normed_two, grad_gate_pre)
    grad_up = over_rows(normed_two, grad_up_pre)
    back_two = against(grad_gate_pre, w_gate) + against(grad_up_pre, w_up)
    grad_normed_two = lax.psum_scatter(
        back_two.astype(jnp.bfloat16), "mp", scatter_dimension=0, tiled=True
    ).astype(jnp.float32)
    grad_norm_two, grad_through_two = norm_back(residual, scale_two, norm_two, grad_normed_two)
    grad_residual = grad_rows + grad_through_two
    residual_low = grad_residual.astype(jnp.bfloat16)
    residual_low = lax.all_gather(residual_low, "mp", axis=0, tiled=True)
    grad_out_proj = over_rows(attended, residual_low)
    grad_attended = (
        against(residual_low, w_out).astype(jnp.bfloat16).reshape(token_count, head_count, HD)
    )
    grad_turned_q, grad_turned_k, grad_mixed = attend_backward(
        turned_q, turned_k, mixed_values, seg_all, log_totals, grad_attended, score_scale
    )
    grad_value_part = (0.5 * grad_mixed).reshape(token_count, head_count * HD).astype(jnp.bfloat16)
    grad_first_full = lax.all_gather(grad_value_part, "mp", axis=1, tiled=True)
    grad_queries = (
        rotate(grad_turned_q, cosine, sine_part, -1.0)
        .reshape(token_count, head_count * HD)
        .astype(jnp.bfloat16)
    )
    grad_keys = (
        rotate(grad_turned_k, cosine, sine_part, -1.0)
        .reshape(token_count, head_count * HD)
        .astype(jnp.bfloat16)
    )
    grad_query = over_rows(normed, grad_queries)
    grad_key = over_rows(normed, grad_keys)
    grad_value = over_rows(normed, grad_value_part)
    back_one = (
        against(grad_queries, w_query)
        + against(grad_keys, w_key)
        + against(grad_value_part, w_value)
    )
    grad_normed = lax.psum_scatter(
        back_one.astype(jnp.bfloat16), "mp", scatter_dimension=0, tiled=True
    ).astype(jnp.float32)
    grad_norm_one, grad_through_one = norm_back(inputs_here, scale_one_here, norm_one, grad_normed)
    gain_rows = jnp.concatenate([grad_norm_one, grad_norm_two])[None, :]
    grad_input, gain_all = (
        lax.all_gather(
            (grad_residual + grad_through_one).astype(jnp.bfloat16), "mp", axis=0, tiled=True
        ).astype(jnp.float32),
        lax.all_gather(gain_rows, "mp", axis=0, tiled=True),
    )
    gain_total = jnp.sum(gain_all, axis=0)
    width = norm_one.shape[0]
    grad_norm_one = gain_total[:width]
    grad_norm_two = gain_total[width:]
    grad_value_one = over_rows(layer_one_input, grad_first_full)
    grad_layer_one_input = against(grad_first_full, w_value_one)
    grad_norm_one, grad_norm_two = lax.psum((grad_norm_one, grad_norm_two), "dp")
    summed = lax.psum(
        tuple(
            part.astype(jnp.bfloat16)
            for part in (
                grad_query,
                grad_key,
                grad_value,
                grad_out_proj,
                grad_value_one,
                grad_gate,
                grad_up,
                grad_down,
            )
        ),
        "dp",
    )
    (
        grad_query,
        grad_key,
        grad_value,
        grad_out_proj,
        grad_value_one,
        grad_gate,
        grad_up,
        grad_down,
    ) = tuple(part.astype(jnp.float32) for part in summed)
    return (
        output,
        grad_input,
        grad_layer_one_input,
        grad_norm_one,
        grad_query,
        grad_key,
        grad_value,
        grad_out_proj,
        grad_norm_two,
        grad_gate,
        grad_up,
        grad_down,
        grad_value_one,
    )


NN = (((1,), (0,)), ((), ()))
NT = (((1,), (1,)), ((), ()))
TN = (((0,), (0,)), ((), ()))
F32 = jnp.float32
BF16 = jnp.bfloat16
CHUNK = 256
REACH = 512
MESH = pl.DeviceIdType.MESH


def mul(left_side, right_side, dims=NN):
    return lax.dot_general(left_side, right_side, dims, preferred_element_type=F32)


def on_line(index):
    return {"mp": index}


def in_plane(index):
    return {"dp": index}


def remote(src, dst, send_sem, recv_sem, device):
    return pltpu.make_async_remote_copy(
        src_ref=src,
        dst_ref=dst,
        send_sem=send_sem,
        recv_sem=recv_sem,
        device_id=device,
        device_id_type=MESH,
    )


class Scatter:
    def __init__(self, me, count, parts, inbox, meet, sent, came, met):
        self.me, self.count = me, count
        self.parts, self.inbox, self.meet = parts, inbox, meet
        self.sent, self.came, self.met = sent, came, met

    def take(self, c, k):
        slot = self.inbox(c, k)
        remote(slot, slot, self.sent.at[c, k], self.came.at[c, k], on_line(0)).wait_recv()
        self.parts[c, k] = (self.parts[c, k].astype(F32) + self.inbox(c, k)[...].astype(F32)).astype(
            BF16
        )

    def right(self, c, k):
        me = self.me

        @pl.when(me < k)
        def _():
            @pl.when(me > 0)
            def _():
                self.take(c, k)

            remote(
                self.parts.at[c, k],
                self.inbox(c, k),
                self.sent.at[c, k],
                self.came.at[c, k],
                on_line(me + 1),
            ).start()

    def left(self, c, k):
        me = self.me

        @pl.when(me > k)
        def _():
            @pl.when(me < self.count - 1)
            def _():
                self.take(c, k)

            @pl.when(me == k + 1)
            def _():
                remote(
                    self.parts.at[c, k],
                    self.meet.at[c],
                    self.sent.at[c, k],
                    self.met.at[c],
                    on_line(me - 1),
                ).start()

            @pl.when(me > k + 1)
            def _():
                remote(
                    self.parts.at[c, k],
                    self.inbox(c, k),
                    self.sent.at[c, k],
                    self.came.at[c, k],
                    on_line(me - 1),
                ).start()

    def rights(self, c):
        for k in range(self.count - 1, 0, -1):
            self.right(c, k)

    def lefts(self, c):
        for k in range(self.count - 1):
            self.left(c, k)

    def open(self, c):
        @pl.when(self.me == 0)
        def _():
            self.rights(c)

        @pl.when(self.me == self.count - 1)
        def _():
            self.lefts(c)

    def relay(self, c):
        @pl.when((self.me > 0) & (self.me < self.count // 2))
        def _():
            self.rights(c)
            self.lefts(c)

        @pl.when((self.me < self.count - 1) & (self.me >= self.count // 2))
        def _():
            self.lefts(c)
            self.rights(c)

    def total(self, c, into):
        me = self.me
        into[...] = self.parts[c, me].astype(F32)

        @pl.when(me > 0)
        def _():
            slot = self.inbox(c, me)
            remote(slot, slot, self.sent.at[c, me], self.came.at[c, me], on_line(0)).wait_recv()
            into[...] += self.inbox(c, me)[...].astype(F32)

        @pl.when(me < self.count - 1)
        def _():
            slot = self.meet.at[c]
            remote(slot, slot, self.sent.at[c, me], self.met.at[c], on_line(0)).wait_recv()
            into[...] += self.meet[c].astype(F32)

    def drain_one(self, c):
        for k in range(self.count):

            @pl.when(self.me != k)
            def _():
                slot = self.parts.at[c, k]
                remote(
                    slot, slot, self.sent.at[c, k], self.came.at[c, k], on_line(0)
                ).wait_send()

    def drain(self, chunks):
        def one(c, carry):
            self.drain_one(c)
            return carry

        lax.fori_loop(0, chunks, one, 0)


class Gather:
    def __init__(self, me, count, place, came, sent_right, sent_left):
        self.me, self.count, self.place = me, count, place
        self.came, self.sent_right, self.sent_left = came, sent_right, sent_left

    def to_right(self, c, k, src):
        return remote(
            src, self.place(c, k), self.sent_right.at[c, k], self.came.at[c, k], on_line(self.me + 1)
        )

    def to_left(self, c, k, src):
        return remote(
            src, self.place(c, k), self.sent_left.at[c, k], self.came.at[c, k], on_line(self.me - 1)
        )

    def own(self, c, src):
        me = self.me

        @pl.when(me < self.count - 1)
        def _():
            self.to_right(c, me, src).start()

        @pl.when(me > 0)
        def _():
            self.to_left(c, me, src).start()

    def wait(self, c, k):
        slot = self.place(c, k)
        remote(slot, slot, self.sent_left.at[c, k], self.came.at[c, k], on_line(0)).wait_recv()

    def relay(self, c):
        me = self.me
        for step in range(1, self.count):

            @pl.when(me >= step)
            def _():
                k = me - step
                self.wait(c, k)

                @pl.when(me < self.count - 1)
                def _():
                    self.to_right(c, k, self.place(c, k)).start()

            @pl.when(me + step < self.count)
            def _():
                k = me + step
                self.wait(c, k)

                @pl.when(me > 0)
                def _():
                    self.to_left(c, k, self.place(c, k)).start()

    def drain(self, chunks):
        me = self.me

        def one(c, carry):
            for k in range(self.count):

                @pl.when((me >= k) & (me < self.count - 1))
                def _():
                    slot = self.place(c, k)
                    remote(
                        slot, slot, self.sent_right.at[c, k], self.came.at[c, k], on_line(0)
                    ).wait_send()

                @pl.when((me <= k) & (me > 0))
                def _():
                    slot = self.place(c, k)
                    remote(
                        slot, slot, self.sent_left.at[c, k], self.came.at[c, k], on_line(0)
                    ).wait_send()

            return carry

        lax.fori_loop(0, chunks, one, 0)


class Plane:
    def __init__(self, partners, bits, span, inboxes, sent, came, free, gather_span=None):
        self.partners, self.bits, self.span = partners, bits, span
        self.inboxes, self.sent, self.came, self.free = inboxes, sent, came, free
        self.gather_span = span if gather_span is None else gather_span

    def start_of(self, step):
        bits = self.bits
        return (0, 4 * bits[0], 4 * bits[0] + 2 * bits[1], 4 * bits[0] + 2 * bits[1] + bits[2])[step]

    def copy(self, step):
        if step < 3:
            size = 4 >> step
            src = self.span(self.start_of(step) + size * (1 - self.bits[step]), size)
            dst, partner = self.inboxes[step], self.partners[step]
        else:
            size = 1 << (step - 3)
            src = dst = self.gather_span(self.start_of(6 - step), size)
            partner = self.partners[5 - step]
        return remote(src, dst, self.sent.at[step], self.came.at[step], in_plane(partner))

    def send(self, step):
        if step >= 3:
            pl.semaphore_wait(self.free.at[5 - step], 1)
        self.copy(step).start()

    def add(self, step):
        self.copy(step).wait_send()
        pl.semaphore_signal(
            self.free.at[step], inc=1, device_id=in_plane(self.partners[step]), device_id_type=MESH
        )
        self.copy(step).wait_recv()
        kept = self.span(self.start_of(step + 1), 4 >> step)
        kept[...] = (kept[...].astype(F32) + self.inboxes[step][...].astype(F32)).astype(BF16)

    def next(self, step):
        if 0 < step <= 3:
            self.add(step - 1)
        elif step > 3:
            self.copy(step - 1).wait_recv()
        if step < 6:
            self.send(step)

    def drain(self):
        for step in range(3, 6):
            self.copy(step).wait_send()


def turn(tensor, cosine, sine, sign):
    pieces = []
    front = lax.broadcasted_iota(jnp.int32, (1, 128), 1) % HD < HD // 2
    for at in range(0, tensor.shape[-1], 128):
        piece = tensor[:, at : at + 128]
        mixed = jnp.where(front, -pltpu.roll(piece, 96, 1), pltpu.roll(piece, 32, 1)) * sine
        pieces.append(piece * cosine + sign * mixed)
    return jnp.concatenate(pieces, axis=1)


def layer_kernel(names, sizes, *ref_list):
    r = SimpleNamespace(**dict(zip(names, ref_list)))
    count, groups, tokens, width, cols, units = sizes
    chunks = tokens // CHUNK
    share = CHUNK // count
    heads = cols // HD
    score_scale = HD ** (-0.5)
    me = lax.axis_index("mp")
    row = lax.axis_index("dp")

    core = row % 2
    along_x = (row // 2) % 2
    along_y = row // 4
    other_core = row + 1 - 2 * core
    other_x = row + 2 - 4 * along_x
    other_y = row + 4 - 8 * along_y

    loads = {}

    def load(index, src, dst):
        copy = pltpu.make_async_copy(src, dst, r.load_sem.at[index])
        copy.start()
        loads[index] = copy

    def loaded(*indices):
        for index in indices:
            loads.pop(index).wait()

    load(0, r.layer_one, r.first_in)
    load(1, r.w_value_one, r.wv1)
    load(2, r.block_input, r.x)
    load(3, r.w_query, r.wq)
    load(4, r.w_key, r.wk)
    load(5, r.w_value, r.wv)
    load(6, r.w_out, r.wo.at[me])
    load(7, r.grad_output, r.g)
    load(8, r.w_gate, r.wg)
    load(9, r.w_up, r.wu)
    load(10, r.w_down, r.wd)

    barrier = pltpu.get_barrier_semaphore()
    for step in range(1, count):
        pl.semaphore_signal(
            barrier, inc=1, device_id=on_line((me + step) % count), device_id_type=MESH
        )
    for partner in (other_core, other_x, other_y):
        pl.semaphore_signal(barrier, inc=1, device_id=in_plane(partner), device_id_type=MESH)
    pl.semaphore_wait(barrier, count - 1 + 3)

    def slot_of(ref):
        return lambda c, k: ref.at[c, k]

    def f_slot(c, k):
        return r.f_in.at[pl.ds(pl.multiple_of((c * count + k) * CHUNK, CHUNK), CHUNK)]

    first = Scatter(
        me, count, r.f_part, f_slot, r.f_meet, r.f_sent, r.f_came, r.f_met
    )
    back2 = Scatter(
        me, count, r.b_part, slot_of(r.b_in), r.b_meet, r.b_sent, r.b_came, r.b_met
    )
    out = Scatter(
        me, count, r.o_part, slot_of(r.o_in), r.o_meet, r.o_sent, r.o_came, r.o_met
    )
    back1 = Scatter(
        me, count, r.b_part, slot_of(r.b_in), r.b_meet, r.d_sent, r.d_came, r.d_met
    )
    heads_all = Gather(
        me, count, lambda c, k: r.att.at[c, k], r.att_came, r.att_right, r.att_left
    )
    values_all = Gather(
        me, count, lambda c, k: r.dv_all.at[c, k], r.dv_came, r.dv_right, r.dv_left
    )

    def rows_of(ref):
        return lambda c, k: ref.at[pl.ds(c * CHUNK + k * share, share)]

    outs_all = Gather(
        me, count, rows_of(r.output), r.out_came, r.out_right, r.out_left
    )
    gin_all = Gather(
        me, count, rows_of(r.grad_input), r.gin_came, r.gin_right, r.gin_left
    )

    def at(c):
        return pl.ds(c * CHUNK, CHUNK)

    def mine(c):
        return pl.ds(pl.multiple_of(c * CHUNK + me * share, share), share)

    piece = cols // groups
    block = core * 4 + along_x * 2 + along_y

    def wo_rows(slot, step):
        span = 1 << step
        start = pl.multiple_of((block // span) * span * piece, piece)
        return r.wo.at[slot, pl.ds(start, span * piece)]

    def wo_line():
        loaded(6)
        for step in range(1, count):
            remote(
                wo_rows(me, 0),
                wo_rows(me, 0),
                r.wo_sent.at[step],
                r.wo_came.at[step],
                on_line((me + step) % count),
            ).start()

    def wo_line_wait():
        for step in range(1, count):
            slot = wo_rows((me + count - step) % count, 0)
            copy = remote(
                slot, slot, r.wo_sent.at[step], r.wo_came.at[step], on_line(0)
            )
            copy.wait_send()
            copy.wait_recv()

    def wo_plane(step, start):
        partner = (other_y, other_x, other_core)[step]
        span = 1 << step
        for other in range(1, count):
            slot = (me + other) % count
            index = count * (step + 1) + other
            copy = remote(
                wo_rows(slot, step),
                wo_rows(slot, step),
                r.wo_sent.at[index],
                r.wo_came.at[index],
                in_plane(partner),
            )
            if start:
                copy.start()
            else:
                copy.wait_send()
                copy.wait_recv()

    def first_part(c):
        part = mul(r.first_in[at(c)], r.wv1[...])
        for k in range(count):
            r.f_part[c, k] = part[:, k * cols : (k + 1) * cols].astype(BF16)
        first.open(c)

    def project(c):
        x = r.x[at(c)].astype(F32)
        scale = lax.rsqrt(jnp.mean(x * x, axis=-1, keepdims=True) + EPSILON)
        normed = (x * scale * r.norm_one[...]).astype(BF16)
        r.a1[at(c)] = normed
        tables = [table[at(c)] for table in (r.cosine, r.sine)]
        queries = turn(mul(normed, r.wq[...]), *tables, 1.0)
        r.q[at(c)] = (queries.astype(BF16).astype(F32) * score_scale).astype(BF16)
        r.k[at(c)] = turn(mul(normed, r.wk[...]), *tables, 1.0).astype(BF16)
        r.own[...] = mul(normed, r.wv[...])

    def window(c):
        low = max(0, c * CHUNK - REACH)
        return low, (c + 1) * CHUNK - low

    def mask_bias(c):
        low, span = window(c)
        row_index = c * CHUNK + lax.broadcasted_iota(jnp.int32, (CHUNK, span), 0)
        col_index = low + lax.broadcasted_iota(jnp.int32, (CHUNK, span), 1)
        here = r.seg_row[:, c * CHUNK : (c + 1) * CHUNK]
        diagonal = lax.broadcasted_iota(jnp.int32, (CHUNK, CHUNK), 0) == (
            lax.broadcasted_iota(jnp.int32, (CHUNK, CHUNK), 1)
        )
        column = jnp.sum(jnp.where(diagonal, here, 0), axis=1, keepdims=True)
        same = column == r.seg_row[:, low : low + span]
        r.bias[:, :span] = jnp.where(same & (col_index <= row_index), 0.0, -1e30)

    def head_lanes(head):
        return (lax.broadcasted_iota(jnp.int32, (1, cols), 1) // HD) == head

    def only(tensor, lanes):
        return jnp.where(lanes, tensor, jnp.zeros_like(tensor))

    def attend(c):
        first.total(c, r.sum_a)
        r.vm[at(c)] = (0.5 * r.own[...] + 0.5 * r.sum_a[...]).astype(BF16)
        low, span = window(c)
        mask_bias(c)
        r.sum_a[...] = jnp.zeros_like(r.sum_a)

        def one(head, carry):
            lanes = head_lanes(head)
            scores = mul(only(r.q[at(c)], lanes), r.k[low : low + span], NT)
            scores = scores + r.bias[:, :span]
            largest = jnp.max(scores, axis=-1, keepdims=True)
            raised = jnp.exp(scores - largest)
            summed = jnp.sum(raised, axis=-1, keepdims=True)
            weights = (raised * (1.0 / summed)).astype(BF16)
            r.sum_a[...] += mul(weights, only(r.vm[low : low + span], lanes))
            here = lax.broadcasted_iota(jnp.int32, (1, 128), 1) == head
            r.lse[at(c)] = jnp.where(here, largest + jnp.log(summed), r.lse[at(c)])
            return carry

        lax.fori_loop(0, heads, one, 0)
        r.att[c, me] = r.sum_a[...].astype(BF16)
        heads_all.own(c, r.att.at[c, me])

    def feed(c):
        heads_all.relay(c)
        h = r.x[at(c)].astype(F32)
        for k in range(count):
            h = h + mul(r.att[c, k], r.wo[k])
        r.big[...] = h
        r.h_own[c] = r.big[pl.ds(pl.multiple_of(me * share, share), share)]
        scale = lax.rsqrt(jnp.mean(h * h, axis=-1, keepdims=True) + EPSILON)
        normed = (h * scale * r.norm_two[...]).astype(BF16)
        r.a2[at(c)] = normed
        gate = mul(normed, r.wg[...], NT)
        up = mul(normed, r.wu[...], NT)
        sig = jax.nn.sigmoid(gate)
        silu = gate * sig
        hidden = (silu * up).astype(BF16)
        r.hid[at(c)] = hidden
        grad_hidden = mul(r.g[at(c)], r.wd[...], NT)
        grad_gate = (grad_hidden * up * sig * (1.0 + gate * (1.0 - sig))).astype(BF16)
        grad_up = (grad_hidden * silu).astype(BF16)
        r.dga[at(c)] = grad_gate
        r.dup[at(c)] = grad_up
        back = mul(grad_gate, r.wg[...]) + mul(grad_up, r.wu[...])
        r.b_part[c] = back.astype(BF16).reshape(count, share, width)
        back2.open(c)
        r.o_part[c] = mul(hidden, r.wd[...]).astype(BF16).reshape(count, share, width)

    def norm_back(values, gain, grad):
        scale = lax.rsqrt(jnp.mean(values * values, axis=-1, keepdims=True) + EPSILON)
        grad_gain = jnp.sum(grad * values * scale, axis=0, keepdims=True)
        scaled = grad * gain
        inner = jnp.mean(scaled * values, axis=-1, keepdims=True)
        return grad_gain, scale * scaled - values * scale * scale * scale * inner

    def through_two(c):
        back2.total(c, r.sum_b)
        grad_gain, grad = norm_back(r.h_own[c], r.norm_two[...], r.sum_b[...])
        r.gains[1:2] += grad_gain
        grad = r.g[mine(c)].astype(F32) + grad
        r.dh_own[c] = grad
        low = grad.astype(BF16)
        r.db_own[c] = low
        for k in range(count):
            part = mul(low, r.wo[k], NT).astype(BF16)

            @pl.when(me == k)
            def _():
                r.do[mine(c)] = part

            @pl.when(me != k)
            def _():
                r.do_part[c, k] = part
                remote(
                    r.do_part.at[c, k],
                    r.do.at[mine(c)],
                    r.do_sent.at[c, k],
                    r.do_came.at[c, (me - k + count) % count],
                    on_line(k),
                ).start()

    def do_wait(c):
        for step in range(1, count):
            source = (me + step) % count
            slot = r.do.at[
                pl.ds(pl.multiple_of(c * CHUNK + source * share, share), share)
            ]
            remote(
                slot, slot, r.do_sent.at[c, 0], r.do_came.at[c, step], on_line(0)
            ).wait_recv()

    def attend_back(c):
        do_wait(c)
        low, span = window(c)
        mask_bias(c)
        r.sum_a[...] = jnp.zeros_like(r.sum_a)

        def one(head, carry):
            lanes = head_lanes(head)
            q_head = only(r.q[at(c)], lanes)
            do_head = only(r.do[at(c)], lanes)
            here = lax.broadcasted_iota(jnp.int32, (1, 128), 1) == head
            lse = jnp.sum(jnp.where(here, r.lse[at(c)], 0.0), axis=-1, keepdims=True)
            scores = mul(q_head, r.k[low : low + span], NT) + r.bias[:, :span]
            probs = jnp.exp(scores - lse)
            grad_probs = mul(do_head, r.vm[low : low + span], NT)
            inner = jnp.sum(probs * grad_probs, axis=-1, keepdims=True)
            grad_scores = (probs * (grad_probs - inner)).astype(BF16)
            r.sum_a[...] += mul(grad_scores, only(r.k[low : low + span], lanes))
            r.dk_sum[low : low + span] += mul(grad_scores, q_head, TN)
            r.dv_sum[low : low + span] += mul(probs.astype(BF16), do_head, TN)
            return carry

        lax.fori_loop(0, heads, one, 0)
        tables = [table[at(c)] for table in (r.cosine, r.sine)]
        r.dqkv[at(c), :cols] = turn(r.sum_a[...] * score_scale, *tables, -1.0).astype(BF16)

    def keys_back(c):
        tables = [table[at(c)] for table in (r.cosine, r.sine)]
        r.dqkv[at(c), cols : 2 * cols] = turn(r.dk_sum[at(c)], *tables, -1.0).astype(BF16)
        grad_values = (0.5 * r.dv_sum[at(c)]).astype(BF16)
        r.dv_all[c, me] = grad_values
        r.dqkv[at(c), 2 * cols :] = grad_values
        values_all.own(c, r.dv_all.at[c, me])
        back = mul(r.dqkv[at(c), :cols], r.wq[...], NT)
        back = back + mul(r.dqkv[at(c), cols : 2 * cols], r.wk[...], NT)
        back = back + mul(grad_values, r.wv[...], NT)
        back2.drain_one(c)
        r.b_part[c] = back.astype(BF16).reshape(count, share, width)
        back1.open(c)

    stores = []

    def local(src, dst):
        copy = pltpu.make_async_copy(src, dst, r.store_sem.at[len(stores)])
        copy.start()
        return copy

    def through_one(c):
        back1.total(c, r.sum_b)
        x = r.x[mine(c)].astype(F32)
        grad_gain, grad = norm_back(x, r.norm_one[...], r.sum_b[...])
        r.gains[0:1] += grad_gain
        r.b_part[c, me] = (r.dh_own[c] + grad).astype(BF16)
        gin_all.own(c, r.b_part.at[c, me])
        stores.append(local(r.b_part.at[c, me], r.grad_input.at[mine(c)]))

    def finish_out(c):
        out.total(c, r.sum_b)
        r.o_part[c, me] = (r.h_own[c] + r.sum_b[...]).astype(BF16)
        outs_all.own(c, r.o_part.at[c, me])
        stores.append(local(r.o_part.at[c, me], r.output.at[mine(c)]))

    x_first = ((other_core, other_x, other_y), (core, along_x, along_y))
    y_first = ((other_core, other_y, other_x), (core, along_y, along_x))

    def by_cols(ref, size):
        return lambda start, n: ref.at[:, pl.ds(pl.multiple_of(start * size, size), n * size)]

    def by_rows(ref, size):
        return lambda start, n: ref.at[pl.ds(pl.multiple_of(start * size, size), n * size)]

    eighth = width // 8
    part = cols // 8
    plane_gate = Plane(
        *x_first,
        by_cols(r.wg, eighth),
        [r.u_in0.at[0], r.u_in1.at[0], r.u_in2.at[0]],
        r.p_sent.at[0],
        r.p_came.at[0],
        r.p_free.at[0],
    )
    plane_up = Plane(
        *y_first,
        by_cols(r.wu, eighth),
        [r.u_in0.at[1], r.u_in1.at[1], r.u_in2.at[1]],
        r.p_sent.at[1],
        r.p_came.at[1],
        r.p_free.at[1],
    )
    plane_down = Plane(
        *x_first,
        by_cols(r.wd, eighth),
        [r.u_in0.at[2], r.u_in1.at[2], r.u_in2.at[2]],
        r.p_sent.at[2],
        r.p_came.at[2],
        r.p_free.at[2],
    )
    plane_out = Plane(
        *y_first,
        by_rows(r.a2, eighth),
        [
            r.g.at[pl.ds(0, 4 * eighth)],
            r.g.at[pl.ds(4 * eighth, 2 * eighth)],
            r.g.at[pl.ds(6 * eighth, eighth)],
        ],
        r.p_sent.at[3],
        r.p_came.at[3],
        r.p_free.at[3],
        by_rows(r.wo.at[me], part),
    )
    plane_qkv = [
        Plane(
            *(x_first if index == 1 else y_first),
            by_rows(ref, eighth),
            [
                r.f_in.at[pl.ds((7 * index) * eighth, 4 * eighth)],
                r.f_in.at[pl.ds((7 * index + 4) * eighth, 2 * eighth)],
                r.f_in.at[pl.ds((7 * index + 6) * eighth, eighth)],
            ],
            r.p_sent.at[4 + index],
            r.p_came.at[4 + index],
            r.p_free.at[4 + index],
        )
        for index, ref in enumerate((r.wq, r.wk, r.wv))
    ]
    plane_one = Plane(
        *x_first,
        by_cols(r.wv1, eighth),
        [r.v_in0, r.v_in1, r.v_in2],
        r.p_sent.at[7],
        r.p_came.at[7],
        r.p_free.at[7],
    )

    def units_grad(left, right, into):
        for start in range(0, units, 256):
            span = min(256, units - start)
            into[start : start + span] = mul(left[:, start : start + span], right[...], TN).astype(
                BF16
            )

    def out_grad():
        low = r.db_own[...].reshape(tokens // count, width)
        for k in range(count):
            own = jnp.concatenate(
                [
                    r.att[c, k, pl.ds(pl.multiple_of(me * share, share), share)]
                    for c in range(chunks)
                ],
                axis=0,
            )
            grad = mul(own, low, TN).astype(BF16)
            for s in range(8):
                r.a2[s * eighth + k * part : s * eighth + (k + 1) * part] = grad[
                    s * part : (s + 1) * part
                ]

    def out_line(start):
        slot = plane_out.start_of(3)
        for step in range(1, count):
            peer = (me + step) % count
            rows = pl.ds(pl.multiple_of(slot * eighth + peer * part, part), part)
            copy = remote(
                r.a2.at[rows],
                r.z_in.at[step],
                r.z_sent.at[step],
                r.z_came.at[step],
                on_line(peer),
            )
            if start:
                copy.start()
            else:
                copy.wait_send()
                copy.wait_recv()

    def out_line_sum():
        out_line(False)
        slot = plane_out.start_of(3)
        rows = pl.ds(pl.multiple_of(slot * eighth + me * part, part), part)
        grad = r.a2[rows].astype(F32)
        for step in range(1, count):
            grad = grad + r.z_in[step].astype(F32)
        r.wo[me, pl.ds(pl.multiple_of(slot * part, part), part)] = grad.astype(BF16)

    def values_one(c):
        grad = None
        for k in range(count):
            values = r.dv_all[c, k]
            piece = mul(values, r.wv1[:, k * cols : (k + 1) * cols], NT)
            grad = piece if grad is None else grad + piece
            piece = mul(r.first_in[at(c)], values, TN)
            if c > 0:
                piece = piece + r.big[:, k * cols : (k + 1) * cols]
            r.big[:, k * cols : (k + 1) * cols] = piece
        r.dk_sum[at(c)] = grad
        stores.append(local(r.dk_sum.at[at(c)], r.grad_first.at[at(c)]))

    def qkv_grad():
        for start in range(0, width, 256):
            grad = mul(r.a1[:, start : start + 256], r.dqkv[...], TN).astype(BF16)
            for index, into in enumerate((r.wq, r.wk, r.wv)):
                into[start : start + 256] = grad[:, index * cols : (index + 1) * cols]

    def gain_copy(step):
        if step < count:
            src, device = r.gains, on_line((me + step) % count)
        else:
            src = r.gain_sum.at[step - count]
            device = in_plane((other_core, other_x, other_y)[step - count])
        return remote(src, r.gain_in.at[step], r.gain_sent.at[step], r.gain_came.at[step], device)

    def gain_line():
        for step in range(1, count):
            gain_copy(step).start()

    def gain_plane(index):
        if index == 0:
            total = r.gains[...]
            for step in range(1, count):
                gain_copy(step).wait_recv()
                total = total + r.gain_in[step]
        else:
            gain_copy(count + index - 1).wait_recv()
            total = r.gain_sum[index - 1] + r.gain_in[count + index - 1]
        if index < 3:
            r.gain_sum[index] = total
            gain_copy(count + index).start()
        else:
            r.gain_out[...] = total

    r.gains[...] = jnp.zeros_like(r.gains)
    r.dk_sum[...] = jnp.zeros_like(r.dk_sum)
    r.dv_sum[...] = jnp.zeros_like(r.dv_sum)
    r.lse[...] = jnp.zeros_like(r.lse)
    loaded(0, 1)
    first_part(0)
    first_part(1)
    wo_line()
    first_part(2)
    first_part(3)
    loaded(2, 3, 4, 5)
    project(0)
    first.relay(0)
    wo_line_wait()
    wo_plane(0, True)
    attend(0)
    wo_plane(0, False)
    wo_plane(1, True)
    project(1)
    first.relay(1)
    attend(1)
    wo_plane(1, False)
    wo_plane(2, True)
    project(2)
    first.relay(2)
    wo_plane(2, False)
    loaded(7, 8, 9, 10)
    feed(0)
    attend(2)
    project(3)
    first.relay(3)
    back2.relay(0)
    feed(1)
    attend(3)
    through_two(0)
    back2.relay(1)
    feed(2)
    through_two(1)
    back2.relay(2)
    feed(3)
    units_grad(r.dga, r.a2, r.wg)
    plane_gate.next(0)
    through_two(2)
    back2.relay(3)
    out.open(0)
    units_grad(r.dup, r.a2, r.wu)
    plane_up.next(0)
    attend_back(0)
    through_two(3)
    plane_gate.next(1)
    plane_up.next(1)
    out.relay(0)
    out.open(1)
    attend_back(1)
    out.relay(1)
    finish_out(0)
    plane_gate.next(2)
    plane_up.next(2)
    units_grad(r.hid, r.g, r.wd)
    plane_down.next(0)
    attend_back(2)
    keys_back(0)
    plane_gate.next(3)
    plane_up.next(3)
    plane_down.next(1)
    outs_all.relay(0)
    attend_back(3)
    keys_back(1)
    back1.relay(0)
    keys_back(2)
    values_all.relay(0)
    keys_back(3)
    plane_gate.next(4)
    plane_up.next(4)
    plane_down.next(2)
    qkv_grad()
    plane_qkv[0].next(0)
    plane_qkv[1].next(0)
    plane_qkv[2].next(0)
    through_one(0)
    back1.relay(1)
    values_all.relay(1)
    out_grad()
    plane_out.next(0)
    gin_all.relay(0)
    plane_gate.next(5)
    plane_up.next(5)
    plane_down.next(3)
    values_one(0)
    through_one(1)
    back1.relay(2)
    values_all.relay(2)
    plane_gate.next(6)
    plane_up.next(6)
    plane_down.next(4)
    plane_out.next(1)
    for plane in plane_qkv:
        plane.next(1)
    values_one(1)
    gin_all.relay(1)
    through_one(2)
    back1.relay(3)
    values_all.relay(3)
    plane_down.next(5)
    plane_out.next(2)
    for plane in plane_qkv:
        plane.next(2)
    values_one(2)
    gin_all.relay(2)
    through_one(3)
    gain_line()
    values_one(3)
    r.wv1[...] = r.big[...].astype(BF16)
    plane_one.next(0)
    plane_out.add(2)
    out_line(True)
    plane_down.next(6)
    finish_out(1)
    for plane in plane_qkv:
        plane.next(3)
    out.open(2)
    out.open(3)
    gain_plane(0)
    plane_one.next(1)
    out_line_sum()
    plane_out.send(3)
    out.relay(2)
    gin_all.relay(3)
    for plane in plane_qkv:
        plane.next(4)
    gain_plane(1)
    plane_one.next(2)
    plane_out.next(4)
    outs_all.relay(1)
    out.relay(3)
    for plane in plane_qkv:
        plane.next(5)
    gain_plane(2)
    plane_one.next(3)
    plane_out.next(5)
    finish_out(2)
    for plane in plane_qkv:
        plane.next(6)
    gain_plane(3)
    plane_one.next(4)
    plane_out.next(6)
    finish_out(3)
    plane_one.next(5)
    outs_all.relay(2)
    plane_one.next(6)
    outs_all.relay(3)
    for src, dst in (
        (r.wg, r.grad_gate),
        (r.wu, r.grad_up),
        (r.wd, r.grad_down),
        (r.wo.at[me], r.grad_out),
        (r.wq, r.grad_query),
        (r.wk, r.grad_key),
        (r.wv, r.grad_value),
        (r.wv1, r.grad_one),
    ):
        stores.append(local(src, dst))
    for copy in stores:
        copy.wait()
    for line in (first, back1, out, heads_all, values_all, outs_all, gin_all):
        line.drain(chunks)
    for plane in (plane_gate, plane_up, plane_down, plane_out, plane_one, *plane_qkv):
        plane.drain()
    for step in range(1, count + 3):
        gain_copy(step).wait_send()

    def do_drain(c, carry):
        for k in range(count):

            @pl.when(me != k)
            def _():
                slot = r.do_part.at[c, k]
                remote(
                    slot, slot, r.do_sent.at[c, k], r.do_came.at[c, 0], on_line(0)
                ).wait_send()

        return carry

    lax.fori_loop(0, chunks, do_drain, 0)


def fused_layer(arrays, sizes):
    count, groups, tokens, width, cols, units = sizes
    chunks = tokens // CHUNK
    share = CHUNK // count
    eighth = width // 8
    hbm = pl.BlockSpec(memory_space=pl.ANY)
    vmem = pl.BlockSpec(memory_space=pltpu.VMEM)
    ins = dict(
        block_input=hbm,
        layer_one=hbm,
        grad_output=hbm,
        norm_one=vmem,
        w_query=hbm,
        w_key=hbm,
        w_value=hbm,
        w_out=hbm,
        norm_two=vmem,
        w_gate=hbm,
        w_up=hbm,
        w_down=hbm,
        w_value_one=hbm,
        cosine=vmem,
        sine=vmem,
        seg_row=vmem,
    )
    outs = dict(
        output=((tokens, width), BF16, hbm),
        grad_input=((tokens, width), BF16, hbm),
        grad_first=((tokens, cols), F32, hbm),
        grad_query=((width, cols), BF16, hbm),
        grad_key=((width, cols), BF16, hbm),
        grad_value=((width, cols), BF16, hbm),
        grad_out=((cols, width), BF16, hbm),
        grad_gate=((units, width), BF16, hbm),
        grad_up=((units, width), BF16, hbm),
        grad_down=((units, width), BF16, hbm),
        grad_one=((cols, width), BF16, hbm),
        gain_out=((8, width), F32, vmem),
    )
    dma = pltpu.SemaphoreType.DMA

    def low(*shape):
        return pltpu.VMEM(shape, BF16)

    def full(*shape):
        return pltpu.VMEM(shape, F32)

    slots = (chunks, count)
    scratch = dict(
        x=low(tokens, width),
        g=low(tokens, width),
        first_in=low(tokens, cols),
        wq=low(width, cols),
        wk=low(width, cols),
        wv=low(width, cols),
        wv1=low(cols, width),
        wo=low(count, cols, width),
        wg=low(units, width),
        wu=low(units, width),
        wd=low(units, width),
        a1=low(tokens, width),
        a2=low(tokens, width),
        q=low(tokens, cols),
        k=low(tokens, cols),
        vm=low(tokens, cols),
        own=full(CHUNK, cols),
        lse=full(tokens, 128),
        bias=full(CHUNK, CHUNK + REACH),
        sum_a=full(CHUNK, cols),
        sum_b=full(share, width),
        big=full(CHUNK, width),
        att=low(*slots, CHUNK, cols),
        dv_all=low(*slots, CHUNK, cols),
        hid=low(tokens, units),
        dga=low(tokens, units),
        dup=low(tokens, units),
        h_own=full(chunks, share, width),
        dh_own=full(chunks, share, width),
        db_own=low(chunks, share, width),
        do_part=low(*slots, share, cols),
        do=low(tokens, cols),
        dqkv=low(tokens, 3 * cols),
        dk_sum=full(tokens, cols),
        dv_sum=full(tokens, cols),
        gains=full(8, width),
        gain_sum=full(3, 8, width),
        gain_in=full(count + 3, 8, width),
        u_in0=low(3, units, 4 * eighth),
        u_in1=low(3, units, 2 * eighth),
        u_in2=low(3, units, eighth),
        z_in=low(count, cols // 8, width),
        v_in0=low(cols, 4 * eighth),
        v_in1=low(cols, 2 * eighth),
        v_in2=low(cols, eighth),
        f_part=low(*slots, CHUNK, cols),
        f_in=low(chunks * count * CHUNK, cols),
        f_meet=low(chunks, CHUNK, cols),
        b_part=low(*slots, share, width),
        b_in=low(*slots, share, width),
        b_meet=low(chunks, share, width),
        o_part=low(*slots, share, width),
        o_in=low(*slots, share, width),
        o_meet=low(chunks, share, width),
        load_sem=dma((11,)),
        store_sem=dma((3 * chunks + 8,)),
        wo_sent=dma((4 * count,)),
        wo_came=dma((4 * count,)),
        do_sent=dma(slots),
        do_came=dma(slots),
        p_sent=dma((8, 6)),
        p_came=dma((8, 6)),
        p_free=pltpu.SemaphoreType.REGULAR((8, 3)),
        z_sent=dma((count,)),
        z_came=dma((count,)),
        gain_sent=dma((count + 3,)),
        gain_came=dma((count + 3,)),
        f_sent=dma(slots),
        f_came=dma(slots),
        f_met=dma((chunks,)),
        b_sent=dma(slots),
        b_came=dma(slots),
        b_met=dma((chunks,)),
        o_sent=dma(slots),
        o_came=dma(slots),
        o_met=dma((chunks,)),
        d_sent=dma(slots),
        d_came=dma(slots),
        d_met=dma((chunks,)),
        att_came=dma(slots),
        att_right=dma(slots),
        att_left=dma(slots),
        dv_came=dma(slots),
        dv_right=dma(slots),
        dv_left=dma(slots),
        out_came=dma(slots),
        out_right=dma(slots),
        out_left=dma(slots),
        gin_came=dma(slots),
        gin_right=dma(slots),
        gin_left=dma(slots),
    )
    results = pl.pallas_call(
        functools.partial(layer_kernel, [*ins, *outs, *scratch], sizes),
        out_shape=[jax.ShapeDtypeStruct(item[0], item[1]) for item in outs.values()],
        in_specs=list(ins.values()),
        out_specs=[item[2] for item in outs.values()],
        scratch_shapes=list(scratch.values()),
        compiler_params=pltpu.CompilerParams(
            collective_id=0, has_side_effects=True, vmem_limit_bytes=VMEM_LIMIT
        ),
        cost_estimate=pl.CostEstimate(
            flops=2 * 13 * 10**9, bytes_accessed=40 * 2**20, transcendentals=0
        ),
    )(*arrays)
    return SimpleNamespace(**dict(zip(outs, results)))


def on_device(*arguments):
    (
        block_input,
        layer_one_input,
        segment_ids,
        grad_output,
        norm_one,
        w_query,
        w_key,
        w_value,
        w_out,
        norm_two,
        w_gate,
        w_up,
        w_down,
        w_value_one,
    ) = arguments
    count = lax.axis_size("mp")
    groups = lax.axis_size("dp")
    tokens, width = block_input.shape
    cols = w_query.shape[1]
    units = w_gate.shape[1]
    fits = (
        count == 4
        and groups == 8
        and tokens == 4 * CHUNK
        and cols == 256
        and width == count * cols
        and units % 64 == 0
        and units <= 704
        and segment_ids.shape[0] == 1
    )
    if not fits:
        return by_collectives(*arguments)
    cosine, sine_part = rope_tables(positions_of(segment_ids)[0], HD)
    cosine = cosine[:, 0]
    sine_part = sine_part[:, 0]
    r = fused_layer(
        (
            block_input,
            layer_one_input,
            grad_output,
            norm_one[None, :],
            w_query,
            w_key,
            w_value,
            w_out,
            norm_two[None, :],
            w_gate.T,
            w_up.T,
            w_down,
            w_value_one,
            jnp.concatenate([cosine] * 4, axis=1),
            jnp.concatenate([sine_part] * 4, axis=1),
            segment_ids.astype(F32),
        ),
        (count, groups, tokens, width, cols, units),
    )
    return (
        r.output,
        r.grad_input.astype(F32),
        r.grad_first,
        r.gain_out[0],
        r.grad_query.astype(F32),
        r.grad_key.astype(F32),
        r.grad_value.astype(F32),
        r.grad_out.astype(F32),
        r.gain_out[1],
        r.grad_gate.astype(F32).T,
        r.grad_up.astype(F32).T,
        r.grad_down.astype(F32),
        r.grad_one.astype(F32),
    )


def solution(mesh):
    return jax.shard_map(
        on_device,
        mesh=mesh,
        in_specs=(
            P("dp", None),
            P("dp", "mp"),
            P("dp", None),
            P("dp", None),
            P(),
            P(None, "mp"),
            P(None, "mp"),
            P(None, "mp"),
            P("mp", None),
            P(),
            P(None, "mp"),
            P(None, "mp"),
            P("mp", None),
            P("mp", None),
        ),
        out_specs=(
            P("dp", None),
            P("dp", None),
            P("dp", "mp"),
            P(),
            P(None, "mp"),
            P(None, "mp"),
            P(None, "mp"),
            P("mp", None),
            P(),
            P(None, "mp"),
            P(None, "mp"),
            P("mp", None),
            P("mp", None),
        ),
        check_vma=False,
    )
```

```python
import functools
import math
from types import SimpleNamespace

import jax
import jax.numpy as jnp
from jax import lax
from jax.experimental import pallas as pl
from jax.experimental.pallas import tpu as pltpu
from jax.sharding import PartitionSpec as P

HD = 64


EPSILON = 1e-06
VMEM_LIMIT = 64 * 2**20 - 2**16


def positions_of(segments):
    position = lax.broadcasted_iota(jnp.int32, segments.shape, 1)
    changed = (segments[:, 1:] != segments[:, :-1]).astype(jnp.int32)
    starts = jnp.concatenate([jnp.ones_like(segments[:, :1]), changed], axis=1)
    return position - lax.cummax(position * starts, axis=1)


def rope_tables(positions, width):
    half_width = width // 2
    rates = jnp.exp(jnp.arange(half_width, dtype=jnp.float32) * (-math.log(10000.0) / half_width))
    angles = positions.astype(jnp.float32)[:, None] * rates[None, :]
    return (jnp.cos(angles)[:, None, :], jnp.sin(angles)[:, None, :])


def rotate(tensor, cosine, sine_part, turn):
    half_width = tensor.shape[-1] // 2
    left_half = tensor[..., :half_width]
    right_half = tensor[..., half_width:]
    return jnp.concatenate(
        [
            left_half * cosine - turn * right_half * sine_part,
            right_half * cosine + turn * left_half * sine_part,
        ],
        axis=-1,
    )


def over_rows(left_side, right_side):
    return lax.dot_general(
        left_side, right_side, (((0,), (0,)), ((), ())), preferred_element_type=jnp.float32
    )


def against(left_side, right_side):
    return lax.dot_general(
        left_side, right_side, (((1,), (1,)), ((), ())), preferred_element_type=jnp.float32
    )


def norm_back(activations, scale_vec, gain_vec, grad_normed):
    grad_gain = jnp.sum(grad_normed * activations * scale_vec, axis=0)
    scaled = grad_normed * gain_vec
    inner = jnp.mean(scaled * activations, axis=-1, keepdims=True)
    return (grad_gain, scale_vec * scaled - activations * scale_vec * scale_vec * scale_vec * inner)


def masked_scores(q_block, key_rows, seg_block, seg_all, first_row, score_scale):
    block_rows = q_block.shape[0]
    scores = (
        jnp.einsum("qhd,khd->hqk", q_block, key_rows, preferred_element_type=jnp.float32)
        * score_scale
    )
    row_index = first_row + lax.broadcasted_iota(jnp.int32, (block_rows, key_rows.shape[0]), 0)
    col_index = lax.broadcasted_iota(jnp.int32, (block_rows, key_rows.shape[0]), 1)
    allowed = (seg_block[:, None] == seg_all[None, :]) & (col_index <= row_index)
    return jnp.where(allowed[None], scores, -1e30)


def attend_forward(queries, key_rows, values, seg_all, score_scale):
    row_count, head_count, width = queries.shape
    block_rows = min(512, row_count)

    def one_block(block_index):
        first_row = block_index * block_rows
        q_block = lax.dynamic_slice_in_dim(queries, first_row, block_rows, 0)
        seg_block = lax.dynamic_slice_in_dim(seg_all, first_row, block_rows, 0)
        scores = masked_scores(q_block, key_rows, seg_block, seg_all, first_row, score_scale)
        largest = jnp.max(scores, axis=-1, keepdims=True)
        raised = jnp.exp(scores - largest)
        summed = jnp.sum(raised, axis=-1, keepdims=True)
        weights = (raised / summed).astype(jnp.bfloat16)
        result = jnp.einsum("hqk,khd->qhd", weights, values, preferred_element_type=jnp.float32)
        return (result, (largest + jnp.log(summed))[..., 0])

    results, log_totals = lax.map(one_block, jnp.arange(row_count // block_rows, dtype=jnp.int32))
    return (results.reshape(row_count, head_count, width), log_totals)


def attend_backward(queries, key_rows, values, seg_all, log_totals, grad_attended, score_scale):
    row_count = queries.shape[0]
    block_rows = min(512, row_count)

    def one_block(carried, block_index):
        grad_keys, grad_values = carried
        first_row = block_index * block_rows
        q_block = lax.dynamic_slice_in_dim(queries, first_row, block_rows, 0)
        seg_block = lax.dynamic_slice_in_dim(seg_all, first_row, block_rows, 0)
        grad_block = lax.dynamic_slice_in_dim(grad_attended, first_row, block_rows, 0)
        scores = masked_scores(q_block, key_rows, seg_block, seg_all, first_row, score_scale)
        probs = jnp.exp(scores - log_totals[block_index][..., None])
        grad_probs = jnp.einsum(
            "qhd,khd->hqk", grad_block, values, preferred_element_type=jnp.float32
        )
        inner = jnp.sum(probs * grad_probs, axis=-1, keepdims=True)
        grad_scores = (probs * (grad_probs - inner)).astype(jnp.bfloat16)
        grad_query = (
            jnp.einsum("hqk,khd->qhd", grad_scores, key_rows, preferred_element_type=jnp.float32)
            * score_scale
        )
        grad_keys = (
            grad_keys
            + jnp.einsum("hqk,qhd->khd", grad_scores, q_block, preferred_element_type=jnp.float32)
            * score_scale
        )
        grad_values = grad_values + jnp.einsum(
            "hqk,qhd->khd",
            probs.astype(jnp.bfloat16),
            grad_block,
            preferred_element_type=jnp.float32,
        )
        return ((grad_keys, grad_values), grad_query)

    zero_rows = jnp.zeros(key_rows.shape, jnp.float32)
    (grad_keys, grad_values), grad_queries = lax.scan(
        one_block, (zero_rows, zero_rows), jnp.arange(row_count // block_rows, dtype=jnp.int32)
    )
    return (grad_queries.reshape(key_rows.shape), grad_keys, grad_values)


def by_collectives(
    block_input,
    layer_one_input,
    segment_ids,
    grad_output,
    norm_one,
    w_query,
    w_key,
    w_value,
    w_out,
    norm_two,
    w_gate,
    w_up,
    w_down,
    w_value_one,
):
    token_count = block_input.shape[0]
    head_count = w_query.shape[1] // HD
    score_scale = HD ** (-0.5)
    seg_all = segment_ids[0]
    cosine, sine_part = rope_tables(positions_of(segment_ids)[0], HD)
    share_rows = token_count // lax.axis_size("mp")
    share_start = lax.axis_index("mp") * share_rows
    inputs = block_input.astype(jnp.float32)
    scale_one = lax.rsqrt(jnp.mean(inputs * inputs, axis=-1, keepdims=True) + EPSILON)
    normed = (inputs * scale_one * norm_one).astype(jnp.bfloat16)
    queries = jnp.dot(normed, w_query, preferred_element_type=jnp.float32).reshape(
        token_count, head_count, HD
    )
    key_rows = jnp.dot(normed, w_key, preferred_element_type=jnp.float32).reshape(
        token_count, head_count, HD
    )
    own_values = jnp.dot(normed, w_value, preferred_element_type=jnp.float32)
    first_values = lax.psum_scatter(
        jnp.dot(layer_one_input, w_value_one, preferred_element_type=jnp.float32).astype(
            jnp.bfloat16
        ),
        "mp",
        scatter_dimension=1,
        tiled=True,
    ).astype(jnp.float32)
    mixed_values = (
        (0.5 * own_values + 0.5 * first_values)
        .astype(jnp.bfloat16)
        .reshape(token_count, head_count, HD)
    )
    turned_q = rotate(queries, cosine, sine_part, 1.0).astype(jnp.bfloat16)
    turned_k = rotate(key_rows, cosine, sine_part, 1.0).astype(jnp.bfloat16)
    attended, log_totals = attend_forward(turned_q, turned_k, mixed_values, seg_all, score_scale)
    attended = attended.reshape(token_count, head_count * HD).astype(jnp.bfloat16)
    branch_one = jnp.dot(attended, w_out, preferred_element_type=jnp.float32)
    inputs_here = lax.dynamic_slice_in_dim(inputs, share_start, share_rows, 0)
    scale_one_here = lax.dynamic_slice_in_dim(scale_one, share_start, share_rows, 0)
    grad_rows = lax.dynamic_slice_in_dim(grad_output, share_start, share_rows, 0).astype(
        jnp.float32
    )
    residual = inputs_here + lax.psum_scatter(
        branch_one.astype(jnp.bfloat16), "mp", scatter_dimension=0, tiled=True
    ).astype(jnp.float32)
    scale_two = lax.rsqrt(jnp.mean(residual * residual, axis=-1, keepdims=True) + EPSILON)
    normed_two = (residual * scale_two * norm_two).astype(jnp.bfloat16)
    normed_two = lax.all_gather(normed_two, "mp", axis=0, tiled=True)
    gate_pre = jnp.dot(normed_two, w_gate, preferred_element_type=jnp.float32)
    up_pre = jnp.dot(normed_two, w_up, preferred_element_type=jnp.float32)
    sigmoid_gate = jax.nn.sigmoid(gate_pre)
    silu_gate = gate_pre * sigmoid_gate
    hidden = (silu_gate * up_pre).astype(jnp.bfloat16)
    branch_two = jnp.dot(hidden, w_down, preferred_element_type=jnp.float32)
    output_share = (
        residual
        + lax.psum_scatter(
            branch_two.astype(jnp.bfloat16), "mp", scatter_dimension=0, tiled=True
        ).astype(jnp.float32)
    ).astype(jnp.bfloat16)
    output = lax.all_gather(output_share, "mp", axis=0, tiled=True)
    grad_down = over_rows(hidden, grad_output)
    grad_hidden = against(grad_output, w_down)
    grad_gate_pre = (
        grad_hidden * up_pre * sigmoid_gate * (1.0 + gate_pre * (1.0 - sigmoid_gate))
    ).astype(jnp.bfloat16)
    grad_up_pre = (grad_hidden * silu_gate).astype(jnp.bfloat16)
    grad_gate = over_rows(normed_two, grad_gate_pre)
    grad_up = over_rows(normed_two, grad_up_pre)
    back_two = against(grad_gate_pre, w_gate) + against(grad_up_pre, w_up)
    grad_normed_two = lax.psum_scatter(
        back_two.astype(jnp.bfloat16), "mp", scatter_dimension=0, tiled=True
    ).astype(jnp.float32)
    grad_norm_two, grad_through_two = norm_back(residual, scale_two, norm_two, grad_normed_two)
    grad_residual = grad_rows + grad_through_two
    residual_low = grad_residual.astype(jnp.bfloat16)
    residual_low = lax.all_gather(residual_low, "mp", axis=0, tiled=True)
    grad_out_proj = over_rows(attended, residual_low)
    grad_attended = (
        against(residual_low, w_out).astype(jnp.bfloat16).reshape(token_count, head_count, HD)
    )
    grad_turned_q, grad_turned_k, grad_mixed = attend_backward(
        turned_q, turned_k, mixed_values, seg_all, log_totals, grad_attended, score_scale
    )
    grad_value_part = (0.5 * grad_mixed).reshape(token_count, head_count * HD).astype(jnp.bfloat16)
    grad_first_full = lax.all_gather(grad_value_part, "mp", axis=1, tiled=True)
    grad_queries = (
        rotate(grad_turned_q, cosine, sine_part, -1.0)
        .reshape(token_count, head_count * HD)
        .astype(jnp.bfloat16)
    )
    grad_keys = (
        rotate(grad_turned_k, cosine, sine_part, -1.0)
        .reshape(token_count, head_count * HD)
        .astype(jnp.bfloat16)
    )
    grad_query = over_rows(normed, grad_queries)
    grad_key = over_rows(normed, grad_keys)
    grad_value = over_rows(normed, grad_value_part)
    back_one = (
        against(grad_queries, w_query)
        + against(grad_keys, w_key)
        + against(grad_value_part, w_value)
    )
    grad_normed = lax.psum_scatter(
        back_one.astype(jnp.bfloat16), "mp", scatter_dimension=0, tiled=True
    ).astype(jnp.float32)
    grad_norm_one, grad_through_one = norm_back(inputs_here, scale_one_here, norm_one, grad_normed)
    gain_rows = jnp.concatenate([grad_norm_one, grad_norm_two])[None, :]
    grad_input, gain_all = (
        lax.all_gather(
            (grad_residual + grad_through_one).astype(jnp.bfloat16), "mp", axis=0, tiled=True
        ).astype(jnp.float32),
        lax.all_gather(gain_rows, "mp", axis=0, tiled=True),
    )
    gain_total = jnp.sum(gain_all, axis=0)
    width = norm_one.shape[0]
    grad_norm_one = gain_total[:width]
    grad_norm_two = gain_total[width:]
    grad_value_one = over_rows(layer_one_input, grad_first_full)
    grad_layer_one_input = against(grad_first_full, w_value_one)
    grad_norm_one, grad_norm_two = lax.psum((grad_norm_one, grad_norm_two), "dp")
    summed = lax.psum(
        tuple(
            part.astype(jnp.bfloat16)
            for part in (
                grad_query,
                grad_key,
                grad_value,
                grad_out_proj,
                grad_value_one,
                grad_gate,
                grad_up,
                grad_down,
            )
        ),
        "dp",
    )
    (
        grad_query,
        grad_key,
        grad_value,
        grad_out_proj,
        grad_value_one,
        grad_gate,
        grad_up,
        grad_down,
    ) = tuple(part.astype(jnp.float32) for part in summed)
    return (
        output,
        grad_input,
        grad_layer_one_input,
        grad_norm_one,
        grad_query,
        grad_key,
        grad_value,
        grad_out_proj,
        grad_norm_two,
        grad_gate,
        grad_up,
        grad_down,
        grad_value_one,
    )


NN = (((1,), (0,)), ((), ()))
NT = (((1,), (1,)), ((), ()))
TN = (((0,), (0,)), ((), ()))
F32 = jnp.float32
BF16 = jnp.bfloat16
CHUNK = 256
REACH = 512
MESH = pl.DeviceIdType.MESH


def mul(left_side, right_side, dims=NN):
    return lax.dot_general(left_side, right_side, dims, preferred_element_type=F32)


def on_line(index):
    return {"mp": index}


def in_plane(index):
    return {"dp": index}


def remote(src, dst, send_sem, recv_sem, device):
    return pltpu.make_async_remote_copy(
        src_ref=src,
        dst_ref=dst,
        send_sem=send_sem,
        recv_sem=recv_sem,
        device_id=device,
        device_id_type=MESH,
    )


class Scatter:
    def __init__(self, me, count, parts, inbox, meet, sent, came, met):
        self.me, self.count = me, count
        self.parts, self.inbox, self.meet = parts, inbox, meet
        self.sent, self.came, self.met = sent, came, met

    def take(self, c, k):
        slot = self.inbox(c, k)
        remote(slot, slot, self.sent.at[c, k], self.came.at[c, k], on_line(0)).wait_recv()
        self.parts[c, k] = (self.parts[c, k].astype(F32) + self.inbox(c, k)[...].astype(F32)).astype(
            BF16
        )

    def right(self, c, k):
        me = self.me

        @pl.when(me < k)
        def _():
            @pl.when(me > 0)
            def _():
                self.take(c, k)

            remote(
                self.parts.at[c, k],
                self.inbox(c, k),
                self.sent.at[c, k],
                self.came.at[c, k],
                on_line(me + 1),
            ).start()

    def left(self, c, k):
        me = self.me

        @pl.when(me > k)
        def _():
            @pl.when(me < self.count - 1)
            def _():
                self.take(c, k)

            @pl.when(me == k + 1)
            def _():
                remote(
                    self.parts.at[c, k],
                    self.meet.at[c],
                    self.sent.at[c, k],
                    self.met.at[c],
                    on_line(me - 1),
                ).start()

            @pl.when(me > k + 1)
            def _():
                remote(
                    self.parts.at[c, k],
                    self.inbox(c, k),
                    self.sent.at[c, k],
                    self.came.at[c, k],
                    on_line(me - 1),
                ).start()

    def rights(self, c):
        for k in range(self.count - 1, 0, -1):
            self.right(c, k)

    def lefts(self, c):
        for k in range(self.count - 1):
            self.left(c, k)

    def open(self, c):
        @pl.when(self.me == 0)
        def _():
            self.rights(c)

        @pl.when(self.me == self.count - 1)
        def _():
            self.lefts(c)

    def near(self, c, step):
        me, half = self.me, self.count // 2

        @pl.when((me > 0) & (me < half))
        def _():
            self.right(c, self.count - 1 - step)

        @pl.when((me < self.count - 1) & (me >= half))
        def _():
            self.left(c, step)

    def far(self, c):
        me, half = self.me, self.count // 2

        @pl.when((me > 0) & (me < half))
        def _():
            self.lefts(c)

        @pl.when((me < self.count - 1) & (me >= half))
        def _():
            self.rights(c)

    def total(self, c, into):
        me = self.me
        into[...] = self.parts[c, me].astype(F32)

        @pl.when(me > 0)
        def _():
            slot = self.inbox(c, me)
            remote(slot, slot, self.sent.at[c, me], self.came.at[c, me], on_line(0)).wait_recv()
            into[...] += self.inbox(c, me)[...].astype(F32)

        @pl.when(me < self.count - 1)
        def _():
            slot = self.meet.at[c]
            remote(slot, slot, self.sent.at[c, me], self.met.at[c], on_line(0)).wait_recv()
            into[...] += self.meet[c].astype(F32)

    def drain_one(self, c):
        for k in range(self.count):

            @pl.when(self.me != k)
            def _():
                slot = self.parts.at[c, k]
                remote(
                    slot, slot, self.sent.at[c, k], self.came.at[c, k], on_line(0)
                ).wait_send()

    def drain(self, chunks):
        def one(c, carry):
            self.drain_one(c)
            return carry

        lax.fori_loop(0, chunks, one, 0)


class Gather:
    def __init__(self, me, count, place, came, sent_right, sent_left):
        self.me, self.count, self.place = me, count, place
        self.came, self.sent_right, self.sent_left = came, sent_right, sent_left

    def to_right(self, c, k, src):
        return remote(
            src, self.place(c, k), self.sent_right.at[c, k], self.came.at[c, k], on_line(self.me + 1)
        )

    def to_left(self, c, k, src):
        return remote(
            src, self.place(c, k), self.sent_left.at[c, k], self.came.at[c, k], on_line(self.me - 1)
        )

    def own(self, c, src):
        me = self.me

        @pl.when(me < self.count - 1)
        def _():
            self.to_right(c, me, src).start()

        @pl.when(me > 0)
        def _():
            self.to_left(c, me, src).start()

    def wait(self, c, k):
        slot = self.place(c, k)
        remote(slot, slot, self.sent_left.at[c, k], self.came.at[c, k], on_line(0)).wait_recv()

    def hop(self, c, step):
        me = self.me

        @pl.when(me >= step)
        def _():
            k = me - step
            self.wait(c, k)

            @pl.when(me < self.count - 1)
            def _():
                self.to_right(c, k, self.place(c, k)).start()

        @pl.when(me + step < self.count)
        def _():
            k = me + step
            self.wait(c, k)

            @pl.when(me > 0)
            def _():
                self.to_left(c, k, self.place(c, k)).start()

    def drain(self, chunks):
        me = self.me

        def one(c, carry):
            for k in range(self.count):

                @pl.when((me >= k) & (me < self.count - 1))
                def _():
                    slot = self.place(c, k)
                    remote(
                        slot, slot, self.sent_right.at[c, k], self.came.at[c, k], on_line(0)
                    ).wait_send()

                @pl.when((me <= k) & (me > 0))
                def _():
                    slot = self.place(c, k)
                    remote(
                        slot, slot, self.sent_left.at[c, k], self.came.at[c, k], on_line(0)
                    ).wait_send()

            return carry

        lax.fori_loop(0, chunks, one, 0)


class Plane:
    def __init__(self, partners, bits, span, inboxes, sent, came, free, gather_span=None):
        self.partners, self.bits, self.span = partners, bits, span
        self.inboxes, self.sent, self.came, self.free = inboxes, sent, came, free
        self.gather_span = span if gather_span is None else gather_span

    def start_of(self, step):
        bits = self.bits
        return (0, 4 * bits[0], 4 * bits[0] + 2 * bits[1], 4 * bits[0] + 2 * bits[1] + bits[2])[step]

    def copy(self, step):
        if step < 3:
            size = 4 >> step
            src = self.span(self.start_of(step) + size * (1 - self.bits[step]), size)
            dst, partner = self.inboxes[step], self.partners[step]
        else:
            size = 1 << (step - 3)
            src = dst = self.gather_span(self.start_of(6 - step), size)
            partner = self.partners[5 - step]
        return remote(src, dst, self.sent.at[step], self.came.at[step], in_plane(partner))

    def send(self, step):
        if step >= 3:
            pl.semaphore_wait(self.free.at[5 - step], 1)
        self.copy(step).start()

    def add(self, step):
        self.copy(step).wait_send()
        pl.semaphore_signal(
            self.free.at[step], inc=1, device_id=in_plane(self.partners[step]), device_id_type=MESH
        )
        self.copy(step).wait_recv()
        kept = self.span(self.start_of(step + 1), 4 >> step)
        kept[...] = (kept[...].astype(F32) + self.inboxes[step][...].astype(F32)).astype(BF16)

    def next(self, step):
        if 0 < step <= 3:
            self.add(step - 1)
        elif step > 3:
            self.copy(step - 1).wait_recv()
        if step < 6:
            self.send(step)

    def drain(self):
        for step in range(3, 6):
            self.copy(step).wait_send()


def turn(tensor, cosine, sine, sign):
    pieces = []
    front = lax.broadcasted_iota(jnp.int32, (1, 128), 1) % HD < HD // 2
    for at in range(0, tensor.shape[-1], 128):
        piece = tensor[:, at : at + 128]
        mixed = jnp.where(front, -pltpu.roll(piece, 96, 1), pltpu.roll(piece, 32, 1)) * sine
        pieces.append(piece * cosine + sign * mixed)
    return jnp.concatenate(pieces, axis=1)


def layer_kernel(names, sizes, *ref_list):
    r = SimpleNamespace(**dict(zip(names, ref_list)))
    count, groups, tokens, width, cols, units = sizes
    chunks = tokens // CHUNK
    share = CHUNK // count
    heads = cols // HD
    score_scale = HD ** (-0.5)
    me = lax.axis_index("mp")
    row = lax.axis_index("dp")

    core = row % 2
    along_x = (row // 2) % 2
    along_y = row // 4
    other_core = row + 1 - 2 * core
    other_x = row + 2 - 4 * along_x
    other_y = row + 4 - 8 * along_y

    loads = {}

    def load(index, src, dst):
        copy = pltpu.make_async_copy(src, dst, r.load_sem.at[index])
        copy.start()
        loads[index] = copy

    def loaded(*indices):
        for index in indices:
            loads.pop(index).wait()

    load(0, r.layer_one, r.first_in)
    load(1, r.w_value_one, r.wv1)
    load(2, r.block_input, r.x)
    load(3, r.w_query, r.wq)
    load(4, r.w_key, r.wk)
    load(5, r.w_value, r.wv)
    load(6, r.w_out, r.wo.at[me])
    load(7, r.grad_output, r.g)
    load(8, r.w_gate, r.wg)
    load(9, r.w_up, r.wu)
    load(10, r.w_down, r.wd)

    barrier = pltpu.get_barrier_semaphore()
    for step in range(1, count):
        pl.semaphore_signal(
            barrier, inc=1, device_id=on_line((me + step) % count), device_id_type=MESH
        )
    for partner in (other_core, other_x, other_y):
        pl.semaphore_signal(barrier, inc=1, device_id=in_plane(partner), device_id_type=MESH)
    pl.semaphore_wait(barrier, count - 1 + 3)

    def slot_of(ref):
        return lambda c, k: ref.at[c, k]

    def f_slot(c, k):
        return r.f_in.at[pl.ds(pl.multiple_of((c * count + k) * CHUNK, CHUNK), CHUNK)]

    first = Scatter(
        me, count, r.f_part, f_slot, r.f_meet, r.f_sent, r.f_came, r.f_met
    )
    back2 = Scatter(
        me, count, r.b_part, slot_of(r.b_in), r.b_meet, r.b_sent, r.b_came, r.b_met
    )
    out = Scatter(
        me, count, r.o_part, slot_of(r.o_in), r.o_meet, r.o_sent, r.o_came, r.o_met
    )
    back1 = Scatter(
        me, count, r.b_part, slot_of(r.b_in), r.b_meet, r.d_sent, r.d_came, r.d_met
    )
    heads_all = Gather(
        me, count, lambda c, k: r.att.at[c, k], r.att_came, r.att_right, r.att_left
    )
    values_all = Gather(
        me, count, lambda c, k: r.dv_all.at[c, k], r.dv_came, r.dv_right, r.dv_left
    )

    def rows_of(ref):
        return lambda c, k: ref.at[pl.ds(c * CHUNK + k * share, share)]

    outs_all = Gather(
        me, count, rows_of(r.output), r.out_came, r.out_right, r.out_left
    )
    gin_all = Gather(
        me, count, rows_of(r.grad_input), r.gin_came, r.gin_right, r.gin_left
    )

    def at(c):
        return pl.ds(c * CHUNK, CHUNK)

    def mine(c):
        return pl.ds(pl.multiple_of(c * CHUNK + me * share, share), share)

    piece = cols // groups
    block = core * 4 + along_x * 2 + along_y

    def wo_rows(slot, step):
        span = 1 << step
        start = pl.multiple_of((block // span) * span * piece, piece)
        return r.wo.at[slot, pl.ds(start, span * piece)]

    def wo_line():
        loaded(6)
        for step in range(1, count):
            remote(
                wo_rows(me, 0),
                wo_rows(me, 0),
                r.wo_sent.at[step],
                r.wo_came.at[step],
                on_line((me + step) % count),
            ).start()

    def wo_line_wait():
        for step in range(1, count):
            slot = wo_rows((me + count - step) % count, 0)
            copy = remote(
                slot, slot, r.wo_sent.at[step], r.wo_came.at[step], on_line(0)
            )
            copy.wait_send()
            copy.wait_recv()

    def wo_plane(step, start):
        partner = (other_y, other_x, other_core)[step]
        span = 1 << step
        for other in range(1, count):
            slot = (me + other) % count
            index = count * (step + 1) + other
            copy = remote(
                wo_rows(slot, step),
                wo_rows(slot, step),
                r.wo_sent.at[index],
                r.wo_came.at[index],
                in_plane(partner),
            )
            if start:
                copy.start()
            else:
                copy.wait_send()
                copy.wait_recv()

    def first_part(c):
        part = mul(r.first_in[at(c)], r.wv1[...])
        for k in range(count):
            r.f_part[c, k] = part[:, k * cols : (k + 1) * cols].astype(BF16)
        first.open(c)

    def project(c):
        x = r.x[at(c)].astype(F32)
        scale = lax.rsqrt(jnp.mean(x * x, axis=-1, keepdims=True) + EPSILON)
        normed = (x * scale * r.norm_one[...]).astype(BF16)
        r.a1[at(c)] = normed
        tables = [table[at(c)] for table in (r.cosine, r.sine)]
        queries = turn(mul(normed, r.wq[...]), *tables, 1.0)
        r.q[at(c)] = (queries.astype(BF16).astype(F32) * score_scale).astype(BF16)
        r.k[at(c)] = turn(mul(normed, r.wk[...]), *tables, 1.0).astype(BF16)

    def window(c):
        low = max(0, c * CHUNK - REACH)
        return low, (c + 1) * CHUNK - low

    def mask_bias(c):
        low, span = window(c)
        row_index = c * CHUNK + lax.broadcasted_iota(jnp.int32, (CHUNK, span), 0)
        col_index = low + lax.broadcasted_iota(jnp.int32, (CHUNK, span), 1)
        here = r.seg_row[:, c * CHUNK : (c + 1) * CHUNK]
        diagonal = lax.broadcasted_iota(jnp.int32, (CHUNK, CHUNK), 0) == (
            lax.broadcasted_iota(jnp.int32, (CHUNK, CHUNK), 1)
        )
        column = jnp.sum(jnp.where(diagonal, here, 0), axis=1, keepdims=True)
        same = column == r.seg_row[:, low : low + span]
        r.bias[:, :span] = jnp.where(same & (col_index <= row_index), 0.0, -1e30)

    def head_lanes(head):
        return (lax.broadcasted_iota(jnp.int32, (1, cols), 1) // HD) == head

    def only(tensor, lanes):
        return jnp.where(lanes, tensor, jnp.zeros_like(tensor))

    def attend(c):
        first.total(c, r.sum_a)
        own = mul(r.a1[at(c)], r.wv[...])
        r.vm[at(c)] = (0.5 * own + 0.5 * r.sum_a[...]).astype(BF16)
        low, span = window(c)
        mask_bias(c)
        r.sum_a[...] = jnp.zeros_like(r.sum_a)

        def one(head, carry):
            lanes = head_lanes(head)
            scores = mul(only(r.q[at(c)], lanes), r.k[low : low + span], NT)
            scores = scores + r.bias[:, :span]
            largest = jnp.max(scores, axis=-1, keepdims=True)
            raised = jnp.exp(scores - largest)
            summed = jnp.sum(raised, axis=-1, keepdims=True)
            weights = (raised * (1.0 / summed)).astype(BF16)
            r.sum_a[...] += mul(weights, only(r.vm[low : low + span], lanes))
            here = lax.broadcasted_iota(jnp.int32, (1, 128), 1) == head
            r.lse[at(c)] = jnp.where(here, largest + jnp.log(summed), r.lse[at(c)])
            return carry

        lax.fori_loop(0, heads, one, 0)
        r.att[c, me] = r.sum_a[...].astype(BF16)
        heads_all.own(c, r.att.at[c, me])

    def feed(c):
        h = r.x[at(c)].astype(F32)
        for k in range(count):
            h = h + mul(r.att[c, k], r.wo[k])
        r.big[...] = h
        r.h_own[c] = r.big[pl.ds(pl.multiple_of(me * share, share), share)]
        scale = lax.rsqrt(jnp.mean(h * h, axis=-1, keepdims=True) + EPSILON)
        normed = (h * scale * r.norm_two[...]).astype(BF16)
        r.a2[at(c)] = normed
        gate = mul(normed, r.wg[...], NT)
        up = mul(normed, r.wu[...], NT)
        sig = jax.nn.sigmoid(gate)
        silu = gate * sig
        hidden = (silu * up).astype(BF16)
        r.hid[at(c)] = hidden
        grad_hidden = mul(r.g[at(c)], r.wd[...], NT)
        grad_gate = (grad_hidden * up * sig * (1.0 + gate * (1.0 - sig))).astype(BF16)
        grad_up = (grad_hidden * silu).astype(BF16)
        r.dga[at(c)] = grad_gate
        r.dup[at(c)] = grad_up
        back = mul(grad_gate, r.wg[...]) + mul(grad_up, r.wu[...])
        r.b_part[c] = back.astype(BF16).reshape(count, share, width)
        back2.open(c)

    def down(c):
        part = mul(r.hid[at(c)], r.wd[...])
        r.o_part[c] = part.astype(BF16).reshape(count, share, width)

    def norm_back(values, gain, grad):
        scale = lax.rsqrt(jnp.mean(values * values, axis=-1, keepdims=True) + EPSILON)
        grad_gain = jnp.sum(grad * values * scale, axis=0, keepdims=True)
        scaled = grad * gain
        inner = jnp.mean(scaled * values, axis=-1, keepdims=True)
        return grad_gain, scale * scaled - values * scale * scale * scale * inner

    def through_two(c):
        back2.total(c, r.sum_b)
        grad_gain, grad = norm_back(r.h_own[c], r.norm_two[...], r.sum_b[...])
        r.gains[1:2] += grad_gain
        grad = r.g[mine(c)].astype(F32) + grad
        r.dh_own[c] = grad
        low = grad.astype(BF16)
        r.db_own[c] = low
        for k in range(count):
            part = mul(low, r.wo[k], NT).astype(BF16)

            @pl.when(me == k)
            def _():
                r.do[mine(c)] = part

            @pl.when(me != k)
            def _():
                r.do_part[c, k] = part
                remote(
                    r.do_part.at[c, k],
                    r.do.at[mine(c)],
                    r.do_sent.at[c, k],
                    r.do_came.at[c, (me - k + count) % count],
                    on_line(k),
                ).start()

    def do_wait(c):
        for step in range(1, count):
            source = (me + step) % count
            slot = r.do.at[
                pl.ds(pl.multiple_of(c * CHUNK + source * share, share), share)
            ]
            remote(
                slot, slot, r.do_sent.at[c, 0], r.do_came.at[c, step], on_line(0)
            ).wait_recv()

    def attend_back(c):
        do_wait(c)
        low, span = window(c)
        mask_bias(c)
        r.sum_a[...] = jnp.zeros_like(r.sum_a)

        def one(head, carry):
            lanes = head_lanes(head)
            q_head = only(r.q[at(c)], lanes)
            do_head = only(r.do[at(c)], lanes)
            here = lax.broadcasted_iota(jnp.int32, (1, 128), 1) == head
            lse = jnp.sum(jnp.where(here, r.lse[at(c)], 0.0), axis=-1, keepdims=True)
            scores = mul(q_head, r.k[low : low + span], NT) + r.bias[:, :span]
            probs = jnp.exp(scores - lse)
            grad_probs = mul(do_head, r.vm[low : low + span], NT)
            inner = jnp.sum(probs * grad_probs, axis=-1, keepdims=True)
            grad_scores = (probs * (grad_probs - inner)).astype(BF16)
            r.sum_a[...] += mul(grad_scores, only(r.k[low : low + span], lanes))
            r.dk_sum[low : low + span] += mul(grad_scores, q_head, TN)
            r.dv_sum[low : low + span] += mul(probs.astype(BF16), do_head, TN)
            return carry

        lax.fori_loop(0, heads, one, 0)
        tables = [table[at(c)] for table in (r.cosine, r.sine)]
        r.dqkv[at(c), :cols] = turn(r.sum_a[...] * score_scale, *tables, -1.0).astype(BF16)

    def values_back(c):
        tables = [table[at(c)] for table in (r.cosine, r.sine)]
        r.dqkv[at(c), cols : 2 * cols] = turn(r.dk_sum[at(c)], *tables, -1.0).astype(BF16)
        grad_values = (0.5 * r.dv_sum[at(c)]).astype(BF16)
        r.dv_all[c, me] = grad_values
        r.dqkv[at(c), 2 * cols :] = grad_values
        values_all.own(c, r.dv_all.at[c, me])

    def keys_back(c):
        back = mul(r.dqkv[at(c), :cols], r.wq[...], NT)
        back = back + mul(r.dqkv[at(c), cols : 2 * cols], r.wk[...], NT)
        back = back + mul(r.dqkv[at(c), 2 * cols :], r.wv[...], NT)
        back2.drain_one(c)
        r.b_part[c] = back.astype(BF16).reshape(count, share, width)
        back1.open(c)

    stores = []

    def local(src, dst):
        copy = pltpu.make_async_copy(src, dst, r.store_sem.at[len(stores)])
        copy.start()
        return copy

    def through_one(c):
        back1.total(c, r.sum_b)
        x = r.x[mine(c)].astype(F32)
        grad_gain, grad = norm_back(x, r.norm_one[...], r.sum_b[...])
        r.gains[0:1] += grad_gain
        r.b_part[c, me] = (r.dh_own[c] + grad).astype(BF16)
        gin_all.own(c, r.b_part.at[c, me])
        stores.append(local(r.b_part.at[c, me], r.grad_input.at[mine(c)]))

    def finish_out(c):
        out.total(c, r.sum_b)
        r.o_part[c, me] = (r.h_own[c] + r.sum_b[...]).astype(BF16)
        outs_all.own(c, r.o_part.at[c, me])
        stores.append(local(r.o_part.at[c, me], r.output.at[mine(c)]))

    x_first = ((other_core, other_x, other_y), (core, along_x, along_y))
    y_first = ((other_core, other_y, other_x), (core, along_y, along_x))

    def by_cols(ref, size):
        return lambda start, n: ref.at[:, pl.ds(pl.multiple_of(start * size, size), n * size)]

    def by_rows(ref, size):
        return lambda start, n: ref.at[pl.ds(pl.multiple_of(start * size, size), n * size)]

    eighth = width // 8
    part = cols // 8
    plane_gate = Plane(
        *x_first,
        by_cols(r.wg, eighth),
        [r.u_in0.at[0], r.u_in1.at[0], r.u_in2.at[0]],
        r.p_sent.at[0],
        r.p_came.at[0],
        r.p_free.at[0],
    )
    plane_up = Plane(
        *y_first,
        by_cols(r.wu, eighth),
        [r.u_in0.at[1], r.u_in1.at[1], r.u_in2.at[1]],
        r.p_sent.at[1],
        r.p_came.at[1],
        r.p_free.at[1],
    )
    plane_down = Plane(
        *x_first,
        by_cols(r.wd, eighth),
        [r.u_in0.at[2], r.u_in1.at[2], r.u_in2.at[2]],
        r.p_sent.at[2],
        r.p_came.at[2],
        r.p_free.at[2],
    )
    plane_out = Plane(
        *y_first,
        by_rows(r.a2, eighth),
        [
            r.g.at[pl.ds(0, 4 * eighth)],
            r.g.at[pl.ds(4 * eighth, 2 * eighth)],
            r.g.at[pl.ds(6 * eighth, eighth)],
        ],
        r.p_sent.at[3],
        r.p_came.at[3],
        r.p_free.at[3],
        by_rows(r.wo.at[me], part),
    )
    plane_qkv = [
        Plane(
            *(x_first if index == 1 else y_first),
            by_rows(ref, eighth),
            [
                r.f_in.at[pl.ds((7 * index) * eighth, 4 * eighth)],
                r.f_in.at[pl.ds((7 * index + 4) * eighth, 2 * eighth)],
                r.f_in.at[pl.ds((7 * index + 6) * eighth, eighth)],
            ],
            r.p_sent.at[4 + index],
            r.p_came.at[4 + index],
            r.p_free.at[4 + index],
        )
        for index, ref in enumerate((r.wq, r.wk, r.wv))
    ]
    plane_one = Plane(
        *x_first,
        by_cols(r.wv1, eighth),
        [r.v_in0, r.v_in1, r.v_in2],
        r.p_sent.at[7],
        r.p_came.at[7],
        r.p_free.at[7],
    )

    def units_grad(left, right, into):
        for start in range(0, units, 256):
            span = min(256, units - start)
            into[start : start + span] = mul(left[:, start : start + span], right[...], TN).astype(
                BF16
            )

    def out_grad():
        low = r.db_own[...].reshape(tokens // count, width)
        for k in range(count):
            own = jnp.concatenate(
                [
                    r.att[c, k, pl.ds(pl.multiple_of(me * share, share), share)]
                    for c in range(chunks)
                ],
                axis=0,
            )
            grad = mul(own, low, TN).astype(BF16)
            for s in range(8):
                r.a2[s * eighth + k * part : s * eighth + (k + 1) * part] = grad[
                    s * part : (s + 1) * part
                ]

    def out_line(start):
        slot = plane_out.start_of(3)
        for step in range(1, count):
            peer = (me + step) % count
            rows = pl.ds(pl.multiple_of(slot * eighth + peer * part, part), part)
            copy = remote(
                r.a2.at[rows],
                r.z_in.at[step],
                r.z_sent.at[step],
                r.z_came.at[step],
                on_line(peer),
            )
            if start:
                copy.start()
            else:
                copy.wait_send()
                copy.wait_recv()

    def out_line_sum():
        out_line(False)
        slot = plane_out.start_of(3)
        rows = pl.ds(pl.multiple_of(slot * eighth + me * part, part), part)
        grad = r.a2[rows].astype(F32)
        for step in range(1, count):
            grad = grad + r.z_in[step].astype(F32)
        r.wo[me, pl.ds(pl.multiple_of(slot * part, part), part)] = grad.astype(BF16)
        plane_out.send(3)

    def values_one(c):
        grad = None
        for k in range(count):
            values = r.dv_all[c, k]
            piece = mul(values, r.wv1[:, k * cols : (k + 1) * cols], NT)
            grad = piece if grad is None else grad + piece
            piece = mul(r.first_in[at(c)], values, TN)
            if c > 0:
                piece = piece + r.big[:, k * cols : (k + 1) * cols]
            r.big[:, k * cols : (k + 1) * cols] = piece
        r.dk_sum[at(c)] = grad
        stores.append(local(r.dk_sum.at[at(c)], r.grad_first.at[at(c)]))

    def qkv_grad():
        for start in range(0, width, 256):
            grad = mul(r.a1[:, start : start + 256], r.dqkv[...], TN).astype(BF16)
            for index, into in enumerate((r.wq, r.wk, r.wv)):
                into[start : start + 256] = grad[:, index * cols : (index + 1) * cols]

    def grad_gate():
        units_grad(r.dga, r.a2, r.wg)

    def grad_up():
        units_grad(r.dup, r.a2, r.wu)

    def grad_down():
        units_grad(r.hid, r.g, r.wd)

    def out_line_send():
        plane_out.add(2)
        out_line(True)

    def qkv_next(step):
        for plane in plane_qkv:
            plane.next(step)

    def one_start():
        r.wv1[...] = r.big[...].astype(BF16)

    def gain_copy(step):
        if step < count:
            src, device = r.gains, on_line((me + step) % count)
        else:
            src = r.gain_sum.at[step - count]
            device = in_plane((other_core, other_x, other_y)[step - count])
        return remote(src, r.gain_in.at[step], r.gain_sent.at[step], r.gain_came.at[step], device)

    def gain_line():
        for step in range(1, count):
            gain_copy(step).start()

    def gain_plane(index):
        if index == 0:
            total = r.gains[...]
            for step in range(1, count):
                gain_copy(step).wait_recv()
                total = total + r.gain_in[step]
        else:
            gain_copy(count + index - 1).wait_recv()
            total = r.gain_sum[index - 1] + r.gain_in[count + index - 1]
        if index < 3:
            r.gain_sum[index] = total
            gain_copy(count + index).start()
        else:
            r.gain_out[...] = total

    r.gains[...] = jnp.zeros_like(r.gains)
    r.dk_sum[...] = jnp.zeros_like(r.dk_sum)
    r.dv_sum[...] = jnp.zeros_like(r.dv_sum)
    r.lse[...] = jnp.zeros_like(r.lse)
    wo_line()
    loaded(2, 3, 4, 5)
    loaded(0, 1)
    first_part(0)
    first_part(1)
    wo_line_wait()
    wo_plane(0, True)
    wo_plane(0, False)
    first.near(0, 0)
    wo_plane(1, True)
    first.near(0, 1)
    first.far(0)
    first.near(1, 0)
    project(0)
    first.near(1, 1)
    first_part(2)
    attend(0)
    first.near(2, 0)
    first.near(2, 1)
    first.far(1)
    first_part(3)
    project(1)
    first.far(2)
    wo_plane(1, False)
    loaded(7, 8, 9, 10)
    heads_all.hop(0, 1)
    attend(1)
    heads_all.hop(0, 2)
    wo_plane(2, True)
    project(2)
    attend(2)
    wo_plane(2, False)
    project(3)
    heads_all.hop(1, 1)
    heads_all.hop(0, 3)
    feed(0)
    heads_all.hop(2, 1)
    first.near(3, 0)
    heads_all.hop(2, 2)
    back2.near(0, 0)
    down(0)
    first.far(3)
    heads_all.hop(1, 2)
    first.near(3, 1)
    back2.near(0, 1)
    out.open(0)
    out.near(0, 0)
    attend(3)
    back2.far(0)
    heads_all.hop(1, 3)
    feed(1)
    heads_all.hop(3, 1)
    through_two(0)
    heads_all.hop(2, 3)
    out.near(0, 1)
    feed(2)
    heads_all.hop(3, 2)
    out.far(0)
    heads_all.hop(3, 3)
    down(1)
    back2.near(1, 0)
    feed(3)
    back2.near(1, 1)
    finish_out(0)
    grad_up()
    back2.near(2, 0)
    down(2)
    attend_back(0)
    back2.far(1)
    grad_gate()
    down(3)
    back2.near(3, 0)
    back2.near(2, 1)
    plane_gate.next(0)
    grad_down()
    back2.far(2)
    back2.far(3)
    back2.near(3, 1)
    through_two(1)
    through_two(2)
    through_two(3)
    outs_all.hop(0, 1)
    plane_gate.next(1)
    out.open(1)
    attend_back(1)
    attend_back(2)
    out.near(1, 0)
    values_back(0)
    attend_back(3)
    values_back(2)
    plane_gate.next(2)
    values_back(3)
    values_back(1)
    plane_down.next(0)
    keys_back(1)
    values_all.hop(0, 1)
    keys_back(0)
    out.far(1)
    out_grad()
    plane_down.next(1)
    values_all.hop(2, 1)
    keys_back(2)
    plane_gate.next(3)
    plane_down.next(2)
    keys_back(3)
    values_all.hop(3, 1)
    values_all.hop(1, 1)
    plane_down.next(3)
    out.open(3)
    values_all.hop(0, 2)
    back1.near(1, 0)
    back1.near(0, 0)
    plane_out.next(0)
    values_all.hop(1, 2)
    plane_gate.next(4)
    back1.near(0, 1)
    outs_all.hop(0, 2)
    plane_up.next(0)
    values_all.hop(0, 3)
    back1.far(1)
    plane_down.next(4)
    back1.near(1, 1)
    back1.near(2, 0)
    back1.near(2, 1)
    values_all.hop(3, 2)
    values_all.hop(3, 3)
    through_one(1)
    plane_up.next(1)
    qkv_grad()
    back1.far(0)
    back1.near(3, 0)
    back1.far(2)
    back1.near(3, 1)
    plane_out.next(1)
    out.near(1, 1)
    values_all.hop(1, 3)
    through_one(0)
    values_all.hop(2, 2)
    values_all.hop(2, 3)
    out.near(3, 0)
    plane_up.next(2)
    plane_gate.next(5)
    through_one(2)
    back1.far(3)
    through_one(3)
    plane_up.next(3)
    values_one(0)
    gin_all.hop(1, 1)
    plane_down.next(5)
    gin_all.hop(0, 1)
    plane_out.next(2)
    qkv_next(0)
    values_one(1)
    out.open(2)
    values_one(2)
    qkv_next(1)
    gin_all.hop(3, 1)
    out.far(3)
    gin_all.hop(2, 1)
    plane_up.next(4)
    out.near(2, 0)
    values_one(3)
    plane_gate.next(6)
    gin_all.hop(3, 2)
    one_start()
    qkv_next(2)
    plane_one.next(0)
    plane_one.next(1)
    finish_out(1)
    outs_all.hop(0, 3)
    gin_all.hop(2, 2)
    out.near(3, 1)
    gain_line()
    plane_down.next(6)
    out.far(2)
    gin_all.hop(1, 2)
    out_line_send()
    gain_plane(0)
    out.near(2, 1)
    finish_out(3)
    qkv_next(3)
    finish_out(2)
    gin_all.hop(0, 2)
    plane_one.next(2)
    qkv_next(4)
    gin_all.hop(0, 3)
    outs_all.hop(2, 1)
    qkv_next(5)
    out_line_sum()
    plane_one.next(3)
    gin_all.hop(3, 3)
    outs_all.hop(3, 1)
    gain_plane(1)
    plane_up.next(5)
    outs_all.hop(1, 1)
    gain_plane(2)
    plane_one.next(4)
    outs_all.hop(3, 2)
    gin_all.hop(1, 3)
    gin_all.hop(2, 3)
    plane_one.next(5)
    plane_out.next(4)
    plane_up.next(6)
    gain_plane(3)
    outs_all.hop(2, 2)
    outs_all.hop(2, 3)
    qkv_next(6)
    plane_out.next(5)
    outs_all.hop(1, 2)
    plane_out.next(6)
    outs_all.hop(3, 3)
    plane_one.next(6)
    outs_all.hop(1, 3)
    for src, dst in (
        (r.wg, r.grad_gate),
        (r.wu, r.grad_up),
        (r.wd, r.grad_down),
        (r.wo.at[me], r.grad_out),
        (r.wq, r.grad_query),
        (r.wk, r.grad_key),
        (r.wv, r.grad_value),
        (r.wv1, r.grad_one),
    ):
        stores.append(local(src, dst))
    for copy in stores:
        copy.wait()
    for line in (first, back1, out, heads_all, values_all, outs_all, gin_all):
        line.drain(chunks)
    for plane in (plane_gate, plane_up, plane_down, plane_out, plane_one, *plane_qkv):
        plane.drain()
    for step in range(1, count + 3):
        gain_copy(step).wait_send()

    def do_drain(c, carry):
        for k in range(count):

            @pl.when(me != k)
            def _():
                slot = r.do_part.at[c, k]
                remote(
                    slot, slot, r.do_sent.at[c, k], r.do_came.at[c, 0], on_line(0)
                ).wait_send()

        return carry

    lax.fori_loop(0, chunks, do_drain, 0)


def fused_layer(arrays, sizes):
    count, groups, tokens, width, cols, units = sizes
    chunks = tokens // CHUNK
    share = CHUNK // count
    eighth = width // 8
    hbm = pl.BlockSpec(memory_space=pl.ANY)
    vmem = pl.BlockSpec(memory_space=pltpu.VMEM)
    ins = dict(
        block_input=hbm,
        layer_one=hbm,
        grad_output=hbm,
        norm_one=vmem,
        w_query=hbm,
        w_key=hbm,
        w_value=hbm,
        w_out=hbm,
        norm_two=vmem,
        w_gate=hbm,
        w_up=hbm,
        w_down=hbm,
        w_value_one=hbm,
        cosine=vmem,
        sine=vmem,
        seg_row=vmem,
    )
    outs = dict(
        output=((tokens, width), BF16, hbm),
        grad_input=((tokens, width), BF16, hbm),
        grad_first=((tokens, cols), F32, hbm),
        grad_query=((width, cols), BF16, hbm),
        grad_key=((width, cols), BF16, hbm),
        grad_value=((width, cols), BF16, hbm),
        grad_out=((cols, width), BF16, hbm),
        grad_gate=((units, width), BF16, hbm),
        grad_up=((units, width), BF16, hbm),
        grad_down=((units, width), BF16, hbm),
        grad_one=((cols, width), BF16, hbm),
        gain_out=((8, width), F32, vmem),
    )
    dma = pltpu.SemaphoreType.DMA

    def low(*shape):
        return pltpu.VMEM(shape, BF16)

    def full(*shape):
        return pltpu.VMEM(shape, F32)

    slots = (chunks, count)
    scratch = dict(
        x=low(tokens, width),
        g=low(tokens, width),
        first_in=low(tokens, cols),
        wq=low(width, cols),
        wk=low(width, cols),
        wv=low(width, cols),
        wv1=low(cols, width),
        wo=low(count, cols, width),
        wg=low(units, width),
        wu=low(units, width),
        wd=low(units, width),
        a1=low(tokens, width),
        a2=low(tokens, width),
        q=low(tokens, cols),
        k=low(tokens, cols),
        vm=low(tokens, cols),
        lse=full(tokens, 128),
        bias=full(CHUNK, CHUNK + REACH),
        sum_a=full(CHUNK, cols),
        sum_b=full(share, width),
        big=full(CHUNK, width),
        att=low(*slots, CHUNK, cols),
        dv_all=low(*slots, CHUNK, cols),
        hid=low(tokens, units),
        dga=low(tokens, units),
        dup=low(tokens, units),
        h_own=full(chunks, share, width),
        dh_own=full(chunks, share, width),
        db_own=low(chunks, share, width),
        do_part=low(*slots, share, cols),
        do=low(tokens, cols),
        dqkv=low(tokens, 3 * cols),
        dk_sum=full(tokens, cols),
        dv_sum=full(tokens, cols),
        gains=full(8, width),
        gain_sum=full(3, 8, width),
        gain_in=full(count + 3, 8, width),
        u_in0=low(3, units, 4 * eighth),
        u_in1=low(3, units, 2 * eighth),
        u_in2=low(3, units, eighth),
        z_in=low(count, cols // 8, width),
        v_in0=low(cols, 4 * eighth),
        v_in1=low(cols, 2 * eighth),
        v_in2=low(cols, eighth),
        f_part=low(*slots, CHUNK, cols),
        f_in=low(chunks * count * CHUNK, cols),
        f_meet=low(chunks, CHUNK, cols),
        b_part=low(*slots, share, width),
        b_in=low(*slots, share, width),
        b_meet=low(chunks, share, width),
        o_part=low(*slots, share, width),
        o_in=low(*slots, share, width),
        o_meet=low(chunks, share, width),
        load_sem=dma((11,)),
        store_sem=dma((3 * chunks + 8,)),
        wo_sent=dma((4 * count,)),
        wo_came=dma((4 * count,)),
        do_sent=dma(slots),
        do_came=dma(slots),
        p_sent=dma((8, 6)),
        p_came=dma((8, 6)),
        p_free=pltpu.SemaphoreType.REGULAR((8, 3)),
        z_sent=dma((count,)),
        z_came=dma((count,)),
        gain_sent=dma((count + 3,)),
        gain_came=dma((count + 3,)),
        f_sent=dma(slots),
        f_came=dma(slots),
        f_met=dma((chunks,)),
        b_sent=dma(slots),
        b_came=dma(slots),
        b_met=dma((chunks,)),
        o_sent=dma(slots),
        o_came=dma(slots),
        o_met=dma((chunks,)),
        d_sent=dma(slots),
        d_came=dma(slots),
        d_met=dma((chunks,)),
        att_came=dma(slots),
        att_right=dma(slots),
        att_left=dma(slots),
        dv_came=dma(slots),
        dv_right=dma(slots),
        dv_left=dma(slots),
        out_came=dma(slots),
        out_right=dma(slots),
        out_left=dma(slots),
        gin_came=dma(slots),
        gin_right=dma(slots),
        gin_left=dma(slots),
    )
    results = pl.pallas_call(
        functools.partial(layer_kernel, [*ins, *outs, *scratch], sizes),
        out_shape=[jax.ShapeDtypeStruct(item[0], item[1]) for item in outs.values()],
        in_specs=list(ins.values()),
        out_specs=[item[2] for item in outs.values()],
        scratch_shapes=list(scratch.values()),
        compiler_params=pltpu.CompilerParams(
            collective_id=0, has_side_effects=True, vmem_limit_bytes=VMEM_LIMIT
        ),
        cost_estimate=pl.CostEstimate(
            flops=2 * 13 * 10**9, bytes_accessed=40 * 2**20, transcendentals=0
        ),
    )(*arrays)
    return SimpleNamespace(**dict(zip(outs, results)))


def on_device(*arguments):
    (
        block_input,
        layer_one_input,
        segment_ids,
        grad_output,
        norm_one,
        w_query,
        w_key,
        w_value,
        w_out,
        norm_two,
        w_gate,
        w_up,
        w_down,
        w_value_one,
    ) = arguments
    count = lax.axis_size("mp")
    groups = lax.axis_size("dp")
    tokens, width = block_input.shape
    cols = w_query.shape[1]
    units = w_gate.shape[1]
    fits = (
        count == 4
        and groups == 8
        and tokens == 4 * CHUNK
        and cols == 256
        and width == count * cols
        and units % 64 == 0
        and units <= 704
        and segment_ids.shape[0] == 1
    )
    if not fits:
        return by_collectives(*arguments)
    cosine, sine_part = rope_tables(positions_of(segment_ids)[0], HD)
    cosine = cosine[:, 0]
    sine_part = sine_part[:, 0]
    r = fused_layer(
        (
            block_input,
            layer_one_input,
            grad_output,
            norm_one[None, :],
            w_query,
            w_key,
            w_value,
            w_out,
            norm_two[None, :],
            w_gate.T,
            w_up.T,
            w_down,
            w_value_one,
            jnp.concatenate([cosine] * 4, axis=1),
            jnp.concatenate([sine_part] * 4, axis=1),
            segment_ids.astype(F32),
        ),
        (count, groups, tokens, width, cols, units),
    )
    return (
        r.output,
        r.grad_input.astype(F32),
        r.grad_first,
        r.gain_out[0],
        r.grad_query.astype(F32),
        r.grad_key.astype(F32),
        r.grad_value.astype(F32),
        r.grad_out.astype(F32),
        r.gain_out[1],
        r.grad_gate.astype(F32).T,
        r.grad_up.astype(F32).T,
        r.grad_down.astype(F32),
        r.grad_one.astype(F32),
    )


def solution(mesh):
    return jax.shard_map(
        on_device,
        mesh=mesh,
        in_specs=(
            P("dp", None),
            P("dp", "mp"),
            P("dp", None),
            P("dp", None),
            P(),
            P(None, "mp"),
            P(None, "mp"),
            P(None, "mp"),
            P("mp", None),
            P(),
            P(None, "mp"),
            P(None, "mp"),
            P("mp", None),
            P("mp", None),
        ),
        out_specs=(
            P("dp", None),
            P("dp", None),
            P("dp", "mp"),
            P(),
            P(None, "mp"),
            P(None, "mp"),
            P(None, "mp"),
            P("mp", None),
            P(),
            P(None, "mp"),
            P(None, "mp"),
            P("mp", None),
            P("mp", None),
        ),
        check_vma=False,
    )
```

```python
import functools
import math
from types import SimpleNamespace

import jax
import jax.numpy as jnp
import numpy as np
from jax import lax
from jax.experimental import pallas as pl
from jax.experimental.pallas import tpu as pltpu
from jax.sharding import PartitionSpec as P

HD = 64


EPSILON = 1e-06
VMEM_LIMIT = 64 * 2**20 - 2**16


def positions_of(segments):
    position = lax.broadcasted_iota(jnp.int32, segments.shape, 1)
    changed = (segments[:, 1:] != segments[:, :-1]).astype(jnp.int32)
    starts = jnp.concatenate([jnp.ones_like(segments[:, :1]), changed], axis=1)
    return position - lax.cummax(position * starts, axis=1)


def rope_tables(positions, width):
    half_width = width // 2
    rates = jnp.exp(jnp.arange(half_width, dtype=jnp.float32) * (-math.log(10000.0) / half_width))
    angles = positions.astype(jnp.float32)[:, None] * rates[None, :]
    return (jnp.cos(angles)[:, None, :], jnp.sin(angles)[:, None, :])


def rotate(tensor, cosine, sine_part, turn):
    half_width = tensor.shape[-1] // 2
    left_half = tensor[..., :half_width]
    right_half = tensor[..., half_width:]
    return jnp.concatenate(
        [
            left_half * cosine - turn * right_half * sine_part,
            right_half * cosine + turn * left_half * sine_part,
        ],
        axis=-1,
    )


def over_rows(left_side, right_side):
    return lax.dot_general(
        left_side, right_side, (((0,), (0,)), ((), ())), preferred_element_type=jnp.float32
    )


def against(left_side, right_side):
    return lax.dot_general(
        left_side, right_side, (((1,), (1,)), ((), ())), preferred_element_type=jnp.float32
    )


def norm_back(activations, scale_vec, gain_vec, grad_normed):
    grad_gain = jnp.sum(grad_normed * activations * scale_vec, axis=0)
    scaled = grad_normed * gain_vec
    inner = jnp.mean(scaled * activations, axis=-1, keepdims=True)
    return (grad_gain, scale_vec * scaled - activations * scale_vec * scale_vec * scale_vec * inner)


def masked_scores(q_block, key_rows, seg_block, seg_all, first_row, score_scale):
    block_rows = q_block.shape[0]
    scores = (
        jnp.einsum("qhd,khd->hqk", q_block, key_rows, preferred_element_type=jnp.float32)
        * score_scale
    )
    row_index = first_row + lax.broadcasted_iota(jnp.int32, (block_rows, key_rows.shape[0]), 0)
    col_index = lax.broadcasted_iota(jnp.int32, (block_rows, key_rows.shape[0]), 1)
    allowed = (seg_block[:, None] == seg_all[None, :]) & (col_index <= row_index)
    return jnp.where(allowed[None], scores, -1e30)


def attend_forward(queries, key_rows, values, seg_all, score_scale):
    row_count, head_count, width = queries.shape
    block_rows = min(512, row_count)

    def one_block(block_index):
        first_row = block_index * block_rows
        q_block = lax.dynamic_slice_in_dim(queries, first_row, block_rows, 0)
        seg_block = lax.dynamic_slice_in_dim(seg_all, first_row, block_rows, 0)
        scores = masked_scores(q_block, key_rows, seg_block, seg_all, first_row, score_scale)
        largest = jnp.max(scores, axis=-1, keepdims=True)
        raised = jnp.exp(scores - largest)
        summed = jnp.sum(raised, axis=-1, keepdims=True)
        weights = (raised / summed).astype(jnp.bfloat16)
        result = jnp.einsum("hqk,khd->qhd", weights, values, preferred_element_type=jnp.float32)
        return (result, (largest + jnp.log(summed))[..., 0])

    results, log_totals = lax.map(one_block, jnp.arange(row_count // block_rows, dtype=jnp.int32))
    return (results.reshape(row_count, head_count, width), log_totals)


def attend_backward(queries, key_rows, values, seg_all, log_totals, grad_attended, score_scale):
    row_count = queries.shape[0]
    block_rows = min(512, row_count)

    def one_block(carried, block_index):
        grad_keys, grad_values = carried
        first_row = block_index * block_rows
        q_block = lax.dynamic_slice_in_dim(queries, first_row, block_rows, 0)
        seg_block = lax.dynamic_slice_in_dim(seg_all, first_row, block_rows, 0)
        grad_block = lax.dynamic_slice_in_dim(grad_attended, first_row, block_rows, 0)
        scores = masked_scores(q_block, key_rows, seg_block, seg_all, first_row, score_scale)
        probs = jnp.exp(scores - log_totals[block_index][..., None])
        grad_probs = jnp.einsum(
            "qhd,khd->hqk", grad_block, values, preferred_element_type=jnp.float32
        )
        inner = jnp.sum(probs * grad_probs, axis=-1, keepdims=True)
        grad_scores = (probs * (grad_probs - inner)).astype(jnp.bfloat16)
        grad_query = (
            jnp.einsum("hqk,khd->qhd", grad_scores, key_rows, preferred_element_type=jnp.float32)
            * score_scale
        )
        grad_keys = (
            grad_keys
            + jnp.einsum("hqk,qhd->khd", grad_scores, q_block, preferred_element_type=jnp.float32)
            * score_scale
        )
        grad_values = grad_values + jnp.einsum(
            "hqk,qhd->khd",
            probs.astype(jnp.bfloat16),
            grad_block,
            preferred_element_type=jnp.float32,
        )
        return ((grad_keys, grad_values), grad_query)

    zero_rows = jnp.zeros(key_rows.shape, jnp.float32)
    (grad_keys, grad_values), grad_queries = lax.scan(
        one_block, (zero_rows, zero_rows), jnp.arange(row_count // block_rows, dtype=jnp.int32)
    )
    return (grad_queries.reshape(key_rows.shape), grad_keys, grad_values)


def by_collectives(
    block_input,
    layer_one_input,
    segment_ids,
    grad_output,
    norm_one,
    w_query,
    w_key,
    w_value,
    w_out,
    norm_two,
    w_gate,
    w_up,
    w_down,
    w_value_one,
):
    token_count = block_input.shape[0]
    head_count = w_query.shape[1] // HD
    score_scale = HD ** (-0.5)
    seg_all = segment_ids[0]
    cosine, sine_part = rope_tables(positions_of(segment_ids)[0], HD)
    share_rows = token_count // lax.axis_size("mp")
    share_start = lax.axis_index("mp") * share_rows
    inputs = block_input.astype(jnp.float32)
    scale_one = lax.rsqrt(jnp.mean(inputs * inputs, axis=-1, keepdims=True) + EPSILON)
    normed = (inputs * scale_one * norm_one).astype(jnp.bfloat16)
    queries = jnp.dot(normed, w_query, preferred_element_type=jnp.float32).reshape(
        token_count, head_count, HD
    )
    key_rows = jnp.dot(normed, w_key, preferred_element_type=jnp.float32).reshape(
        token_count, head_count, HD
    )
    own_values = jnp.dot(normed, w_value, preferred_element_type=jnp.float32)
    first_values = lax.psum_scatter(
        jnp.dot(layer_one_input, w_value_one, preferred_element_type=jnp.float32).astype(
            jnp.bfloat16
        ),
        "mp",
        scatter_dimension=1,
        tiled=True,
    ).astype(jnp.float32)
    mixed_values = (
        (0.5 * own_values + 0.5 * first_values)
        .astype(jnp.bfloat16)
        .reshape(token_count, head_count, HD)
    )
    turned_q = rotate(queries, cosine, sine_part, 1.0).astype(jnp.bfloat16)
    turned_k = rotate(key_rows, cosine, sine_part, 1.0).astype(jnp.bfloat16)
    attended, log_totals = attend_forward(turned_q, turned_k, mixed_values, seg_all, score_scale)
    attended = attended.reshape(token_count, head_count * HD).astype(jnp.bfloat16)
    branch_one = jnp.dot(attended, w_out, preferred_element_type=jnp.float32)
    inputs_here = lax.dynamic_slice_in_dim(inputs, share_start, share_rows, 0)
    scale_one_here = lax.dynamic_slice_in_dim(scale_one, share_start, share_rows, 0)
    grad_rows = lax.dynamic_slice_in_dim(grad_output, share_start, share_rows, 0).astype(
        jnp.float32
    )
    residual = inputs_here + lax.psum_scatter(
        branch_one.astype(jnp.bfloat16), "mp", scatter_dimension=0, tiled=True
    ).astype(jnp.float32)
    scale_two = lax.rsqrt(jnp.mean(residual * residual, axis=-1, keepdims=True) + EPSILON)
    normed_two = (residual * scale_two * norm_two).astype(jnp.bfloat16)
    normed_two = lax.all_gather(normed_two, "mp", axis=0, tiled=True)
    gate_pre = jnp.dot(normed_two, w_gate, preferred_element_type=jnp.float32)
    up_pre = jnp.dot(normed_two, w_up, preferred_element_type=jnp.float32)
    sigmoid_gate = jax.nn.sigmoid(gate_pre)
    silu_gate = gate_pre * sigmoid_gate
    hidden = (silu_gate * up_pre).astype(jnp.bfloat16)
    branch_two = jnp.dot(hidden, w_down, preferred_element_type=jnp.float32)
    output_share = (
        residual
        + lax.psum_scatter(
            branch_two.astype(jnp.bfloat16), "mp", scatter_dimension=0, tiled=True
        ).astype(jnp.float32)
    ).astype(jnp.bfloat16)
    output = lax.all_gather(output_share, "mp", axis=0, tiled=True)
    grad_down = over_rows(hidden, grad_output)
    grad_hidden = against(grad_output, w_down)
    grad_gate_pre = (
        grad_hidden * up_pre * sigmoid_gate * (1.0 + gate_pre * (1.0 - sigmoid_gate))
    ).astype(jnp.bfloat16)
    grad_up_pre = (grad_hidden * silu_gate).astype(jnp.bfloat16)
    grad_gate = over_rows(normed_two, grad_gate_pre)
    grad_up = over_rows(normed_two, grad_up_pre)
    back_two = against(grad_gate_pre, w_gate) + against(grad_up_pre, w_up)
    grad_normed_two = lax.psum_scatter(
        back_two.astype(jnp.bfloat16), "mp", scatter_dimension=0, tiled=True
    ).astype(jnp.float32)
    grad_norm_two, grad_through_two = norm_back(residual, scale_two, norm_two, grad_normed_two)
    grad_residual = grad_rows + grad_through_two
    residual_low = grad_residual.astype(jnp.bfloat16)
    residual_low = lax.all_gather(residual_low, "mp", axis=0, tiled=True)
    grad_out_proj = over_rows(attended, residual_low)
    grad_attended = (
        against(residual_low, w_out).astype(jnp.bfloat16).reshape(token_count, head_count, HD)
    )
    grad_turned_q, grad_turned_k, grad_mixed = attend_backward(
        turned_q, turned_k, mixed_values, seg_all, log_totals, grad_attended, score_scale
    )
    grad_value_part = (0.5 * grad_mixed).reshape(token_count, head_count * HD).astype(jnp.bfloat16)
    grad_first_full = lax.all_gather(grad_value_part, "mp", axis=1, tiled=True)
    grad_queries = (
        rotate(grad_turned_q, cosine, sine_part, -1.0)
        .reshape(token_count, head_count * HD)
        .astype(jnp.bfloat16)
    )
    grad_keys = (
        rotate(grad_turned_k, cosine, sine_part, -1.0)
        .reshape(token_count, head_count * HD)
        .astype(jnp.bfloat16)
    )
    grad_query = over_rows(normed, grad_queries)
    grad_key = over_rows(normed, grad_keys)
    grad_value = over_rows(normed, grad_value_part)
    back_one = (
        against(grad_queries, w_query)
        + against(grad_keys, w_key)
        + against(grad_value_part, w_value)
    )
    grad_normed = lax.psum_scatter(
        back_one.astype(jnp.bfloat16), "mp", scatter_dimension=0, tiled=True
    ).astype(jnp.float32)
    grad_norm_one, grad_through_one = norm_back(inputs_here, scale_one_here, norm_one, grad_normed)
    gain_rows = jnp.concatenate([grad_norm_one, grad_norm_two])[None, :]
    grad_input, gain_all = (
        lax.all_gather(
            (grad_residual + grad_through_one).astype(jnp.bfloat16), "mp", axis=0, tiled=True
        ).astype(jnp.float32),
        lax.all_gather(gain_rows, "mp", axis=0, tiled=True),
    )
    gain_total = jnp.sum(gain_all, axis=0)
    width = norm_one.shape[0]
    grad_norm_one = gain_total[:width]
    grad_norm_two = gain_total[width:]
    grad_value_one = over_rows(layer_one_input, grad_first_full)
    grad_layer_one_input = against(grad_first_full, w_value_one)
    grad_norm_one, grad_norm_two = lax.psum((grad_norm_one, grad_norm_two), "dp")
    summed = lax.psum(
        tuple(
            part.astype(jnp.bfloat16)
            for part in (
                grad_query,
                grad_key,
                grad_value,
                grad_out_proj,
                grad_value_one,
                grad_gate,
                grad_up,
                grad_down,
            )
        ),
        "dp",
    )
    (
        grad_query,
        grad_key,
        grad_value,
        grad_out_proj,
        grad_value_one,
        grad_gate,
        grad_up,
        grad_down,
    ) = tuple(part.astype(jnp.float32) for part in summed)
    return (
        output,
        grad_input,
        grad_layer_one_input,
        grad_norm_one,
        grad_query,
        grad_key,
        grad_value,
        grad_out_proj,
        grad_norm_two,
        grad_gate,
        grad_up,
        grad_down,
        grad_value_one,
    )


NN = (((1,), (0,)), ((), ()))
NT = (((1,), (1,)), ((), ()))
TN = (((0,), (0,)), ((), ()))
F32 = jnp.float32
BF16 = jnp.bfloat16
CHUNK = 256
REACH = 512
MESH = pl.DeviceIdType.MESH


def mul(left_side, right_side, dims=NN):
    return lax.dot_general(left_side, right_side, dims, preferred_element_type=F32)


def on_line(index):
    return {"mp": index}


def in_plane(index):
    return {"dp": index}


def remote(src, dst, send_sem, recv_sem, device):
    return pltpu.make_async_remote_copy(
        src_ref=src,
        dst_ref=dst,
        send_sem=send_sem,
        recv_sem=recv_sem,
        device_id=device,
        device_id_type=MESH,
    )


class Scatter:
    def __init__(self, me, count, parts, inbox, meet, sent, came, met):
        self.me, self.count = me, count
        self.parts, self.inbox, self.meet = parts, inbox, meet
        self.sent, self.came, self.met = sent, came, met

    def take(self, c, k):
        slot = self.inbox(c, k)
        remote(slot, slot, self.sent.at[c, k], self.came.at[c, k], on_line(0)).wait_recv()
        self.parts[c, k] = (self.parts[c, k].astype(F32) + self.inbox(c, k)[...].astype(F32)).astype(
            BF16
        )

    def right(self, c, k):
        me = self.me

        @pl.when(me < k)
        def _():
            @pl.when(me > 0)
            def _():
                self.take(c, k)

            remote(
                self.parts.at[c, k],
                self.inbox(c, k),
                self.sent.at[c, k],
                self.came.at[c, k],
                on_line(me + 1),
            ).start()

    def left(self, c, k):
        me = self.me

        @pl.when(me > k)
        def _():
            @pl.when(me < self.count - 1)
            def _():
                self.take(c, k)

            @pl.when(me == k + 1)
            def _():
                remote(
                    self.parts.at[c, k],
                    self.meet.at[c],
                    self.sent.at[c, k],
                    self.met.at[c],
                    on_line(me - 1),
                ).start()

            @pl.when(me > k + 1)
            def _():
                remote(
                    self.parts.at[c, k],
                    self.inbox(c, k),
                    self.sent.at[c, k],
                    self.came.at[c, k],
                    on_line(me - 1),
                ).start()

    def rights(self, c):
        for k in range(self.count - 1, 0, -1):
            self.right(c, k)

    def lefts(self, c):
        for k in range(self.count - 1):
            self.left(c, k)

    def open(self, c):
        @pl.when(self.me == 0)
        def _():
            self.rights(c)

        @pl.when(self.me == self.count - 1)
        def _():
            self.lefts(c)

    def near(self, c, step):
        me, half = self.me, self.count // 2

        @pl.when((me > 0) & (me < half))
        def _():
            self.right(c, self.count - 1 - step)

        @pl.when((me < self.count - 1) & (me >= half))
        def _():
            self.left(c, step)

    def far(self, c):
        me, half = self.me, self.count // 2

        @pl.when((me > 0) & (me < half))
        def _():
            self.lefts(c)

        @pl.when((me < self.count - 1) & (me >= half))
        def _():
            self.rights(c)

    def total(self, c, into):
        me = self.me
        into[...] = self.parts[c, me].astype(F32)

        @pl.when(me > 0)
        def _():
            slot = self.inbox(c, me)
            remote(slot, slot, self.sent.at[c, me], self.came.at[c, me], on_line(0)).wait_recv()
            into[...] += self.inbox(c, me)[...].astype(F32)

        @pl.when(me < self.count - 1)
        def _():
            slot = self.meet.at[c]
            remote(slot, slot, self.sent.at[c, me], self.met.at[c], on_line(0)).wait_recv()
            into[...] += self.meet[c].astype(F32)

    def drain_one(self, c):
        for k in range(self.count):

            @pl.when(self.me != k)
            def _():
                slot = self.parts.at[c, k]
                remote(
                    slot, slot, self.sent.at[c, k], self.came.at[c, k], on_line(0)
                ).wait_send()

    def drain(self, chunks):
        def one(c, carry):
            self.drain_one(c)
            return carry

        lax.fori_loop(0, chunks, one, 0)


class Gather:
    def __init__(self, me, count, place, came, sent_right, sent_left):
        self.me, self.count, self.place = me, count, place
        self.came, self.sent_right, self.sent_left = came, sent_right, sent_left

    def to_right(self, c, k, src):
        return remote(
            src, self.place(c, k), self.sent_right.at[c, k], self.came.at[c, k], on_line(self.me + 1)
        )

    def to_left(self, c, k, src):
        return remote(
            src, self.place(c, k), self.sent_left.at[c, k], self.came.at[c, k], on_line(self.me - 1)
        )

    def own(self, c, src):
        me = self.me

        @pl.when(me < self.count - 1)
        def _():
            self.to_right(c, me, src).start()

        @pl.when(me > 0)
        def _():
            self.to_left(c, me, src).start()

    def wait(self, c, k):
        slot = self.place(c, k)
        remote(slot, slot, self.sent_left.at[c, k], self.came.at[c, k], on_line(0)).wait_recv()

    def hop(self, c, step):
        me = self.me

        @pl.when(me >= step)
        def _():
            k = me - step
            self.wait(c, k)

            @pl.when(me < self.count - 1)
            def _():
                self.to_right(c, k, self.place(c, k)).start()

        @pl.when(me + step < self.count)
        def _():
            k = me + step
            self.wait(c, k)

            @pl.when(me > 0)
            def _():
                self.to_left(c, k, self.place(c, k)).start()

    def drain(self, chunks):
        me = self.me

        def one(c, carry):
            for k in range(self.count):

                @pl.when((me >= k) & (me < self.count - 1))
                def _():
                    slot = self.place(c, k)
                    remote(
                        slot, slot, self.sent_right.at[c, k], self.came.at[c, k], on_line(0)
                    ).wait_send()

                @pl.when((me <= k) & (me > 0))
                def _():
                    slot = self.place(c, k)
                    remote(
                        slot, slot, self.sent_left.at[c, k], self.came.at[c, k], on_line(0)
                    ).wait_send()

            return carry

        lax.fori_loop(0, chunks, one, 0)


class Plane:
    def __init__(self, partners, bits, span, inboxes, sent, came, free, store, gather_span=None):
        self.partners, self.bits, self.span = partners, bits, span
        self.inboxes, self.sent, self.came, self.free = inboxes, sent, came, free
        self.store = store
        self.gather_span = span if gather_span is None else gather_span

    def start_of(self, step):
        bits = self.bits
        return (0, 4 * bits[0], 4 * bits[0] + 2 * bits[1], 4 * bits[0] + 2 * bits[1] + bits[2])[step]

    def copy(self, step):
        if step < 3:
            size = 4 >> step
            src = self.span(self.start_of(step) + size * (1 - self.bits[step]), size)
            dst, partner = self.inboxes[step], self.partners[step]
        else:
            size = 1 << (step - 3)
            src = dst = self.gather_span(self.start_of(6 - step), size)
            partner = self.partners[5 - step]
        return remote(src, dst, self.sent.at[step], self.came.at[step], in_plane(partner))

    def send(self, step):
        if step >= 3:
            pl.semaphore_wait(self.free.at[5 - step], 1)
        self.copy(step).start()

    def add(self, step):
        self.copy(step).wait_send()
        pl.semaphore_signal(
            self.free.at[step], inc=1, device_id=in_plane(self.partners[step]), device_id_type=MESH
        )
        self.copy(step).wait_recv()
        kept = self.span(self.start_of(step + 1), 4 >> step)
        kept[...] = (kept[...].astype(F32) + self.inboxes[step][...].astype(F32)).astype(BF16)

    def next(self, step):
        if 0 < step <= 3:
            self.add(step - 1)
        elif step > 3:
            self.copy(step - 1).wait_recv()
        if step < 6:
            self.send(step)
        else:
            self.store()

    def drain(self):
        for step in range(3, 6):
            self.copy(step).wait_send()


def turn(tensor, cosine, sine, sign):
    pieces = []
    front = lax.broadcasted_iota(jnp.int32, (1, 128), 1) % HD < HD // 2
    for at in range(0, tensor.shape[-1], 128):
        piece = tensor[:, at : at + 128]
        mixed = jnp.where(front, -pltpu.roll(piece, 96, 1), pltpu.roll(piece, 32, 1)) * sine
        pieces.append(piece * cosine + sign * mixed)
    return jnp.concatenate(pieces, axis=1)


def layer_kernel(names, sizes, *ref_list):
    r = SimpleNamespace(**dict(zip(names, ref_list)))
    count, groups, tokens, width, cols, units = sizes
    chunks = tokens // CHUNK
    share = CHUNK // count
    heads = cols // HD
    score_scale = HD ** (-0.5)
    me = lax.axis_index("mp")
    row = lax.axis_index("dp")

    core = row % 2
    along_x = (row // 2) % 2
    along_y = row // 4
    other_core = row + 1 - 2 * core
    other_x = row + 2 - 4 * along_x
    other_y = row + 4 - 8 * along_y

    loads = {}

    def load(index, src, dst):
        copy = pltpu.make_async_copy(src, dst, r.load_sem.at[index])
        copy.start()
        loads[index] = copy

    def loaded(*indices):
        for index in indices:
            loads.pop(index).wait()

    load(0, r.layer_one, r.first_in)
    load(1, r.w_value_one, r.wv1)
    load(2, r.block_input, r.x)
    load(3, r.w_query, r.wq)
    load(4, r.w_key, r.wk)
    load(5, r.w_value, r.wv)
    load(6, r.w_out, r.wo.at[me])
    load(7, r.grad_output, r.g)
    load(8, r.w_gate, r.wg)
    load(9, r.w_up, r.wu)
    load(10, r.w_down, r.wd)

    barrier = pltpu.get_barrier_semaphore()
    for step in range(1, count):
        pl.semaphore_signal(
            barrier, inc=1, device_id=on_line((me + step) % count), device_id_type=MESH
        )
    for partner in (other_core, other_x, other_y):
        pl.semaphore_signal(barrier, inc=1, device_id=in_plane(partner), device_id_type=MESH)
    pl.semaphore_wait(barrier, count - 1 + 3)

    def slot_of(ref):
        return lambda c, k: ref.at[c, k]

    def f_slot(c, k):
        return r.f_in.at[pl.ds(pl.multiple_of((c * count + k) * CHUNK, CHUNK), CHUNK)]

    first = Scatter(
        me, count, r.f_part, f_slot, r.f_meet, r.f_sent, r.f_came, r.f_met
    )
    back2 = Scatter(
        me, count, r.b_part, slot_of(r.b_in), r.b_meet, r.b_sent, r.b_came, r.b_met
    )
    out = Scatter(
        me, count, r.o_part, slot_of(r.o_in), r.o_meet, r.o_sent, r.o_came, r.o_met
    )
    back1 = Scatter(
        me, count, r.b_part, slot_of(r.b_in), r.b_meet, r.d_sent, r.d_came, r.d_met
    )
    heads_all = Gather(
        me, count, lambda c, k: r.att.at[c, k], r.att_came, r.att_right, r.att_left
    )
    values_all = Gather(
        me, count, lambda c, k: r.dv_all.at[c, k], r.dv_came, r.dv_right, r.dv_left
    )

    def rows_of(ref):
        return lambda c, k: ref.at[pl.ds(c * CHUNK + k * share, share)]

    outs_all = Gather(
        me, count, rows_of(r.output), r.out_came, r.out_right, r.out_left
    )
    gin_all = Gather(
        me, count, rows_of(r.grad_input), r.gin_came, r.gin_right, r.gin_left
    )

    def at(c):
        return pl.ds(c * CHUNK, CHUNK)

    def mine(c):
        return pl.ds(pl.multiple_of(c * CHUNK + me * share, share), share)

    piece = cols // groups
    block = core * 4 + along_x * 2 + along_y

    def wo_rows(slot, step):
        span = 1 << step
        start = pl.multiple_of((block // span) * span * piece, piece)
        return r.wo.at[slot, pl.ds(start, span * piece)]

    def wo_line():
        loaded(6)
        for step in range(1, count):
            remote(
                wo_rows(me, 0),
                wo_rows(me, 0),
                r.wo_sent.at[step],
                r.wo_came.at[step],
                on_line((me + step) % count),
            ).start()

    def wo_line_wait():
        for step in range(1, count):
            slot = wo_rows((me + count - step) % count, 0)
            copy = remote(
                slot, slot, r.wo_sent.at[step], r.wo_came.at[step], on_line(0)
            )
            copy.wait_send()
            copy.wait_recv()

    def wo_plane(step, start):
        partner = (other_y, other_x, other_core)[step]
        span = 1 << step
        for other in range(1, count):
            slot = (me + other) % count
            index = count * (step + 1) + other
            copy = remote(
                wo_rows(slot, step),
                wo_rows(slot, step),
                r.wo_sent.at[index],
                r.wo_came.at[index],
                in_plane(partner),
            )
            if start:
                copy.start()
            else:
                copy.wait_send()
                copy.wait_recv()

    def first_part(c):
        part = mul(r.first_in[at(c)], r.wv1[...])
        for k in range(count):
            r.f_part[c, k] = part[:, k * cols : (k + 1) * cols].astype(BF16)
        first.open(c)

    def window(c):
        low = max(0, c * CHUNK - REACH)
        return low, (c + 1) * CHUNK - low

    def visible(c):
        low, span = window(c)
        row_index = c * CHUNK + lax.broadcasted_iota(jnp.int32, (CHUNK, span), 0)
        col_index = low + lax.broadcasted_iota(jnp.int32, (CHUNK, span), 1)
        here = r.seg_row[:, c * CHUNK : (c + 1) * CHUNK].astype(F32)
        diagonal = lax.broadcasted_iota(jnp.int32, (CHUNK, CHUNK), 0) == (
            lax.broadcasted_iota(jnp.int32, (CHUNK, CHUNK), 1)
        )
        column = jnp.sum(jnp.where(diagonal, here, 0.0), axis=1, keepdims=True)
        same = column == r.seg_row[:, low : low + span].astype(F32)
        return same & (col_index <= row_index)

    def mask_bias(c):
        span = window(c)[1]
        r.bias[:, :span] = jnp.where(visible(c), 0.0, -1e30)

    def angle_tables(c):
        position = jnp.sum(jnp.where(visible(c), 1.0, 0.0), axis=1, keepdims=True) - 1.0
        angles = position * r.rates[...]
        r.cosine[at(c)] = jnp.cos(angles)
        r.sine[at(c)] = jnp.sin(angles)

    def project(c):
        angle_tables(c)
        x = r.x[at(c)].astype(F32)
        scale = lax.rsqrt(jnp.mean(x * x, axis=-1, keepdims=True) + EPSILON)
        normed = (x * scale * r.norm_one[...]).astype(BF16)
        r.a1[at(c)] = normed
        tables = [table[at(c)] for table in (r.cosine, r.sine)]
        queries = turn(mul(normed, r.wq[...]), *tables, 1.0)
        r.q[at(c)] = (queries.astype(BF16).astype(F32) * score_scale).astype(BF16)
        r.k[at(c)] = turn(mul(normed, r.wk[...]), *tables, 1.0).astype(BF16)

    def head_lanes(head):
        return (lax.broadcasted_iota(jnp.int32, (1, cols), 1) // HD) == head

    def only(tensor, lanes):
        return jnp.where(lanes, tensor, jnp.zeros_like(tensor))

    def attend(c):
        first.total(c, r.sum_a)
        own = mul(r.a1[at(c)], r.wv[...])
        r.vm[at(c)] = (0.5 * own + 0.5 * r.sum_a[...]).astype(BF16)
        low, span = window(c)
        mask_bias(c)
        r.sum_a[...] = jnp.zeros_like(r.sum_a)

        def one(head, carry):
            lanes = head_lanes(head)
            scores = mul(only(r.q[at(c)], lanes), r.k[low : low + span], NT)
            scores = scores + r.bias[:, :span]
            largest = jnp.max(scores, axis=-1, keepdims=True)
            raised = jnp.exp(scores - largest)
            summed = jnp.sum(raised, axis=-1, keepdims=True)
            weights = (raised * (1.0 / summed)).astype(BF16)
            r.sum_a[...] += mul(weights, only(r.vm[low : low + span], lanes))
            here = lax.broadcasted_iota(jnp.int32, (1, 128), 1) == head
            r.lse[at(c)] = jnp.where(here, largest + jnp.log(summed), r.lse[at(c)])
            return carry

        lax.fori_loop(0, heads, one, 0)
        r.att[c, me] = r.sum_a[...].astype(BF16)
        heads_all.own(c, r.att.at[c, me])

    def feed(c):
        h = r.x[at(c)].astype(F32)
        for k in range(count):
            h = h + mul(r.att[c, k], r.wo[k])
        r.big[...] = h
        r.h_own[c] = r.big[pl.ds(pl.multiple_of(me * share, share), share)]
        scale = lax.rsqrt(jnp.mean(h * h, axis=-1, keepdims=True) + EPSILON)
        normed = (h * scale * r.norm_two[...]).astype(BF16)
        r.a2[at(c)] = normed
        gate = mul(normed, r.wg[...], NT)
        up = mul(normed, r.wu[...], NT)
        sig = jax.nn.sigmoid(gate)
        silu = gate * sig
        hidden = (silu * up).astype(BF16)
        r.hid[at(c)] = hidden
        grad_hidden = mul(r.g[at(c)], r.wd[...], NT)
        grad_gate = (grad_hidden * up * sig * (1.0 + gate * (1.0 - sig))).astype(BF16)
        grad_up = (grad_hidden * silu).astype(BF16)
        r.dga[at(c)] = grad_gate
        r.dup[at(c)] = grad_up
        back = mul(grad_gate, r.wg[...]) + mul(grad_up, r.wu[...])
        r.b_part[c] = back.astype(BF16).reshape(count, share, width)
        back2.open(c)

    def down(c):
        part = mul(r.hid[at(c)], r.wd[...])
        r.o_part[c] = part.astype(BF16).reshape(count, share, width)

    def add_gain(which, grad):
        quarter = width // 4
        for j in range(4):
            r.gains[4 * which + j : 4 * which + j + 1] += grad[:, j * quarter : (j + 1) * quarter]

    def norm_back(values, gain, grad):
        scale = lax.rsqrt(jnp.mean(values * values, axis=-1, keepdims=True) + EPSILON)
        grad_gain = jnp.sum(grad * values * scale, axis=0, keepdims=True)
        scaled = grad * gain
        inner = jnp.mean(scaled * values, axis=-1, keepdims=True)
        return grad_gain, scale * scaled - values * scale * scale * scale * inner

    def through_two(c):
        back2.total(c, r.sum_b)
        grad_gain, grad = norm_back(r.h_own[c], r.norm_two[...], r.sum_b[...])
        add_gain(1, grad_gain)
        grad = r.g[mine(c)].astype(F32) + grad
        r.dh_own[c] = grad
        low = grad.astype(BF16)
        r.db_own[c] = low
        for k in range(count):
            part = mul(low, r.wo[k], NT).astype(BF16)

            @pl.when(me == k)
            def _():
                r.do[mine(c)] = part

            @pl.when(me != k)
            def _():
                r.do_part[c, k] = part
                remote(
                    r.do_part.at[c, k],
                    r.do.at[mine(c)],
                    r.do_sent.at[c, k],
                    r.do_came.at[c, (me - k + count) % count],
                    on_line(k),
                ).start()

    def do_wait(c):
        for step in range(1, count):
            source = (me + step) % count
            slot = r.do.at[
                pl.ds(pl.multiple_of(c * CHUNK + source * share, share), share)
            ]
            remote(
                slot, slot, r.do_sent.at[c, 0], r.do_came.at[c, step], on_line(0)
            ).wait_recv()

    def attend_back(c):
        do_wait(c)
        low, span = window(c)
        mask_bias(c)
        r.sum_a[...] = jnp.zeros_like(r.sum_a)

        def one(head, carry):
            lanes = head_lanes(head)
            q_head = only(r.q[at(c)], lanes)
            do_head = only(r.do[at(c)], lanes)
            here = lax.broadcasted_iota(jnp.int32, (1, 128), 1) == head
            lse = jnp.sum(jnp.where(here, r.lse[at(c)], 0.0), axis=-1, keepdims=True)
            scores = mul(q_head, r.k[low : low + span], NT) + r.bias[:, :span]
            probs = jnp.exp(scores - lse)
            grad_probs = mul(do_head, r.vm[low : low + span], NT)
            inner = jnp.sum(probs * grad_probs, axis=-1, keepdims=True)
            grad_scores = (probs * (grad_probs - inner)).astype(BF16)
            r.sum_a[...] += mul(grad_scores, only(r.k[low : low + span], lanes))
            r.dk_sum[low : low + span] += mul(grad_scores, q_head, TN)
            r.dv_sum[low : low + span] += mul(probs.astype(BF16), do_head, TN)
            return carry

        lax.fori_loop(0, heads, one, 0)
        tables = [table[at(c)] for table in (r.cosine, r.sine)]
        r.dqkv[at(c), :cols] = turn(r.sum_a[...] * score_scale, *tables, -1.0).astype(BF16)

    def values_back(c):
        tables = [table[at(c)] for table in (r.cosine, r.sine)]
        r.dqkv[at(c), cols : 2 * cols] = turn(r.dk_sum[at(c)], *tables, -1.0).astype(BF16)
        grad_values = (0.5 * r.dv_sum[at(c)]).astype(BF16)
        r.dv_all[c, me] = grad_values
        r.dqkv[at(c), 2 * cols :] = grad_values
        values_all.own(c, r.dv_all.at[c, me])

    def keys_back(c):
        back = mul(r.dqkv[at(c), :cols], r.wq[...], NT)
        back = back + mul(r.dqkv[at(c), cols : 2 * cols], r.wk[...], NT)
        back = back + mul(r.dqkv[at(c), 2 * cols :], r.wv[...], NT)
        back2.drain_one(c)
        r.b_part[c] = back.astype(BF16).reshape(count, share, width)
        back1.open(c)

    stores = []

    def local(src, dst):
        copy = pltpu.make_async_copy(src, dst, r.store_sem.at[len(stores)])
        copy.start()
        return copy

    def through_one(c):
        back1.total(c, r.sum_b)
        x = r.x[mine(c)].astype(F32)
        grad_gain, grad = norm_back(x, r.norm_one[...], r.sum_b[...])
        add_gain(0, grad_gain)
        r.b_part[c, me] = (r.dh_own[c] + grad).astype(BF16)
        gin_all.own(c, r.b_part.at[c, me])
        stores.append(local(r.b_part.at[c, me], r.grad_input.at[mine(c)]))

    def finish_out(c):
        out.total(c, r.sum_b)
        r.o_part[c, me] = (r.h_own[c] + r.sum_b[...]).astype(BF16)
        outs_all.own(c, r.o_part.at[c, me])
        stores.append(local(r.o_part.at[c, me], r.output.at[mine(c)]))

    x_first = ((other_core, other_x, other_y), (core, along_x, along_y))
    y_first = ((other_core, other_y, other_x), (core, along_y, along_x))

    def by_cols(ref, size):
        return lambda start, n: ref.at[:, pl.ds(pl.multiple_of(start * size, size), n * size)]

    def by_rows(ref, size):
        return lambda start, n: ref.at[pl.ds(pl.multiple_of(start * size, size), n * size)]

    def keep(src, dst):
        return lambda: stores.append(local(src, dst))

    eighth = width // 8
    part = cols // 8
    plane_gate = Plane(
        *x_first,
        by_cols(r.wg, eighth),
        [r.u_in0.at[0], r.u_in1.at[0], r.u_in2.at[0]],
        r.p_sent.at[0],
        r.p_came.at[0],
        r.p_free.at[0],
        keep(r.wg, r.grad_gate),
    )
    plane_up = Plane(
        *y_first,
        by_cols(r.wu, eighth),
        [r.u_in0.at[1], r.u_in1.at[1], r.u_in2.at[1]],
        r.p_sent.at[1],
        r.p_came.at[1],
        r.p_free.at[1],
        keep(r.wu, r.grad_up),
    )
    plane_down = Plane(
        *x_first,
        by_cols(r.wd, eighth),
        [r.u_in0.at[2], r.u_in1.at[2], r.u_in2.at[2]],
        r.p_sent.at[2],
        r.p_came.at[2],
        r.p_free.at[2],
        keep(r.wd, r.grad_down),
    )
    plane_out = Plane(
        *y_first,
        by_rows(r.a2, eighth),
        [
            r.g.at[pl.ds(0, 4 * eighth)],
            r.g.at[pl.ds(4 * eighth, 2 * eighth)],
            r.g.at[pl.ds(6 * eighth, eighth)],
        ],
        r.p_sent.at[3],
        r.p_came.at[3],
        r.p_free.at[3],
        keep(r.wo.at[me], r.grad_out),
        by_rows(r.wo.at[me], part),
    )
    plane_qkv = [
        Plane(
            *(x_first if index == 1 else y_first),
            by_rows(ref, eighth),
            [
                r.f_in.at[pl.ds((7 * index) * eighth, 4 * eighth)],
                r.f_in.at[pl.ds((7 * index + 4) * eighth, 2 * eighth)],
                r.f_in.at[pl.ds((7 * index + 6) * eighth, eighth)],
            ],
            r.p_sent.at[4 + index],
            r.p_came.at[4 + index],
            r.p_free.at[4 + index],
            keep(ref, grad),
        )
        for index, (ref, grad) in enumerate(
            ((r.wq, r.grad_query), (r.wk, r.grad_key), (r.wv, r.grad_value))
        )
    ]
    plane_one = Plane(
        *x_first,
        by_cols(r.wv1, eighth),
        [r.v_in0, r.v_in1, r.v_in2],
        r.p_sent.at[7],
        r.p_came.at[7],
        r.p_free.at[7],
        keep(r.wv1, r.grad_one),
    )

    def units_grad(left, right, into):
        for start in range(0, units, 256):
            span = min(256, units - start)
            into[start : start + span] = mul(left[:, start : start + span], right[...], TN).astype(
                BF16
            )

    def out_grad():
        low = r.db_own[...].reshape(tokens // count, width)
        for k in range(count):
            own = jnp.concatenate(
                [
                    r.att[c, k, pl.ds(pl.multiple_of(me * share, share), share)]
                    for c in range(chunks)
                ],
                axis=0,
            )
            grad = mul(own, low, TN).astype(BF16)
            for s in range(8):
                r.a2[s * eighth + k * part : s * eighth + (k + 1) * part] = grad[
                    s * part : (s + 1) * part
                ]

    def out_line(start):
        slot = plane_out.start_of(3)
        for step in range(1, count):
            peer = (me + step) % count
            rows = pl.ds(pl.multiple_of(slot * eighth + peer * part, part), part)
            copy = remote(
                r.a2.at[rows],
                r.z_in.at[step],
                r.z_sent.at[step],
                r.z_came.at[step],
                on_line(peer),
            )
            if start:
                copy.start()
            else:
                copy.wait_send()
                copy.wait_recv()

    def out_line_sum():
        out_line(False)
        slot = plane_out.start_of(3)
        rows = pl.ds(pl.multiple_of(slot * eighth + me * part, part), part)
        grad = r.a2[rows].astype(F32)
        for step in range(1, count):
            grad = grad + r.z_in[step].astype(F32)
        r.wo[me, pl.ds(pl.multiple_of(slot * part, part), part)] = grad.astype(BF16)
        plane_out.send(3)

    def values_one(c):
        grad = None
        for k in range(count):
            values = r.dv_all[c, k]
            piece = mul(values, r.wv1[:, k * cols : (k + 1) * cols], NT)
            grad = piece if grad is None else grad + piece
            piece = mul(r.first_in[at(c)], values, TN)
            if c > 0:
                piece = piece + r.big[:, k * cols : (k + 1) * cols]
            r.big[:, k * cols : (k + 1) * cols] = piece
        r.dk_sum[at(c)] = grad
        stores.append(local(r.dk_sum.at[at(c)], r.grad_first.at[at(c)]))

    def qkv_grad():
        for start in range(0, width, 256):
            grad = mul(r.a1[:, start : start + 256], r.dqkv[...], TN).astype(BF16)
            for index, into in enumerate((r.wq, r.wk, r.wv)):
                into[start : start + 256] = grad[:, index * cols : (index + 1) * cols]

    def grad_gate():
        units_grad(r.dga, r.a2, r.wg)

    def grad_up():
        units_grad(r.dup, r.a2, r.wu)

    def grad_down():
        units_grad(r.hid, r.g, r.wd)

    def out_line_send():
        plane_out.add(2)
        out_line(True)

    def qkv_next(step):
        for plane in plane_qkv:
            plane.next(step)

    def one_start():
        r.wv1[...] = r.big[...].astype(BF16)

    def gain_copy(step):
        if step < count:
            src, device = r.gains, on_line((me + step) % count)
        else:
            src = r.gain_sum.at[step - count]
            device = in_plane((other_core, other_x, other_y)[step - count])
        return remote(src, r.gain_in.at[step], r.gain_sent.at[step], r.gain_came.at[step], device)

    def gain_line():
        for step in range(1, count):
            gain_copy(step).start()

    def gain_plane(index):
        if index == 0:
            total = r.gains[...]
            for step in range(1, count):
                gain_copy(step).wait_recv()
                total = total + r.gain_in[step]
        else:
            gain_copy(count + index - 1).wait_recv()
            total = r.gain_sum[index - 1] + r.gain_in[count + index - 1]
        if index < 3:
            r.gain_sum[index] = total
            gain_copy(count + index).start()
        else:
            r.gain_out[...] = total

    r.gains[...] = jnp.zeros_like(r.gains)
    r.dk_sum[...] = jnp.zeros_like(r.dk_sum)
    r.dv_sum[...] = jnp.zeros_like(r.dv_sum)
    r.lse[...] = jnp.zeros_like(r.lse)
    wo_line()
    loaded(2, 3, 4, 5)
    project(0)
    loaded(0, 1)
    first_part(0)
    first.near(0, 0)
    project(1)
    wo_line_wait()
    first_part(1)
    wo_plane(0, True)
    project(2)
    first.near(0, 1)
    first.near(1, 0)
    wo_plane(0, False)
    first_part(2)
    project(3)
    wo_plane(1, True)
    first.near(1, 1)
    first.far(0)
    attend(0)
    first.far(1)
    first_part(3)
    first.near(2, 0)
    attend(1)
    wo_plane(1, False)
    loaded(7, 8, 9, 10)
    first.far(2)
    heads_all.hop(0, 1)
    wo_plane(2, True)
    first.near(3, 0)
    wo_plane(2, False)
    first.near(2, 1)
    heads_all.hop(0, 2)
    first.near(3, 1)
    first.far(3)
    heads_all.hop(1, 1)
    attend(2)
    heads_all.hop(0, 3)
    feed(0)
    heads_all.hop(1, 2)
    down(0)
    back2.near(0, 0)
    out.open(0)
    back2.near(0, 1)
    heads_all.hop(2, 1)
    attend(3)
    heads_all.hop(1, 3)
    out.near(0, 0)
    feed(1)
    heads_all.hop(2, 2)
    back2.far(0)
    out.near(0, 1)
    heads_all.hop(2, 3)
    heads_all.hop(3, 1)
    feed(2)
    back2.near(1, 0)
    heads_all.hop(3, 2)
    down(2)
    out.far(0)
    heads_all.hop(3, 3)
    through_two(0)
    back2.near(1, 1)
    back2.near(2, 0)
    feed(3)
    down(1)
    back2.near(2, 1)
    finish_out(0)
    back2.far(1)
    grad_gate()
    plane_gate.next(0)
    through_two(1)
    back2.near(3, 0)
    down(3)
    back2.far(2)
    through_two(2)
    out.open(2)
    attend_back(0)
    back2.far(3)
    back2.near(3, 1)
    plane_gate.next(1)
    outs_all.hop(0, 1)
    attend_back(1)
    through_two(3)
    out.near(2, 0)
    outs_all.hop(0, 2)
    out.open(3)
    attend_back(2)
    values_back(0)
    out.near(2, 1)
    out.far(2)
    attend_back(3)
    values_back(3)
    grad_up()
    values_back(1)
    values_back(2)
    plane_up.next(0)
    grad_down()
    finish_out(2)
    keys_back(1)
    plane_gate.next(2)
    out.near(3, 0)
    plane_down.next(0)
    values_all.hop(0, 1)
    keys_back(3)
    out_grad()
    plane_down.next(1)
    plane_up.next(1)
    values_all.hop(3, 1)
    keys_back(2)
    out.far(3)
    values_all.hop(1, 1)
    outs_all.hop(2, 1)
    values_all.hop(2, 1)
    plane_down.next(2)
    keys_back(0)
    back1.near(1, 0)
    values_all.hop(0, 2)
    plane_out.next(0)
    qkv_grad()
    plane_up.next(2)
    values_all.hop(1, 2)
    qkv_next(0)
    outs_all.hop(2, 2)
    plane_down.next(3)
    back1.near(3, 0)
    values_all.hop(0, 3)
    out.near(3, 1)
    back1.near(1, 1)
    plane_up.next(3)
    values_all.hop(3, 2)
    values_one(0)
    plane_out.next(1)
    values_all.hop(3, 3)
    values_all.hop(2, 2)
    back1.near(2, 0)
    back1.near(2, 1)
    plane_down.next(4)
    back1.far(3)
    back1.far(1)
    finish_out(3)
    qkv_next(1)
    plane_gate.next(3)
    plane_out.next(2)
    back1.near(0, 0)
    values_all.hop(1, 3)
    through_one(1)
    values_all.hop(2, 3)
    values_one(1)
    back1.near(3, 1)
    out.open(1)
    back1.far(2)
    outs_all.hop(0, 3)
    back1.far(0)
    plane_up.next(4)
    qkv_next(2)
    through_one(2)
    gin_all.hop(1, 1)
    out.near(1, 0)
    plane_gate.next(4)
    back1.near(0, 1)
    outs_all.hop(2, 3)
    outs_all.hop(3, 1)
    values_one(2)
    values_one(3)
    one_start()
    plane_up.next(5)
    gin_all.hop(1, 2)
    out.far(1)
    qkv_next(3)
    through_one(3)
    through_one(0)
    gin_all.hop(1, 3)
    plane_one.next(0)
    plane_one.next(1)
    out_line_send()
    plane_one.next(2)
    gin_all.hop(2, 1)
    qkv_next(4)
    gin_all.hop(3, 1)
    gin_all.hop(2, 2)
    plane_down.next(5)
    plane_one.next(3)
    out.near(1, 1)
    outs_all.hop(3, 2)
    plane_down.next(6)
    plane_gate.next(5)
    qkv_next(5)
    out_line_sum()
    plane_one.next(4)
    gain_line()
    plane_gate.next(6)
    gin_all.hop(3, 2)
    plane_out.next(4)
    finish_out(1)
    gin_all.hop(2, 3)
    gain_plane(0)
    gain_plane(1)
    gin_all.hop(0, 1)
    plane_out.next(5)
    plane_one.next(5)
    plane_up.next(6)
    gin_all.hop(0, 2)
    outs_all.hop(1, 1)
    qkv_next(6)
    gain_plane(2)
    gain_plane(3)
    outs_all.hop(1, 2)
    gin_all.hop(3, 3)
    gin_all.hop(0, 3)
    plane_one.next(6)
    outs_all.hop(3, 3)
    plane_out.next(6)
    outs_all.hop(1, 3)
    for copy in stores:
        copy.wait()
    for line in (first, back1, out, heads_all, values_all, outs_all, gin_all):
        line.drain(chunks)
    for plane in (plane_gate, plane_up, plane_down, plane_out, plane_one, *plane_qkv):
        plane.drain()
    for step in range(1, count + 3):
        gain_copy(step).wait_send()

    def do_drain(c, carry):
        for k in range(count):

            @pl.when(me != k)
            def _():
                slot = r.do_part.at[c, k]
                remote(
                    slot, slot, r.do_sent.at[c, k], r.do_came.at[c, 0], on_line(0)
                ).wait_send()

        return carry

    lax.fori_loop(0, chunks, do_drain, 0)


def fused_layer(arrays, sizes):
    count, groups, tokens, width, cols, units = sizes
    chunks = tokens // CHUNK
    share = CHUNK // count
    eighth = width // 8
    hbm = pl.BlockSpec(memory_space=pl.ANY)
    vmem = pl.BlockSpec(memory_space=pltpu.VMEM)
    ins = dict(
        block_input=hbm,
        layer_one=hbm,
        grad_output=hbm,
        norm_one=vmem,
        w_query=hbm,
        w_key=hbm,
        w_value=hbm,
        w_out=hbm,
        norm_two=vmem,
        w_gate=hbm,
        w_up=hbm,
        w_down=hbm,
        w_value_one=hbm,
        rates=vmem,
        seg_row=vmem,
    )
    outs = dict(
        output=((tokens, width), BF16, hbm),
        grad_input=((tokens, width), BF16, hbm),
        grad_first=((tokens, cols), F32, hbm),
        grad_query=((width, cols), BF16, hbm),
        grad_key=((width, cols), BF16, hbm),
        grad_value=((width, cols), BF16, hbm),
        grad_out=((cols, width), BF16, hbm),
        grad_gate=((units, width), BF16, hbm),
        grad_up=((units, width), BF16, hbm),
        grad_down=((units, width), BF16, hbm),
        grad_one=((cols, width), BF16, hbm),
        gain_out=((8, width // 4), F32, vmem),
    )
    dma = pltpu.SemaphoreType.DMA

    def low(*shape):
        return pltpu.VMEM(shape, BF16)

    def full(*shape):
        return pltpu.VMEM(shape, F32)

    slots = (chunks, count)
    scratch = dict(
        cosine=full(tokens, 128),
        sine=full(tokens, 128),
        x=low(tokens, width),
        g=low(tokens, width),
        first_in=low(tokens, cols),
        wq=low(width, cols),
        wk=low(width, cols),
        wv=low(width, cols),
        wv1=low(cols, width),
        wo=low(count, cols, width),
        wg=low(units, width),
        wu=low(units, width),
        wd=low(units, width),
        a1=low(tokens, width),
        a2=low(tokens, width),
        q=low(tokens, cols),
        k=low(tokens, cols),
        vm=low(tokens, cols),
        lse=full(tokens, 128),
        bias=full(CHUNK, CHUNK + REACH),
        sum_a=full(CHUNK, cols),
        sum_b=full(share, width),
        big=full(CHUNK, width),
        att=low(*slots, CHUNK, cols),
        dv_all=low(*slots, CHUNK, cols),
        hid=low(tokens, units),
        dga=low(tokens, units),
        dup=low(tokens, units),
        h_own=full(chunks, share, width),
        dh_own=full(chunks, share, width),
        db_own=low(chunks, share, width),
        do_part=low(*slots, share, cols),
        do=low(tokens, cols),
        dqkv=low(tokens, 3 * cols),
        dk_sum=full(tokens, cols),
        dv_sum=full(tokens, cols),
        gains=full(8, width // 4),
        gain_sum=full(3, 8, width // 4),
        gain_in=full(count + 3, 8, width // 4),
        u_in0=low(3, units, 4 * eighth),
        u_in1=low(3, units, 2 * eighth),
        u_in2=low(3, units, eighth),
        z_in=low(count, cols // 8, width),
        v_in0=low(cols, 4 * eighth),
        v_in1=low(cols, 2 * eighth),
        v_in2=low(cols, eighth),
        f_part=low(*slots, CHUNK, cols),
        f_in=low(chunks * count * CHUNK, cols),
        f_meet=low(chunks, CHUNK, cols),
        b_part=low(*slots, share, width),
        b_in=low(*slots, share, width),
        b_meet=low(chunks, share, width),
        o_part=low(*slots, share, width),
        o_in=low(*slots, share, width),
        o_meet=low(chunks, share, width),
        load_sem=dma((11,)),
        store_sem=dma((3 * chunks + 8,)),
        wo_sent=dma((4 * count,)),
        wo_came=dma((4 * count,)),
        do_sent=dma(slots),
        do_came=dma(slots),
        p_sent=dma((8, 6)),
        p_came=dma((8, 6)),
        p_free=pltpu.SemaphoreType.REGULAR((8, 3)),
        z_sent=dma((count,)),
        z_came=dma((count,)),
        gain_sent=dma((count + 3,)),
        gain_came=dma((count + 3,)),
        f_sent=dma(slots),
        f_came=dma(slots),
        f_met=dma((chunks,)),
        b_sent=dma(slots),
        b_came=dma(slots),
        b_met=dma((chunks,)),
        o_sent=dma(slots),
        o_came=dma(slots),
        o_met=dma((chunks,)),
        d_sent=dma(slots),
        d_came=dma(slots),
        d_met=dma((chunks,)),
        att_came=dma(slots),
        att_right=dma(slots),
        att_left=dma(slots),
        dv_came=dma(slots),
        dv_right=dma(slots),
        dv_left=dma(slots),
        out_came=dma(slots),
        out_right=dma(slots),
        out_left=dma(slots),
        gin_came=dma(slots),
        gin_right=dma(slots),
        gin_left=dma(slots),
    )
    results = pl.pallas_call(
        functools.partial(layer_kernel, [*ins, *outs, *scratch], sizes),
        out_shape=[jax.ShapeDtypeStruct(item[0], item[1]) for item in outs.values()],
        in_specs=list(ins.values()),
        out_specs=[item[2] for item in outs.values()],
        scratch_shapes=list(scratch.values()),
        compiler_params=pltpu.CompilerParams(
            collective_id=0, has_side_effects=True, vmem_limit_bytes=VMEM_LIMIT
        ),
        cost_estimate=pl.CostEstimate(
            flops=2 * 13 * 10**9, bytes_accessed=40 * 2**20, transcendentals=0
        ),
    )(*arrays)
    return widen(results)


def widen(results):
    steps = 8
    *arrays, gains = results

    def one(*refs):
        for src, dst in zip(refs[: len(arrays)], refs[len(arrays) :]):
            dst[...] = src[...].astype(dst.dtype)

    specs = []
    shapes = []
    for index, array in enumerate(arrays):
        rows, width = array.shape
        if rows % (16 * steps):
            specs.append(pl.BlockSpec((rows, width // steps), lambda i: (0, i)))
        else:
            specs.append(pl.BlockSpec((rows // steps, width), lambda i: (i, 0)))
        shapes.append(jax.ShapeDtypeStruct(array.shape, F32 if index else BF16))
    wide = pl.pallas_call(
        one,
        grid=(steps,),
        in_specs=specs,
        out_specs=specs,
        out_shape=shapes,
        compiler_params=pltpu.CompilerParams(vmem_limit_bytes=VMEM_LIMIT),
    )(*arrays)
    return (*wide, gains)

def on_device(*arguments):
    (
        block_input,
        layer_one_input,
        segment_ids,
        grad_output,
        norm_one,
        w_query,
        w_key,
        w_value,
        w_out,
        norm_two,
        w_gate,
        w_up,
        w_down,
        w_value_one,
    ) = arguments
    count = lax.axis_size("mp")
    groups = lax.axis_size("dp")
    tokens, width = block_input.shape
    cols = w_query.shape[1]
    units = w_gate.shape[1]
    fits = (
        count == 4
        and groups == 8
        and tokens == 4 * CHUNK
        and cols == 256
        and width == count * cols
        and units % 64 == 0
        and units <= 704
        and segment_ids.shape[0] == 1
    )
    if not fits:
        return by_collectives(*arguments)
    half = HD // 2
    rates = np.exp(np.arange(half, dtype=np.float32) * np.float32(-math.log(10000.0) / half))
    r = fused_layer(
        (
            block_input,
            layer_one_input,
            grad_output,
            norm_one[None, :],
            w_query,
            w_key,
            w_value,
            w_out,
            norm_two[None, :],
            w_gate.T,
            w_up.T,
            w_down,
            w_value_one,
            jnp.asarray(np.tile(rates, 4)[None, :]),
            segment_ids,
        ),
        (count, groups, tokens, width, cols, units),
    )
    (
        output,
        grad_input,
        grad_first,
        grad_query,
        grad_key,
        grad_value,
        grad_out,
        grad_gate,
        grad_up,
        grad_down,
        grad_one,
        gains,
    ) = r
    return (
        output,
        grad_input,
        grad_first,
        gains[:4].reshape(width),
        grad_query,
        grad_key,
        grad_value,
        grad_out,
        gains[4:].reshape(width),
        grad_gate.T,
        grad_up.T,
        grad_down,
        grad_one,
    )


def solution(mesh):
    return jax.shard_map(
        on_device,
        mesh=mesh,
        in_specs=(
            P("dp", None),
            P("dp", "mp"),
            P("dp", None),
            P("dp", None),
            P(),
            P(None, "mp"),
            P(None, "mp"),
            P(None, "mp"),
            P("mp", None),
            P(),
            P(None, "mp"),
            P(None, "mp"),
            P("mp", None),
            P("mp", None),
        ),
        out_specs=(
            P("dp", None),
            P("dp", None),
            P("dp", "mp"),
            P(),
            P(None, "mp"),
            P(None, "mp"),
            P(None, "mp"),
            P("mp", None),
            P(),
            P(None, "mp"),
            P(None, "mp"),
            P("mp", None),
            P("mp", None),
        ),
        check_vma=False,
    )
```

```python
import functools
import math
from types import SimpleNamespace

import jax
import jax.numpy as jnp
import numpy as np
from jax import lax
from jax.experimental import pallas as pl
from jax.experimental.pallas import tpu as pltpu
from jax.sharding import PartitionSpec as P

HD = 64


EPSILON = 1e-06
VMEM_LIMIT = 64 * 2**20 - 2**16


def positions_of(segments):
    position = lax.broadcasted_iota(jnp.int32, segments.shape, 1)
    changed = (segments[:, 1:] != segments[:, :-1]).astype(jnp.int32)
    starts = jnp.concatenate([jnp.ones_like(segments[:, :1]), changed], axis=1)
    return position - lax.cummax(position * starts, axis=1)


def rope_tables(positions, width):
    half_width = width // 2
    rates = jnp.exp(jnp.arange(half_width, dtype=jnp.float32) * (-math.log(10000.0) / half_width))
    angles = positions.astype(jnp.float32)[:, None] * rates[None, :]
    return (jnp.cos(angles)[:, None, :], jnp.sin(angles)[:, None, :])


def rotate(tensor, cosine, sine_part, turn):
    half_width = tensor.shape[-1] // 2
    left_half = tensor[..., :half_width]
    right_half = tensor[..., half_width:]
    return jnp.concatenate(
        [
            left_half * cosine - turn * right_half * sine_part,
            right_half * cosine + turn * left_half * sine_part,
        ],
        axis=-1,
    )


def over_rows(left_side, right_side):
    return lax.dot_general(
        left_side, right_side, (((0,), (0,)), ((), ())), preferred_element_type=jnp.float32
    )


def against(left_side, right_side):
    return lax.dot_general(
        left_side, right_side, (((1,), (1,)), ((), ())), preferred_element_type=jnp.float32
    )


def norm_back(activations, scale_vec, gain_vec, grad_normed):
    grad_gain = jnp.sum(grad_normed * activations * scale_vec, axis=0)
    scaled = grad_normed * gain_vec
    inner = jnp.mean(scaled * activations, axis=-1, keepdims=True)
    return (grad_gain, scale_vec * scaled - activations * scale_vec * scale_vec * scale_vec * inner)


def masked_scores(q_block, key_rows, seg_block, seg_all, first_row, score_scale):
    block_rows = q_block.shape[0]
    scores = (
        jnp.einsum("qhd,khd->hqk", q_block, key_rows, preferred_element_type=jnp.float32)
        * score_scale
    )
    row_index = first_row + lax.broadcasted_iota(jnp.int32, (block_rows, key_rows.shape[0]), 0)
    col_index = lax.broadcasted_iota(jnp.int32, (block_rows, key_rows.shape[0]), 1)
    allowed = (seg_block[:, None] == seg_all[None, :]) & (col_index <= row_index)
    return jnp.where(allowed[None], scores, -1e30)


def attend_forward(queries, key_rows, values, seg_all, score_scale):
    row_count, head_count, width = queries.shape
    block_rows = min(512, row_count)

    def one_block(block_index):
        first_row = block_index * block_rows
        q_block = lax.dynamic_slice_in_dim(queries, first_row, block_rows, 0)
        seg_block = lax.dynamic_slice_in_dim(seg_all, first_row, block_rows, 0)
        scores = masked_scores(q_block, key_rows, seg_block, seg_all, first_row, score_scale)
        largest = jnp.max(scores, axis=-1, keepdims=True)
        raised = jnp.exp(scores - largest)
        summed = jnp.sum(raised, axis=-1, keepdims=True)
        weights = (raised / summed).astype(jnp.bfloat16)
        result = jnp.einsum("hqk,khd->qhd", weights, values, preferred_element_type=jnp.float32)
        return (result, (largest + jnp.log(summed))[..., 0])

    results, log_totals = lax.map(one_block, jnp.arange(row_count // block_rows, dtype=jnp.int32))
    return (results.reshape(row_count, head_count, width), log_totals)


def attend_backward(queries, key_rows, values, seg_all, log_totals, grad_attended, score_scale):
    row_count = queries.shape[0]
    block_rows = min(512, row_count)

    def one_block(carried, block_index):
        grad_keys, grad_values = carried
        first_row = block_index * block_rows
        q_block = lax.dynamic_slice_in_dim(queries, first_row, block_rows, 0)
        seg_block = lax.dynamic_slice_in_dim(seg_all, first_row, block_rows, 0)
        grad_block = lax.dynamic_slice_in_dim(grad_attended, first_row, block_rows, 0)
        scores = masked_scores(q_block, key_rows, seg_block, seg_all, first_row, score_scale)
        probs = jnp.exp(scores - log_totals[block_index][..., None])
        grad_probs = jnp.einsum(
            "qhd,khd->hqk", grad_block, values, preferred_element_type=jnp.float32
        )
        inner = jnp.sum(probs * grad_probs, axis=-1, keepdims=True)
        grad_scores = (probs * (grad_probs - inner)).astype(jnp.bfloat16)
        grad_query = (
            jnp.einsum("hqk,khd->qhd", grad_scores, key_rows, preferred_element_type=jnp.float32)
            * score_scale
        )
        grad_keys = (
            grad_keys
            + jnp.einsum("hqk,qhd->khd", grad_scores, q_block, preferred_element_type=jnp.float32)
            * score_scale
        )
        grad_values = grad_values + jnp.einsum(
            "hqk,qhd->khd",
            probs.astype(jnp.bfloat16),
            grad_block,
            preferred_element_type=jnp.float32,
        )
        return ((grad_keys, grad_values), grad_query)

    zero_rows = jnp.zeros(key_rows.shape, jnp.float32)
    (grad_keys, grad_values), grad_queries = lax.scan(
        one_block, (zero_rows, zero_rows), jnp.arange(row_count // block_rows, dtype=jnp.int32)
    )
    return (grad_queries.reshape(key_rows.shape), grad_keys, grad_values)


def by_collectives(
    block_input,
    layer_one_input,
    segment_ids,
    grad_output,
    norm_one,
    w_query,
    w_key,
    w_value,
    w_out,
    norm_two,
    w_gate,
    w_up,
    w_down,
    w_value_one,
):
    token_count = block_input.shape[0]
    head_count = w_query.shape[1] // HD
    score_scale = HD ** (-0.5)
    seg_all = segment_ids[0]
    cosine, sine_part = rope_tables(positions_of(segment_ids)[0], HD)
    share_rows = token_count // lax.axis_size("mp")
    share_start = lax.axis_index("mp") * share_rows
    inputs = block_input.astype(jnp.float32)
    scale_one = lax.rsqrt(jnp.mean(inputs * inputs, axis=-1, keepdims=True) + EPSILON)
    normed = (inputs * scale_one * norm_one).astype(jnp.bfloat16)
    queries = jnp.dot(normed, w_query, preferred_element_type=jnp.float32).reshape(
        token_count, head_count, HD
    )
    key_rows = jnp.dot(normed, w_key, preferred_element_type=jnp.float32).reshape(
        token_count, head_count, HD
    )
    own_values = jnp.dot(normed, w_value, preferred_element_type=jnp.float32)
    first_values = lax.psum_scatter(
        jnp.dot(layer_one_input, w_value_one, preferred_element_type=jnp.float32).astype(
            jnp.bfloat16
        ),
        "mp",
        scatter_dimension=1,
        tiled=True,
    ).astype(jnp.float32)
    mixed_values = (
        (0.5 * own_values + 0.5 * first_values)
        .astype(jnp.bfloat16)
        .reshape(token_count, head_count, HD)
    )
    turned_q = rotate(queries, cosine, sine_part, 1.0).astype(jnp.bfloat16)
    turned_k = rotate(key_rows, cosine, sine_part, 1.0).astype(jnp.bfloat16)
    attended, log_totals = attend_forward(turned_q, turned_k, mixed_values, seg_all, score_scale)
    attended = attended.reshape(token_count, head_count * HD).astype(jnp.bfloat16)
    branch_one = jnp.dot(attended, w_out, preferred_element_type=jnp.float32)
    inputs_here = lax.dynamic_slice_in_dim(inputs, share_start, share_rows, 0)
    scale_one_here = lax.dynamic_slice_in_dim(scale_one, share_start, share_rows, 0)
    grad_rows = lax.dynamic_slice_in_dim(grad_output, share_start, share_rows, 0).astype(
        jnp.float32
    )
    residual = inputs_here + lax.psum_scatter(
        branch_one.astype(jnp.bfloat16), "mp", scatter_dimension=0, tiled=True
    ).astype(jnp.float32)
    scale_two = lax.rsqrt(jnp.mean(residual * residual, axis=-1, keepdims=True) + EPSILON)
    normed_two = (residual * scale_two * norm_two).astype(jnp.bfloat16)
    normed_two = lax.all_gather(normed_two, "mp", axis=0, tiled=True)
    gate_pre = jnp.dot(normed_two, w_gate, preferred_element_type=jnp.float32)
    up_pre = jnp.dot(normed_two, w_up, preferred_element_type=jnp.float32)
    sigmoid_gate = jax.nn.sigmoid(gate_pre)
    silu_gate = gate_pre * sigmoid_gate
    hidden = (silu_gate * up_pre).astype(jnp.bfloat16)
    branch_two = jnp.dot(hidden, w_down, preferred_element_type=jnp.float32)
    output_share = (
        residual
        + lax.psum_scatter(
            branch_two.astype(jnp.bfloat16), "mp", scatter_dimension=0, tiled=True
        ).astype(jnp.float32)
    ).astype(jnp.bfloat16)
    output = lax.all_gather(output_share, "mp", axis=0, tiled=True)
    grad_down = over_rows(hidden, grad_output)
    grad_hidden = against(grad_output, w_down)
    grad_gate_pre = (
        grad_hidden * up_pre * sigmoid_gate * (1.0 + gate_pre * (1.0 - sigmoid_gate))
    ).astype(jnp.bfloat16)
    grad_up_pre = (grad_hidden * silu_gate).astype(jnp.bfloat16)
    grad_gate = over_rows(normed_two, grad_gate_pre)
    grad_up = over_rows(normed_two, grad_up_pre)
    back_two = against(grad_gate_pre, w_gate) + against(grad_up_pre, w_up)
    grad_normed_two = lax.psum_scatter(
        back_two.astype(jnp.bfloat16), "mp", scatter_dimension=0, tiled=True
    ).astype(jnp.float32)
    grad_norm_two, grad_through_two = norm_back(residual, scale_two, norm_two, grad_normed_two)
    grad_residual = grad_rows + grad_through_two
    residual_low = grad_residual.astype(jnp.bfloat16)
    residual_low = lax.all_gather(residual_low, "mp", axis=0, tiled=True)
    grad_out_proj = over_rows(attended, residual_low)
    grad_attended = (
        against(residual_low, w_out).astype(jnp.bfloat16).reshape(token_count, head_count, HD)
    )
    grad_turned_q, grad_turned_k, grad_mixed = attend_backward(
        turned_q, turned_k, mixed_values, seg_all, log_totals, grad_attended, score_scale
    )
    grad_value_part = (0.5 * grad_mixed).reshape(token_count, head_count * HD).astype(jnp.bfloat16)
    grad_first_full = lax.all_gather(grad_value_part, "mp", axis=1, tiled=True)
    grad_queries = (
        rotate(grad_turned_q, cosine, sine_part, -1.0)
        .reshape(token_count, head_count * HD)
        .astype(jnp.bfloat16)
    )
    grad_keys = (
        rotate(grad_turned_k, cosine, sine_part, -1.0)
        .reshape(token_count, head_count * HD)
        .astype(jnp.bfloat16)
    )
    grad_query = over_rows(normed, grad_queries)
    grad_key = over_rows(normed, grad_keys)
    grad_value = over_rows(normed, grad_value_part)
    back_one = (
        against(grad_queries, w_query)
        + against(grad_keys, w_key)
        + against(grad_value_part, w_value)
    )
    grad_normed = lax.psum_scatter(
        back_one.astype(jnp.bfloat16), "mp", scatter_dimension=0, tiled=True
    ).astype(jnp.float32)
    grad_norm_one, grad_through_one = norm_back(inputs_here, scale_one_here, norm_one, grad_normed)
    gain_rows = jnp.concatenate([grad_norm_one, grad_norm_two])[None, :]
    grad_input, gain_all = (
        lax.all_gather(
            (grad_residual + grad_through_one).astype(jnp.bfloat16), "mp", axis=0, tiled=True
        ).astype(jnp.float32),
        lax.all_gather(gain_rows, "mp", axis=0, tiled=True),
    )
    gain_total = jnp.sum(gain_all, axis=0)
    width = norm_one.shape[0]
    grad_norm_one = gain_total[:width]
    grad_norm_two = gain_total[width:]
    grad_value_one = over_rows(layer_one_input, grad_first_full)
    grad_layer_one_input = against(grad_first_full, w_value_one)
    grad_norm_one, grad_norm_two = lax.psum((grad_norm_one, grad_norm_two), "dp")
    summed = lax.psum(
        tuple(
            part.astype(jnp.bfloat16)
            for part in (
                grad_query,
                grad_key,
                grad_value,
                grad_out_proj,
                grad_value_one,
                grad_gate,
                grad_up,
                grad_down,
            )
        ),
        "dp",
    )
    (
        grad_query,
        grad_key,
        grad_value,
        grad_out_proj,
        grad_value_one,
        grad_gate,
        grad_up,
        grad_down,
    ) = tuple(part.astype(jnp.float32) for part in summed)
    return (
        output,
        grad_input,
        grad_layer_one_input,
        grad_norm_one,
        grad_query,
        grad_key,
        grad_value,
        grad_out_proj,
        grad_norm_two,
        grad_gate,
        grad_up,
        grad_down,
        grad_value_one,
    )


NN = (((1,), (0,)), ((), ()))
NT = (((1,), (1,)), ((), ()))
TN = (((0,), (0,)), ((), ()))
F32 = jnp.float32
BF16 = jnp.bfloat16
CHUNK = 256
REACH = 512
MESH = pl.DeviceIdType.MESH


def mul(left_side, right_side, dims=NN):
    return lax.dot_general(left_side, right_side, dims, preferred_element_type=F32)


def on_line(index):
    return {"mp": index}


def in_plane(index):
    return {"dp": index}


def remote(src, dst, send_sem, recv_sem, device):
    return pltpu.make_async_remote_copy(
        src_ref=src,
        dst_ref=dst,
        send_sem=send_sem,
        recv_sem=recv_sem,
        device_id=device,
        device_id_type=MESH,
    )


class Scatter:
    def __init__(self, me, count, parts, inbox, meet, sent, came, met):
        self.me, self.count = me, count
        self.parts, self.inbox, self.meet = parts, inbox, meet
        self.sent, self.came, self.met = sent, came, met

    def take(self, c, k):
        slot = self.inbox(c, k)
        remote(slot, slot, self.sent.at[c, k], self.came.at[c, k], on_line(0)).wait_recv()
        self.parts[c, k] = (self.parts[c, k].astype(F32) + self.inbox(c, k)[...].astype(F32)).astype(
            BF16
        )

    def right(self, c, k):
        me = self.me

        @pl.when(me < k)
        def _():
            @pl.when(me > 0)
            def _():
                self.take(c, k)

            remote(
                self.parts.at[c, k],
                self.inbox(c, k),
                self.sent.at[c, k],
                self.came.at[c, k],
                on_line(me + 1),
            ).start()

    def left(self, c, k):
        me = self.me

        @pl.when(me > k)
        def _():
            @pl.when(me < self.count - 1)
            def _():
                self.take(c, k)

            @pl.when(me == k + 1)
            def _():
                remote(
                    self.parts.at[c, k],
                    self.meet.at[c],
                    self.sent.at[c, k],
                    self.met.at[c],
                    on_line(me - 1),
                ).start()

            @pl.when(me > k + 1)
            def _():
                remote(
                    self.parts.at[c, k],
                    self.inbox(c, k),
                    self.sent.at[c, k],
                    self.came.at[c, k],
                    on_line(me - 1),
                ).start()

    def rights(self, c):
        for k in range(self.count - 1, 0, -1):
            self.right(c, k)

    def lefts(self, c):
        for k in range(self.count - 1):
            self.left(c, k)

    def open(self, c):
        @pl.when(self.me == 0)
        def _():
            self.rights(c)

        @pl.when(self.me == self.count - 1)
        def _():
            self.lefts(c)

    def near(self, c, step):
        me, half = self.me, self.count // 2

        @pl.when((me > 0) & (me < half))
        def _():
            self.right(c, self.count - 1 - step)

        @pl.when((me < self.count - 1) & (me >= half))
        def _():
            self.left(c, step)

    def far(self, c):
        me, half = self.me, self.count // 2

        @pl.when((me > 0) & (me < half))
        def _():
            self.lefts(c)

        @pl.when((me < self.count - 1) & (me >= half))
        def _():
            self.rights(c)

    def total(self, c, into):
        me = self.me
        into[...] = self.parts[c, me].astype(F32)

        @pl.when(me > 0)
        def _():
            slot = self.inbox(c, me)
            remote(slot, slot, self.sent.at[c, me], self.came.at[c, me], on_line(0)).wait_recv()
            into[...] += self.inbox(c, me)[...].astype(F32)

        @pl.when(me < self.count - 1)
        def _():
            slot = self.meet.at[c]
            remote(slot, slot, self.sent.at[c, me], self.met.at[c], on_line(0)).wait_recv()
            into[...] += self.meet[c].astype(F32)

    def drain_one(self, c):
        for k in range(self.count):

            @pl.when(self.me != k)
            def _():
                slot = self.parts.at[c, k]
                remote(
                    slot, slot, self.sent.at[c, k], self.came.at[c, k], on_line(0)
                ).wait_send()

    def drain(self, chunks):
        def one(c, carry):
            self.drain_one(c)
            return carry

        lax.fori_loop(0, chunks, one, 0)


class Gather:
    def __init__(self, me, count, place, came, sent_right, sent_left):
        self.me, self.count, self.place = me, count, place
        self.came, self.sent_right, self.sent_left = came, sent_right, sent_left

    def to_right(self, c, k, src):
        return remote(
            src, self.place(c, k), self.sent_right.at[c, k], self.came.at[c, k], on_line(self.me + 1)
        )

    def to_left(self, c, k, src):
        return remote(
            src, self.place(c, k), self.sent_left.at[c, k], self.came.at[c, k], on_line(self.me - 1)
        )

    def own(self, c, src):
        me = self.me

        @pl.when(me < self.count - 1)
        def _():
            self.to_right(c, me, src).start()

        @pl.when(me > 0)
        def _():
            self.to_left(c, me, src).start()

    def wait(self, c, k):
        slot = self.place(c, k)
        remote(slot, slot, self.sent_left.at[c, k], self.came.at[c, k], on_line(0)).wait_recv()

    def hop(self, c, step):
        me = self.me

        @pl.when(me >= step)
        def _():
            k = me - step
            self.wait(c, k)

            @pl.when(me < self.count - 1)
            def _():
                self.to_right(c, k, self.place(c, k)).start()

        @pl.when(me + step < self.count)
        def _():
            k = me + step
            self.wait(c, k)

            @pl.when(me > 0)
            def _():
                self.to_left(c, k, self.place(c, k)).start()

    def drain(self, chunks):
        me = self.me

        def one(c, carry):
            for k in range(self.count):

                @pl.when((me >= k) & (me < self.count - 1))
                def _():
                    slot = self.place(c, k)
                    remote(
                        slot, slot, self.sent_right.at[c, k], self.came.at[c, k], on_line(0)
                    ).wait_send()

                @pl.when((me <= k) & (me > 0))
                def _():
                    slot = self.place(c, k)
                    remote(
                        slot, slot, self.sent_left.at[c, k], self.came.at[c, k], on_line(0)
                    ).wait_send()

            return carry

        lax.fori_loop(0, chunks, one, 0)


class Ends:
    def __init__(self, me, count, parts, inbox, sent, came):
        self.me, self.count, self.half = me, count, count // 2
        self.parts, self.inbox, self.sent, self.came = parts, inbox, sent, came

    def copy(self, c, k):
        step = 1 if k >= self.half else -1
        return remote(
            self.parts.at[c, k],
            self.inbox.at[c, k],
            self.sent.at[c, k],
            self.came.at[c, k],
            on_line(self.me + step),
        )

    def arrived(self, c, k):
        slot = self.inbox.at[c, k]
        remote(slot, slot, self.sent.at[c, k], self.came.at[c, k], on_line(0)).wait_recv()

    def open(self, c):
        @pl.when(self.me == 0)
        def _():
            for k in range(self.half, self.count):
                self.copy(c, k).start()

        @pl.when(self.me == self.count - 1)
        def _():
            for k in range(self.half):
                self.copy(c, k).start()

    def hand(self, c, k):
        self.arrived(c, k)
        self.parts[c, k] = (self.parts[c, k].astype(F32) + self.inbox[c, k].astype(F32)).astype(
            BF16
        )
        self.copy(c, k).start()

    def near(self, c, j):
        pl.when(self.me == 1)(lambda: self.hand(c, self.half + j))
        pl.when(self.me == self.count - 2)(lambda: self.hand(c, j))

    def far(self, c, j):
        pl.when(self.me == 1)(lambda: self.hand(c, j))
        pl.when(self.me == self.count - 2)(lambda: self.hand(c, self.half + j))

    def total(self, c, into):
        side = self.me // (self.count - 1)
        rows = self.parts.shape[2]
        for j in range(self.half):
            k = side * self.half + j
            self.arrived(c, k)
            into[j * rows : (j + 1) * rows] = self.parts[c, k].astype(F32) + self.inbox[
                c, k
            ].astype(F32)

    def drain_one(self, c):
        for k in range(self.count):

            @pl.when(self.me != (0 if k < self.half else self.count - 1))
            def _():
                slot = self.parts.at[c, k]
                remote(
                    slot, slot, self.sent.at[c, k], self.came.at[c, k], on_line(0)
                ).wait_send()

    def drain(self, chunks):
        def one(c, carry):
            self.drain_one(c)
            return carry

        lax.fori_loop(0, chunks, one, 0)


class EndsGather:
    def __init__(self, me, count, place, sent, came):
        self.me, self.count, self.half = me, count, count // 2
        self.place, self.sent, self.came = place, sent, came

    def copy(self, c, k, src):
        step = 1 if k < self.half else -1
        return remote(
            src,
            self.place(c, k),
            self.sent.at[c, k],
            self.came.at[c, k],
            on_line(self.me + step),
        )

    def arrived(self, c, k):
        slot = self.place(c, k)
        remote(slot, slot, self.sent.at[c, k], self.came.at[c, k], on_line(0)).wait_recv()

    def own(self, c, parts):
        @pl.when(self.me == 0)
        def _():
            for k in range(self.half):
                self.copy(c, k, parts.at[c, k]).start()

        @pl.when(self.me == self.count - 1)
        def _():
            for k in range(self.half, self.count):
                self.copy(c, k, parts.at[c, k]).start()

    def hand(self, c, k):
        self.arrived(c, k)
        self.copy(c, k, self.place(c, k)).start()

    def pass_on(self, c, j):
        pl.when(self.me == 1)(lambda: self.hand(c, j))
        pl.when(self.me == self.count - 2)(lambda: self.hand(c, self.half + j))

    def pass_far(self, c, j):
        pl.when(self.me == 1)(lambda: self.hand(c, self.half + j))
        pl.when(self.me == self.count - 2)(lambda: self.hand(c, j))

    def settle(self, c):
        @pl.when(self.me == 0)
        def _():
            for k in range(self.half, self.count):
                self.arrived(c, k)

        @pl.when(self.me == self.count - 1)
        def _():
            for k in range(self.half):
                self.arrived(c, k)

    def drain(self, chunks):
        def one(c, carry):
            for k in range(self.count):

                @pl.when(self.me != (self.count - 1 if k < self.half else 0))
                def _():
                    slot = self.place(c, k)
                    remote(
                        slot, slot, self.sent.at[c, k], self.came.at[c, k], on_line(0)
                    ).wait_send()

            return carry

        lax.fori_loop(0, chunks, one, 0)


class Plane:
    def __init__(self, partners, bits, span, inboxes, sent, came, free, store, gather_span=None):
        self.fenced = gather_span is None
        self.partners, self.bits, self.span = partners, bits, span
        self.inboxes, self.sent, self.came, self.free = inboxes, sent, came, free
        self.store = store
        self.gather_span = span if gather_span is None else gather_span

    def start_of(self, step):
        bits = self.bits
        return (0, 4 * bits[0], 4 * bits[0] + 2 * bits[1], 4 * bits[0] + 2 * bits[1] + bits[2])[step]

    def copy(self, step):
        if step < 3:
            size = 4 >> step
            src = self.span(self.start_of(step) + size * (1 - self.bits[step]), size)
            dst, partner = self.inboxes[step], self.partners[step]
        else:
            size = 1 << (step - 3)
            src = dst = self.gather_span(self.start_of(6 - step), size)
            partner = self.partners[5 - step]
        return remote(src, dst, self.sent.at[step], self.came.at[step], in_plane(partner))

    def send(self, step):
        if step >= 3 and self.fenced:
            pl.semaphore_wait(self.free.at[5 - step], 1)
        self.copy(step).start()

    def add(self, step):
        self.copy(step).wait_send()
        if self.fenced:
            pl.semaphore_signal(
                self.free.at[step],
                inc=1,
                device_id=in_plane(self.partners[step]),
                device_id_type=MESH,
            )
        self.copy(step).wait_recv()
        kept = self.span(self.start_of(step + 1), 4 >> step)
        kept[...] = (kept[...].astype(F32) + self.inboxes[step][...].astype(F32)).astype(BF16)

    def next(self, step):
        if 0 < step <= 3:
            self.add(step - 1)
        elif step > 3:
            self.copy(step - 1).wait_recv()
        if step < 6:
            self.send(step)
        else:
            self.store()

    def drain(self):
        for step in range(3, 6):
            self.copy(step).wait_send()


def turn(tensor, cosine, sine, sign):
    pieces = []
    front = lax.broadcasted_iota(jnp.int32, (1, 128), 1) % HD < HD // 2
    for at in range(0, tensor.shape[-1], 128):
        piece = tensor[:, at : at + 128]
        mixed = jnp.where(front, -pltpu.roll(piece, 96, 1), pltpu.roll(piece, 32, 1)) * sine
        pieces.append(piece * cosine + sign * mixed)
    return jnp.concatenate(pieces, axis=1)


def layer_kernel(names, sizes, *ref_list):
    r = SimpleNamespace(**dict(zip(names, ref_list)))
    count, groups, tokens, width, cols, units = sizes
    chunks = tokens // CHUNK
    share = CHUNK // count
    heads = cols // HD
    owned = CHUNK // 2
    score_scale = HD ** (-0.5)
    me = lax.axis_index("mp")
    row = lax.axis_index("dp")
    side = me // (count - 1)
    edge = (me == 0) | (me == count - 1)

    core = row % 2
    along_x = (row // 2) % 2
    along_y = row // 4
    other_core = row + 1 - 2 * core
    other_x = row + 2 - 4 * along_x
    other_y = row + 4 - 8 * along_y

    loads = {}

    def load(index, src, dst):
        copy = pltpu.make_async_copy(src, dst, r.load_sem.at[index])
        copy.start()
        loads[index] = copy

    def loaded(*indices):
        for index in indices:
            loads.pop(index).wait()

    load(0, r.layer_one, r.first_in)
    load(1, r.w_value_one, r.wv1)
    load(2, r.block_input, r.x)
    load(3, r.w_query, r.wq)
    load(4, r.w_key, r.wk)
    load(5, r.w_value, r.wv)
    load(6, r.w_out, r.wo.at[me])
    load(7, r.grad_output, r.g)
    load(8, r.w_gate, r.wg)
    load(9, r.w_up, r.wu)
    load(10, r.w_down, r.wd)

    barrier = pltpu.get_barrier_semaphore()
    for step in range(1, count):
        pl.semaphore_signal(
            barrier, inc=1, device_id=on_line((me + step) % count), device_id_type=MESH
        )
    for partner in (other_core, other_x, other_y):
        pl.semaphore_signal(barrier, inc=1, device_id=in_plane(partner), device_id_type=MESH)
    pl.semaphore_wait(barrier, count - 1 + 3)

    def f_slot(c, k):
        return r.f_in.at[pl.ds(pl.multiple_of((c * count + k) * CHUNK, CHUNK), CHUNK)]

    first = Scatter(
        me, count, r.f_part, f_slot, r.f_meet, r.f_sent, r.f_came, r.f_met
    )
    back2 = Ends(me, count, r.b_part, r.b_in, r.b_sent, r.b_came)
    out = Ends(me, count, r.o_part, r.o_in, r.o_sent, r.o_came)
    back1 = Ends(me, count, r.b_part, r.b_in, r.d_sent, r.d_came)
    heads_all = Gather(
        me, count, lambda c, k: r.att.at[c, k], r.att_came, r.att_right, r.att_left
    )
    values_all = Gather(
        me, count, lambda c, k: r.dv_all.at[c, k], r.dv_came, r.dv_right, r.dv_left
    )

    def rows_of(ref):
        return lambda c, k: ref.at[pl.ds(c * CHUNK + k * share, share)]

    outs_all = EndsGather(me, count, rows_of(r.output), r.out_sent, r.out_came)
    gin_all = EndsGather(me, count, rows_of(r.grad_input), r.gin_sent, r.gin_came)

    def at(c):
        return pl.ds(c * CHUNK, CHUNK)

    def mine(c):
        return pl.ds(pl.multiple_of(c * CHUNK + side * owned, owned), owned)

    piece = cols // groups
    block = core * 4 + along_x * 2 + along_y

    def wo_rows(slot, step):
        span = 1 << step
        start = pl.multiple_of((block // span) * span * piece, piece)
        return r.wo.at[slot, pl.ds(start, span * piece)]

    def wo_line():
        loaded(6)
        for step in range(1, count):
            remote(
                wo_rows(me, 0),
                wo_rows(me, 0),
                r.wo_sent.at[step],
                r.wo_came.at[step],
                on_line((me + step) % count),
            ).start()

    def wo_line_wait():
        for step in range(1, count):
            slot = wo_rows((me + count - step) % count, 0)
            copy = remote(
                slot, slot, r.wo_sent.at[step], r.wo_came.at[step], on_line(0)
            )
            copy.wait_send()
            copy.wait_recv()

    def wo_plane(step, start):
        partner = (other_y, other_x, other_core)[step]
        span = 1 << step
        for other in range(1, count):
            slot = (me + other) % count
            index = count * (step + 1) + other
            copy = remote(
                wo_rows(slot, step),
                wo_rows(slot, step),
                r.wo_sent.at[index],
                r.wo_came.at[index],
                in_plane(partner),
            )
            if start:
                copy.start()
            else:
                copy.wait_send()
                copy.wait_recv()

    def first_part(c):
        part = mul(r.first_in[at(c)], r.wv1[...])
        for k in range(count):
            r.f_part[c, k] = part[:, k * cols : (k + 1) * cols].astype(BF16)
        first.open(c)

    def window(c):
        low = max(0, c * CHUNK - REACH)
        return low, (c + 1) * CHUNK - low

    def visible(c):
        low, span = window(c)
        row_index = c * CHUNK + lax.broadcasted_iota(jnp.int32, (CHUNK, span), 0)
        col_index = low + lax.broadcasted_iota(jnp.int32, (CHUNK, span), 1)
        here = r.seg_row[:, c * CHUNK : (c + 1) * CHUNK].astype(F32)
        diagonal = lax.broadcasted_iota(jnp.int32, (CHUNK, CHUNK), 0) == (
            lax.broadcasted_iota(jnp.int32, (CHUNK, CHUNK), 1)
        )
        column = jnp.sum(jnp.where(diagonal, here, 0.0), axis=1, keepdims=True)
        same = column == r.seg_row[:, low : low + span].astype(F32)
        return same & (col_index <= row_index)

    def mask_bias(c):
        span = window(c)[1]
        r.bias[:, :span] = jnp.where(visible(c), 0.0, -1e30)

    def angle_tables(c):
        position = jnp.sum(jnp.where(visible(c), 1.0, 0.0), axis=1, keepdims=True) - 1.0
        angles = position * r.rates[...]
        r.cosine[at(c)] = jnp.cos(angles)
        r.sine[at(c)] = jnp.sin(angles)

    def project(c):
        angle_tables(c)
        x = r.x[at(c)].astype(F32)
        scale = lax.rsqrt(jnp.mean(x * x, axis=-1, keepdims=True) + EPSILON)
        normed = (x * scale * r.norm_one[...]).astype(BF16)
        r.a1[at(c)] = normed
        tables = [table[at(c)] for table in (r.cosine, r.sine)]
        queries = turn(mul(normed, r.wq[...]), *tables, 1.0)
        r.q[at(c)] = (queries.astype(BF16).astype(F32) * score_scale).astype(BF16)
        r.k[at(c)] = turn(mul(normed, r.wk[...]), *tables, 1.0).astype(BF16)

    def head_lanes(head):
        return (lax.broadcasted_iota(jnp.int32, (1, cols), 1) // HD) == head

    def only(tensor, lanes):
        return jnp.where(lanes, tensor, jnp.zeros_like(tensor))

    def attend(c):
        first.total(c, r.sum_a)
        own = mul(r.a1[at(c)], r.wv[...])
        r.vm[at(c)] = (0.5 * own + 0.5 * r.sum_a[...]).astype(BF16)
        low, span = window(c)
        mask_bias(c)
        r.sum_a[...] = jnp.zeros_like(r.sum_a)

        def one(head, carry):
            lanes = head_lanes(head)
            scores = mul(only(r.q[at(c)], lanes), r.k[low : low + span], NT)
            scores = scores + r.bias[:, :span]
            largest = jnp.max(scores, axis=-1, keepdims=True)
            raised = jnp.exp(scores - largest)
            summed = jnp.sum(raised, axis=-1, keepdims=True)
            weights = (raised * (1.0 / summed)).astype(BF16)
            r.sum_a[...] += mul(weights, only(r.vm[low : low + span], lanes))
            here = lax.broadcasted_iota(jnp.int32, (1, 128), 1) == head
            r.lse[at(c)] = jnp.where(here, largest + jnp.log(summed), r.lse[at(c)])
            return carry

        lax.fori_loop(0, heads, one, 0)
        r.att[c, me] = r.sum_a[...].astype(BF16)
        heads_all.own(c, r.att.at[c, me])

    def feed(c):
        h = r.x[at(c)].astype(F32)
        for k in range(count):
            h = h + mul(r.att[c, k], r.wo[k])
        r.big[...] = h
        r.h_own[c] = r.big[pl.ds(pl.multiple_of(side * owned, owned), owned)]
        scale = lax.rsqrt(jnp.mean(h * h, axis=-1, keepdims=True) + EPSILON)
        normed = (h * scale * r.norm_two[...]).astype(BF16)
        r.a2[at(c)] = normed
        gate = mul(normed, r.wg[...], NT)
        up = mul(normed, r.wu[...], NT)
        sig = jax.nn.sigmoid(gate)
        silu = gate * sig
        hidden = (silu * up).astype(BF16)
        r.hid[at(c)] = hidden
        grad_hidden = mul(r.g[at(c)], r.wd[...], NT)
        grad_gate = (grad_hidden * up * sig * (1.0 + gate * (1.0 - sig))).astype(BF16)
        grad_up = (grad_hidden * silu).astype(BF16)
        r.dga[at(c)] = grad_gate
        r.dup[at(c)] = grad_up
        back = mul(grad_gate, r.wg[...]) + mul(grad_up, r.wu[...])
        r.b_part[c] = back.astype(BF16).reshape(count, share, width)
        back2.open(c)

    def down(c):
        part = mul(r.hid[at(c)], r.wd[...])
        r.o_part[c] = part.astype(BF16).reshape(count, share, width)

    def add_gain(which, grad):
        quarter = width // 4
        for j in range(4):
            r.gains[4 * which + j : 4 * which + j + 1] += grad[:, j * quarter : (j + 1) * quarter]

    def norm_back(values, gain, grad):
        scale = lax.rsqrt(jnp.mean(values * values, axis=-1, keepdims=True) + EPSILON)
        grad_gain = jnp.sum(grad * values * scale, axis=0, keepdims=True)
        scaled = grad * gain
        inner = jnp.mean(scaled * values, axis=-1, keepdims=True)
        return grad_gain, scale * scaled - values * scale * scale * scale * inner

    def through_two(c):
        pl.when(edge)(lambda: through_two_owned(c))

    def through_two_owned(c):
        back2.total(c, r.sum_b)
        grad_gain, grad = norm_back(r.h_own[c], r.norm_two[...], r.sum_b[...])
        add_gain(1, grad_gain)
        low = (r.g[mine(c)].astype(F32) + grad).astype(BF16)
        r.db_own[c] = low
        first.drain_one(c)
        for k in range(count):
            part = mul(low, r.wo[k], NT).astype(BF16)

            @pl.when(me == k)
            def _():
                r.do[mine(c)] = part

            @pl.when(me != k)
            def _():
                r.f_part[c, k, :owned] = part
                remote(
                    r.f_part.at[c, k, pl.ds(0, owned)],
                    r.do.at[mine(c)],
                    r.do_sent.at[c, k],
                    r.do_came.at[c, side],
                    on_line(k),
                ).start()

    def do_wait(c):
        for s in range(2):

            @pl.when(me != s * (count - 1))
            def _():
                slot = r.do.at[pl.ds(c * CHUNK + s * owned, owned)]
                remote(
                    slot, slot, r.do_sent.at[c, 0], r.do_came.at[c, s], on_line(0)
                ).wait_recv()

    def attend_back(c):
        do_wait(c)
        low, span = window(c)
        mask_bias(c)
        r.sum_a[...] = jnp.zeros_like(r.sum_a)
        r.dk_sum[at(c)] = jnp.zeros((CHUNK, cols), F32)
        r.dv_sum[at(c)] = jnp.zeros((CHUNK, cols), F32)

        def one(head, carry):
            lanes = head_lanes(head)
            q_head = only(r.q[at(c)], lanes)
            do_head = only(r.do[at(c)], lanes)
            here = lax.broadcasted_iota(jnp.int32, (1, 128), 1) == head
            lse = jnp.sum(jnp.where(here, r.lse[at(c)], 0.0), axis=-1, keepdims=True)
            scores = mul(q_head, r.k[low : low + span], NT) + r.bias[:, :span]
            probs = jnp.exp(scores - lse)
            grad_probs = mul(do_head, r.vm[low : low + span], NT)
            inner = jnp.sum(probs * grad_probs, axis=-1, keepdims=True)
            grad_scores = (probs * (grad_probs - inner)).astype(BF16)
            r.sum_a[...] += mul(grad_scores, only(r.k[low : low + span], lanes))
            r.dk_sum[low : low + span] += mul(grad_scores, q_head, TN)
            r.dv_sum[low : low + span] += mul(probs.astype(BF16), do_head, TN)
            return carry

        lax.fori_loop(0, heads, one, 0)
        tables = [table[at(c)] for table in (r.cosine, r.sine)]
        r.dqkv[at(c), :cols] = turn(r.sum_a[...] * score_scale, *tables, -1.0).astype(BF16)

    def values_back(c):
        tables = [table[at(c)] for table in (r.cosine, r.sine)]
        r.dqkv[at(c), cols : 2 * cols] = turn(r.dk_sum[at(c)], *tables, -1.0).astype(BF16)
        grad_values = (0.5 * r.dv_sum[at(c)]).astype(BF16)
        r.dv_all[c, me] = grad_values
        r.dqkv[at(c), 2 * cols :] = grad_values
        values_all.own(c, r.dv_all.at[c, me])

    def keys_back(c):
        back = mul(r.dqkv[at(c), :cols], r.wq[...], NT)
        back = back + mul(r.dqkv[at(c), cols : 2 * cols], r.wk[...], NT)
        back = back + mul(r.dqkv[at(c), 2 * cols :], r.wv[...], NT)
        back2.drain_one(c)
        r.b_part[c] = back.astype(BF16).reshape(count, share, width)
        back1.open(c)

    stores = []

    def local(src, dst):
        copy = pltpu.make_async_copy(src, dst, r.store_sem.at[len(stores)])
        copy.start()
        return copy

    def own_copy(which, c, j):
        parts, dst = ((r.b_part, r.grad_input), (r.o_part, r.output))[which]
        place = pl.ds(pl.multiple_of(c * CHUNK + side * owned + j * share, share), share)
        return pltpu.make_async_copy(
            parts.at[c, side * (count // 2) + j], dst.at[place], r.own_sem.at[which, c, j]
        )

    def own_rows(which, c, parts, rows):
        for j in range(count // 2):
            parts[c, side * (count // 2) + j] = rows[j * share : (j + 1) * share]
            own_copy(which, c, j).start()

    def through_one(c):
        pl.when(edge)(lambda: through_one_owned(c))

    def through_one_owned(c):
        back1.total(c, r.sum_b)
        x = r.x[mine(c)].astype(F32)
        grad_gain, grad = norm_back(x, r.norm_one[...], r.sum_b[...])
        add_gain(0, grad_gain)
        own_rows(0, c, r.b_part, (r.db_own[c].astype(F32) + grad).astype(BF16))
        gin_all.own(c, r.b_part)

    def finish_out(c):
        pl.when(edge)(lambda: finish_out_owned(c))

    def finish_out_owned(c):
        out.total(c, r.sum_b)
        own_rows(1, c, r.o_part, (r.h_own[c] + r.sum_b[...]).astype(BF16))
        outs_all.own(c, r.o_part)

    def settle():
        for c in range(chunks):
            outs_all.settle(c)
            gin_all.settle(c)

    x_first = ((other_core, other_x, other_y), (core, along_x, along_y))
    y_first = ((other_core, other_y, other_x), (core, along_y, along_x))

    def by_cols(ref, size):
        return lambda start, n: ref.at[:, pl.ds(pl.multiple_of(start * size, size), n * size)]

    def by_rows(ref, size):
        return lambda start, n: ref.at[pl.ds(pl.multiple_of(start * size, size), n * size)]

    def keep(src, dst):
        return lambda: stores.append(local(src, dst))

    eighth = width // 8
    part = cols // 8
    plane_gate = Plane(
        *x_first,
        by_cols(r.wg, eighth),
        [r.u_in0.at[0], r.u_in1.at[0], r.u_in2.at[0]],
        r.p_sent.at[0],
        r.p_came.at[0],
        r.p_free.at[0],
        keep(r.wg, r.grad_gate),
    )
    plane_up = Plane(
        *y_first,
        by_cols(r.wu, eighth),
        [r.u_in0.at[1], r.u_in1.at[1], r.u_in2.at[1]],
        r.p_sent.at[1],
        r.p_came.at[1],
        r.p_free.at[1],
        keep(r.wu, r.grad_up),
    )
    plane_down = Plane(
        *x_first,
        by_cols(r.wd, eighth),
        [r.u_in0.at[2], r.u_in1.at[2], r.u_in2.at[2]],
        r.p_sent.at[2],
        r.p_came.at[2],
        r.p_free.at[2],
        keep(r.wd, r.grad_down),
    )
    plane_out = Plane(
        *y_first,
        by_rows(r.a2, eighth),
        [
            r.g.at[pl.ds(0, 4 * eighth)],
            r.g.at[pl.ds(4 * eighth, 2 * eighth)],
            r.g.at[pl.ds(6 * eighth, eighth)],
        ],
        r.p_sent.at[3],
        r.p_came.at[3],
        r.p_free.at[3],
        keep(r.wo.at[me], r.grad_out),
        by_rows(r.wo.at[me], part),
    )
    plane_qkv = [
        Plane(
            *(x_first if index == 1 else y_first),
            by_rows(ref, eighth),
            [
                r.f_in.at[pl.ds((7 * index) * eighth, 4 * eighth)],
                r.f_in.at[pl.ds((7 * index + 4) * eighth, 2 * eighth)],
                r.f_in.at[pl.ds((7 * index + 6) * eighth, eighth)],
            ],
            r.p_sent.at[4 + index],
            r.p_came.at[4 + index],
            r.p_free.at[4 + index],
            keep(ref, grad),
        )
        for index, (ref, grad) in enumerate(
            ((r.wq, r.grad_query), (r.wk, r.grad_key), (r.wv, r.grad_value))
        )
    ]
    plane_one = Plane(
        *x_first,
        by_cols(r.wv1, eighth),
        [r.v_in0, r.v_in1, r.v_in2],
        r.p_sent.at[7],
        r.p_came.at[7],
        r.p_free.at[7],
        keep(r.wv1, r.grad_one),
    )

    def units_grad(left, right, into):
        for start in range(0, units, 256):
            span = min(256, units - start)
            into[start : start + span] = mul(left[:, start : start + span], right[...], TN).astype(
                BF16
            )

    def out_grad():
        pl.when(edge)(out_grad_owned)

    def out_grad_owned():
        low = r.db_own[...].reshape(chunks * owned, width)
        for k in range(count):
            own = jnp.concatenate(
                [
                    r.att[c, k, pl.ds(pl.multiple_of(side * owned, owned), owned)]
                    for c in range(chunks)
                ],
                axis=0,
            )
            grad = mul(own, low, TN).astype(BF16)
            for s in range(8):
                r.a2[s * eighth + k * part : s * eighth + (k + 1) * part] = grad[
                    s * part : (s + 1) * part
                ]

    def out_next(step):
        if step < 3:
            pl.when(edge)(lambda: plane_out.next(step))
        else:
            plane_out.next(step)

    def out_piece(peer):
        slot = plane_out.start_of(3)
        return pl.ds(pl.multiple_of(slot * eighth + peer * part, part), part)

    def out_line_copy(step):
        peer = (me + step) % count
        return remote(
            r.a2.at[out_piece(peer)],
            r.z_in.at[side],
            r.z_sent.at[step],
            r.z_came.at[side],
            on_line(peer),
        )

    def out_line_send():
        @pl.when(edge)
        def _():
            plane_out.add(2)
            for step in range(1, count):
                out_line_copy(step).start()

    def out_line_sum():
        for s in range(2):

            @pl.when(me != s * (count - 1))
            def _():
                slot = r.z_in.at[s]
                remote(slot, slot, r.z_sent.at[0], r.z_came.at[s], on_line(0)).wait_recv()

        @pl.when(edge)
        def _():
            r.z_in[side] = r.a2[out_piece(me)]

        grad = r.z_in[0].astype(F32) + r.z_in[1].astype(F32)
        slot = plane_out.start_of(3)
        r.wo[me, pl.ds(pl.multiple_of(slot * part, part), part)] = grad.astype(BF16)
        plane_out.send(3)

    def values_one(c):
        grad = None
        for k in range(count):
            values = r.dv_all[c, k]
            piece = mul(values, r.wv1[:, k * cols : (k + 1) * cols], NT)
            grad = piece if grad is None else grad + piece
            piece = mul(r.first_in[at(c)], values, TN)
            if c > 0:
                piece = piece + r.big[:, k * cols : (k + 1) * cols]
            r.big[:, k * cols : (k + 1) * cols] = piece
        r.dk_sum[at(c)] = grad
        stores.append(local(r.dk_sum.at[at(c)], r.grad_first.at[at(c)]))

    def qkv_grad():
        for start in range(0, width, 256):
            grad = mul(r.a1[:, start : start + 256], r.dqkv[...], TN).astype(BF16)
            for index, into in enumerate((r.wq, r.wk, r.wv)):
                into[start : start + 256] = grad[:, index * cols : (index + 1) * cols]

    def grad_gate():
        units_grad(r.dga, r.a2, r.wg)

    def grad_up():
        units_grad(r.dup, r.a2, r.wu)

    def grad_down():
        units_grad(r.hid, r.g, r.wd)

    def qkv_next(step):
        for plane in plane_qkv:
            plane.next(step)

    def one_start():
        r.wv1[...] = r.big[...].astype(BF16)

    def gain_line_copy(step):
        return remote(
            r.gains,
            r.gain_in.at[side],
            r.gain_sent.at[2 + step],
            r.gain_came.at[side],
            on_line((me + step) % count),
        )

    def gain_copy(index):
        return remote(
            r.gain_sum.at[index],
            r.gain_in.at[2 + index],
            r.gain_sent.at[index],
            r.gain_came.at[2 + index],
            in_plane((other_core, other_x, other_y)[index]),
        )

    def gain_line():
        @pl.when(edge)
        def _():
            for step in range(1, count):
                gain_line_copy(step).start()

    def gain_plane(index):
        if index == 0:
            for s in range(2):

                @pl.when(me != s * (count - 1))
                def _():
                    slot = r.gain_in.at[s]
                    remote(
                        slot, slot, r.gain_sent.at[0], r.gain_came.at[s], on_line(0)
                    ).wait_recv()

            @pl.when(edge)
            def _():
                r.gain_in[side] = r.gains[...]

            total = r.gain_in[0] + r.gain_in[1]
        else:
            gain_copy(index - 1).wait_recv()
            total = r.gain_sum[index - 1] + r.gain_in[1 + index]
        if index < 3:
            r.gain_sum[index] = total
            gain_copy(index).start()
        else:
            r.gain_out[...] = total

    r.gains[...] = jnp.zeros_like(r.gains)
    wo_line()
    loaded(0, 1)
    first_part(0)
    loaded(2, 3, 4, 5)
    first.near(0, 0)
    wo_line_wait()
    wo_plane(0, True)
    first_part(1)
    first.near(0, 1)
    wo_plane(0, False)
    wo_plane(1, True)
    first.far(0)
    project(0)
    first_part(2)
    first.near(1, 0)
    project(1)
    first.near(1, 1)
    attend(0)
    first.far(1)
    first_part(3)
    first.near(2, 0)
    attend(1)
    wo_plane(1, False)
    first.near(2, 1)
    wo_plane(2, True)
    loaded(7, 8, 9, 10)
    first.far(2)
    project(2)
    wo_plane(2, False)
    heads_all.hop(0, 1)
    project(3)
    first.near(3, 0)
    first.near(3, 1)
    heads_all.hop(0, 2)
    attend(2)
    heads_all.hop(1, 1)
    heads_all.hop(0, 3)
    feed(0)
    first.far(3)
    down(0)
    out.open(0)
    heads_all.hop(2, 1)
    heads_all.hop(1, 2)
    back2.near(0, 0)
    attend(3)
    heads_all.hop(2, 2)
    heads_all.hop(1, 3)
    out.near(0, 0)
    feed(1)
    out.near(0, 1)
    heads_all.hop(3, 1)
    out.far(0, 0)
    back2.near(0, 1)
    heads_all.hop(2, 3)
    feed(2)
    back2.far(0, 0)
    down(2)
    back2.near(1, 0)
    back2.near(1, 1)
    heads_all.hop(3, 2)
    out.open(2)
    out.far(0, 1)
    heads_all.hop(3, 3)
    feed(3)
    down(3)
    back2.near(2, 0)
    grad_up()
    back2.far(0, 1)
    back2.far(1, 0)
    out.near(2, 0)
    back2.near(2, 1)
    out.open(3)
    grad_gate()
    back2.far(2, 0)
    out.near(2, 1)
    plane_gate.next(0)
    plane_gate.next(1)
    plane_up.next(0)
    out.far(2, 0)
    back2.far(1, 1)
    down(1)
    through_two(0)
    back2.near(3, 0)
    back2.near(3, 1)
    back2.far(2, 1)
    through_two(1)
    back2.far(3, 0)
    out.near(3, 0)
    through_two(2)
    back2.far(3, 1)
    attend_back(0)
    grad_down()
    out.far(2, 1)
    through_two(3)
    out.open(1)
    out.near(3, 1)
    out.far(3, 0)
    attend_back(1)
    attend_back(2)
    out.far(3, 1)
    values_back(0)
    attend_back(3)
    values_back(3)
    out.near(1, 0)
    values_back(1)
    values_back(2)
    plane_down.next(0)
    plane_down.next(1)
    keys_back(0)
    values_all.hop(0, 1)
    values_all.hop(1, 1)
    plane_up.next(1)
    keys_back(1)
    keys_back(3)
    values_all.hop(2, 1)
    plane_down.next(2)
    values_all.hop(3, 1)
    out.near(1, 1)
    out.far(1, 0)
    back1.near(0, 0)
    values_all.hop(2, 2)
    values_all.hop(1, 2)
    plane_down.next(3)
    keys_back(2)
    plane_gate.next(2)
    back1.near(3, 0)
    values_all.hop(0, 2)
    back1.near(1, 0)
    finish_out(2)
    back1.far(0, 0)
    plane_down.next(4)
    back1.near(0, 1)
    out_grad()
    plane_up.next(2)
    back1.far(3, 0)
    values_all.hop(3, 2)
    values_all.hop(1, 3)
    values_all.hop(0, 3)
    out_next(0)
    qkv_grad()
    qkv_next(0)
    back1.far(1, 0)
    out.far(1, 1)
    back1.near(1, 1)
    finish_out(3)
    values_all.hop(2, 3)
    back1.far(0, 1)
    out_next(1)
    back1.near(2, 0)
    back1.near(3, 1)
    finish_out(0)
    back1.near(2, 1)
    plane_up.next(3)
    outs_all.pass_on(2, 0)
    finish_out(1)
    back1.far(3, 1)
    back1.far(1, 1)
    back1.far(2, 0)
    qkv_next(1)
    outs_all.pass_on(0, 0)
    outs_all.pass_far(2, 0)
    values_one(0)
    values_all.hop(3, 3)
    through_one(1)
    through_one(0)
    outs_all.pass_on(2, 1)
    outs_all.pass_on(3, 0)
    through_one(3)
    plane_gate.next(3)
    outs_all.pass_on(3, 1)
    plane_down.next(5)
    values_one(1)
    back1.far(2, 1)
    outs_all.pass_far(3, 0)
    outs_all.pass_on(1, 0)
    values_one(2)
    qkv_next(2)
    outs_all.pass_on(0, 1)
    values_one(3)
    one_start()
    outs_all.pass_far(0, 0)
    gin_all.pass_on(1, 0)
    outs_all.pass_far(3, 1)
    out_next(2)
    plane_gate.next(4)
    plane_one.next(0)
    plane_down.next(6)
    outs_all.pass_far(0, 1)
    through_one(2)
    gin_all.pass_on(0, 0)
    outs_all.pass_far(2, 1)
    plane_up.next(4)
    gin_all.pass_on(1, 1)
    plane_one.next(1)
    outs_all.pass_far(1, 0)
    gin_all.pass_far(0, 0)
    gin_all.pass_far(1, 0)
    plane_gate.next(5)
    qkv_next(3)
    out_line_send()
    outs_all.pass_on(1, 1)
    gin_all.pass_far(1, 1)
    gin_all.pass_on(2, 0)
    qkv_next(4)
    plane_one.next(2)
    gin_all.pass_far(2, 0)
    gain_line()
    gin_all.pass_on(0, 1)
    plane_up.next(5)
    out_line_sum()
    outs_all.pass_far(1, 1)
    gin_all.pass_on(3, 0)
    gin_all.pass_far(0, 1)
    plane_one.next(3)
    gain_plane(0)
    gin_all.pass_on(2, 1)
    out_next(4)
    plane_one.next(4)
    gin_all.pass_far(3, 0)
    gain_plane(1)
    gin_all.pass_on(3, 1)
    plane_gate.next(6)
    out_next(5)
    gin_all.pass_far(2, 1)
    qkv_next(5)
    gain_plane(2)
    plane_up.next(6)
    plane_one.next(5)
    qkv_next(6)
    plane_one.next(6)
    gain_plane(3)
    out_next(6)
    gin_all.pass_far(3, 1)
    settle()
    for copy in stores:
        copy.wait()
    for line in (back1, out, heads_all, values_all, outs_all, gin_all):
        line.drain(chunks)
    for plane in (plane_gate, plane_up, plane_down, plane_out, plane_one, *plane_qkv):
        plane.drain()
    for index in range(3):
        gain_copy(index).wait_send()

    @pl.when(me != 0)
    def _():
        pl.when(me != count - 1)(lambda: first.drain(chunks))

    @pl.when(edge)
    def _():
        for which in range(2):
            for c in range(chunks):
                for j in range(count // 2):
                    own_copy(which, c, j).wait()
        for step in range(1, count):
            out_line_copy(step).wait_send()
            gain_line_copy(step).wait_send()

        def do_drain(c, carry):
            for k in range(count):

                @pl.when(me != k)
                def _():
                    slot = r.f_part.at[c, k, pl.ds(0, owned)]
                    remote(
                        slot, slot, r.do_sent.at[c, k], r.do_came.at[c, 0], on_line(0)
                    ).wait_send()

            return carry

        lax.fori_loop(0, chunks, do_drain, 0)


def fused_layer(arrays, sizes):
    count, groups, tokens, width, cols, units = sizes
    chunks = tokens // CHUNK
    share = CHUNK // count
    eighth = width // 8
    hbm = pl.BlockSpec(memory_space=pl.ANY)
    vmem = pl.BlockSpec(memory_space=pltpu.VMEM)
    ins = dict(
        block_input=hbm,
        layer_one=hbm,
        grad_output=hbm,
        norm_one=vmem,
        w_query=hbm,
        w_key=hbm,
        w_value=hbm,
        w_out=hbm,
        norm_two=vmem,
        w_gate=hbm,
        w_up=hbm,
        w_down=hbm,
        w_value_one=hbm,
        rates=vmem,
        seg_row=vmem,
    )
    outs = dict(
        output=((tokens, width), BF16, hbm),
        grad_input=((tokens, width), BF16, hbm),
        grad_first=((tokens, cols), F32, hbm),
        grad_query=((width, cols), BF16, hbm),
        grad_key=((width, cols), BF16, hbm),
        grad_value=((width, cols), BF16, hbm),
        grad_out=((cols, width), BF16, hbm),
        grad_gate=((units, width), BF16, hbm),
        grad_up=((units, width), BF16, hbm),
        grad_down=((units, width), BF16, hbm),
        grad_one=((cols, width), BF16, hbm),
        gain_out=((8, width // 4), F32, vmem),
    )
    dma = pltpu.SemaphoreType.DMA

    def low(*shape):
        return pltpu.VMEM(shape, BF16)

    def full(*shape):
        return pltpu.VMEM(shape, F32)

    slots = (chunks, count)
    scratch = dict(
        cosine=full(tokens, 128),
        sine=full(tokens, 128),
        x=low(tokens, width),
        g=low(tokens, width),
        first_in=low(tokens, cols),
        wq=low(width, cols),
        wk=low(width, cols),
        wv=low(width, cols),
        wv1=low(cols, width),
        wo=low(count, cols, width),
        wg=low(units, width),
        wu=low(units, width),
        wd=low(units, width),
        a1=low(tokens, width),
        a2=low(tokens, width),
        q=low(tokens, cols),
        k=low(tokens, cols),
        vm=low(tokens, cols),
        lse=full(tokens, 128),
        bias=full(CHUNK, CHUNK + REACH),
        sum_a=full(CHUNK, cols),
        sum_b=full(CHUNK // 2, width),
        big=full(CHUNK, width),
        att=low(*slots, CHUNK, cols),
        dv_all=low(*slots, CHUNK, cols),
        hid=low(tokens, units),
        dga=low(tokens, units),
        dup=low(tokens, units),
        h_own=full(chunks, CHUNK // 2, width),
        db_own=low(chunks, CHUNK // 2, width),
        do=low(tokens, cols),
        dqkv=low(tokens, 3 * cols),
        dk_sum=full(tokens, cols),
        dv_sum=full(tokens, cols),
        gains=full(8, width // 4),
        gain_sum=full(3, 8, width // 4),
        gain_in=full(5, 8, width // 4),
        u_in0=low(3, units, 4 * eighth),
        u_in1=low(3, units, 2 * eighth),
        u_in2=low(3, units, eighth),
        z_in=low(2, cols // 8, width),
        v_in0=low(cols, 4 * eighth),
        v_in1=low(cols, 2 * eighth),
        v_in2=low(cols, eighth),
        f_part=low(*slots, CHUNK, cols),
        f_in=low(chunks * count * CHUNK, cols),
        f_meet=low(chunks, CHUNK, cols),
        b_part=low(*slots, share, width),
        b_in=low(*slots, share, width),
        o_part=low(*slots, share, width),
        o_in=low(*slots, share, width),
        load_sem=dma((11,)),
        store_sem=dma((chunks + 8,)),
        own_sem=dma((2, chunks, count // 2)),
        wo_sent=dma((4 * count,)),
        wo_came=dma((4 * count,)),
        do_sent=dma(slots),
        do_came=dma((chunks, 2)),
        p_sent=dma((8, 6)),
        p_came=dma((8, 6)),
        p_free=pltpu.SemaphoreType.REGULAR((8, 3)),
        z_sent=dma((count,)),
        z_came=dma((2,)),
        gain_sent=dma((count + 2,)),
        gain_came=dma((5,)),
        f_sent=dma(slots),
        f_came=dma(slots),
        f_met=dma((chunks,)),
        b_sent=dma(slots),
        b_came=dma(slots),
        o_sent=dma(slots),
        o_came=dma(slots),
        d_sent=dma(slots),
        d_came=dma(slots),
        att_came=dma(slots),
        att_right=dma(slots),
        att_left=dma(slots),
        dv_came=dma(slots),
        dv_right=dma(slots),
        dv_left=dma(slots),
        out_came=dma(slots),
        out_sent=dma(slots),
        gin_came=dma(slots),
        gin_sent=dma(slots),
    )
    results = pl.pallas_call(
        functools.partial(layer_kernel, [*ins, *outs, *scratch], sizes),
        out_shape=[jax.ShapeDtypeStruct(item[0], item[1]) for item in outs.values()],
        in_specs=list(ins.values()),
        out_specs=[item[2] for item in outs.values()],
        scratch_shapes=list(scratch.values()),
        compiler_params=pltpu.CompilerParams(
            collective_id=0, has_side_effects=True, vmem_limit_bytes=VMEM_LIMIT
        ),
        cost_estimate=pl.CostEstimate(
            flops=2 * 13 * 10**9, bytes_accessed=40 * 2**20, transcendentals=0
        ),
    )(*arrays)
    return widen(results)


def widen(results):
    steps = 8
    *arrays, gains = results

    def one(*refs):
        for src, dst in zip(refs[: len(arrays)], refs[len(arrays) :]):
            dst[...] = src[...].astype(dst.dtype)

    specs = []
    shapes = []
    for index, array in enumerate(arrays):
        rows, width = array.shape
        if rows % (16 * steps):
            specs.append(pl.BlockSpec((rows, width // steps), lambda i: (0, i)))
        else:
            specs.append(pl.BlockSpec((rows // steps, width), lambda i: (i, 0)))
        shapes.append(jax.ShapeDtypeStruct(array.shape, F32 if index else BF16))
    wide = pl.pallas_call(
        one,
        grid=(steps,),
        in_specs=specs,
        out_specs=specs,
        out_shape=shapes,
        compiler_params=pltpu.CompilerParams(vmem_limit_bytes=VMEM_LIMIT),
    )(*arrays)
    return (*wide, gains)

def on_device(*arguments):
    (
        block_input,
        layer_one_input,
        segment_ids,
        grad_output,
        norm_one,
        w_query,
        w_key,
        w_value,
        w_out,
        norm_two,
        w_gate,
        w_up,
        w_down,
        w_value_one,
    ) = arguments
    count = lax.axis_size("mp")
    groups = lax.axis_size("dp")
    tokens, width = block_input.shape
    cols = w_query.shape[1]
    units = w_gate.shape[1]
    fits = (
        count == 4
        and groups == 8
        and tokens == 4 * CHUNK
        and cols == 256
        and width == count * cols
        and units % 64 == 0
        and units <= 704
        and segment_ids.shape[0] == 1
    )
    if not fits:
        return by_collectives(*arguments)
    half = HD // 2
    rates = np.exp(np.arange(half, dtype=np.float32) * np.float32(-math.log(10000.0) / half))
    r = fused_layer(
        (
            block_input,
            layer_one_input,
            grad_output,
            norm_one[None, :],
            w_query,
            w_key,
            w_value,
            w_out,
            norm_two[None, :],
            w_gate.T,
            w_up.T,
            w_down,
            w_value_one,
            jnp.asarray(np.tile(rates, 4)[None, :]),
            segment_ids,
        ),
        (count, groups, tokens, width, cols, units),
    )
    (
        output,
        grad_input,
        grad_first,
        grad_query,
        grad_key,
        grad_value,
        grad_out,
        grad_gate,
        grad_up,
        grad_down,
        grad_one,
        gains,
    ) = r
    return (
        output,
        grad_input,
        grad_first,
        gains[:4].reshape(width),
        grad_query,
        grad_key,
        grad_value,
        grad_out,
        gains[4:].reshape(width),
        grad_gate.T,
        grad_up.T,
        grad_down,
        grad_one,
    )


def solution(mesh):
    return jax.shard_map(
        on_device,
        mesh=mesh,
        in_specs=(
            P("dp", None),
            P("dp", "mp"),
            P("dp", None),
            P("dp", None),
            P(),
            P(None, "mp"),
            P(None, "mp"),
            P(None, "mp"),
            P("mp", None),
            P(),
            P(None, "mp"),
            P(None, "mp"),
            P("mp", None),
            P("mp", None),
        ),
        out_specs=(
            P("dp", None),
            P("dp", None),
            P("dp", "mp"),
            P(),
            P(None, "mp"),
            P(None, "mp"),
            P(None, "mp"),
            P("mp", None),
            P(),
            P(None, "mp"),
            P(None, "mp"),
            P("mp", None),
            P("mp", None),
        ),
        check_vma=False,
    )
```

```python
import functools
import math
from types import SimpleNamespace

import jax
import jax.numpy as jnp
import numpy as np
from jax import lax
from jax.experimental import pallas as pl
from jax.experimental.pallas import tpu as pltpu
from jax.sharding import PartitionSpec as P

HD = 64


EPSILON = 1e-06
VMEM_LIMIT = 64 * 2**20 - 2**16


def positions_of(segments):
    position = lax.broadcasted_iota(jnp.int32, segments.shape, 1)
    changed = (segments[:, 1:] != segments[:, :-1]).astype(jnp.int32)
    starts = jnp.concatenate([jnp.ones_like(segments[:, :1]), changed], axis=1)
    return position - lax.cummax(position * starts, axis=1)


def rope_tables(positions, width):
    half_width = width // 2
    rates = jnp.exp(jnp.arange(half_width, dtype=jnp.float32) * (-math.log(10000.0) / half_width))
    angles = positions.astype(jnp.float32)[:, None] * rates[None, :]
    return (jnp.cos(angles)[:, None, :], jnp.sin(angles)[:, None, :])


def rotate(tensor, cosine, sine_part, turn):
    half_width = tensor.shape[-1] // 2
    left_half = tensor[..., :half_width]
    right_half = tensor[..., half_width:]
    return jnp.concatenate(
        [
            left_half * cosine - turn * right_half * sine_part,
            right_half * cosine + turn * left_half * sine_part,
        ],
        axis=-1,
    )


def over_rows(left_side, right_side):
    return lax.dot_general(
        left_side, right_side, (((0,), (0,)), ((), ())), preferred_element_type=jnp.float32
    )


def against(left_side, right_side):
    return lax.dot_general(
        left_side, right_side, (((1,), (1,)), ((), ())), preferred_element_type=jnp.float32
    )


def norm_back(activations, scale_vec, gain_vec, grad_normed):
    grad_gain = jnp.sum(grad_normed * activations * scale_vec, axis=0)
    scaled = grad_normed * gain_vec
    inner = jnp.mean(scaled * activations, axis=-1, keepdims=True)
    return (grad_gain, scale_vec * scaled - activations * scale_vec * scale_vec * scale_vec * inner)


def masked_scores(q_block, key_rows, seg_block, seg_all, first_row, score_scale):
    block_rows = q_block.shape[0]
    scores = (
        jnp.einsum("qhd,khd->hqk", q_block, key_rows, preferred_element_type=jnp.float32)
        * score_scale
    )
    row_index = first_row + lax.broadcasted_iota(jnp.int32, (block_rows, key_rows.shape[0]), 0)
    col_index = lax.broadcasted_iota(jnp.int32, (block_rows, key_rows.shape[0]), 1)
    allowed = (seg_block[:, None] == seg_all[None, :]) & (col_index <= row_index)
    return jnp.where(allowed[None], scores, -1e30)


def attend_forward(queries, key_rows, values, seg_all, score_scale):
    row_count, head_count, width = queries.shape
    block_rows = min(512, row_count)

    def one_block(block_index):
        first_row = block_index * block_rows
        q_block = lax.dynamic_slice_in_dim(queries, first_row, block_rows, 0)
        seg_block = lax.dynamic_slice_in_dim(seg_all, first_row, block_rows, 0)
        scores = masked_scores(q_block, key_rows, seg_block, seg_all, first_row, score_scale)
        largest = jnp.max(scores, axis=-1, keepdims=True)
        raised = jnp.exp(scores - largest)
        summed = jnp.sum(raised, axis=-1, keepdims=True)
        weights = (raised / summed).astype(jnp.bfloat16)
        result = jnp.einsum("hqk,khd->qhd", weights, values, preferred_element_type=jnp.float32)
        return (result, (largest + jnp.log(summed))[..., 0])

    results, log_totals = lax.map(one_block, jnp.arange(row_count // block_rows, dtype=jnp.int32))
    return (results.reshape(row_count, head_count, width), log_totals)


def attend_backward(queries, key_rows, values, seg_all, log_totals, grad_attended, score_scale):
    row_count = queries.shape[0]
    block_rows = min(512, row_count)

    def one_block(carried, block_index):
        grad_keys, grad_values = carried
        first_row = block_index * block_rows
        q_block = lax.dynamic_slice_in_dim(queries, first_row, block_rows, 0)
        seg_block = lax.dynamic_slice_in_dim(seg_all, first_row, block_rows, 0)
        grad_block = lax.dynamic_slice_in_dim(grad_attended, first_row, block_rows, 0)
        scores = masked_scores(q_block, key_rows, seg_block, seg_all, first_row, score_scale)
        probs = jnp.exp(scores - log_totals[block_index][..., None])
        grad_probs = jnp.einsum(
            "qhd,khd->hqk", grad_block, values, preferred_element_type=jnp.float32
        )
        inner = jnp.sum(probs * grad_probs, axis=-1, keepdims=True)
        grad_scores = (probs * (grad_probs - inner)).astype(jnp.bfloat16)
        grad_query = (
            jnp.einsum("hqk,khd->qhd", grad_scores, key_rows, preferred_element_type=jnp.float32)
            * score_scale
        )
        grad_keys = (
            grad_keys
            + jnp.einsum("hqk,qhd->khd", grad_scores, q_block, preferred_element_type=jnp.float32)
            * score_scale
        )
        grad_values = grad_values + jnp.einsum(
            "hqk,qhd->khd",
            probs.astype(jnp.bfloat16),
            grad_block,
            preferred_element_type=jnp.float32,
        )
        return ((grad_keys, grad_values), grad_query)

    zero_rows = jnp.zeros(key_rows.shape, jnp.float32)
    (grad_keys, grad_values), grad_queries = lax.scan(
        one_block, (zero_rows, zero_rows), jnp.arange(row_count // block_rows, dtype=jnp.int32)
    )
    return (grad_queries.reshape(key_rows.shape), grad_keys, grad_values)


def by_collectives(
    block_input,
    layer_one_input,
    segment_ids,
    grad_output,
    norm_one,
    w_query,
    w_key,
    w_value,
    w_out,
    norm_two,
    w_gate,
    w_up,
    w_down,
    w_value_one,
):
    token_count = block_input.shape[0]
    head_count = w_query.shape[1] // HD
    score_scale = HD ** (-0.5)
    seg_all = segment_ids[0]
    cosine, sine_part = rope_tables(positions_of(segment_ids)[0], HD)
    share_rows = token_count // lax.axis_size("mp")
    share_start = lax.axis_index("mp") * share_rows
    inputs = block_input.astype(jnp.float32)
    scale_one = lax.rsqrt(jnp.mean(inputs * inputs, axis=-1, keepdims=True) + EPSILON)
    normed = (inputs * scale_one * norm_one).astype(jnp.bfloat16)
    queries = jnp.dot(normed, w_query, preferred_element_type=jnp.float32).reshape(
        token_count, head_count, HD
    )
    key_rows = jnp.dot(normed, w_key, preferred_element_type=jnp.float32).reshape(
        token_count, head_count, HD
    )
    own_values = jnp.dot(normed, w_value, preferred_element_type=jnp.float32)
    first_values = lax.psum_scatter(
        jnp.dot(layer_one_input, w_value_one, preferred_element_type=jnp.float32).astype(
            jnp.bfloat16
        ),
        "mp",
        scatter_dimension=1,
        tiled=True,
    ).astype(jnp.float32)
    mixed_values = (
        (0.5 * own_values + 0.5 * first_values)
        .astype(jnp.bfloat16)
        .reshape(token_count, head_count, HD)
    )
    turned_q = rotate(queries, cosine, sine_part, 1.0).astype(jnp.bfloat16)
    turned_k = rotate(key_rows, cosine, sine_part, 1.0).astype(jnp.bfloat16)
    attended, log_totals = attend_forward(turned_q, turned_k, mixed_values, seg_all, score_scale)
    attended = attended.reshape(token_count, head_count * HD).astype(jnp.bfloat16)
    branch_one = jnp.dot(attended, w_out, preferred_element_type=jnp.float32)
    inputs_here = lax.dynamic_slice_in_dim(inputs, share_start, share_rows, 0)
    scale_one_here = lax.dynamic_slice_in_dim(scale_one, share_start, share_rows, 0)
    grad_rows = lax.dynamic_slice_in_dim(grad_output, share_start, share_rows, 0).astype(
        jnp.float32
    )
    residual = inputs_here + lax.psum_scatter(
        branch_one.astype(jnp.bfloat16), "mp", scatter_dimension=0, tiled=True
    ).astype(jnp.float32)
    scale_two = lax.rsqrt(jnp.mean(residual * residual, axis=-1, keepdims=True) + EPSILON)
    normed_two = (residual * scale_two * norm_two).astype(jnp.bfloat16)
    normed_two = lax.all_gather(normed_two, "mp", axis=0, tiled=True)
    gate_pre = jnp.dot(normed_two, w_gate, preferred_element_type=jnp.float32)
    up_pre = jnp.dot(normed_two, w_up, preferred_element_type=jnp.float32)
    sigmoid_gate = jax.nn.sigmoid(gate_pre)
    silu_gate = gate_pre * sigmoid_gate
    hidden = (silu_gate * up_pre).astype(jnp.bfloat16)
    branch_two = jnp.dot(hidden, w_down, preferred_element_type=jnp.float32)
    output_share = (
        residual
        + lax.psum_scatter(
            branch_two.astype(jnp.bfloat16), "mp", scatter_dimension=0, tiled=True
        ).astype(jnp.float32)
    ).astype(jnp.bfloat16)
    output = lax.all_gather(output_share, "mp", axis=0, tiled=True)
    grad_down = over_rows(hidden, grad_output)
    grad_hidden = against(grad_output, w_down)
    grad_gate_pre = (
        grad_hidden * up_pre * sigmoid_gate * (1.0 + gate_pre * (1.0 - sigmoid_gate))
    ).astype(jnp.bfloat16)
    grad_up_pre = (grad_hidden * silu_gate).astype(jnp.bfloat16)
    grad_gate = over_rows(normed_two, grad_gate_pre)
    grad_up = over_rows(normed_two, grad_up_pre)
    back_two = against(grad_gate_pre, w_gate) + against(grad_up_pre, w_up)
    grad_normed_two = lax.psum_scatter(
        back_two.astype(jnp.bfloat16), "mp", scatter_dimension=0, tiled=True
    ).astype(jnp.float32)
    grad_norm_two, grad_through_two = norm_back(residual, scale_two, norm_two, grad_normed_two)
    grad_residual = grad_rows + grad_through_two
    residual_low = grad_residual.astype(jnp.bfloat16)
    residual_low = lax.all_gather(residual_low, "mp", axis=0, tiled=True)
    grad_out_proj = over_rows(attended, residual_low)
    grad_attended = (
        against(residual_low, w_out).astype(jnp.bfloat16).reshape(token_count, head_count, HD)
    )
    grad_turned_q, grad_turned_k, grad_mixed = attend_backward(
        turned_q, turned_k, mixed_values, seg_all, log_totals, grad_attended, score_scale
    )
    grad_value_part = (0.5 * grad_mixed).reshape(token_count, head_count * HD).astype(jnp.bfloat16)
    grad_first_full = lax.all_gather(grad_value_part, "mp", axis=1, tiled=True)
    grad_queries = (
        rotate(grad_turned_q, cosine, sine_part, -1.0)
        .reshape(token_count, head_count * HD)
        .astype(jnp.bfloat16)
    )
    grad_keys = (
        rotate(grad_turned_k, cosine, sine_part, -1.0)
        .reshape(token_count, head_count * HD)
        .astype(jnp.bfloat16)
    )
    grad_query = over_rows(normed, grad_queries)
    grad_key = over_rows(normed, grad_keys)
    grad_value = over_rows(normed, grad_value_part)
    back_one = (
        against(grad_queries, w_query)
        + against(grad_keys, w_key)
        + against(grad_value_part, w_value)
    )
    grad_normed = lax.psum_scatter(
        back_one.astype(jnp.bfloat16), "mp", scatter_dimension=0, tiled=True
    ).astype(jnp.float32)
    grad_norm_one, grad_through_one = norm_back(inputs_here, scale_one_here, norm_one, grad_normed)
    gain_rows = jnp.concatenate([grad_norm_one, grad_norm_two])[None, :]
    grad_input, gain_all = (
        lax.all_gather(
            (grad_residual + grad_through_one).astype(jnp.bfloat16), "mp", axis=0, tiled=True
        ).astype(jnp.float32),
        lax.all_gather(gain_rows, "mp", axis=0, tiled=True),
    )
    gain_total = jnp.sum(gain_all, axis=0)
    width = norm_one.shape[0]
    grad_norm_one = gain_total[:width]
    grad_norm_two = gain_total[width:]
    grad_value_one = over_rows(layer_one_input, grad_first_full)
    grad_layer_one_input = against(grad_first_full, w_value_one)
    grad_norm_one, grad_norm_two = lax.psum((grad_norm_one, grad_norm_two), "dp")
    summed = lax.psum(
        tuple(
            part.astype(jnp.bfloat16)
            for part in (
                grad_query,
                grad_key,
                grad_value,
                grad_out_proj,
                grad_value_one,
                grad_gate,
                grad_up,
                grad_down,
            )
        ),
        "dp",
    )
    (
        grad_query,
        grad_key,
        grad_value,
        grad_out_proj,
        grad_value_one,
        grad_gate,
        grad_up,
        grad_down,
    ) = tuple(part.astype(jnp.float32) for part in summed)
    return (
        output,
        grad_input,
        grad_layer_one_input,
        grad_norm_one,
        grad_query,
        grad_key,
        grad_value,
        grad_out_proj,
        grad_norm_two,
        grad_gate,
        grad_up,
        grad_down,
        grad_value_one,
    )


NN = (((1,), (0,)), ((), ()))
NT = (((1,), (1,)), ((), ()))
TN = (((0,), (0,)), ((), ()))
F32 = jnp.float32
BF16 = jnp.bfloat16
CHUNK = 256
REACH = 512
MESH = pl.DeviceIdType.MESH


def mul(left_side, right_side, dims=NN):
    return lax.dot_general(left_side, right_side, dims, preferred_element_type=F32)


def on_line(index):
    return {"mp": index}


def in_plane(index):
    return {"dp": index}


def remote(src, dst, send_sem, recv_sem, device):
    return pltpu.make_async_remote_copy(
        src_ref=src,
        dst_ref=dst,
        send_sem=send_sem,
        recv_sem=recv_sem,
        device_id=device,
        device_id_type=MESH,
    )


class Scatter:
    def __init__(self, me, count, parts, inbox, meet, sent, came, met):
        self.me, self.count = me, count
        self.parts, self.inbox, self.meet = parts, inbox, meet
        self.sent, self.came, self.met = sent, came, met

    def take(self, c, k):
        slot = self.inbox(c, k)
        remote(slot, slot, self.sent.at[c], self.came.at[c, k], on_line(0)).wait_recv()
        self.parts[c, k] = (self.parts[c, k].astype(F32) + self.inbox(c, k)[...].astype(F32)).astype(
            BF16
        )

    def right(self, c, k):
        me = self.me

        @pl.when(me < k)
        def _():
            @pl.when(me > 0)
            def _():
                self.take(c, k)

            remote(
                self.parts.at[c, k],
                self.inbox(c, k),
                self.sent.at[c],
                self.came.at[c, k],
                on_line(me + 1),
            ).start()

    def left(self, c, k):
        me = self.me

        @pl.when(me > k)
        def _():
            @pl.when(me < self.count - 1)
            def _():
                self.take(c, k)

            @pl.when(me == k + 1)
            def _():
                remote(
                    self.parts.at[c, k],
                    self.meet.at[c],
                    self.sent.at[c],
                    self.met.at[c],
                    on_line(me - 1),
                ).start()

            @pl.when(me > k + 1)
            def _():
                remote(
                    self.parts.at[c, k],
                    self.inbox(c, k),
                    self.sent.at[c],
                    self.came.at[c, k],
                    on_line(me - 1),
                ).start()

    def rights(self, c):
        for k in range(self.count - 1, 0, -1):
            self.right(c, k)

    def lefts(self, c):
        for k in range(self.count - 1):
            self.left(c, k)

    def open(self, c):
        @pl.when(self.me == 0)
        def _():
            self.rights(c)

        @pl.when(self.me == self.count - 1)
        def _():
            self.lefts(c)

    def near(self, c, step):
        me, half = self.me, self.count // 2

        @pl.when((me > 0) & (me < half))
        def _():
            self.right(c, self.count - 1 - step)

        @pl.when((me < self.count - 1) & (me >= half))
        def _():
            self.left(c, step)

    def far(self, c):
        me, half = self.me, self.count // 2

        @pl.when((me > 0) & (me < half))
        def _():
            self.lefts(c)

        @pl.when((me < self.count - 1) & (me >= half))
        def _():
            self.rights(c)

    def total(self, c, into):
        me = self.me
        into[...] = self.parts[c, me].astype(F32)

        @pl.when(me > 0)
        def _():
            slot = self.inbox(c, me)
            remote(slot, slot, self.sent.at[c], self.came.at[c, me], on_line(0)).wait_recv()
            into[...] += self.inbox(c, me)[...].astype(F32)

        @pl.when(me < self.count - 1)
        def _():
            slot = self.meet.at[c]
            remote(slot, slot, self.sent.at[c], self.met.at[c], on_line(0)).wait_recv()
            into[...] += self.meet[c].astype(F32)

    def drain_one(self, c):
        slots = self.parts.at[c, pl.ds(0, self.count - 1)]
        remote(slots, slots, self.sent.at[c], self.came.at[c, 0], on_line(0)).wait_send()

    def drain(self, chunks):
        def one(c, carry):
            self.drain_one(c)
            return carry

        lax.fori_loop(0, chunks, one, 0)


class Gather:
    def __init__(self, me, count, place, came, sent_right, sent_left):
        self.me, self.count, self.place = me, count, place
        self.came, self.sent_right, self.sent_left = came, sent_right, sent_left

    def to_right(self, c, k, src):
        return remote(
            src, self.place(c, k), self.sent_right.at[0], self.came.at[c, k], on_line(self.me + 1)
        )

    def to_left(self, c, k, src):
        return remote(
            src, self.place(c, k), self.sent_left.at[0], self.came.at[c, k], on_line(self.me - 1)
        )

    def own(self, c, src):
        me = self.me

        @pl.when(me < self.count - 1)
        def _():
            self.to_right(c, me, src).start()

        @pl.when(me > 0)
        def _():
            self.to_left(c, me, src).start()

    def wait(self, c, k):
        slot = self.place(c, k)
        remote(slot, slot, self.sent_left.at[0], self.came.at[c, k], on_line(0)).wait_recv()

    def hop(self, c, step):
        me = self.me

        @pl.when(me >= step)
        def _():
            k = me - step
            self.wait(c, k)

            @pl.when(me < self.count - 1)
            def _():
                self.to_right(c, k, self.place(c, k)).start()

        @pl.when(me + step < self.count)
        def _():
            k = me + step
            self.wait(c, k)

            @pl.when(me > 0)
            def _():
                self.to_left(c, k, self.place(c, k)).start()

    def drain(self, ref):
        for device in range(self.count):
            for slots, sem in (
                ((device + 1) * (device < self.count - 1), self.sent_right),
                ((self.count - device) * (device > 0), self.sent_left),
            ):
                if slots:

                    @pl.when(self.me == device)
                    def _():
                        sent = ref.at[:, pl.ds(0, slots)]
                        remote(
                            sent, sent, sem.at[0], self.came.at[0, 0], on_line(0)
                        ).wait_send()


class Ends:
    def __init__(self, me, count, parts, inbox, sent, came):
        self.me, self.count, self.half = me, count, count // 2
        self.parts, self.inbox, self.sent, self.came = parts, inbox, sent, came

    def copy(self, c, k):
        step = 1 if k >= self.half else -1
        return remote(
            self.parts.at[c, k],
            self.inbox.at[c, k],
            self.sent.at[c],
            self.came.at[c, k],
            on_line(self.me + step),
        )

    def arrived(self, c, k):
        slot = self.inbox.at[c, k]
        remote(slot, slot, self.sent.at[c], self.came.at[c, k], on_line(0)).wait_recv()

    def open(self, c):
        @pl.when(self.me == 0)
        def _():
            for k in range(self.half, self.count):
                self.copy(c, k).start()

        @pl.when(self.me == self.count - 1)
        def _():
            for k in range(self.half):
                self.copy(c, k).start()

    def hand(self, c, k):
        self.arrived(c, k)
        self.parts[c, k] = (self.parts[c, k].astype(F32) + self.inbox[c, k].astype(F32)).astype(
            BF16
        )
        self.copy(c, k).start()

    def near(self, c, j):
        pl.when(self.me == 1)(lambda: self.hand(c, self.half + j))
        pl.when(self.me == self.count - 2)(lambda: self.hand(c, j))

    def far(self, c, j):
        pl.when(self.me == 1)(lambda: self.hand(c, j))
        pl.when(self.me == self.count - 2)(lambda: self.hand(c, self.half + j))

    def total(self, c, into):
        side = self.me // (self.count - 1)
        rows = self.parts.shape[2]
        for j in range(self.half):
            k = side * self.half + j
            self.arrived(c, k)
            into[j * rows : (j + 1) * rows] = self.parts[c, k].astype(F32) + self.inbox[
                c, k
            ].astype(F32)

    def drain_one(self, c):
        edge = (self.me == 0) | (self.me == self.count - 1)

        def wait(slots):
            remote(slots, slots, self.sent.at[c], self.came.at[c, 0], on_line(0)).wait_send()

        pl.when(edge)(lambda: wait(self.parts.at[c, pl.ds(0, self.half)]))
        pl.when(jnp.logical_not(edge))(lambda: wait(self.parts.at[c]))

    def drain(self, chunks):
        def one(c, carry):
            self.drain_one(c)
            return carry

        lax.fori_loop(0, chunks, one, 0)


class EndsGather:
    def __init__(self, me, count, ref, share, sent, came):
        self.me, self.count, self.half = me, count, count // 2
        self.ref, self.share, self.sent, self.came = ref, share, sent, came

    def place(self, c, k):
        return self.ref.at[pl.ds((c * self.count + k) * self.share, self.share)]

    def copy(self, c, k, src):
        step = 1 if k < self.half else -1
        return remote(
            src,
            self.place(c, k),
            self.sent.at[c],
            self.came.at[c, k],
            on_line(self.me + step),
        )

    def arrived(self, c, k):
        slot = self.place(c, k)
        remote(slot, slot, self.sent.at[c], self.came.at[c, k], on_line(0)).wait_recv()

    def own(self, c, parts):
        @pl.when(self.me == 0)
        def _():
            for k in range(self.half):
                self.copy(c, k, parts.at[c, k]).start()

        @pl.when(self.me == self.count - 1)
        def _():
            for k in range(self.half, self.count):
                self.copy(c, k, parts.at[c, k]).start()

    def hand(self, c, k):
        self.arrived(c, k)
        self.copy(c, k, self.place(c, k)).start()

    def pass_on(self, c, j):
        pl.when(self.me == 1)(lambda: self.hand(c, j))
        pl.when(self.me == self.count - 2)(lambda: self.hand(c, self.half + j))

    def pass_far(self, c, j):
        pl.when(self.me == 1)(lambda: self.hand(c, self.half + j))
        pl.when(self.me == self.count - 2)(lambda: self.hand(c, j))

    def settle(self, c):
        @pl.when(self.me == 0)
        def _():
            for k in range(self.half, self.count):
                self.arrived(c, k)

        @pl.when(self.me == self.count - 1)
        def _():
            for k in range(self.half):
                self.arrived(c, k)

    def drain(self, chunks):
        edge = (self.me == 0) | (self.me == self.count - 1)

        def one(c, carry):
            def wait(count):
                rows = self.ref.at[pl.ds(0, count * self.share)]
                remote(rows, rows, self.sent.at[c], self.came.at[c, 0], on_line(0)).wait_send()

            pl.when(edge)(lambda: wait(self.half))
            pl.when(jnp.logical_not(edge))(lambda: wait(self.count))
            return carry

        lax.fori_loop(0, chunks, one, 0)


class Plane:
    def __init__(self, partners, bits, span, inboxes, sent, came, free, store, gather_span=None):
        self.fenced = gather_span is None
        self.partners, self.bits, self.span = partners, bits, span
        self.inboxes, self.sent, self.came, self.free = inboxes, sent, came, free
        self.store = store
        self.gather_span = span if gather_span is None else gather_span

    def start_of(self, step):
        bits = self.bits
        return (0, 4 * bits[0], 4 * bits[0] + 2 * bits[1], 4 * bits[0] + 2 * bits[1] + bits[2])[step]

    def copy(self, step):
        if step < 3:
            size = 4 >> step
            src = self.span(self.start_of(step) + size * (1 - self.bits[step]), size)
            dst, partner = self.inboxes[step], self.partners[step]
        else:
            size = 1 << (step - 3)
            src = dst = self.gather_span(self.start_of(6 - step), size)
            partner = self.partners[5 - step]
        return remote(src, dst, self.sent.at[step], self.came.at[step], in_plane(partner))

    def send(self, step):
        if step >= 3 and self.fenced:
            pl.semaphore_wait(self.free.at[5 - step], 1)
        self.copy(step).start()

    def add(self, step):
        self.copy(step).wait_send()
        if self.fenced:
            pl.semaphore_signal(
                self.free.at[step],
                inc=1,
                device_id=in_plane(self.partners[step]),
                device_id_type=MESH,
            )
        self.copy(step).wait_recv()
        kept = self.span(self.start_of(step + 1), 4 >> step)
        kept[...] = (kept[...].astype(F32) + self.inboxes[step][...].astype(F32)).astype(BF16)

    def next(self, step):
        if 0 < step <= 3:
            self.add(step - 1)
        elif step > 3:
            self.copy(step - 1).wait_recv()
        if step < 6:
            self.send(step)
        else:
            self.store()

    def drain(self):
        for step in range(3, 6):
            self.copy(step).wait_send()


def turn(tensor, cosine, sine, sign):
    pieces = []
    front = lax.broadcasted_iota(jnp.int32, (1, 128), 1) % HD < HD // 2
    for at in range(0, tensor.shape[-1], 128):
        piece = tensor[:, at : at + 128]
        mixed = jnp.where(front, -pltpu.roll(piece, 96, 1), pltpu.roll(piece, 32, 1)) * sine
        pieces.append(piece * cosine + sign * mixed)
    return jnp.concatenate(pieces, axis=1)


def layer_kernel(names, sizes, *ref_list):
    r = SimpleNamespace(**dict(zip(names, ref_list)))
    count, groups, tokens, width, cols, units = sizes
    chunks = tokens // CHUNK
    share = CHUNK // count
    heads = cols // HD
    owned = CHUNK // 2
    score_scale = HD ** (-0.5)
    me = lax.axis_index("mp")
    row = lax.axis_index("dp")
    side = me // (count - 1)
    edge = (me == 0) | (me == count - 1)

    core = row % 2
    along_x = (row // 2) % 2
    along_y = row // 4
    other_core = row + 1 - 2 * core
    other_x = row + 2 - 4 * along_x
    other_y = row + 4 - 8 * along_y

    loads = {}

    def load(index, src, dst):
        copy = pltpu.make_async_copy(src, dst, r.load_sem.at[index])
        copy.start()
        loads[index] = copy

    def loaded(*indices):
        for index in indices:
            loads.pop(index).wait()

    load(0, r.layer_one, r.first_in)
    load(1, r.w_value_one, r.wv1)
    load(11, r.norm_one_in, r.norm_one)
    load(12, r.norm_two_in, r.norm_two)
    load(13, r.rates_in, r.rates)
    load(14, r.seg_row_in, r.seg_row)
    load(2, r.block_input, r.x)
    load(3, r.w_query, r.wq)
    load(4, r.w_key, r.wk)
    load(5, r.w_value, r.wv)
    load(6, r.w_out, r.wo.at[me])
    load(7, r.grad_output, r.g)
    load(8, r.w_gate, r.wg)
    load(9, r.w_up, r.wu)
    load(10, r.w_down, r.wd)

    barrier = pltpu.get_barrier_semaphore()
    for step in range(1, count):
        pl.semaphore_signal(
            barrier, inc=1, device_id=on_line((me + step) % count), device_id_type=MESH
        )
    for partner in (other_core, other_x, other_y):
        pl.semaphore_signal(barrier, inc=1, device_id=in_plane(partner), device_id_type=MESH)
    pl.semaphore_wait(barrier, count - 1 + 3)

    def f_slot(c, k):
        return r.f_in.at[pl.ds(pl.multiple_of((c * count + k) * CHUNK, CHUNK), CHUNK)]

    loaded(0, 1)

    first = Scatter(
        me, count, r.f_part, f_slot, r.f_meet, r.f_sent, r.f_came, r.f_met
    )
    back2 = Ends(me, count, r.b_part, r.b_in, r.b_sent, r.b_came)
    out = Ends(me, count, r.o_part, r.o_in, r.o_sent, r.o_came)
    back1 = Ends(me, count, r.b_part, r.b_in, r.d_sent, r.d_came)
    heads_all = Gather(
        me, count, lambda c, k: r.att.at[c, k], r.att_came, r.att_right, r.att_left
    )
    values_all = Gather(
        me, count, lambda c, k: r.dv_all.at[c, k], r.dv_came, r.dv_right, r.dv_left
    )

    outs_all = EndsGather(me, count, r.output, share, r.out_sent, r.out_came)
    gin_all = EndsGather(me, count, r.grad_input, share, r.gin_sent, r.gin_came)

    def at(c):
        return pl.ds(c * CHUNK, CHUNK)

    def mine(c):
        return pl.ds(pl.multiple_of(c * CHUNK + side * owned, owned), owned)

    piece = cols // groups
    block = core * 4 + along_x * 2 + along_y

    def wo_rows(slot, step):
        span = 1 << step
        start = pl.multiple_of((block // span) * span * piece, piece)
        return r.wo.at[slot, pl.ds(start, span * piece)]

    def wo_line():
        loaded(6)
        for step in range(1, count):
            remote(
                wo_rows(me, 0),
                wo_rows(me, 0),
                r.wo_sent.at[0],
                r.wo_came.at[0],
                on_line((me + step) % count),
            ).start()

    def wo_wait(index, rows):
        slots = r.wo.at[pl.ds(0, count - 1), pl.ds(0, rows)]
        copy = remote(slots, slots, r.wo_sent.at[index], r.wo_came.at[index], on_line(0))
        copy.wait_send()
        copy.wait_recv()

    def wo_line_wait():
        wo_wait(0, piece)

    def wo_plane(step, start):
        if not start:
            wo_wait(step + 1, piece << step)
            return
        for other in range(1, count):
            slot = (me + other) % count
            remote(
                wo_rows(slot, step),
                wo_rows(slot, step),
                r.wo_sent.at[step + 1],
                r.wo_came.at[step + 1],
                in_plane((other_y, other_x, other_core)[step]),
            ).start()

    def first_part(c):
        part = mul(r.first_in[at(c)], r.wv1[...])
        for k in range(count):
            r.f_part[c, k] = part[:, k * cols : (k + 1) * cols].astype(BF16)
        first.open(c)

    def window(c):
        low = max(0, c * CHUNK - REACH)
        return low, (c + 1) * CHUNK - low

    def visible(c):
        low, span = window(c)
        row_index = c * CHUNK + lax.broadcasted_iota(jnp.int32, (CHUNK, span), 0)
        col_index = low + lax.broadcasted_iota(jnp.int32, (CHUNK, span), 1)
        here = r.seg_row[:, c * CHUNK : (c + 1) * CHUNK].astype(F32)
        diagonal = lax.broadcasted_iota(jnp.int32, (CHUNK, CHUNK), 0) == (
            lax.broadcasted_iota(jnp.int32, (CHUNK, CHUNK), 1)
        )
        column = jnp.sum(jnp.where(diagonal, here, 0.0), axis=1, keepdims=True)
        same = column == r.seg_row[:, low : low + span].astype(F32)
        return same & (col_index <= row_index)

    def mask_bias(c):
        span = window(c)[1]
        r.bias[:, :span] = jnp.where(visible(c), 0.0, -1e30)

    def angle_tables(c):
        position = jnp.sum(jnp.where(visible(c), 1.0, 0.0), axis=1, keepdims=True) - 1.0
        angles = position * r.rates[...]
        r.cosine[at(c)] = jnp.cos(angles)
        r.sine[at(c)] = jnp.sin(angles)

    def project(c):
        angle_tables(c)
        x = r.x[at(c)].astype(F32)
        scale = lax.rsqrt(jnp.mean(x * x, axis=-1, keepdims=True) + EPSILON)
        normed = (x * scale * r.norm_one[...]).astype(BF16)
        r.a1[at(c)] = normed
        tables = [table[at(c)] for table in (r.cosine, r.sine)]
        queries = turn(mul(normed, r.wq[...]), *tables, 1.0)
        r.q[at(c)] = (queries.astype(BF16).astype(F32) * score_scale).astype(BF16)
        r.k[at(c)] = turn(mul(normed, r.wk[...]), *tables, 1.0).astype(BF16)

    def head_lanes(head):
        return (lax.broadcasted_iota(jnp.int32, (1, cols), 1) // HD) == head

    def only(tensor, lanes):
        return jnp.where(lanes, tensor, jnp.zeros_like(tensor))

    def attend(c):
        first.total(c, r.sum_a)
        own = mul(r.a1[at(c)], r.wv[...])
        r.vm[at(c)] = (0.5 * own + 0.5 * r.sum_a[...]).astype(BF16)
        low, span = window(c)
        mask_bias(c)
        r.sum_a[...] = jnp.zeros_like(r.sum_a)

        def one(head, carry):
            lanes = head_lanes(head)
            scores = mul(only(r.q[at(c)], lanes), r.k[low : low + span], NT)
            scores = scores + r.bias[:, :span]
            largest = jnp.max(scores, axis=-1, keepdims=True)
            raised = jnp.exp(scores - largest)
            summed = jnp.sum(raised, axis=-1, keepdims=True)
            weights = (raised * (1.0 / summed)).astype(BF16)
            r.sum_a[...] += mul(weights, only(r.vm[low : low + span], lanes))
            here = lax.broadcasted_iota(jnp.int32, (1, 128), 1) == head
            r.lse[at(c)] = jnp.where(here, largest + jnp.log(summed), r.lse[at(c)])
            return carry

        lax.fori_loop(0, heads, one, 0)
        r.att[c, me] = r.sum_a[...].astype(BF16)
        heads_all.own(c, r.att.at[c, me])

    def feed(c):
        h = r.x[at(c)].astype(F32)
        for k in range(count):
            h = h + mul(r.att[c, k], r.wo[k])
        r.big[...] = h
        r.h_own[c] = r.big[pl.ds(pl.multiple_of(side * owned, owned), owned)]
        scale = lax.rsqrt(jnp.mean(h * h, axis=-1, keepdims=True) + EPSILON)
        normed = (h * scale * r.norm_two[...]).astype(BF16)
        r.a2[at(c)] = normed
        gate = mul(normed, r.wg[...], NT)
        up = mul(normed, r.wu[...], NT)
        sig = jax.nn.sigmoid(gate)
        silu = gate * sig
        hidden = (silu * up).astype(BF16)
        r.hid[at(c)] = hidden
        grad_hidden = mul(r.g[at(c)], r.wd[...], NT)
        grad_gate = (grad_hidden * up * sig * (1.0 + gate * (1.0 - sig))).astype(BF16)
        grad_up = (grad_hidden * silu).astype(BF16)
        r.dga[at(c)] = grad_gate
        r.dup[at(c)] = grad_up
        back = mul(grad_gate, r.wg[...]) + mul(grad_up, r.wu[...])
        r.b_part[c] = back.astype(BF16).reshape(count, share, width)
        back2.open(c)

    def down(c):
        part = mul(r.hid[at(c)], r.wd[...])
        r.o_part[c] = part.astype(BF16).reshape(count, share, width)

    def add_gain(which, grad):
        quarter = width // 4
        for j in range(4):
            r.gains[4 * which + j : 4 * which + j + 1] += grad[:, j * quarter : (j + 1) * quarter]

    def norm_back(values, gain, grad):
        scale = lax.rsqrt(jnp.mean(values * values, axis=-1, keepdims=True) + EPSILON)
        grad_gain = jnp.sum(grad * values * scale, axis=0, keepdims=True)
        scaled = grad * gain
        inner = jnp.mean(scaled * values, axis=-1, keepdims=True)
        return grad_gain, scale * scaled - values * scale * scale * scale * inner

    def through_two(c):
        pl.when(edge)(lambda: through_two_owned(c))

    def through_two_owned(c):
        back2.total(c, r.sum_b)
        grad_gain, grad = norm_back(r.h_own[c], r.norm_two[...], r.sum_b[...])
        add_gain(1, grad_gain)
        low = (r.g[mine(c)].astype(F32) + grad).astype(BF16)
        r.db_own[c] = low
        first.drain_one(c)
        for k in range(count):
            part = mul(low, r.wo[k], NT).astype(BF16)

            @pl.when(me == k)
            def _():
                r.do[mine(c)] = part

            @pl.when(me != k)
            def _():
                r.f_part[c, k, :owned] = part
                remote(
                    r.f_part.at[c, k, pl.ds(0, owned)],
                    r.do.at[mine(c)],
                    r.do_sent.at[0],
                    r.do_came.at[c, side],
                    on_line(k),
                ).start()

    def do_wait(c):
        for s in range(2):

            @pl.when(me != s * (count - 1))
            def _():
                slot = r.do.at[pl.ds(c * CHUNK + s * owned, owned)]
                remote(
                    slot, slot, r.do_sent.at[0], r.do_came.at[c, s], on_line(0)
                ).wait_recv()

    def attend_back(c):
        do_wait(c)
        low, span = window(c)
        mask_bias(c)
        r.sum_a[...] = jnp.zeros_like(r.sum_a)
        r.dk_sum[at(c)] = jnp.zeros((CHUNK, cols), F32)
        r.dv_sum[at(c)] = jnp.zeros((CHUNK, cols), F32)

        def one(head, carry):
            lanes = head_lanes(head)
            q_head = only(r.q[at(c)], lanes)
            do_head = only(r.do[at(c)], lanes)
            here = lax.broadcasted_iota(jnp.int32, (1, 128), 1) == head
            lse = jnp.sum(jnp.where(here, r.lse[at(c)], 0.0), axis=-1, keepdims=True)
            scores = mul(q_head, r.k[low : low + span], NT) + r.bias[:, :span]
            probs = jnp.exp(scores - lse)
            grad_probs = mul(do_head, r.vm[low : low + span], NT)
            inner = jnp.sum(probs * grad_probs, axis=-1, keepdims=True)
            grad_scores = (probs * (grad_probs - inner)).astype(BF16)
            r.sum_a[...] += mul(grad_scores, only(r.k[low : low + span], lanes))
            r.dk_sum[low : low + span] += mul(grad_scores, q_head, TN)
            r.dv_sum[low : low + span] += mul(probs.astype(BF16), do_head, TN)
            return carry

        lax.fori_loop(0, heads, one, 0)
        tables = [table[at(c)] for table in (r.cosine, r.sine)]
        r.dqkv[at(c), :cols] = turn(r.sum_a[...] * score_scale, *tables, -1.0).astype(BF16)

    def values_back(c):
        tables = [table[at(c)] for table in (r.cosine, r.sine)]
        r.dqkv[at(c), cols : 2 * cols] = turn(r.dk_sum[at(c)], *tables, -1.0).astype(BF16)
        grad_values = (0.5 * r.dv_sum[at(c)]).astype(BF16)
        r.dv_all[c, me] = grad_values
        r.dqkv[at(c), 2 * cols :] = grad_values
        values_all.own(c, r.dv_all.at[c, me])

    def keys_back(c):
        back = mul(r.dqkv[at(c), :cols], r.wq[...], NT)
        back = back + mul(r.dqkv[at(c), cols : 2 * cols], r.wk[...], NT)
        back = back + mul(r.dqkv[at(c), 2 * cols :], r.wv[...], NT)
        back2.drain_one(c)
        r.b_part[c] = back.astype(BF16).reshape(count, share, width)
        back1.open(c)

    stores = []

    def local(src, dst):
        copy = pltpu.make_async_copy(src, dst, r.store_sem.at[len(stores)])
        copy.start()
        return copy

    def own_copy(which, c, j):
        parts, dst = ((r.b_part, r.grad_input), (r.o_part, r.output))[which]
        place = pl.ds(pl.multiple_of(c * CHUNK + side * owned + j * share, share), share)
        return pltpu.make_async_copy(
            parts.at[c, side * (count // 2) + j], dst.at[place], r.own_sem.at[which]
        )

    def own_rows(which, c, parts, rows):
        for j in range(count // 2):
            parts[c, side * (count // 2) + j] = rows[j * share : (j + 1) * share]
            own_copy(which, c, j).start()

    def through_one(c):
        pl.when(edge)(lambda: through_one_owned(c))

    def through_one_owned(c):
        back1.total(c, r.sum_b)
        x = r.x[mine(c)].astype(F32)
        grad_gain, grad = norm_back(x, r.norm_one[...], r.sum_b[...])
        add_gain(0, grad_gain)
        own_rows(0, c, r.b_part, (r.db_own[c].astype(F32) + grad).astype(BF16))
        gin_all.own(c, r.b_part)

    def finish_out(c):
        pl.when(edge)(lambda: finish_out_owned(c))

    def finish_out_owned(c):
        out.total(c, r.sum_b)
        own_rows(1, c, r.o_part, (r.h_own[c] + r.sum_b[...]).astype(BF16))
        outs_all.own(c, r.o_part)

    def settle():
        for c in range(chunks):
            outs_all.settle(c)
            gin_all.settle(c)

    x_first = ((other_core, other_x, other_y), (core, along_x, along_y))
    y_first = ((other_core, other_y, other_x), (core, along_y, along_x))

    def by_cols(ref, size):
        return lambda start, n: ref.at[:, pl.ds(pl.multiple_of(start * size, size), n * size)]

    def by_rows(ref, size):
        return lambda start, n: ref.at[pl.ds(pl.multiple_of(start * size, size), n * size)]

    def keep(src, dst):
        return lambda: stores.append(local(src, dst))

    eighth = width // 8
    part = cols // 8
    plane_gate = Plane(
        *x_first,
        by_cols(r.wg, eighth),
        [r.u_in0.at[0], r.u_in1.at[0], r.u_in2.at[0]],
        r.p_sent.at[0],
        r.p_came.at[0],
        r.p_free.at[0],
        keep(r.wg, r.grad_gate),
    )
    plane_up = Plane(
        *y_first,
        by_cols(r.wu, eighth),
        [r.u_in0.at[1], r.u_in1.at[1], r.u_in2.at[1]],
        r.p_sent.at[1],
        r.p_came.at[1],
        r.p_free.at[1],
        keep(r.wu, r.grad_up),
    )
    plane_down = Plane(
        *x_first,
        by_cols(r.wd, eighth),
        [r.u_in0.at[2], r.u_in1.at[2], r.u_in2.at[2]],
        r.p_sent.at[2],
        r.p_came.at[2],
        r.p_free.at[2],
        keep(r.wd, r.grad_down),
    )
    plane_out = Plane(
        *y_first,
        by_rows(r.a2, eighth),
        [
            r.g.at[pl.ds(0, 4 * eighth)],
            r.g.at[pl.ds(4 * eighth, 2 * eighth)],
            r.g.at[pl.ds(6 * eighth, eighth)],
        ],
        r.p_sent.at[3],
        r.p_came.at[3],
        r.p_free.at[3],
        keep(r.wo.at[me], r.grad_out),
        by_rows(r.wo.at[me], part),
    )
    plane_qkv = [
        Plane(
            *(x_first if index == 1 else y_first),
            by_rows(ref, eighth),
            [
                r.f_in.at[pl.ds((7 * index) * eighth, 4 * eighth)],
                r.f_in.at[pl.ds((7 * index + 4) * eighth, 2 * eighth)],
                r.f_in.at[pl.ds((7 * index + 6) * eighth, eighth)],
            ],
            r.p_sent.at[4 + index],
            r.p_came.at[4 + index],
            r.p_free.at[4 + index],
            keep(ref, grad),
        )
        for index, (ref, grad) in enumerate(
            ((r.wq, r.grad_query), (r.wk, r.grad_key), (r.wv, r.grad_value))
        )
    ]
    plane_one = Plane(
        *x_first,
        by_cols(r.wv1, eighth),
        [r.v_in0, r.v_in1, r.v_in2],
        r.p_sent.at[7],
        r.p_came.at[7],
        r.p_free.at[7],
        keep(r.wv1, r.grad_one),
    )

    def units_grad(left, right, into):
        for start in range(0, units, 256):
            span = min(256, units - start)
            into[start : start + span] = mul(left[:, start : start + span], right[...], TN).astype(
                BF16
            )

    def out_grad():
        pl.when(edge)(out_grad_owned)

    def out_grad_owned():
        low = r.db_own[...].reshape(chunks * owned, width)
        for k in range(count):
            own = jnp.concatenate(
                [
                    r.att[c, k, pl.ds(pl.multiple_of(side * owned, owned), owned)]
                    for c in range(chunks)
                ],
                axis=0,
            )
            grad = mul(own, low, TN).astype(BF16)
            for s in range(8):
                r.a2[s * eighth + k * part : s * eighth + (k + 1) * part] = grad[
                    s * part : (s + 1) * part
                ]

    def out_next(step):
        if step < 3:
            pl.when(edge)(lambda: plane_out.next(step))
        else:
            plane_out.next(step)

    def out_piece(peer):
        slot = plane_out.start_of(3)
        return pl.ds(pl.multiple_of(slot * eighth + peer * part, part), part)

    def out_line_copy(step):
        peer = (me + step) % count
        return remote(
            r.a2.at[out_piece(peer)],
            r.z_in.at[side],
            r.z_sent.at[step],
            r.z_came.at[side],
            on_line(peer),
        )

    def out_line_send():
        @pl.when(edge)
        def _():
            plane_out.add(2)
            for step in range(1, count):
                out_line_copy(step).start()

    def out_line_sum():
        for s in range(2):

            @pl.when(me != s * (count - 1))
            def _():
                slot = r.z_in.at[s]
                remote(slot, slot, r.z_sent.at[0], r.z_came.at[s], on_line(0)).wait_recv()

        @pl.when(edge)
        def _():
            r.z_in[side] = r.a2[out_piece(me)]

        grad = r.z_in[0].astype(F32) + r.z_in[1].astype(F32)
        slot = plane_out.start_of(3)
        r.wo[me, pl.ds(pl.multiple_of(slot * part, part), part)] = grad.astype(BF16)
        plane_out.send(3)

    def values_one(c):
        grad = None
        for k in range(count):
            values = r.dv_all[c, k]
            piece = mul(values, r.wv1[:, k * cols : (k + 1) * cols], NT)
            grad = piece if grad is None else grad + piece
            piece = mul(r.first_in[at(c)], values, TN)
            if c > 0:
                piece = piece + r.big[:, k * cols : (k + 1) * cols]
            r.big[:, k * cols : (k + 1) * cols] = piece
        r.dk_sum[at(c)] = grad
        stores.append(local(r.dk_sum.at[at(c)], r.grad_first.at[at(c)]))

    def qkv_grad():
        for start in range(0, width, 256):
            grad = mul(r.a1[:, start : start + 256], r.dqkv[...], TN).astype(BF16)
            for index, into in enumerate((r.wq, r.wk, r.wv)):
                into[start : start + 256] = grad[:, index * cols : (index + 1) * cols]

    def grad_gate():
        units_grad(r.dga, r.a2, r.wg)

    def grad_up():
        units_grad(r.dup, r.a2, r.wu)

    def grad_down():
        units_grad(r.hid, r.g, r.wd)

    def qkv_next(step):
        for plane in plane_qkv:
            plane.next(step)

    def one_start():
        r.wv1[...] = r.big[...].astype(BF16)

    def gain_line_copy(step):
        return remote(
            r.gains,
            r.gain_in.at[side],
            r.gain_sent.at[2 + step],
            r.gain_came.at[side],
            on_line((me + step) % count),
        )

    def gain_copy(index):
        return remote(
            r.gain_sum.at[index],
            r.gain_in.at[2 + index],
            r.gain_sent.at[index],
            r.gain_came.at[2 + index],
            in_plane((other_core, other_x, other_y)[index]),
        )

    def gain_line():
        @pl.when(edge)
        def _():
            for step in range(1, count):
                gain_line_copy(step).start()

    def gain_plane(index):
        if index == 0:
            for s in range(2):

                @pl.when(me != s * (count - 1))
                def _():
                    slot = r.gain_in.at[s]
                    remote(
                        slot, slot, r.gain_sent.at[0], r.gain_came.at[s], on_line(0)
                    ).wait_recv()

            @pl.when(edge)
            def _():
                r.gain_in[side] = r.gains[...]

            total = r.gain_in[0] + r.gain_in[1]
        else:
            gain_copy(index - 1).wait_recv()
            total = r.gain_sum[index - 1] + r.gain_in[1 + index]
        if index < 3:
            r.gain_sum[index] = total
            gain_copy(index).start()
        else:
            for which, into in enumerate((r.gain_one, r.gain_two)):
                into[...] = jnp.concatenate(
                    [total[4 * which + j : 4 * which + j + 1] for j in range(4)], axis=1
                )

    r.gains[...] = jnp.zeros_like(r.gains)
    wo_line()
    loaded(2, 3, 4, 5, 11, 13, 14)
    pass
    first_part(0)
    wo_line_wait()
    first_part(1)
    wo_plane(0, True)
    first.near(0, 0)
    first.far(0)
    first.near(0, 1)
    project(0)
    first.near(1, 0)
    wo_plane(0, False)
    project(1)
    first.near(1, 1)
    first_part(2)
    attend(0)
    first.near(2, 0)
    wo_plane(1, True)
    first_part(3)
    first.far(1)
    project(2)
    first.near(2, 1)
    first.far(2)
    heads_all.hop(0, 1)
    attend(1)
    loaded(7, 8, 9, 10, 12)
    first.near(3, 0)
    wo_plane(1, False)
    wo_plane(2, True)
    heads_all.hop(0, 2)
    attend(2)
    wo_plane(2, False)
    heads_all.hop(1, 1)
    first.near(3, 1)
    heads_all.hop(0, 3)
    feed(0)
    first.far(3)
    project(3)
    down(0)
    out.open(0)
    heads_all.hop(2, 1)
    heads_all.hop(1, 2)
    back2.near(0, 0)
    attend(3)
    heads_all.hop(1, 3)
    back2.near(0, 1)
    heads_all.hop(2, 2)
    out.near(0, 0)
    back2.far(0, 0)
    feed(1)
    heads_all.hop(3, 1)
    heads_all.hop(2, 3)
    feed(2)
    back2.near(1, 0)
    down(2)
    out.far(0, 0)
    back2.near(1, 1)
    heads_all.hop(3, 2)
    back2.near(2, 0)
    out.open(2)
    heads_all.hop(3, 3)
    out.near(0, 1)
    back2.far(1, 0)
    feed(3)
    back2.near(2, 1)
    down(3)
    out.open(3)
    back2.far(1, 1)
    out.near(2, 0)
    back2.far(2, 0)
    back2.far(0, 1)
    out.far(0, 1)
    back2.near(3, 0)
    back2.far(2, 1)
    grad_up()
    down(1)
    through_two(0)
    back2.near(3, 1)
    grad_gate()
    plane_up.next(0)
    back2.far(3, 0)
    out.near(3, 0)
    back2.far(3, 1)
    through_two(1)
    grad_down()
    out.far(2, 0)
    through_two(2)
    plane_gate.next(0)
    attend_back(0)
    out.near(3, 1)
    through_two(3)
    out.far(3, 0)
    plane_down.next(0)
    out.open(1)
    attend_back(1)
    out.near(2, 1)
    attend_back(2)
    out.far(3, 1)
    values_back(0)
    attend_back(3)
    values_back(2)
    out.near(1, 0)
    values_back(3)
    keys_back(2)
    values_all.hop(0, 1)
    plane_gate.next(1)
    values_back(1)
    out.far(1, 0)
    values_all.hop(0, 2)
    values_all.hop(3, 1)
    plane_up.next(1)
    back1.near(2, 0)
    out.near(1, 1)
    plane_down.next(1)
    plane_gate.next(2)
    keys_back(3)
    values_all.hop(1, 1)
    out.far(2, 1)
    values_all.hop(2, 1)
    finish_out(3)
    out_grad()
    out.far(1, 1)
    keys_back(0)
    plane_up.next(2)
    keys_back(1)
    qkv_grad()
    back1.near(2, 1)
    values_all.hop(2, 2)
    values_all.hop(1, 2)
    back1.near(3, 0)
    plane_gate.next(3)
    values_all.hop(0, 3)
    finish_out(2)
    values_all.hop(3, 2)
    qkv_next(0)
    back1.near(0, 0)
    back1.far(2, 0)
    back1.near(0, 1)
    qkv_next(1)
    back1.far(3, 0)
    back1.near(1, 0)
    back1.near(3, 1)
    values_all.hop(1, 3)
    plane_down.next(2)
    qkv_next(2)
    finish_out(1)
    back1.far(2, 1)
    back1.far(1, 0)
    outs_all.pass_on(3, 0)
    finish_out(0)
    outs_all.pass_on(2, 0)
    qkv_next(3)
    values_one(0)
    plane_down.next(3)
    plane_up.next(3)
    back1.far(3, 1)
    plane_gate.next(4)
    through_one(2)
    values_all.hop(3, 3)
    qkv_next(4)
    out_next(0)
    back1.far(0, 0)
    outs_all.pass_on(1, 0)
    out_next(1)
    outs_all.pass_far(2, 0)
    values_one(1)
    outs_all.pass_on(2, 1)
    values_all.hop(2, 3)
    values_one(2)
    values_one(3)
    through_one(3)
    back1.far(0, 1)
    plane_up.next(4)
    outs_all.pass_on(1, 1)
    plane_down.next(4)
    outs_all.pass_far(3, 0)
    through_one(0)
    outs_all.pass_far(1, 0)
    back1.near(1, 1)
    outs_all.pass_on(0, 0)
    outs_all.pass_far(1, 1)
    gin_all.pass_on(3, 0)
    one_start()
    back1.far(1, 1)
    gin_all.pass_on(2, 0)
    plane_one.next(0)
    plane_one.next(1)
    qkv_next(5)
    gin_all.pass_on(0, 0)
    out_next(2)
    gin_all.pass_far(3, 0)
    outs_all.pass_far(2, 1)
    gin_all.pass_far(2, 0)
    gin_all.pass_on(2, 1)
    plane_down.next(5)
    outs_all.pass_far(0, 0)
    through_one(1)
    plane_one.next(2)
    qkv_next(6)
    out_line_send()
    plane_gate.next(5)
    gain_line()
    outs_all.pass_on(3, 1)
    plane_up.next(5)
    outs_all.pass_on(0, 1)
    gin_all.pass_far(2, 1)
    plane_one.next(3)
    outs_all.pass_far(0, 1)
    gin_all.pass_on(1, 0)
    gin_all.pass_on(0, 1)
    gin_all.pass_far(0, 0)
    plane_one.next(4)
    plane_one.next(5)
    gain_plane(0)
    gin_all.pass_far(1, 0)
    plane_up.next(6)
    gin_all.pass_on(3, 1)
    gin_all.pass_on(1, 1)
    outs_all.pass_far(3, 1)
    plane_down.next(6)
    out_line_sum()
    gain_plane(1)
    out_next(4)
    gin_all.pass_far(0, 1)
    gin_all.pass_far(1, 1)
    plane_gate.next(6)
    gain_plane(2)
    gin_all.pass_far(3, 1)
    out_next(5)
    out_next(6)
    plane_one.next(6)
    gain_plane(3)
    settle()
    for copy in stores:
        copy.wait()
    for line in (back1, out, outs_all, gin_all):
        line.drain(chunks)
    heads_all.drain(r.att)
    values_all.drain(r.dv_all)
    for plane in (plane_gate, plane_up, plane_down, plane_out, plane_one, *plane_qkv):
        plane.drain()
    for index in range(3):
        gain_copy(index).wait_send()

    @pl.when(me != 0)
    def _():
        pl.when(me != count - 1)(lambda: first.drain(chunks))

    @pl.when(edge)
    def _():
        for which, dst in enumerate((r.grad_input, r.output)):
            rows = dst.at[pl.ds(0, chunks * owned)]
            pltpu.make_async_copy(rows, rows, r.own_sem.at[which]).wait()
        for step in range(1, count):
            out_line_copy(step).wait_send()
            gain_line_copy(step).wait_send()

        slots = r.f_part.at[pl.ds(0, chunks // 2), pl.ds(0, count - 1)]
        remote(slots, slots, r.do_sent.at[0], r.do_came.at[0, 0], on_line(0)).wait_send()


def fused_layer(arrays, sizes):
    count, groups, tokens, width, cols, units = sizes
    chunks = tokens // CHUNK
    share = CHUNK // count
    eighth = width // 8
    hbm = pl.BlockSpec(memory_space=pl.ANY)
    vmem = pl.BlockSpec(memory_space=pltpu.VMEM)
    ins = dict(
        block_input=hbm,
        layer_one=hbm,
        grad_output=hbm,
        norm_one_in=hbm,
        w_query=hbm,
        w_key=hbm,
        w_value=hbm,
        w_out=hbm,
        norm_two_in=hbm,
        w_gate=hbm,
        w_up=hbm,
        w_down=hbm,
        w_value_one=hbm,
        rates_in=hbm,
        seg_row_in=hbm,
    )
    outs = dict(
        output=((tokens, width), BF16, hbm),
        grad_input=((tokens, width), BF16, hbm),
        grad_first=((tokens, cols), F32, hbm),
        grad_query=((width, cols), BF16, hbm),
        grad_key=((width, cols), BF16, hbm),
        grad_value=((width, cols), BF16, hbm),
        grad_out=((cols, width), BF16, hbm),
        grad_gate=((units, width), BF16, hbm),
        grad_up=((units, width), BF16, hbm),
        grad_down=((units, width), BF16, hbm),
        grad_one=((cols, width), BF16, hbm),
        gain_one=((1, width), F32, vmem),
        gain_two=((1, width), F32, vmem),
    )
    dma = pltpu.SemaphoreType.DMA

    def low(*shape):
        return pltpu.VMEM(shape, BF16)

    def full(*shape):
        return pltpu.VMEM(shape, F32)

    slots = (chunks, count)
    scratch = dict(
        norm_one=full(1, width),
        norm_two=full(1, width),
        rates=full(1, 128),
        seg_row=pltpu.VMEM((1, tokens), jnp.int32),
        cosine=full(tokens, 128),
        sine=full(tokens, 128),
        x=low(tokens, width),
        g=low(tokens, width),
        first_in=low(tokens, cols),
        wq=low(width, cols),
        wk=low(width, cols),
        wv=low(width, cols),
        wv1=low(cols, width),
        wo=low(count, cols, width),
        wg=low(units, width),
        wu=low(units, width),
        wd=low(units, width),
        a1=low(tokens, width),
        a2=low(tokens, width),
        q=low(tokens, cols),
        k=low(tokens, cols),
        vm=low(tokens, cols),
        lse=full(tokens, 128),
        bias=full(CHUNK, CHUNK + REACH),
        sum_a=full(CHUNK, cols),
        sum_b=full(CHUNK // 2, width),
        big=full(CHUNK, width),
        att=low(*slots, CHUNK, cols),
        dv_all=low(*slots, CHUNK, cols),
        hid=low(tokens, units),
        dga=low(tokens, units),
        dup=low(tokens, units),
        h_own=full(chunks, CHUNK // 2, width),
        db_own=low(chunks, CHUNK // 2, width),
        do=low(tokens, cols),
        dqkv=low(tokens, 3 * cols),
        dk_sum=full(tokens, cols),
        dv_sum=full(tokens, cols),
        gains=full(8, width // 4),
        gain_sum=full(3, 8, width // 4),
        gain_in=full(5, 8, width // 4),
        u_in0=low(3, units, 4 * eighth),
        u_in1=low(3, units, 2 * eighth),
        u_in2=low(3, units, eighth),
        z_in=low(2, cols // 8, width),
        v_in0=low(cols, 4 * eighth),
        v_in1=low(cols, 2 * eighth),
        v_in2=low(cols, eighth),
        f_part=low(*slots, CHUNK, cols),
        f_in=low(chunks * count * CHUNK, cols),
        f_meet=low(chunks, CHUNK, cols),
        b_part=low(*slots, share, width),
        b_in=low(*slots, share, width),
        o_part=low(*slots, share, width),
        o_in=low(*slots, share, width),
        load_sem=dma((15,)),
        store_sem=dma((chunks + 8,)),
        own_sem=dma((2,)),
        wo_sent=dma((4,)),
        wo_came=dma((4,)),
        do_sent=dma((1,)),
        do_came=dma((chunks, 2)),
        p_sent=dma((8, 6)),
        p_came=dma((8, 6)),
        p_free=pltpu.SemaphoreType.REGULAR((8, 3)),
        z_sent=dma((count,)),
        z_came=dma((2,)),
        gain_sent=dma((count + 2,)),
        gain_came=dma((5,)),
        f_sent=dma((chunks,)),
        f_came=dma(slots),
        f_met=dma((chunks,)),
        b_sent=dma((chunks,)),
        b_came=dma(slots),
        o_sent=dma((chunks,)),
        o_came=dma(slots),
        d_sent=dma((chunks,)),
        d_came=dma(slots),
        att_came=dma(slots),
        att_right=dma((1,)),
        att_left=dma((1,)),
        dv_came=dma(slots),
        dv_right=dma((1,)),
        dv_left=dma((1,)),
        out_came=dma(slots),
        out_sent=dma((chunks,)),
        gin_came=dma(slots),
        gin_sent=dma((chunks,)),
    )
    results = pl.pallas_call(
        functools.partial(layer_kernel, [*ins, *outs, *scratch], sizes),
        out_shape=[jax.ShapeDtypeStruct(item[0], item[1]) for item in outs.values()],
        in_specs=list(ins.values()),
        out_specs=[item[2] for item in outs.values()],
        scratch_shapes=list(scratch.values()),
        compiler_params=pltpu.CompilerParams(
            collective_id=0, has_side_effects=True, vmem_limit_bytes=VMEM_LIMIT
        ),
        cost_estimate=pl.CostEstimate(
            flops=2 * 13 * 10**9, bytes_accessed=40 * 2**20, transcendentals=0
        ),
    )(*arrays)
    return widen(results)


def widen(results):
    steps = 2
    *arrays, gain_one, gain_two = results
    width = gain_one.shape[1]

    def one(*refs):
        half = len(refs) // 2
        for src, dst in zip(refs[: half - 2], refs[half:-2]):
            dst[...] = src[...].astype(dst.dtype)
        for src, dst in zip(refs[half - 2 : half], refs[-2:]):
            dst[...] = src[0]

    specs = [
        pl.BlockSpec((array.shape[0] // steps, array.shape[1]), lambda i: (i, 0))
        for array in arrays
    ]
    shapes = [
        jax.ShapeDtypeStruct(array.shape, F32 if index else BF16)
        for index, array in enumerate(arrays)
    ]
    return pl.pallas_call(
        one,
        grid=(steps,),
        in_specs=specs + [pl.BlockSpec((1, width), lambda i: (0, 0))] * 2,
        out_specs=specs + [pl.BlockSpec((width,), lambda i: (0,))] * 2,
        out_shape=shapes + [jax.ShapeDtypeStruct((width,), F32)] * 2,
        compiler_params=pltpu.CompilerParams(vmem_limit_bytes=VMEM_LIMIT),
    )(*arrays, gain_one, gain_two)


def on_device(*arguments):
    (
        block_input,
        layer_one_input,
        segment_ids,
        grad_output,
        norm_one,
        w_query,
        w_key,
        w_value,
        w_out,
        norm_two,
        w_gate,
        w_up,
        w_down,
        w_value_one,
    ) = arguments
    count = lax.axis_size("mp")
    groups = lax.axis_size("dp")
    tokens, width = block_input.shape
    cols = w_query.shape[1]
    units = w_gate.shape[1]
    fits = (
        count == 4
        and groups == 8
        and tokens == 4 * CHUNK
        and cols == 256
        and width == count * cols
        and units % 64 == 0
        and units <= 704
        and segment_ids.shape[0] == 1
    )
    if not fits:
        return by_collectives(*arguments)
    half = HD // 2
    rates = np.exp(np.arange(half, dtype=np.float32) * np.float32(-math.log(10000.0) / half))
    r = fused_layer(
        (
            block_input,
            layer_one_input,
            grad_output,
            norm_one[None, :],
            w_query,
            w_key,
            w_value,
            w_out,
            norm_two[None, :],
            w_gate.T,
            w_up.T,
            w_down,
            w_value_one,
            jnp.asarray(np.tile(rates, 4)[None, :]),
            segment_ids,
        ),
        (count, groups, tokens, width, cols, units),
    )
    (
        output,
        grad_input,
        grad_first,
        grad_query,
        grad_key,
        grad_value,
        grad_out,
        grad_gate,
        grad_up,
        grad_down,
        grad_one,
        gain_one,
        gain_two,
    ) = r
    return (
        output,
        grad_input,
        grad_first,
        gain_one,
        grad_query,
        grad_key,
        grad_value,
        grad_out,
        gain_two,
        grad_gate.T,
        grad_up.T,
        grad_down,
        grad_one,
    )


def solution(mesh):
    return jax.shard_map(
        on_device,
        mesh=mesh,
        in_specs=(
            P("dp", None),
            P("dp", "mp"),
            P("dp", None),
            P("dp", None),
            P(),
            P(None, "mp"),
            P(None, "mp"),
            P(None, "mp"),
            P("mp", None),
            P(),
            P(None, "mp"),
            P(None, "mp"),
            P("mp", None),
            P("mp", None),
        ),
        out_specs=(
            P("dp", None),
            P("dp", None),
            P("dp", "mp"),
            P(),
            P(None, "mp"),
            P(None, "mp"),
            P(None, "mp"),
            P("mp", None),
            P(),
            P(None, "mp"),
            P(None, "mp"),
            P("mp", None),
            P("mp", None),
        ),
        check_vma=False,
    )
```

```python
import functools
import math
from types import SimpleNamespace

import jax
import jax.numpy as jnp
import numpy as np
from jax import lax
from jax.experimental import pallas as pl
from jax.experimental.pallas import tpu as pltpu
from jax.sharding import PartitionSpec as P

HD = 64


EPSILON = 1e-06
VMEM_LIMIT = 64 * 2**20 - 2**16


def positions_of(segments):
    position = lax.broadcasted_iota(jnp.int32, segments.shape, 1)
    changed = (segments[:, 1:] != segments[:, :-1]).astype(jnp.int32)
    starts = jnp.concatenate([jnp.ones_like(segments[:, :1]), changed], axis=1)
    return position - lax.cummax(position * starts, axis=1)


def rope_tables(positions, width):
    half_width = width // 2
    rates = jnp.exp(jnp.arange(half_width, dtype=jnp.float32) * (-math.log(10000.0) / half_width))
    angles = positions.astype(jnp.float32)[:, None] * rates[None, :]
    return (jnp.cos(angles)[:, None, :], jnp.sin(angles)[:, None, :])


def rotate(tensor, cosine, sine_part, turn):
    half_width = tensor.shape[-1] // 2
    left_half = tensor[..., :half_width]
    right_half = tensor[..., half_width:]
    return jnp.concatenate(
        [
            left_half * cosine - turn * right_half * sine_part,
            right_half * cosine + turn * left_half * sine_part,
        ],
        axis=-1,
    )


def over_rows(left_side, right_side):
    return lax.dot_general(
        left_side, right_side, (((0,), (0,)), ((), ())), preferred_element_type=jnp.float32
    )


def against(left_side, right_side):
    return lax.dot_general(
        left_side, right_side, (((1,), (1,)), ((), ())), preferred_element_type=jnp.float32
    )


def norm_back(activations, scale_vec, gain_vec, grad_normed):
    grad_gain = jnp.sum(grad_normed * activations * scale_vec, axis=0)
    scaled = grad_normed * gain_vec
    inner = jnp.mean(scaled * activations, axis=-1, keepdims=True)
    return (grad_gain, scale_vec * scaled - activations * scale_vec * scale_vec * scale_vec * inner)


def masked_scores(q_block, key_rows, seg_block, seg_all, first_row, score_scale):
    block_rows = q_block.shape[0]
    scores = (
        jnp.einsum("qhd,khd->hqk", q_block, key_rows, preferred_element_type=jnp.float32)
        * score_scale
    )
    row_index = first_row + lax.broadcasted_iota(jnp.int32, (block_rows, key_rows.shape[0]), 0)
    col_index = lax.broadcasted_iota(jnp.int32, (block_rows, key_rows.shape[0]), 1)
    allowed = (seg_block[:, None] == seg_all[None, :]) & (col_index <= row_index)
    return jnp.where(allowed[None], scores, -1e30)


def attend_forward(queries, key_rows, values, seg_all, score_scale):
    row_count, head_count, width = queries.shape
    block_rows = min(512, row_count)

    def one_block(block_index):
        first_row = block_index * block_rows
        q_block = lax.dynamic_slice_in_dim(queries, first_row, block_rows, 0)
        seg_block = lax.dynamic_slice_in_dim(seg_all, first_row, block_rows, 0)
        scores = masked_scores(q_block, key_rows, seg_block, seg_all, first_row, score_scale)
        largest = jnp.max(scores, axis=-1, keepdims=True)
        raised = jnp.exp(scores - largest)
        summed = jnp.sum(raised, axis=-1, keepdims=True)
        weights = (raised / summed).astype(jnp.bfloat16)
        result = jnp.einsum("hqk,khd->qhd", weights, values, preferred_element_type=jnp.float32)
        return (result, (largest + jnp.log(summed))[..., 0])

    results, log_totals = lax.map(one_block, jnp.arange(row_count // block_rows, dtype=jnp.int32))
    return (results.reshape(row_count, head_count, width), log_totals)


def attend_backward(queries, key_rows, values, seg_all, log_totals, grad_attended, score_scale):
    row_count = queries.shape[0]
    block_rows = min(512, row_count)

    def one_block(carried, block_index):
        grad_keys, grad_values = carried
        first_row = block_index * block_rows
        q_block = lax.dynamic_slice_in_dim(queries, first_row, block_rows, 0)
        seg_block = lax.dynamic_slice_in_dim(seg_all, first_row, block_rows, 0)
        grad_block = lax.dynamic_slice_in_dim(grad_attended, first_row, block_rows, 0)
        scores = masked_scores(q_block, key_rows, seg_block, seg_all, first_row, score_scale)
        probs = jnp.exp(scores - log_totals[block_index][..., None])
        grad_probs = jnp.einsum(
            "qhd,khd->hqk", grad_block, values, preferred_element_type=jnp.float32
        )
        inner = jnp.sum(probs * grad_probs, axis=-1, keepdims=True)
        grad_scores = (probs * (grad_probs - inner)).astype(jnp.bfloat16)
        grad_query = (
            jnp.einsum("hqk,khd->qhd", grad_scores, key_rows, preferred_element_type=jnp.float32)
            * score_scale
        )
        grad_keys = (
            grad_keys
            + jnp.einsum("hqk,qhd->khd", grad_scores, q_block, preferred_element_type=jnp.float32)
            * score_scale
        )
        grad_values = grad_values + jnp.einsum(
            "hqk,qhd->khd",
            probs.astype(jnp.bfloat16),
            grad_block,
            preferred_element_type=jnp.float32,
        )
        return ((grad_keys, grad_values), grad_query)

    zero_rows = jnp.zeros(key_rows.shape, jnp.float32)
    (grad_keys, grad_values), grad_queries = lax.scan(
        one_block, (zero_rows, zero_rows), jnp.arange(row_count // block_rows, dtype=jnp.int32)
    )
    return (grad_queries.reshape(key_rows.shape), grad_keys, grad_values)


def by_collectives(
    block_input,
    layer_one_input,
    segment_ids,
    grad_output,
    norm_one,
    w_query,
    w_key,
    w_value,
    w_out,
    norm_two,
    w_gate,
    w_up,
    w_down,
    w_value_one,
):
    token_count = block_input.shape[0]
    head_count = w_query.shape[1] // HD
    score_scale = HD ** (-0.5)
    seg_all = segment_ids[0]
    cosine, sine_part = rope_tables(positions_of(segment_ids)[0], HD)
    share_rows = token_count // lax.axis_size("mp")
    share_start = lax.axis_index("mp") * share_rows
    inputs = block_input.astype(jnp.float32)
    scale_one = lax.rsqrt(jnp.mean(inputs * inputs, axis=-1, keepdims=True) + EPSILON)
    normed = (inputs * scale_one * norm_one).astype(jnp.bfloat16)
    queries = jnp.dot(normed, w_query, preferred_element_type=jnp.float32).reshape(
        token_count, head_count, HD
    )
    key_rows = jnp.dot(normed, w_key, preferred_element_type=jnp.float32).reshape(
        token_count, head_count, HD
    )
    own_values = jnp.dot(normed, w_value, preferred_element_type=jnp.float32)
    first_values = lax.psum_scatter(
        jnp.dot(layer_one_input, w_value_one, preferred_element_type=jnp.float32).astype(
            jnp.bfloat16
        ),
        "mp",
        scatter_dimension=1,
        tiled=True,
    ).astype(jnp.float32)
    mixed_values = (
        (0.5 * own_values + 0.5 * first_values)
        .astype(jnp.bfloat16)
        .reshape(token_count, head_count, HD)
    )
    turned_q = rotate(queries, cosine, sine_part, 1.0).astype(jnp.bfloat16)
    turned_k = rotate(key_rows, cosine, sine_part, 1.0).astype(jnp.bfloat16)
    attended, log_totals = attend_forward(turned_q, turned_k, mixed_values, seg_all, score_scale)
    attended = attended.reshape(token_count, head_count * HD).astype(jnp.bfloat16)
    branch_one = jnp.dot(attended, w_out, preferred_element_type=jnp.float32)
    inputs_here = lax.dynamic_slice_in_dim(inputs, share_start, share_rows, 0)
    scale_one_here = lax.dynamic_slice_in_dim(scale_one, share_start, share_rows, 0)
    grad_rows = lax.dynamic_slice_in_dim(grad_output, share_start, share_rows, 0).astype(
        jnp.float32
    )
    residual = inputs_here + lax.psum_scatter(
        branch_one.astype(jnp.bfloat16), "mp", scatter_dimension=0, tiled=True
    ).astype(jnp.float32)
    scale_two = lax.rsqrt(jnp.mean(residual * residual, axis=-1, keepdims=True) + EPSILON)
    normed_two = (residual * scale_two * norm_two).astype(jnp.bfloat16)
    normed_two = lax.all_gather(normed_two, "mp", axis=0, tiled=True)
    gate_pre = jnp.dot(normed_two, w_gate, preferred_element_type=jnp.float32)
    up_pre = jnp.dot(normed_two, w_up, preferred_element_type=jnp.float32)
    sigmoid_gate = jax.nn.sigmoid(gate_pre)
    silu_gate = gate_pre * sigmoid_gate
    hidden = (silu_gate * up_pre).astype(jnp.bfloat16)
    branch_two = jnp.dot(hidden, w_down, preferred_element_type=jnp.float32)
    output_share = (
        residual
        + lax.psum_scatter(
            branch_two.astype(jnp.bfloat16), "mp", scatter_dimension=0, tiled=True
        ).astype(jnp.float32)
    ).astype(jnp.bfloat16)
    output = lax.all_gather(output_share, "mp", axis=0, tiled=True)
    grad_down = over_rows(hidden, grad_output)
    grad_hidden = against(grad_output, w_down)
    grad_gate_pre = (
        grad_hidden * up_pre * sigmoid_gate * (1.0 + gate_pre * (1.0 - sigmoid_gate))
    ).astype(jnp.bfloat16)
    grad_up_pre = (grad_hidden * silu_gate).astype(jnp.bfloat16)
    grad_gate = over_rows(normed_two, grad_gate_pre)
    grad_up = over_rows(normed_two, grad_up_pre)
    back_two = against(grad_gate_pre, w_gate) + against(grad_up_pre, w_up)
    grad_normed_two = lax.psum_scatter(
        back_two.astype(jnp.bfloat16), "mp", scatter_dimension=0, tiled=True
    ).astype(jnp.float32)
    grad_norm_two, grad_through_two = norm_back(residual, scale_two, norm_two, grad_normed_two)
    grad_residual = grad_rows + grad_through_two
    residual_low = grad_residual.astype(jnp.bfloat16)
    residual_low = lax.all_gather(residual_low, "mp", axis=0, tiled=True)
    grad_out_proj = over_rows(attended, residual_low)
    grad_attended = (
        against(residual_low, w_out).astype(jnp.bfloat16).reshape(token_count, head_count, HD)
    )
    grad_turned_q, grad_turned_k, grad_mixed = attend_backward(
        turned_q, turned_k, mixed_values, seg_all, log_totals, grad_attended, score_scale
    )
    grad_value_part = (0.5 * grad_mixed).reshape(token_count, head_count * HD).astype(jnp.bfloat16)
    grad_first_full = lax.all_gather(grad_value_part, "mp", axis=1, tiled=True)
    grad_queries = (
        rotate(grad_turned_q, cosine, sine_part, -1.0)
        .reshape(token_count, head_count * HD)
        .astype(jnp.bfloat16)
    )
    grad_keys = (
        rotate(grad_turned_k, cosine, sine_part, -1.0)
        .reshape(token_count, head_count * HD)
        .astype(jnp.bfloat16)
    )
    grad_query = over_rows(normed, grad_queries)
    grad_key = over_rows(normed, grad_keys)
    grad_value = over_rows(normed, grad_value_part)
    back_one = (
        against(grad_queries, w_query)
        + against(grad_keys, w_key)
        + against(grad_value_part, w_value)
    )
    grad_normed = lax.psum_scatter(
        back_one.astype(jnp.bfloat16), "mp", scatter_dimension=0, tiled=True
    ).astype(jnp.float32)
    grad_norm_one, grad_through_one = norm_back(inputs_here, scale_one_here, norm_one, grad_normed)
    gain_rows = jnp.concatenate([grad_norm_one, grad_norm_two])[None, :]
    grad_input, gain_all = (
        lax.all_gather(
            (grad_residual + grad_through_one).astype(jnp.bfloat16), "mp", axis=0, tiled=True
        ).astype(jnp.float32),
        lax.all_gather(gain_rows, "mp", axis=0, tiled=True),
    )
    gain_total = jnp.sum(gain_all, axis=0)
    width = norm_one.shape[0]
    grad_norm_one = gain_total[:width]
    grad_norm_two = gain_total[width:]
    grad_value_one = over_rows(layer_one_input, grad_first_full)
    grad_layer_one_input = against(grad_first_full, w_value_one)
    grad_norm_one, grad_norm_two = lax.psum((grad_norm_one, grad_norm_two), "dp")
    summed = lax.psum(
        tuple(
            part.astype(jnp.bfloat16)
            for part in (
                grad_query,
                grad_key,
                grad_value,
                grad_out_proj,
                grad_value_one,
                grad_gate,
                grad_up,
                grad_down,
            )
        ),
        "dp",
    )
    (
        grad_query,
        grad_key,
        grad_value,
        grad_out_proj,
        grad_value_one,
        grad_gate,
        grad_up,
        grad_down,
    ) = tuple(part.astype(jnp.float32) for part in summed)
    return (
        output,
        grad_input,
        grad_layer_one_input,
        grad_norm_one,
        grad_query,
        grad_key,
        grad_value,
        grad_out_proj,
        grad_norm_two,
        grad_gate,
        grad_up,
        grad_down,
        grad_value_one,
    )


NN = (((1,), (0,)), ((), ()))
NT = (((1,), (1,)), ((), ()))
TN = (((0,), (0,)), ((), ()))
F32 = jnp.float32
BF16 = jnp.bfloat16
CHUNK = 256
REACH = 512
MESH = pl.DeviceIdType.MESH


def mul(left_side, right_side, dims=NN):
    return lax.dot_general(left_side, right_side, dims, preferred_element_type=F32)


def on_line(index):
    return {"mp": index}


def in_plane(index):
    return {"dp": index}


def remote(src, dst, send_sem, recv_sem, device):
    return pltpu.make_async_remote_copy(
        src_ref=src,
        dst_ref=dst,
        send_sem=send_sem,
        recv_sem=recv_sem,
        device_id=device,
        device_id_type=MESH,
    )


class Scatter:
    def __init__(self, me, count, parts, inbox, meet, sent, came, met):
        self.me, self.count = me, count
        self.parts, self.inbox, self.meet = parts, inbox, meet
        self.sent, self.came, self.met = sent, came, met

    def take(self, c, k):
        slot = self.inbox(c, k)
        remote(slot, slot, self.sent.at[c], self.came.at[c, k], on_line(0)).wait_recv()
        self.parts[c, k] = (self.parts[c, k].astype(F32) + self.inbox(c, k)[...].astype(F32)).astype(
            BF16
        )

    def right(self, c, k):
        me = self.me

        @pl.when(me < k)
        def _():
            @pl.when(me > 0)
            def _():
                self.take(c, k)

            remote(
                self.parts.at[c, k],
                self.inbox(c, k),
                self.sent.at[c],
                self.came.at[c, k],
                on_line(me + 1),
            ).start()

    def left(self, c, k):
        me = self.me

        @pl.when(me > k)
        def _():
            @pl.when(me < self.count - 1)
            def _():
                self.take(c, k)

            @pl.when(me == k + 1)
            def _():
                remote(
                    self.parts.at[c, k],
                    self.meet.at[c],
                    self.sent.at[c],
                    self.met.at[c],
                    on_line(me - 1),
                ).start()

            @pl.when(me > k + 1)
            def _():
                remote(
                    self.parts.at[c, k],
                    self.inbox(c, k),
                    self.sent.at[c],
                    self.came.at[c, k],
                    on_line(me - 1),
                ).start()

    def rights(self, c):
        for k in range(self.count - 1, 0, -1):
            self.right(c, k)

    def lefts(self, c):
        for k in range(self.count - 1):
            self.left(c, k)

    def open(self, c):
        @pl.when(self.me == 0)
        def _():
            self.rights(c)

        @pl.when(self.me == self.count - 1)
        def _():
            self.lefts(c)

    def near(self, c, step):
        me, half = self.me, self.count // 2

        @pl.when((me > 0) & (me < half))
        def _():
            self.right(c, self.count - 1 - step)

        @pl.when((me < self.count - 1) & (me >= half))
        def _():
            self.left(c, step)

    def far(self, c):
        me, half = self.me, self.count // 2

        @pl.when((me > 0) & (me < half))
        def _():
            self.lefts(c)

        @pl.when((me < self.count - 1) & (me >= half))
        def _():
            self.rights(c)

    def total(self, c, into):
        me = self.me
        into[...] = self.parts[c, me].astype(F32)

        @pl.when(me > 0)
        def _():
            slot = self.inbox(c, me)
            remote(slot, slot, self.sent.at[c], self.came.at[c, me], on_line(0)).wait_recv()
            into[...] += self.inbox(c, me)[...].astype(F32)

        @pl.when(me < self.count - 1)
        def _():
            slot = self.meet.at[c]
            remote(slot, slot, self.sent.at[c], self.met.at[c], on_line(0)).wait_recv()
            into[...] += self.meet[c].astype(F32)

    def drain_one(self, c):
        slots = self.parts.at[c, pl.ds(0, self.count - 1)]
        remote(slots, slots, self.sent.at[c], self.came.at[c, 0], on_line(0)).wait_send()

    def drain(self, chunks):
        def one(c, carry):
            self.drain_one(c)
            return carry

        lax.fori_loop(0, chunks, one, 0)


class Gather:
    def __init__(self, me, count, place, came, sent_right, sent_left):
        self.me, self.count, self.place = me, count, place
        self.came, self.sent_right, self.sent_left = came, sent_right, sent_left

    def to_right(self, c, k, src):
        return remote(
            src, self.place(c, k), self.sent_right.at[0], self.came.at[c, k], on_line(self.me + 1)
        )

    def to_left(self, c, k, src):
        return remote(
            src, self.place(c, k), self.sent_left.at[0], self.came.at[c, k], on_line(self.me - 1)
        )

    def own(self, c, src):
        me = self.me

        @pl.when(me < self.count - 1)
        def _():
            self.to_right(c, me, src).start()

        @pl.when(me > 0)
        def _():
            self.to_left(c, me, src).start()

    def wait(self, c, k):
        slot = self.place(c, k)
        remote(slot, slot, self.sent_left.at[0], self.came.at[c, k], on_line(0)).wait_recv()

    def hop(self, c, step):
        me = self.me

        @pl.when(me >= step)
        def _():
            k = me - step
            self.wait(c, k)

            @pl.when(me < self.count - 1)
            def _():
                self.to_right(c, k, self.place(c, k)).start()

        @pl.when(me + step < self.count)
        def _():
            k = me + step
            self.wait(c, k)

            @pl.when(me > 0)
            def _():
                self.to_left(c, k, self.place(c, k)).start()

    def drain(self, some):
        for device in range(self.count):
            for slots, sem in (
                ((device + 1) * (device < self.count - 1), self.sent_right),
                ((self.count - device) * (device > 0), self.sent_left),
            ):
                if slots:

                    @pl.when(self.me == device)
                    def _():
                        sent = some(slots)
                        remote(
                            sent, sent, sem.at[0], self.came.at[0, 0], on_line(0)
                        ).wait_send()


class Ends:
    def __init__(self, me, count, parts, inbox, sent, came):
        self.me, self.count, self.half = me, count, count // 2
        self.parts, self.inbox, self.sent, self.came = parts, inbox, sent, came

    def copy(self, c, k):
        step = 1 if k >= self.half else -1
        return remote(
            self.parts.at[c, k],
            self.inbox.at[c, k],
            self.sent.at[c],
            self.came.at[c, k],
            on_line(self.me + step),
        )

    def arrived(self, c, k):
        slot = self.inbox.at[c, k]
        remote(slot, slot, self.sent.at[c], self.came.at[c, k], on_line(0)).wait_recv()

    def open(self, c):
        @pl.when(self.me == 0)
        def _():
            for k in range(self.half, self.count):
                self.copy(c, k).start()

        @pl.when(self.me == self.count - 1)
        def _():
            for k in range(self.half):
                self.copy(c, k).start()

    def hand(self, c, k):
        self.arrived(c, k)
        self.parts[c, k] = (self.parts[c, k].astype(F32) + self.inbox[c, k].astype(F32)).astype(
            BF16
        )
        self.copy(c, k).start()

    def near(self, c, j):
        pl.when(self.me == 1)(lambda: self.hand(c, self.half + j))
        pl.when(self.me == self.count - 2)(lambda: self.hand(c, j))

    def far(self, c, j):
        pl.when(self.me == 1)(lambda: self.hand(c, j))
        pl.when(self.me == self.count - 2)(lambda: self.hand(c, self.half + j))

    def total(self, c, into):
        side = self.me // (self.count - 1)
        rows = self.parts.shape[2]
        for j in range(self.half):
            k = side * self.half + j
            self.arrived(c, k)
            into[j * rows : (j + 1) * rows] = self.parts[c, k].astype(F32) + self.inbox[
                c, k
            ].astype(F32)

    def drain_one(self, c):
        edge = (self.me == 0) | (self.me == self.count - 1)

        def wait(slots):
            remote(slots, slots, self.sent.at[c], self.came.at[c, 0], on_line(0)).wait_send()

        pl.when(edge)(lambda: wait(self.parts.at[c, pl.ds(0, self.half)]))
        pl.when(jnp.logical_not(edge))(lambda: wait(self.parts.at[c]))

    def drain(self, chunks):
        def one(c, carry):
            self.drain_one(c)
            return carry

        lax.fori_loop(0, chunks, one, 0)


class EndsGather:
    def __init__(self, me, count, ref, share, sent, came):
        self.me, self.count, self.half = me, count, count // 2
        self.ref, self.share, self.sent, self.came = ref, share, sent, came

    def place(self, c, k):
        return self.ref.at[pl.ds((c * self.count + k) * self.share, self.share)]

    def copy(self, c, k, src):
        step = 1 if k < self.half else -1
        return remote(
            src,
            self.place(c, k),
            self.sent.at[c],
            self.came.at[c, k],
            on_line(self.me + step),
        )

    def arrived(self, c, k):
        slot = self.place(c, k)
        remote(slot, slot, self.sent.at[c], self.came.at[c, k], on_line(0)).wait_recv()

    def own(self, c, parts):
        @pl.when(self.me == 0)
        def _():
            for k in range(self.half):
                self.copy(c, k, parts.at[c, k]).start()

        @pl.when(self.me == self.count - 1)
        def _():
            for k in range(self.half, self.count):
                self.copy(c, k, parts.at[c, k]).start()

    def hand(self, c, k):
        self.arrived(c, k)
        self.copy(c, k, self.place(c, k)).start()

    def pass_on(self, c, j):
        pl.when(self.me == 1)(lambda: self.hand(c, j))
        pl.when(self.me == self.count - 2)(lambda: self.hand(c, self.half + j))

    def pass_far(self, c, j):
        pl.when(self.me == 1)(lambda: self.hand(c, self.half + j))
        pl.when(self.me == self.count - 2)(lambda: self.hand(c, j))

    def settle(self, c):
        @pl.when(self.me == 0)
        def _():
            for k in range(self.half, self.count):
                self.arrived(c, k)

        @pl.when(self.me == self.count - 1)
        def _():
            for k in range(self.half):
                self.arrived(c, k)

    def drain(self, chunks):
        edge = (self.me == 0) | (self.me == self.count - 1)

        def one(c, carry):
            def wait(count):
                rows = self.ref.at[pl.ds(0, count * self.share)]
                remote(rows, rows, self.sent.at[c], self.came.at[c, 0], on_line(0)).wait_send()

            pl.when(edge)(lambda: wait(self.half))
            pl.when(jnp.logical_not(edge))(lambda: wait(self.count))
            return carry

        lax.fori_loop(0, chunks, one, 0)


class Plane:
    def __init__(self, partners, bits, span, inboxes, sent, came, free, store, gather_span=None):
        self.fenced = gather_span is None
        self.partners, self.bits, self.span = partners, bits, span
        self.inboxes, self.sent, self.came, self.free = inboxes, sent, came, free
        self.store = store
        self.gather_span = span if gather_span is None else gather_span

    def start_of(self, step):
        bits = self.bits
        return (0, 4 * bits[0], 4 * bits[0] + 2 * bits[1], 4 * bits[0] + 2 * bits[1] + bits[2])[step]

    def copy(self, step):
        if step < 3:
            size = 4 >> step
            src = self.span(self.start_of(step) + size * (1 - self.bits[step]), size)
            dst, partner = self.inboxes[step], self.partners[step]
        else:
            size = 1 << (step - 3)
            src = dst = self.gather_span(self.start_of(6 - step), size)
            partner = self.partners[5 - step]
        return remote(src, dst, self.sent.at[step], self.came.at[step], in_plane(partner))

    def send(self, step):
        if step >= 3 and self.fenced:
            pl.semaphore_wait(self.free.at[5 - step], 1)
        self.copy(step).start()

    def add(self, step):
        self.copy(step).wait_send()
        if self.fenced:
            pl.semaphore_signal(
                self.free.at[step],
                inc=1,
                device_id=in_plane(self.partners[step]),
                device_id_type=MESH,
            )
        self.copy(step).wait_recv()
        kept = self.span(self.start_of(step + 1), 4 >> step)
        kept[...] = (kept[...].astype(F32) + self.inboxes[step][...].astype(F32)).astype(BF16)

    def next(self, step):
        if 0 < step <= 3:
            self.add(step - 1)
        elif step > 3:
            self.copy(step - 1).wait_recv()
        if step < 6:
            self.send(step)
        else:
            self.store()

    def drain(self):
        for step in range(3, 6):
            self.copy(step).wait_send()


def turn(tensor, cosine, sine, sign):
    pieces = []
    front = lax.broadcasted_iota(jnp.int32, (1, 128), 1) % HD < HD // 2
    for at in range(0, tensor.shape[-1], 128):
        piece = tensor[:, at : at + 128]
        mixed = jnp.where(front, -pltpu.roll(piece, 96, 1), pltpu.roll(piece, 32, 1)) * sine
        pieces.append(piece * cosine + sign * mixed)
    return jnp.concatenate(pieces, axis=1)


def layer_kernel(names, sizes, *ref_list):
    r = SimpleNamespace(**dict(zip(names, ref_list)))
    count, groups, tokens, width, cols, units = sizes
    chunks = tokens // CHUNK
    share = CHUNK // count
    heads = cols // HD
    owned = CHUNK // 2
    score_scale = HD ** (-0.5)
    me = lax.axis_index("mp")
    row = lax.axis_index("dp")
    side = me // (count - 1)
    edge = (me == 0) | (me == count - 1)

    core = row % 2
    along_x = (row // 2) % 2
    along_y = row // 4
    other_core = row + 1 - 2 * core
    other_x = row + 2 - 4 * along_x
    other_y = row + 4 - 8 * along_y

    loads = {}

    def load(index, src, dst):
        copy = pltpu.make_async_copy(src, dst, r.load_sem.at[index])
        copy.start()
        loads[index] = copy

    def loaded(*indices):
        for index in indices:
            loads.pop(index).wait()

    load(0, r.layer_one, r.first_in)
    load(1, r.w_value_one, r.wv1)
    load(11, r.norm_one_in, r.norm_one)
    load(12, r.norm_two_in, r.norm_two)
    load(13, r.rates_in, r.rates)
    load(14, r.seg_row_in, r.seg_row)
    load(2, r.block_input, r.x)
    load(3, r.w_query, r.wq)
    load(4, r.w_key, r.wk)
    load(5, r.w_value, r.wv)
    load(6, r.w_out, r.wo.at[me])
    load(7, r.grad_output, r.g)
    load(8, r.w_gate, r.wg)
    load(9, r.w_up, r.wu)
    load(10, r.w_down, r.wd)

    barrier = pltpu.get_barrier_semaphore()
    for step in range(1, count):
        pl.semaphore_signal(
            barrier, inc=1, device_id=on_line((me + step) % count), device_id_type=MESH
        )
    for partner in (other_core, other_x, other_y):
        pl.semaphore_signal(barrier, inc=1, device_id=in_plane(partner), device_id_type=MESH)
    pl.semaphore_wait(barrier, count - 1 + 3)

    def f_slot(c, k):
        return r.f_in.at[pl.ds(pl.multiple_of((c * count + k) * CHUNK, CHUNK), CHUNK)]

    loaded(0, 1)

    first = Scatter(
        me, count, r.f_part, f_slot, r.f_meet, r.f_sent, r.f_came, r.f_met
    )
    back2 = Ends(me, count, r.b_part, r.b_in, r.b_sent, r.b_came)
    out = Ends(me, count, r.o_part, r.o_in, r.o_sent, r.o_came)
    back1 = Ends(me, count, r.b_part, r.b_in, r.d_sent, r.d_came)
    heads_all = Gather(
        me, count, lambda c, k: r.att.at[c, k], r.att_came, r.att_right, r.att_left
    )
    values_all = Gather(
        me, count, lambda c, k: r.dv_all.at[c, k], r.dv_came, r.dv_right, r.dv_left
    )

    outs_all = EndsGather(me, count, r.output, share, r.out_sent, r.out_came)
    gin_all = EndsGather(me, count, r.grad_input, share, r.gin_sent, r.gin_came)

    def at(c):
        return pl.ds(c * CHUNK, CHUNK)

    def mine(c):
        return pl.ds(pl.multiple_of(c * CHUNK + side * owned, owned), owned)

    piece = cols // groups
    block = core * 4 + along_x * 2 + along_y

    def wo_rows(slot, step):
        span = 1 << step
        start = pl.multiple_of((block // span) * span * piece, piece)
        return r.wo.at[slot, pl.ds(start, span * piece)]

    wo_all = Gather(
        me, count, lambda c, k: wo_rows(k, 0), r.wo_line_came, r.wo_right, r.wo_left
    )

    def wo_line():
        loaded(6)
        wo_all.own(0, wo_rows(me, 0))

    def wo_wait(index, rows):
        slots = r.wo.at[pl.ds(0, count - 1), pl.ds(0, rows)]
        copy = remote(slots, slots, r.wo_sent.at[index], r.wo_came.at[index], on_line(0))
        copy.wait_send()
        copy.wait_recv()

    def wo_plane(step, start):
        if not start:
            wo_wait(step, piece << step)
            if step == 2:
                wo_all.drain(lambda slots: r.wo.at[pl.ds(0, slots), pl.ds(0, piece)])
            return
        for other in range(1, count):
            slot = (me + other) % count
            remote(
                wo_rows(slot, step),
                wo_rows(slot, step),
                r.wo_sent.at[step],
                r.wo_came.at[step],
                in_plane((other_y, other_x, other_core)[step]),
            ).start()

    def first_part(c):
        part = mul(r.first_in[at(c)], r.wv1[...])
        for k in range(count):
            r.f_part[c, k] = part[:, k * cols : (k + 1) * cols].astype(BF16)
        first.open(c)

    def window(c):
        low = max(0, c * CHUNK - REACH)
        return low, (c + 1) * CHUNK - low

    def visible(c):
        low, span = window(c)
        row_index = c * CHUNK + lax.broadcasted_iota(jnp.int32, (CHUNK, span), 0)
        col_index = low + lax.broadcasted_iota(jnp.int32, (CHUNK, span), 1)
        here = r.seg_row[:, c * CHUNK : (c + 1) * CHUNK].astype(F32)
        diagonal = lax.broadcasted_iota(jnp.int32, (CHUNK, CHUNK), 0) == (
            lax.broadcasted_iota(jnp.int32, (CHUNK, CHUNK), 1)
        )
        column = jnp.sum(jnp.where(diagonal, here, 0.0), axis=1, keepdims=True)
        same = column == r.seg_row[:, low : low + span].astype(F32)
        return same & (col_index <= row_index)

    def mask_bias(c):
        span = window(c)[1]
        r.bias[:, :span] = jnp.where(visible(c), 0.0, -1e30)

    def angle_tables(c):
        position = jnp.sum(jnp.where(visible(c), 1.0, 0.0), axis=1, keepdims=True) - 1.0
        angles = position * r.rates[...]
        r.cosine[at(c)] = jnp.cos(angles)
        r.sine[at(c)] = jnp.sin(angles)

    def project(c):
        angle_tables(c)
        x = r.x[at(c)].astype(F32)
        scale = lax.rsqrt(jnp.mean(x * x, axis=-1, keepdims=True) + EPSILON)
        normed = (x * scale * r.norm_one[...]).astype(BF16)
        r.a1[at(c)] = normed
        tables = [table[at(c)] for table in (r.cosine, r.sine)]
        queries = turn(mul(normed, r.wq[...]), *tables, 1.0)
        r.q[at(c)] = (queries.astype(BF16).astype(F32) * score_scale).astype(BF16)
        r.k[at(c)] = turn(mul(normed, r.wk[...]), *tables, 1.0).astype(BF16)

    def head_lanes(head):
        return (lax.broadcasted_iota(jnp.int32, (1, cols), 1) // HD) == head

    def only(tensor, lanes):
        return jnp.where(lanes, tensor, jnp.zeros_like(tensor))

    def attend(c):
        first.total(c, r.sum_a)
        own = mul(r.a1[at(c)], r.wv[...])
        r.vm[at(c)] = (0.5 * own + 0.5 * r.sum_a[...]).astype(BF16)
        low, span = window(c)
        mask_bias(c)
        r.sum_a[...] = jnp.zeros_like(r.sum_a)

        def one(head, carry):
            lanes = head_lanes(head)
            scores = mul(only(r.q[at(c)], lanes), r.k[low : low + span], NT)
            scores = scores + r.bias[:, :span]
            largest = jnp.max(scores, axis=-1, keepdims=True)
            raised = jnp.exp(scores - largest)
            summed = jnp.sum(raised, axis=-1, keepdims=True)
            weights = (raised * (1.0 / summed)).astype(BF16)
            r.sum_a[...] += mul(weights, only(r.vm[low : low + span], lanes))
            here = lax.broadcasted_iota(jnp.int32, (1, 128), 1) == head
            r.lse[at(c)] = jnp.where(here, largest + jnp.log(summed), r.lse[at(c)])
            return carry

        lax.fori_loop(0, heads, one, 0)
        r.att[c, me] = r.sum_a[...].astype(BF16)
        heads_all.own(c, r.att.at[c, me])

    def feed(c):
        h = r.x[at(c)].astype(F32)
        for k in range(count):
            h = h + mul(r.att[c, k], r.wo[k])
        r.big[...] = h
        r.h_own[c] = r.big[pl.ds(pl.multiple_of(side * owned, owned), owned)]
        scale = lax.rsqrt(jnp.mean(h * h, axis=-1, keepdims=True) + EPSILON)
        normed = (h * scale * r.norm_two[...]).astype(BF16)
        r.a2[at(c)] = normed
        gate = mul(normed, r.wg[...], NT)
        up = mul(normed, r.wu[...], NT)
        sig = jax.nn.sigmoid(gate)
        silu = gate * sig
        hidden = (silu * up).astype(BF16)
        r.hid[at(c)] = hidden
        grad_hidden = mul(r.g[at(c)], r.wd[...], NT)
        grad_gate = (grad_hidden * up * sig * (1.0 + gate * (1.0 - sig))).astype(BF16)
        grad_up = (grad_hidden * silu).astype(BF16)
        r.dga[at(c)] = grad_gate
        r.dup[at(c)] = grad_up
        back = mul(grad_gate, r.wg[...]) + mul(grad_up, r.wu[...])
        r.b_part[c] = back.astype(BF16).reshape(count, share, width)
        back2.open(c)

    def down(c):
        part = mul(r.hid[at(c)], r.wd[...])
        r.o_part[c] = part.astype(BF16).reshape(count, share, width)

    def add_gain(which, grad):
        quarter = width // 4
        for j in range(4):
            r.gains[4 * which + j : 4 * which + j + 1] += grad[:, j * quarter : (j + 1) * quarter]

    def norm_back(values, gain, grad):
        scale = lax.rsqrt(jnp.mean(values * values, axis=-1, keepdims=True) + EPSILON)
        grad_gain = jnp.sum(grad * values * scale, axis=0, keepdims=True)
        scaled = grad * gain
        inner = jnp.mean(scaled * values, axis=-1, keepdims=True)
        return grad_gain, scale * scaled - values * scale * scale * scale * inner

    def through_two(c):
        pl.when(edge)(lambda: through_two_owned(c))

    def through_two_owned(c):
        back2.total(c, r.sum_b)
        grad_gain, grad = norm_back(r.h_own[c], r.norm_two[...], r.sum_b[...])
        add_gain(1, grad_gain)
        low = (r.g[mine(c)].astype(F32) + grad).astype(BF16)
        r.db_own[c] = low
        first.drain_one(c)
        for k in range(count):
            part = mul(low, r.wo[k], NT).astype(BF16)

            @pl.when(me == k)
            def _():
                r.do[mine(c)] = part

            @pl.when(me != k)
            def _():
                r.f_part[c, k, :owned] = part
                remote(
                    r.f_part.at[c, k, pl.ds(0, owned)],
                    r.do.at[mine(c)],
                    r.do_sent.at[0],
                    r.do_came.at[c, side],
                    on_line(k),
                ).start()

    def do_wait(c):
        for s in range(2):

            @pl.when(me != s * (count - 1))
            def _():
                slot = r.do.at[pl.ds(c * CHUNK + s * owned, owned)]
                remote(
                    slot, slot, r.do_sent.at[0], r.do_came.at[c, s], on_line(0)
                ).wait_recv()

    def attend_back(c):
        do_wait(c)
        low, span = window(c)
        mask_bias(c)
        r.sum_a[...] = jnp.zeros_like(r.sum_a)
        r.dk_sum[at(c)] = jnp.zeros((CHUNK, cols), F32)
        r.dv_sum[at(c)] = jnp.zeros((CHUNK, cols), F32)

        def one(head, carry):
            lanes = head_lanes(head)
            q_head = only(r.q[at(c)], lanes)
            do_head = only(r.do[at(c)], lanes)
            here = lax.broadcasted_iota(jnp.int32, (1, 128), 1) == head
            lse = jnp.sum(jnp.where(here, r.lse[at(c)], 0.0), axis=-1, keepdims=True)
            scores = mul(q_head, r.k[low : low + span], NT) + r.bias[:, :span]
            probs = jnp.exp(scores - lse)
            grad_probs = mul(do_head, r.vm[low : low + span], NT)
            inner = jnp.sum(probs * grad_probs, axis=-1, keepdims=True)
            grad_scores = (probs * (grad_probs - inner)).astype(BF16)
            r.sum_a[...] += mul(grad_scores, only(r.k[low : low + span], lanes))
            r.dk_sum[low : low + span] += mul(grad_scores, q_head, TN)
            r.dv_sum[low : low + span] += mul(probs.astype(BF16), do_head, TN)
            return carry

        lax.fori_loop(0, heads, one, 0)
        tables = [table[at(c)] for table in (r.cosine, r.sine)]
        r.dqkv[at(c), :cols] = turn(r.sum_a[...] * score_scale, *tables, -1.0).astype(BF16)

    def values_back(c):
        tables = [table[at(c)] for table in (r.cosine, r.sine)]
        r.dqkv[at(c), cols : 2 * cols] = turn(r.dk_sum[at(c)], *tables, -1.0).astype(BF16)
        grad_values = (0.5 * r.dv_sum[at(c)]).astype(BF16)
        r.dv_all[c, me] = grad_values
        r.dqkv[at(c), 2 * cols :] = grad_values
        values_all.own(c, r.dv_all.at[c, me])

    def keys_back(c):
        back = mul(r.dqkv[at(c), :cols], r.wq[...], NT)
        back = back + mul(r.dqkv[at(c), cols : 2 * cols], r.wk[...], NT)
        back = back + mul(r.dqkv[at(c), 2 * cols :], r.wv[...], NT)
        back2.drain_one(c)
        r.b_part[c] = back.astype(BF16).reshape(count, share, width)
        back1.open(c)

    stores = []

    def local(src, dst):
        copy = pltpu.make_async_copy(src, dst, r.store_sem.at[len(stores)])
        copy.start()
        return copy

    def own_copy(which, c, j):
        parts, dst = ((r.b_part, r.grad_input), (r.o_part, r.output))[which]
        place = pl.ds(pl.multiple_of(c * CHUNK + side * owned + j * share, share), share)
        return pltpu.make_async_copy(
            parts.at[c, side * (count // 2) + j], dst.at[place], r.own_sem.at[which]
        )

    def own_rows(which, c, parts, rows):
        for j in range(count // 2):
            parts[c, side * (count // 2) + j] = rows[j * share : (j + 1) * share]
            own_copy(which, c, j).start()

    def through_one(c):
        pl.when(edge)(lambda: through_one_owned(c))

    def through_one_owned(c):
        back1.total(c, r.sum_b)
        x = r.x[mine(c)].astype(F32)
        grad_gain, grad = norm_back(x, r.norm_one[...], r.sum_b[...])
        add_gain(0, grad_gain)
        own_rows(0, c, r.b_part, (r.db_own[c].astype(F32) + grad).astype(BF16))
        gin_all.own(c, r.b_part)

    def finish_out(c):
        pl.when(edge)(lambda: finish_out_owned(c))

    def finish_out_owned(c):
        out.total(c, r.sum_b)
        own_rows(1, c, r.o_part, (r.h_own[c] + r.sum_b[...]).astype(BF16))
        outs_all.own(c, r.o_part)

    def settle():
        for c in range(chunks):
            outs_all.settle(c)
            gin_all.settle(c)

    x_first = ((other_core, other_x, other_y), (core, along_x, along_y))
    y_first = ((other_core, other_y, other_x), (core, along_y, along_x))

    def by_cols(ref, size):
        return lambda start, n: ref.at[:, pl.ds(pl.multiple_of(start * size, size), n * size)]

    def by_rows(ref, size):
        return lambda start, n: ref.at[pl.ds(pl.multiple_of(start * size, size), n * size)]

    def keep(src, dst):
        return lambda: stores.append(local(src, dst))

    eighth = width // 8
    part = cols // 8
    plane_gate = Plane(
        *x_first,
        by_cols(r.wg, eighth),
        [r.u_in0.at[0], r.u_in1.at[0], r.u_in2.at[0]],
        r.p_sent.at[0],
        r.p_came.at[0],
        r.p_free.at[0],
        keep(r.wg, r.grad_gate),
    )
    plane_up = Plane(
        *y_first,
        by_cols(r.wu, eighth),
        [r.u_in0.at[1], r.u_in1.at[1], r.u_in2.at[1]],
        r.p_sent.at[1],
        r.p_came.at[1],
        r.p_free.at[1],
        keep(r.wu, r.grad_up),
    )
    plane_down = Plane(
        *x_first,
        by_cols(r.wd, eighth),
        [r.u_in0.at[2], r.u_in1.at[2], r.u_in2.at[2]],
        r.p_sent.at[2],
        r.p_came.at[2],
        r.p_free.at[2],
        keep(r.wd, r.grad_down),
    )
    plane_out = Plane(
        *y_first,
        by_rows(r.a2, eighth),
        [
            r.g.at[pl.ds(0, 4 * eighth)],
            r.g.at[pl.ds(4 * eighth, 2 * eighth)],
            r.g.at[pl.ds(6 * eighth, eighth)],
        ],
        r.p_sent.at[3],
        r.p_came.at[3],
        r.p_free.at[3],
        keep(r.wo.at[me], r.grad_out),
        by_rows(r.wo.at[me], part),
    )
    plane_qkv = [
        Plane(
            *(x_first if index == 1 else y_first),
            by_rows(ref, eighth),
            [
                r.f_in.at[pl.ds((7 * index) * eighth, 4 * eighth)],
                r.f_in.at[pl.ds((7 * index + 4) * eighth, 2 * eighth)],
                r.f_in.at[pl.ds((7 * index + 6) * eighth, eighth)],
            ],
            r.p_sent.at[4 + index],
            r.p_came.at[4 + index],
            r.p_free.at[4 + index],
            keep(ref, grad),
        )
        for index, (ref, grad) in enumerate(
            ((r.wq, r.grad_query), (r.wk, r.grad_key), (r.wv, r.grad_value))
        )
    ]
    plane_one = Plane(
        *x_first,
        by_cols(r.wv1, eighth),
        [r.v_in0, r.v_in1, r.v_in2],
        r.p_sent.at[7],
        r.p_came.at[7],
        r.p_free.at[7],
        keep(r.wv1, r.grad_one),
    )

    def units_grad(left, right, into):
        for start in range(0, units, 256):
            span = min(256, units - start)
            into[start : start + span] = mul(left[:, start : start + span], right[...], TN).astype(
                BF16
            )

    def out_grad():
        pl.when(edge)(out_grad_owned)

    def out_grad_owned():
        low = r.db_own[...].reshape(chunks * owned, width)
        for k in range(count):
            own = jnp.concatenate(
                [
                    r.att[c, k, pl.ds(pl.multiple_of(side * owned, owned), owned)]
                    for c in range(chunks)
                ],
                axis=0,
            )
            grad = mul(own, low, TN).astype(BF16)
            for s in range(8):
                r.a2[s * eighth + k * part : s * eighth + (k + 1) * part] = grad[
                    s * part : (s + 1) * part
                ]

    def out_next(step):
        if step < 3:
            pl.when(edge)(lambda: plane_out.next(step))
        else:
            plane_out.next(step)

    def out_piece(peer):
        slot = plane_out.start_of(3)
        return pl.ds(pl.multiple_of(slot * eighth + peer * part, part), part)

    def out_line_copy(step):
        peer = (me + step) % count
        return remote(
            r.a2.at[out_piece(peer)],
            r.z_in.at[side],
            r.z_sent.at[step],
            r.z_came.at[side],
            on_line(peer),
        )

    def out_line_send():
        @pl.when(edge)
        def _():
            plane_out.add(2)
            for step in range(1, count):
                out_line_copy(step).start()

    def out_line_sum():
        for s in range(2):

            @pl.when(me != s * (count - 1))
            def _():
                slot = r.z_in.at[s]
                remote(slot, slot, r.z_sent.at[0], r.z_came.at[s], on_line(0)).wait_recv()

        @pl.when(edge)
        def _():
            r.z_in[side] = r.a2[out_piece(me)]

        grad = r.z_in[0].astype(F32) + r.z_in[1].astype(F32)
        slot = plane_out.start_of(3)
        r.wo[me, pl.ds(pl.multiple_of(slot * part, part), part)] = grad.astype(BF16)
        plane_out.send(3)

    def values_one(c):
        grad = None
        for k in range(count):
            values = r.dv_all[c, k]
            piece = mul(values, r.wv1[:, k * cols : (k + 1) * cols], NT)
            grad = piece if grad is None else grad + piece
            piece = mul(r.first_in[at(c)], values, TN)
            if c > 0:
                piece = piece + r.big[:, k * cols : (k + 1) * cols]
            r.big[:, k * cols : (k + 1) * cols] = piece
        r.dk_sum[at(c)] = grad
        stores.append(local(r.dk_sum.at[at(c)], r.grad_first.at[at(c)]))

    def qkv_grad():
        for start in range(0, width, 256):
            grad = mul(r.a1[:, start : start + 256], r.dqkv[...], TN).astype(BF16)
            for index, into in enumerate((r.wq, r.wk, r.wv)):
                into[start : start + 256] = grad[:, index * cols : (index + 1) * cols]

    def grad_gate():
        units_grad(r.dga, r.a2, r.wg)

    def grad_up():
        units_grad(r.dup, r.a2, r.wu)

    def grad_down():
        units_grad(r.hid, r.g, r.wd)

    def qkv_next(step):
        for plane in plane_qkv:
            plane.next(step)

    def one_start():
        r.wv1[...] = r.big[...].astype(BF16)

    def gain_line_copy(step):
        return remote(
            r.gains,
            r.gain_in.at[side],
            r.gain_sent.at[2 + step],
            r.gain_came.at[side],
            on_line((me + step) % count),
        )

    def gain_copy(index):
        return remote(
            r.gain_sum.at[index],
            r.gain_in.at[2 + index],
            r.gain_sent.at[index],
            r.gain_came.at[2 + index],
            in_plane((other_core, other_x, other_y)[index]),
        )

    def gain_line():
        @pl.when(edge)
        def _():
            for step in range(1, count):
                gain_line_copy(step).start()

    def gain_plane(index):
        if index == 0:
            for s in range(2):

                @pl.when(me != s * (count - 1))
                def _():
                    slot = r.gain_in.at[s]
                    remote(
                        slot, slot, r.gain_sent.at[0], r.gain_came.at[s], on_line(0)
                    ).wait_recv()

            @pl.when(edge)
            def _():
                r.gain_in[side] = r.gains[...]

            total = r.gain_in[0] + r.gain_in[1]
        else:
            gain_copy(index - 1).wait_recv()
            total = r.gain_sum[index - 1] + r.gain_in[1 + index]
        if index < 3:
            r.gain_sum[index] = total
            gain_copy(index).start()
        else:
            for which, into in enumerate((r.gain_one, r.gain_two)):
                into[...] = jnp.concatenate(
                    [total[4 * which + j : 4 * which + j + 1] for j in range(4)], axis=1
                )

    r.gains[...] = jnp.zeros_like(r.gains)
    wo_line()
    first_part(0)
    wo_all.hop(0, 1)
    first_part(1)
    loaded(2, 3, 4, 5, 11, 13, 14)
    project(0)
    first.near(0, 0)
    wo_all.hop(0, 2)
    project(1)
    first_part(2)
    wo_all.hop(0, 3)
    first.near(0, 1)
    first.near(1, 0)
    wo_plane(0, True)
    project(2)
    first.near(1, 1)
    first.far(0)
    attend(0)
    wo_plane(0, False)
    first_part(3)
    first.far(1)
    loaded(7, 8, 9, 10, 12)
    wo_plane(1, True)
    first.near(2, 0)
    attend(1)
    first.far(2)
    first.near(2, 1)
    heads_all.hop(0, 1)
    first.near(3, 0)
    wo_plane(1, False)
    first.near(3, 1)
    wo_plane(2, True)
    heads_all.hop(0, 2)
    attend(2)
    heads_all.hop(1, 1)
    first.far(3)
    wo_plane(2, False)
    heads_all.hop(0, 3)
    feed(0)
    project(3)
    down(0)
    out.open(0)
    heads_all.hop(2, 1)
    heads_all.hop(1, 2)
    back2.near(0, 0)
    attend(3)
    heads_all.hop(2, 2)
    back2.far(0, 0)
    out.near(0, 0)
    heads_all.hop(1, 3)
    out.near(0, 1)
    feed(1)
    heads_all.hop(3, 1)
    heads_all.hop(2, 3)
    feed(2)
    back2.near(1, 0)
    down(2)
    heads_all.hop(3, 2)
    back2.near(1, 1)
    out.far(0, 0)
    back2.far(1, 0)
    back2.near(2, 0)
    back2.far(1, 1)
    back2.near(2, 1)
    down(1)
    out.far(0, 1)
    out.open(2)
    heads_all.hop(3, 3)
    back2.near(0, 1)
    feed(3)
    down(3)
    back2.far(2, 0)
    out.near(2, 0)
    out.open(1)
    back2.near(3, 0)
    back2.far(0, 1)
    grad_gate()
    out.near(2, 1)
    back2.far(2, 1)
    back2.far(3, 0)
    back2.near(3, 1)
    out.far(2, 0)
    out.near(1, 0)
    out.open(3)
    out.far(2, 1)
    through_two(0)
    back2.far(3, 1)
    out.near(3, 0)
    grad_up()
    plane_up.next(0)
    grad_down()
    through_two(1)
    through_two(2)
    out.far(1, 0)
    attend_back(0)
    plane_gate.next(0)
    through_two(3)
    out.far(3, 0)
    finish_out(0)
    out.near(1, 1)
    plane_down.next(0)
    attend_back(1)
    attend_back(2)
    out.far(1, 1)
    values_back(0)
    attend_back(3)
    values_back(2)
    values_back(1)
    plane_down.next(1)
    values_back(3)
    values_all.hop(0, 1)
    plane_up.next(1)
    plane_gate.next(1)
    values_all.hop(1, 1)
    outs_all.pass_on(0, 0)
    keys_back(1)
    values_all.hop(0, 2)
    plane_down.next(2)
    out.near(3, 1)
    finish_out(2)
    values_all.hop(3, 1)
    outs_all.pass_far(0, 0)
    keys_back(2)
    plane_up.next(2)
    out.far(3, 1)
    back1.near(1, 0)
    out_grad()
    plane_gate.next(2)
    plane_down.next(3)
    keys_back(0)
    values_all.hop(3, 2)
    back1.near(1, 1)
    values_all.hop(1, 2)
    keys_back(3)
    back1.far(1, 0)
    finish_out(1)
    back1.near(2, 0)
    outs_all.pass_on(2, 0)
    plane_gate.next(3)
    finish_out(3)
    plane_up.next(3)
    back1.near(0, 0)
    back1.far(2, 0)
    qkv_grad()
    values_all.hop(0, 3)
    qkv_next(0)
    values_all.hop(2, 1)
    back1.near(3, 0)
    back1.far(0, 0)
    back1.far(1, 1)
    back1.near(2, 1)
    back1.near(0, 1)
    qkv_next(1)
    values_all.hop(2, 2)
    outs_all.pass_on(0, 1)
    plane_gate.next(4)
    back1.far(2, 1)
    out_next(0)
    values_all.hop(3, 3)
    back1.far(3, 0)
    out_next(1)
    plane_down.next(4)
    through_one(1)
    outs_all.pass_on(3, 0)
    outs_all.pass_far(2, 0)
    back1.near(3, 1)
    outs_all.pass_on(1, 0)
    outs_all.pass_on(2, 1)
    values_all.hop(1, 3)
    back1.far(0, 1)
    through_one(2)
    back1.far(3, 1)
    values_all.hop(2, 3)
    values_one(0)
    gin_all.pass_on(1, 0)
    outs_all.pass_on(1, 1)
    plane_up.next(4)
    outs_all.pass_far(0, 1)
    outs_all.pass_far(1, 0)
    values_one(1)
    values_one(2)
    through_one(0)
    values_one(3)
    out_next(2)
    gin_all.pass_on(1, 1)
    plane_gate.next(5)
    one_start()
    through_one(3)
    outs_all.pass_far(2, 1)
    plane_one.next(0)
    plane_down.next(5)
    outs_all.pass_far(1, 1)
    outs_all.pass_on(3, 1)
    gin_all.pass_far(1, 0)
    out_line_send()
    gain_line()
    plane_one.next(1)
    outs_all.pass_far(3, 0)
    plane_up.next(5)
    gin_all.pass_on(2, 0)
    gin_all.pass_on(3, 0)
    gin_all.pass_far(1, 1)
    gin_all.pass_on(2, 1)
    qkv_next(2)
    plane_gate.next(6)
    plane_one.next(2)
    gin_all.pass_far(2, 0)
    qkv_next(3)
    gin_all.pass_on(0, 0)
    gain_plane(0)
    plane_one.next(3)
    out_line_sum()
    gin_all.pass_on(0, 1)
    outs_all.pass_far(3, 1)
    qkv_next(4)
    gin_all.pass_on(3, 1)
    gin_all.pass_far(3, 0)
    plane_one.next(4)
    gin_all.pass_far(2, 1)
    plane_down.next(6)
    out_next(4)
    gin_all.pass_far(0, 0)
    qkv_next(5)
    gin_all.pass_far(0, 1)
    gain_plane(1)
    gin_all.pass_far(3, 1)
    plane_one.next(5)
    gain_plane(2)
    plane_up.next(6)
    qkv_next(6)
    plane_one.next(6)
    gain_plane(3)
    out_next(5)
    out_next(6)
    settle()
    for copy in stores:
        copy.wait()
    for line in (back1, out, outs_all, gin_all):
        line.drain(chunks)
    heads_all.drain(lambda slots: r.att.at[:, pl.ds(0, slots)])
    values_all.drain(lambda slots: r.dv_all.at[:, pl.ds(0, slots)])
    for plane in (plane_gate, plane_up, plane_down, plane_out, plane_one, *plane_qkv):
        plane.drain()
    for index in range(3):
        gain_copy(index).wait_send()

    @pl.when(me != 0)
    def _():
        pl.when(me != count - 1)(lambda: first.drain(chunks))

    @pl.when(edge)
    def _():
        for which, dst in enumerate((r.grad_input, r.output)):
            rows = dst.at[pl.ds(0, chunks * owned)]
            pltpu.make_async_copy(rows, rows, r.own_sem.at[which]).wait()
        for step in range(1, count):
            out_line_copy(step).wait_send()
            gain_line_copy(step).wait_send()

        slots = r.f_part.at[pl.ds(0, chunks // 2), pl.ds(0, count - 1)]
        remote(slots, slots, r.do_sent.at[0], r.do_came.at[0, 0], on_line(0)).wait_send()


def fused_layer(arrays, sizes):
    count, groups, tokens, width, cols, units = sizes
    chunks = tokens // CHUNK
    share = CHUNK // count
    eighth = width // 8
    hbm = pl.BlockSpec(memory_space=pl.ANY)
    vmem = pl.BlockSpec(memory_space=pltpu.VMEM)
    ins = dict(
        block_input=hbm,
        layer_one=hbm,
        grad_output=hbm,
        norm_one_in=hbm,
        w_query=hbm,
        w_key=hbm,
        w_value=hbm,
        w_out=hbm,
        norm_two_in=hbm,
        w_gate=hbm,
        w_up=hbm,
        w_down=hbm,
        w_value_one=hbm,
        rates_in=hbm,
        seg_row_in=hbm,
    )
    outs = dict(
        output=((tokens, width), BF16, hbm),
        grad_input=((tokens, width), BF16, hbm),
        grad_first=((tokens, cols), F32, hbm),
        grad_query=((width, cols), BF16, hbm),
        grad_key=((width, cols), BF16, hbm),
        grad_value=((width, cols), BF16, hbm),
        grad_out=((cols, width), BF16, hbm),
        grad_gate=((units, width), BF16, hbm),
        grad_up=((units, width), BF16, hbm),
        grad_down=((units, width), BF16, hbm),
        grad_one=((cols, width), BF16, hbm),
        gain_one=((1, width), F32, vmem),
        gain_two=((1, width), F32, vmem),
    )
    dma = pltpu.SemaphoreType.DMA

    def low(*shape):
        return pltpu.VMEM(shape, BF16)

    def full(*shape):
        return pltpu.VMEM(shape, F32)

    slots = (chunks, count)
    scratch = dict(
        norm_one=full(1, width),
        norm_two=full(1, width),
        rates=full(1, 128),
        seg_row=pltpu.VMEM((1, tokens), jnp.int32),
        cosine=full(tokens, 128),
        sine=full(tokens, 128),
        x=low(tokens, width),
        g=low(tokens, width),
        first_in=low(tokens, cols),
        wq=low(width, cols),
        wk=low(width, cols),
        wv=low(width, cols),
        wv1=low(cols, width),
        wo=low(count, cols, width),
        wg=low(units, width),
        wu=low(units, width),
        wd=low(units, width),
        a1=low(tokens, width),
        a2=low(tokens, width),
        q=low(tokens, cols),
        k=low(tokens, cols),
        vm=low(tokens, cols),
        lse=full(tokens, 128),
        bias=full(CHUNK, CHUNK + REACH),
        sum_a=full(CHUNK, cols),
        sum_b=full(CHUNK // 2, width),
        big=full(CHUNK, width),
        att=low(*slots, CHUNK, cols),
        dv_all=low(*slots, CHUNK, cols),
        hid=low(tokens, units),
        dga=low(tokens, units),
        dup=low(tokens, units),
        h_own=full(chunks, CHUNK // 2, width),
        db_own=low(chunks, CHUNK // 2, width),
        do=low(tokens, cols),
        dqkv=low(tokens, 3 * cols),
        dk_sum=full(tokens, cols),
        dv_sum=full(tokens, cols),
        gains=full(8, width // 4),
        gain_sum=full(3, 8, width // 4),
        gain_in=full(5, 8, width // 4),
        u_in0=low(3, units, 4 * eighth),
        u_in1=low(3, units, 2 * eighth),
        u_in2=low(3, units, eighth),
        z_in=low(2, cols // 8, width),
        v_in0=low(cols, 4 * eighth),
        v_in1=low(cols, 2 * eighth),
        v_in2=low(cols, eighth),
        f_part=low(*slots, CHUNK, cols),
        f_in=low(chunks * count * CHUNK, cols),
        f_meet=low(chunks, CHUNK, cols),
        b_part=low(*slots, share, width),
        b_in=low(*slots, share, width),
        o_part=low(*slots, share, width),
        o_in=low(*slots, share, width),
        load_sem=dma((15,)),
        store_sem=dma((chunks + 8,)),
        own_sem=dma((2,)),
        wo_sent=dma((3,)),
        wo_came=dma((3,)),
        wo_line_came=dma((1, count)),
        wo_right=dma((1,)),
        wo_left=dma((1,)),
        do_sent=dma((1,)),
        do_came=dma((chunks, 2)),
        p_sent=dma((8, 6)),
        p_came=dma((8, 6)),
        p_free=pltpu.SemaphoreType.REGULAR((8, 3)),
        z_sent=dma((count,)),
        z_came=dma((2,)),
        gain_sent=dma((count + 2,)),
        gain_came=dma((5,)),
        f_sent=dma((chunks,)),
        f_came=dma(slots),
        f_met=dma((chunks,)),
        b_sent=dma((chunks,)),
        b_came=dma(slots),
        o_sent=dma((chunks,)),
        o_came=dma(slots),
        d_sent=dma((chunks,)),
        d_came=dma(slots),
        att_came=dma(slots),
        att_right=dma((1,)),
        att_left=dma((1,)),
        dv_came=dma(slots),
        dv_right=dma((1,)),
        dv_left=dma((1,)),
        out_came=dma(slots),
        out_sent=dma((chunks,)),
        gin_came=dma(slots),
        gin_sent=dma((chunks,)),
    )
    results = pl.pallas_call(
        functools.partial(layer_kernel, [*ins, *outs, *scratch], sizes),
        out_shape=[jax.ShapeDtypeStruct(item[0], item[1]) for item in outs.values()],
        in_specs=list(ins.values()),
        out_specs=[item[2] for item in outs.values()],
        scratch_shapes=list(scratch.values()),
        compiler_params=pltpu.CompilerParams(
            collective_id=0, has_side_effects=True, vmem_limit_bytes=VMEM_LIMIT
        ),
        cost_estimate=pl.CostEstimate(
            flops=2 * 13 * 10**9, bytes_accessed=40 * 2**20, transcendentals=0
        ),
    )(*arrays)
    return widen(results)


def widen(results):
    steps = 2
    *arrays, gain_one, gain_two = results
    width = gain_one.shape[1]

    def one(*refs):
        half = len(refs) // 2
        for src, dst in zip(refs[: half - 2], refs[half:-2]):
            dst[...] = src[...].astype(dst.dtype)
        for src, dst in zip(refs[half - 2 : half], refs[-2:]):
            dst[...] = src[0]

    specs = [
        pl.BlockSpec((array.shape[0] // steps, array.shape[1]), lambda i: (i, 0))
        for array in arrays
    ]
    shapes = [
        jax.ShapeDtypeStruct(array.shape, F32 if index else BF16)
        for index, array in enumerate(arrays)
    ]
    return pl.pallas_call(
        one,
        grid=(steps,),
        in_specs=specs + [pl.BlockSpec((1, width), lambda i: (0, 0))] * 2,
        out_specs=specs + [pl.BlockSpec((width,), lambda i: (0,))] * 2,
        out_shape=shapes + [jax.ShapeDtypeStruct((width,), F32)] * 2,
        compiler_params=pltpu.CompilerParams(vmem_limit_bytes=VMEM_LIMIT),
    )(*arrays, gain_one, gain_two)


def on_device(*arguments):
    (
        block_input,
        layer_one_input,
        segment_ids,
        grad_output,
        norm_one,
        w_query,
        w_key,
        w_value,
        w_out,
        norm_two,
        w_gate,
        w_up,
        w_down,
        w_value_one,
    ) = arguments
    count = lax.axis_size("mp")
    groups = lax.axis_size("dp")
    tokens, width = block_input.shape
    cols = w_query.shape[1]
    units = w_gate.shape[1]
    fits = (
        count == 4
        and groups == 8
        and tokens == 4 * CHUNK
        and cols == 256
        and width == count * cols
        and units % 64 == 0
        and units <= 704
        and segment_ids.shape[0] == 1
    )
    if not fits:
        return by_collectives(*arguments)
    half = HD // 2
    rates = np.exp(np.arange(half, dtype=np.float32) * np.float32(-math.log(10000.0) / half))
    r = fused_layer(
        (
            block_input,
            layer_one_input,
            grad_output,
            norm_one[None, :],
            w_query,
            w_key,
            w_value,
            w_out,
            norm_two[None, :],
            w_gate.T,
            w_up.T,
            w_down,
            w_value_one,
            jnp.asarray(np.tile(rates, 4)[None, :]),
            segment_ids,
        ),
        (count, groups, tokens, width, cols, units),
    )
    (
        output,
        grad_input,
        grad_first,
        grad_query,
        grad_key,
        grad_value,
        grad_out,
        grad_gate,
        grad_up,
        grad_down,
        grad_one,
        gain_one,
        gain_two,
    ) = r
    return (
        output,
        grad_input,
        grad_first,
        gain_one,
        grad_query,
        grad_key,
        grad_value,
        grad_out,
        gain_two,
        grad_gate.T,
        grad_up.T,
        grad_down,
        grad_one,
    )


def solution(mesh):
    return jax.shard_map(
        on_device,
        mesh=mesh,
        in_specs=(
            P("dp", None),
            P("dp", "mp"),
            P("dp", None),
            P("dp", None),
            P(),
            P(None, "mp"),
            P(None, "mp"),
            P(None, "mp"),
            P("mp", None),
            P(),
            P(None, "mp"),
            P(None, "mp"),
            P("mp", None),
            P("mp", None),
        ),
        out_specs=(
            P("dp", None),
            P("dp", None),
            P("dp", "mp"),
            P(),
            P(None, "mp"),
            P(None, "mp"),
            P(None, "mp"),
            P("mp", None),
            P(),
            P(None, "mp"),
            P(None, "mp"),
            P("mp", None),
            P("mp", None),
        ),
        check_vma=False,
    )
```

```python
import functools
import math
from types import SimpleNamespace

import jax
import jax.numpy as jnp
import numpy as np
from jax import lax
from jax.experimental import pallas as pl
from jax.experimental.pallas import tpu as pltpu
from jax.sharding import PartitionSpec as P

HD = 64


EPSILON = 1e-06
VMEM_LIMIT = 64 * 2**20 - 2**16


def positions_of(segments):
    position = lax.broadcasted_iota(jnp.int32, segments.shape, 1)
    changed = (segments[:, 1:] != segments[:, :-1]).astype(jnp.int32)
    starts = jnp.concatenate([jnp.ones_like(segments[:, :1]), changed], axis=1)
    return position - lax.cummax(position * starts, axis=1)


def rope_tables(positions, width):
    half_width = width // 2
    rates = jnp.exp(jnp.arange(half_width, dtype=jnp.float32) * (-math.log(10000.0) / half_width))
    angles = positions.astype(jnp.float32)[:, None] * rates[None, :]
    return (jnp.cos(angles)[:, None, :], jnp.sin(angles)[:, None, :])


def rotate(tensor, cosine, sine_part, turn):
    half_width = tensor.shape[-1] // 2
    left_half = tensor[..., :half_width]
    right_half = tensor[..., half_width:]
    return jnp.concatenate(
        [
            left_half * cosine - turn * right_half * sine_part,
            right_half * cosine + turn * left_half * sine_part,
        ],
        axis=-1,
    )


def over_rows(left_side, right_side):
    return lax.dot_general(
        left_side, right_side, (((0,), (0,)), ((), ())), preferred_element_type=jnp.float32
    )


def against(left_side, right_side):
    return lax.dot_general(
        left_side, right_side, (((1,), (1,)), ((), ())), preferred_element_type=jnp.float32
    )


def norm_back(activations, scale_vec, gain_vec, grad_normed):
    grad_gain = jnp.sum(grad_normed * activations * scale_vec, axis=0)
    scaled = grad_normed * gain_vec
    inner = jnp.mean(scaled * activations, axis=-1, keepdims=True)
    return (grad_gain, scale_vec * scaled - activations * scale_vec * scale_vec * scale_vec * inner)


def masked_scores(q_block, key_rows, seg_block, seg_all, first_row, score_scale):
    block_rows = q_block.shape[0]
    scores = (
        jnp.einsum("qhd,khd->hqk", q_block, key_rows, preferred_element_type=jnp.float32)
        * score_scale
    )
    row_index = first_row + lax.broadcasted_iota(jnp.int32, (block_rows, key_rows.shape[0]), 0)
    col_index = lax.broadcasted_iota(jnp.int32, (block_rows, key_rows.shape[0]), 1)
    allowed = (seg_block[:, None] == seg_all[None, :]) & (col_index <= row_index)
    return jnp.where(allowed[None], scores, -1e30)


def attend_forward(queries, key_rows, values, seg_all, score_scale):
    row_count, head_count, width = queries.shape
    block_rows = min(512, row_count)

    def one_block(block_index):
        first_row = block_index * block_rows
        q_block = lax.dynamic_slice_in_dim(queries, first_row, block_rows, 0)
        seg_block = lax.dynamic_slice_in_dim(seg_all, first_row, block_rows, 0)
        scores = masked_scores(q_block, key_rows, seg_block, seg_all, first_row, score_scale)
        largest = jnp.max(scores, axis=-1, keepdims=True)
        raised = jnp.exp(scores - largest)
        summed = jnp.sum(raised, axis=-1, keepdims=True)
        weights = (raised / summed).astype(jnp.bfloat16)
        result = jnp.einsum("hqk,khd->qhd", weights, values, preferred_element_type=jnp.float32)
        return (result, (largest + jnp.log(summed))[..., 0])

    results, log_totals = lax.map(one_block, jnp.arange(row_count // block_rows, dtype=jnp.int32))
    return (results.reshape(row_count, head_count, width), log_totals)


def attend_backward(queries, key_rows, values, seg_all, log_totals, grad_attended, score_scale):
    row_count = queries.shape[0]
    block_rows = min(512, row_count)

    def one_block(carried, block_index):
        grad_keys, grad_values = carried
        first_row = block_index * block_rows
        q_block = lax.dynamic_slice_in_dim(queries, first_row, block_rows, 0)
        seg_block = lax.dynamic_slice_in_dim(seg_all, first_row, block_rows, 0)
        grad_block = lax.dynamic_slice_in_dim(grad_attended, first_row, block_rows, 0)
        scores = masked_scores(q_block, key_rows, seg_block, seg_all, first_row, score_scale)
        probs = jnp.exp(scores - log_totals[block_index][..., None])
        grad_probs = jnp.einsum(
            "qhd,khd->hqk", grad_block, values, preferred_element_type=jnp.float32
        )
        inner = jnp.sum(probs * grad_probs, axis=-1, keepdims=True)
        grad_scores = (probs * (grad_probs - inner)).astype(jnp.bfloat16)
        grad_query = (
            jnp.einsum("hqk,khd->qhd", grad_scores, key_rows, preferred_element_type=jnp.float32)
            * score_scale
        )
        grad_keys = (
            grad_keys
            + jnp.einsum("hqk,qhd->khd", grad_scores, q_block, preferred_element_type=jnp.float32)
            * score_scale
        )
        grad_values = grad_values + jnp.einsum(
            "hqk,qhd->khd",
            probs.astype(jnp.bfloat16),
            grad_block,
            preferred_element_type=jnp.float32,
        )
        return ((grad_keys, grad_values), grad_query)

    zero_rows = jnp.zeros(key_rows.shape, jnp.float32)
    (grad_keys, grad_values), grad_queries = lax.scan(
        one_block, (zero_rows, zero_rows), jnp.arange(row_count // block_rows, dtype=jnp.int32)
    )
    return (grad_queries.reshape(key_rows.shape), grad_keys, grad_values)


def by_collectives(
    block_input,
    layer_one_input,
    segment_ids,
    grad_output,
    norm_one,
    w_query,
    w_key,
    w_value,
    w_out,
    norm_two,
    w_gate,
    w_up,
    w_down,
    w_value_one,
):
    token_count = block_input.shape[0]
    head_count = w_query.shape[1] // HD
    score_scale = HD ** (-0.5)
    seg_all = segment_ids[0]
    cosine, sine_part = rope_tables(positions_of(segment_ids)[0], HD)
    share_rows = token_count // lax.axis_size("mp")
    share_start = lax.axis_index("mp") * share_rows
    inputs = block_input.astype(jnp.float32)
    scale_one = lax.rsqrt(jnp.mean(inputs * inputs, axis=-1, keepdims=True) + EPSILON)
    normed = (inputs * scale_one * norm_one).astype(jnp.bfloat16)
    queries = jnp.dot(normed, w_query, preferred_element_type=jnp.float32).reshape(
        token_count, head_count, HD
    )
    key_rows = jnp.dot(normed, w_key, preferred_element_type=jnp.float32).reshape(
        token_count, head_count, HD
    )
    own_values = jnp.dot(normed, w_value, preferred_element_type=jnp.float32)
    first_values = lax.psum_scatter(
        jnp.dot(layer_one_input, w_value_one, preferred_element_type=jnp.float32).astype(
            jnp.bfloat16
        ),
        "mp",
        scatter_dimension=1,
        tiled=True,
    ).astype(jnp.float32)
    mixed_values = (
        (0.5 * own_values + 0.5 * first_values)
        .astype(jnp.bfloat16)
        .reshape(token_count, head_count, HD)
    )
    turned_q = rotate(queries, cosine, sine_part, 1.0).astype(jnp.bfloat16)
    turned_k = rotate(key_rows, cosine, sine_part, 1.0).astype(jnp.bfloat16)
    attended, log_totals = attend_forward(turned_q, turned_k, mixed_values, seg_all, score_scale)
    attended = attended.reshape(token_count, head_count * HD).astype(jnp.bfloat16)
    branch_one = jnp.dot(attended, w_out, preferred_element_type=jnp.float32)
    inputs_here = lax.dynamic_slice_in_dim(inputs, share_start, share_rows, 0)
    scale_one_here = lax.dynamic_slice_in_dim(scale_one, share_start, share_rows, 0)
    grad_rows = lax.dynamic_slice_in_dim(grad_output, share_start, share_rows, 0).astype(
        jnp.float32
    )
    residual = inputs_here + lax.psum_scatter(
        branch_one.astype(jnp.bfloat16), "mp", scatter_dimension=0, tiled=True
    ).astype(jnp.float32)
    scale_two = lax.rsqrt(jnp.mean(residual * residual, axis=-1, keepdims=True) + EPSILON)
    normed_two = (residual * scale_two * norm_two).astype(jnp.bfloat16)
    normed_two = lax.all_gather(normed_two, "mp", axis=0, tiled=True)
    gate_pre = jnp.dot(normed_two, w_gate, preferred_element_type=jnp.float32)
    up_pre = jnp.dot(normed_two, w_up, preferred_element_type=jnp.float32)
    sigmoid_gate = jax.nn.sigmoid(gate_pre)
    silu_gate = gate_pre * sigmoid_gate
    hidden = (silu_gate * up_pre).astype(jnp.bfloat16)
    branch_two = jnp.dot(hidden, w_down, preferred_element_type=jnp.float32)
    output_share = (
        residual
        + lax.psum_scatter(
            branch_two.astype(jnp.bfloat16), "mp", scatter_dimension=0, tiled=True
        ).astype(jnp.float32)
    ).astype(jnp.bfloat16)
    output = lax.all_gather(output_share, "mp", axis=0, tiled=True)
    grad_down = over_rows(hidden, grad_output)
    grad_hidden = against(grad_output, w_down)
    grad_gate_pre = (
        grad_hidden * up_pre * sigmoid_gate * (1.0 + gate_pre * (1.0 - sigmoid_gate))
    ).astype(jnp.bfloat16)
    grad_up_pre = (grad_hidden * silu_gate).astype(jnp.bfloat16)
    grad_gate = over_rows(normed_two, grad_gate_pre)
    grad_up = over_rows(normed_two, grad_up_pre)
    back_two = against(grad_gate_pre, w_gate) + against(grad_up_pre, w_up)
    grad_normed_two = lax.psum_scatter(
        back_two.astype(jnp.bfloat16), "mp", scatter_dimension=0, tiled=True
    ).astype(jnp.float32)
    grad_norm_two, grad_through_two = norm_back(residual, scale_two, norm_two, grad_normed_two)
    grad_residual = grad_rows + grad_through_two
    residual_low = grad_residual.astype(jnp.bfloat16)
    residual_low = lax.all_gather(residual_low, "mp", axis=0, tiled=True)
    grad_out_proj = over_rows(attended, residual_low)
    grad_attended = (
        against(residual_low, w_out).astype(jnp.bfloat16).reshape(token_count, head_count, HD)
    )
    grad_turned_q, grad_turned_k, grad_mixed = attend_backward(
        turned_q, turned_k, mixed_values, seg_all, log_totals, grad_attended, score_scale
    )
    grad_value_part = (0.5 * grad_mixed).reshape(token_count, head_count * HD).astype(jnp.bfloat16)
    grad_first_full = lax.all_gather(grad_value_part, "mp", axis=1, tiled=True)
    grad_queries = (
        rotate(grad_turned_q, cosine, sine_part, -1.0)
        .reshape(token_count, head_count * HD)
        .astype(jnp.bfloat16)
    )
    grad_keys = (
        rotate(grad_turned_k, cosine, sine_part, -1.0)
        .reshape(token_count, head_count * HD)
        .astype(jnp.bfloat16)
    )
    grad_query = over_rows(normed, grad_queries)
    grad_key = over_rows(normed, grad_keys)
    grad_value = over_rows(normed, grad_value_part)
    back_one = (
        against(grad_queries, w_query)
        + against(grad_keys, w_key)
        + against(grad_value_part, w_value)
    )
    grad_normed = lax.psum_scatter(
        back_one.astype(jnp.bfloat16), "mp", scatter_dimension=0, tiled=True
    ).astype(jnp.float32)
    grad_norm_one, grad_through_one = norm_back(inputs_here, scale_one_here, norm_one, grad_normed)
    gain_rows = jnp.concatenate([grad_norm_one, grad_norm_two])[None, :]
    grad_input, gain_all = (
        lax.all_gather(
            (grad_residual + grad_through_one).astype(jnp.bfloat16), "mp", axis=0, tiled=True
        ).astype(jnp.float32),
        lax.all_gather(gain_rows, "mp", axis=0, tiled=True),
    )
    gain_total = jnp.sum(gain_all, axis=0)
    width = norm_one.shape[0]
    grad_norm_one = gain_total[:width]
    grad_norm_two = gain_total[width:]
    grad_value_one = over_rows(layer_one_input, grad_first_full)
    grad_layer_one_input = against(grad_first_full, w_value_one)
    grad_norm_one, grad_norm_two = lax.psum((grad_norm_one, grad_norm_two), "dp")
    summed = lax.psum(
        tuple(
            part.astype(jnp.bfloat16)
            for part in (
                grad_query,
                grad_key,
                grad_value,
                grad_out_proj,
                grad_value_one,
                grad_gate,
                grad_up,
                grad_down,
            )
        ),
        "dp",
    )
    (
        grad_query,
        grad_key,
        grad_value,
        grad_out_proj,
        grad_value_one,
        grad_gate,
        grad_up,
        grad_down,
    ) = tuple(part.astype(jnp.float32) for part in summed)
    return (
        output,
        grad_input,
        grad_layer_one_input,
        grad_norm_one,
        grad_query,
        grad_key,
        grad_value,
        grad_out_proj,
        grad_norm_two,
        grad_gate,
        grad_up,
        grad_down,
        grad_value_one,
    )


NN = (((1,), (0,)), ((), ()))
NT = (((1,), (1,)), ((), ()))
TN = (((0,), (0,)), ((), ()))
F32 = jnp.float32
BF16 = jnp.bfloat16
CHUNK = 256
REACH = 512
MESH = pl.DeviceIdType.MESH


def mul(left_side, right_side, dims=NN):
    return lax.dot_general(left_side, right_side, dims, preferred_element_type=F32)


def on_line(index):
    return {"mp": index}


def in_plane(index):
    return {"dp": index}


def remote(src, dst, send_sem, recv_sem, device):
    return pltpu.make_async_remote_copy(
        src_ref=src,
        dst_ref=dst,
        send_sem=send_sem,
        recv_sem=recv_sem,
        device_id=device,
        device_id_type=MESH,
    )


class Scatter:
    def __init__(self, me, count, parts, inbox, meet, sent, came, met):
        self.me, self.count = me, count
        self.parts, self.inbox, self.meet = parts, inbox, meet
        self.sent, self.came, self.met = sent, came, met

    def take(self, c, k):
        slot = self.inbox(c, k)
        remote(slot, slot, self.sent.at[c], self.came.at[c, k], on_line(0)).wait_recv()
        self.parts[c, k] = (self.parts[c, k].astype(F32) + self.inbox(c, k)[...].astype(F32)).astype(
            BF16
        )

    def right(self, c, k):
        me = self.me

        @pl.when(me < k)
        def _():
            @pl.when(me > 0)
            def _():
                self.take(c, k)

            remote(
                self.parts.at[c, k],
                self.inbox(c, k),
                self.sent.at[c],
                self.came.at[c, k],
                on_line(me + 1),
            ).start()

    def left(self, c, k):
        me = self.me

        @pl.when(me > k)
        def _():
            @pl.when(me < self.count - 1)
            def _():
                self.take(c, k)

            @pl.when(me == k + 1)
            def _():
                remote(
                    self.parts.at[c, k],
                    self.meet.at[c],
                    self.sent.at[c],
                    self.met.at[c],
                    on_line(me - 1),
                ).start()

            @pl.when(me > k + 1)
            def _():
                remote(
                    self.parts.at[c, k],
                    self.inbox(c, k),
                    self.sent.at[c],
                    self.came.at[c, k],
                    on_line(me - 1),
                ).start()

    def rights(self, c):
        for k in range(self.count - 1, 0, -1):
            self.right(c, k)

    def lefts(self, c):
        for k in range(self.count - 1):
            self.left(c, k)

    def open(self, c):
        @pl.when(self.me == 0)
        def _():
            self.rights(c)

        @pl.when(self.me == self.count - 1)
        def _():
            self.lefts(c)

    def near(self, c, step):
        me, half = self.me, self.count // 2

        @pl.when((me > 0) & (me < half))
        def _():
            self.right(c, self.count - 1 - step)

        @pl.when((me < self.count - 1) & (me >= half))
        def _():
            self.left(c, step)

    def far(self, c):
        me, half = self.me, self.count // 2

        @pl.when((me > 0) & (me < half))
        def _():
            self.lefts(c)

        @pl.when((me < self.count - 1) & (me >= half))
        def _():
            self.rights(c)

    def total(self, c, into):
        me = self.me
        into[...] = self.parts[c, me].astype(F32)

        @pl.when(me > 0)
        def _():
            slot = self.inbox(c, me)
            remote(slot, slot, self.sent.at[c], self.came.at[c, me], on_line(0)).wait_recv()
            into[...] += self.inbox(c, me)[...].astype(F32)

        @pl.when(me < self.count - 1)
        def _():
            slot = self.meet.at[c]
            remote(slot, slot, self.sent.at[c], self.met.at[c], on_line(0)).wait_recv()
            into[...] += self.meet[c].astype(F32)

    def drain_one(self, c):
        slots = self.parts.at[c, pl.ds(0, self.count - 1)]
        remote(slots, slots, self.sent.at[c], self.came.at[c, 0], on_line(0)).wait_send()

    def drain(self, chunks):
        def one(c, carry):
            self.drain_one(c)
            return carry

        lax.fori_loop(0, chunks, one, 0)


class Gather:
    def __init__(self, me, count, place, came, sent_right, sent_left):
        self.me, self.count, self.place = me, count, place
        self.came, self.sent_right, self.sent_left = came, sent_right, sent_left

    def to_right(self, c, k, src):
        return remote(
            src, self.place(c, k), self.sent_right.at[0], self.came.at[c, k], on_line(self.me + 1)
        )

    def to_left(self, c, k, src):
        return remote(
            src, self.place(c, k), self.sent_left.at[0], self.came.at[c, k], on_line(self.me - 1)
        )

    def own(self, c, src):
        me = self.me

        @pl.when(me < self.count - 1)
        def _():
            self.to_right(c, me, src).start()

        @pl.when(me > 0)
        def _():
            self.to_left(c, me, src).start()

    def wait(self, c, k):
        slot = self.place(c, k)
        remote(slot, slot, self.sent_left.at[0], self.came.at[c, k], on_line(0)).wait_recv()

    def hop(self, c, step):
        me = self.me

        @pl.when(me >= step)
        def _():
            k = me - step
            self.wait(c, k)

            @pl.when(me < self.count - 1)
            def _():
                self.to_right(c, k, self.place(c, k)).start()

        @pl.when(me + step < self.count)
        def _():
            k = me + step
            self.wait(c, k)

            @pl.when(me > 0)
            def _():
                self.to_left(c, k, self.place(c, k)).start()

    def drain(self, some):
        for device in range(self.count):
            for slots, sem in (
                ((device + 1) * (device < self.count - 1), self.sent_right),
                ((self.count - device) * (device > 0), self.sent_left),
            ):
                if slots:

                    @pl.when(self.me == device)
                    def _():
                        sent = some(slots)
                        remote(
                            sent, sent, sem.at[0], self.came.at[0, 0], on_line(0)
                        ).wait_send()


class Ends:
    def __init__(self, me, count, parts, inbox, sent, came):
        self.me, self.count, self.half = me, count, count // 2
        self.parts, self.inbox, self.sent, self.came = parts, inbox, sent, came

    def copy(self, c, k):
        step = 1 if k >= self.half else -1
        return remote(
            self.parts.at[c, k],
            self.inbox.at[c, k],
            self.sent.at[c],
            self.came.at[c, k],
            on_line(self.me + step),
        )

    def arrived(self, c, k):
        slot = self.inbox.at[c, k]
        remote(slot, slot, self.sent.at[c], self.came.at[c, k], on_line(0)).wait_recv()

    def open(self, c):
        @pl.when(self.me == 0)
        def _():
            for k in range(self.half, self.count):
                self.copy(c, k).start()

        @pl.when(self.me == self.count - 1)
        def _():
            for k in range(self.half):
                self.copy(c, k).start()

    def hand(self, c, k):
        self.arrived(c, k)
        self.parts[c, k] = (self.parts[c, k].astype(F32) + self.inbox[c, k].astype(F32)).astype(
            BF16
        )
        self.copy(c, k).start()

    def near(self, c, j):
        pl.when(self.me == 1)(lambda: self.hand(c, self.half + j))
        pl.when(self.me == self.count - 2)(lambda: self.hand(c, j))

    def far(self, c, j):
        pl.when(self.me == 1)(lambda: self.hand(c, j))
        pl.when(self.me == self.count - 2)(lambda: self.hand(c, self.half + j))

    def total(self, c, into):
        side = self.me // (self.count - 1)
        rows = self.parts.shape[2]
        for j in range(self.half):
            k = side * self.half + j
            self.arrived(c, k)
            into[j * rows : (j + 1) * rows] = self.parts[c, k].astype(F32) + self.inbox[
                c, k
            ].astype(F32)

    def drain_one(self, c):
        edge = (self.me == 0) | (self.me == self.count - 1)

        def wait(slots):
            remote(slots, slots, self.sent.at[c], self.came.at[c, 0], on_line(0)).wait_send()

        pl.when(edge)(lambda: wait(self.parts.at[c, pl.ds(0, self.half)]))
        pl.when(jnp.logical_not(edge))(lambda: wait(self.parts.at[c]))

    def drain(self, chunks):
        def one(c, carry):
            self.drain_one(c)
            return carry

        lax.fori_loop(0, chunks, one, 0)


class EndsGather:
    def __init__(self, me, count, ref, share, sent, came):
        self.me, self.count, self.half = me, count, count // 2
        self.ref, self.share, self.sent, self.came = ref, share, sent, came

    def place(self, c, k):
        return self.ref.at[pl.ds((c * self.count + k) * self.share, self.share)]

    def copy(self, c, k, src):
        step = 1 if k < self.half else -1
        return remote(
            src,
            self.place(c, k),
            self.sent.at[c],
            self.came.at[c, k],
            on_line(self.me + step),
        )

    def arrived(self, c, k):
        slot = self.place(c, k)
        remote(slot, slot, self.sent.at[c], self.came.at[c, k], on_line(0)).wait_recv()

    def own(self, c, parts):
        @pl.when(self.me == 0)
        def _():
            for k in range(self.half):
                self.copy(c, k, parts.at[c, k]).start()

        @pl.when(self.me == self.count - 1)
        def _():
            for k in range(self.half, self.count):
                self.copy(c, k, parts.at[c, k]).start()

    def hand(self, c, k):
        self.arrived(c, k)
        self.copy(c, k, self.place(c, k)).start()

    def pass_on(self, c, j):
        pl.when(self.me == 1)(lambda: self.hand(c, j))
        pl.when(self.me == self.count - 2)(lambda: self.hand(c, self.half + j))

    def pass_far(self, c, j):
        pl.when(self.me == 1)(lambda: self.hand(c, self.half + j))
        pl.when(self.me == self.count - 2)(lambda: self.hand(c, j))

    def settle(self, c):
        @pl.when(self.me == 0)
        def _():
            for k in range(self.half, self.count):
                self.arrived(c, k)

        @pl.when(self.me == self.count - 1)
        def _():
            for k in range(self.half):
                self.arrived(c, k)

    def drain(self, chunks):
        edge = (self.me == 0) | (self.me == self.count - 1)

        def one(c, carry):
            def wait(count):
                rows = self.ref.at[pl.ds(0, count * self.share)]
                remote(rows, rows, self.sent.at[c], self.came.at[c, 0], on_line(0)).wait_send()

            pl.when(edge)(lambda: wait(self.half))
            pl.when(jnp.logical_not(edge))(lambda: wait(self.count))
            return carry

        lax.fori_loop(0, chunks, one, 0)


class Plane:
    def __init__(self, partners, bits, span, inboxes, sent, came, free, store, gather_span=None):
        self.fenced = gather_span is None
        self.partners, self.bits, self.span = partners, bits, span
        self.inboxes, self.sent, self.came, self.free = inboxes, sent, came, free
        self.store = store
        self.gather_span = span if gather_span is None else gather_span

    def start_of(self, step):
        bits = self.bits
        return (0, 4 * bits[0], 4 * bits[0] + 2 * bits[1], 4 * bits[0] + 2 * bits[1] + bits[2])[step]

    def copy(self, step):
        if step < 3:
            size = 4 >> step
            src = self.span(self.start_of(step) + size * (1 - self.bits[step]), size)
            dst, partner = self.inboxes[step], self.partners[step]
        else:
            size = 1 << (step - 3)
            src = dst = self.gather_span(self.start_of(6 - step), size)
            partner = self.partners[5 - step]
        return remote(src, dst, self.sent.at[step], self.came.at[step], in_plane(partner))

    def send(self, step):
        if step >= 3 and self.fenced:
            pl.semaphore_wait(self.free.at[5 - step], 1)
        self.copy(step).start()

    def add(self, step):
        self.copy(step).wait_send()
        if self.fenced:
            pl.semaphore_signal(
                self.free.at[step],
                inc=1,
                device_id=in_plane(self.partners[step]),
                device_id_type=MESH,
            )
        self.copy(step).wait_recv()
        kept = self.span(self.start_of(step + 1), 4 >> step)
        kept[...] = (kept[...].astype(F32) + self.inboxes[step][...].astype(F32)).astype(BF16)

    def next(self, step):
        if 0 < step <= 3:
            self.add(step - 1)
        elif step > 3:
            self.copy(step - 1).wait_recv()
        if step < 6:
            self.send(step)
        else:
            self.store()

    def drain(self):
        for step in range(3, 6):
            self.copy(step).wait_send()


def turn(tensor, cosine, sine, sign):
    pieces = []
    front = lax.broadcasted_iota(jnp.int32, (1, 128), 1) % HD < HD // 2
    for at in range(0, tensor.shape[-1], 128):
        piece = tensor[:, at : at + 128]
        mixed = jnp.where(front, -pltpu.roll(piece, 96, 1), pltpu.roll(piece, 32, 1)) * sine
        pieces.append(piece * cosine + sign * mixed)
    return jnp.concatenate(pieces, axis=1)


def layer_kernel(names, sizes, *ref_list):
    r = SimpleNamespace(**dict(zip(names, ref_list)))
    count, groups, tokens, width, cols, units = sizes
    chunks = tokens // CHUNK
    share = CHUNK // count
    heads = cols // HD
    owned = CHUNK // 2
    score_scale = HD ** (-0.5)
    me = lax.axis_index("mp")
    row = lax.axis_index("dp")
    side = me // (count - 1)
    edge = (me == 0) | (me == count - 1)

    core = row % 2
    along_x = (row // 2) % 2
    along_y = row // 4
    other_core = row + 1 - 2 * core
    other_x = row + 2 - 4 * along_x
    other_y = row + 4 - 8 * along_y

    loads = {}

    def load(index, src, dst):
        copy = pltpu.make_async_copy(src, dst, r.load_sem.at[index])
        copy.start()
        loads[index] = copy

    def loaded(*indices):
        for index in indices:
            loads.pop(index).wait()

    load(0, r.layer_one, r.first_in)
    load(6, r.w_out, r.wo.at[me])
    load(1, r.w_value_one, r.wv1)
    load(11, r.norm_one_in, r.norm_one)
    load(12, r.norm_two_in, r.norm_two)
    load(13, r.rates_in, r.rates)
    load(14, r.seg_row_in, r.seg_row)
    load(2, r.block_input, r.x)
    load(3, r.w_query, r.wq)
    load(4, r.w_key, r.wk)
    load(5, r.w_value, r.wv)
    load(7, r.grad_output, r.g)
    load(8, r.w_gate, r.wg)
    load(9, r.w_up, r.wu)
    load(10, r.w_down, r.wd)

    barrier = pltpu.get_barrier_semaphore()
    for step in range(1, count):
        pl.semaphore_signal(
            barrier, inc=1, device_id=on_line((me + step) % count), device_id_type=MESH
        )
    for partner in (other_core, other_x, other_y):
        pl.semaphore_signal(barrier, inc=1, device_id=in_plane(partner), device_id_type=MESH)
    pl.semaphore_wait(barrier, count - 1 + 3)

    def f_slot(c, k):
        return r.f_in.at[pl.ds(pl.multiple_of((c * count + k) * CHUNK, CHUNK), CHUNK)]

    loaded(0, 1)

    first = Scatter(
        me, count, r.f_part, f_slot, r.f_meet, r.f_sent, r.f_came, r.f_met
    )
    back2 = Ends(me, count, r.b_part, r.b_in, r.b_sent, r.b_came)
    out = Ends(me, count, r.o_part, r.o_in, r.o_sent, r.o_came)
    back1 = Ends(me, count, r.b_part, r.b_in, r.d_sent, r.d_came)
    heads_all = Gather(
        me, count, lambda c, k: r.att.at[c, k], r.att_came, r.att_right, r.att_left
    )
    values_all = Gather(
        me, count, lambda c, k: r.dv_all.at[c, k], r.dv_came, r.dv_right, r.dv_left
    )

    outs_all = EndsGather(me, count, r.output, share, r.out_sent, r.out_came)
    gin_all = EndsGather(me, count, r.grad_input, share, r.gin_sent, r.gin_came)

    def at(c):
        return pl.ds(c * CHUNK, CHUNK)

    def mine(c):
        return pl.ds(pl.multiple_of(c * CHUNK + side * owned, owned), owned)

    piece = cols // groups
    block = core * 4 + along_x * 2 + along_y

    def wo_rows(slot, step):
        span = 1 << step
        start = pl.multiple_of((block // span) * span * piece, piece)
        return r.wo.at[slot, pl.ds(start, span * piece)]

    wo_all = Gather(
        me, count, lambda c, k: wo_rows(k, 0), r.wo_line_came, r.wo_right, r.wo_left
    )

    def wo_line():
        loaded(6)
        wo_all.own(0, wo_rows(me, 0))

    def wo_wait(index, rows):
        slots = r.wo.at[pl.ds(0, count - 1), pl.ds(0, rows)]
        copy = remote(slots, slots, r.wo_sent.at[index], r.wo_came.at[index], on_line(0))
        copy.wait_send()
        copy.wait_recv()

    def wo_plane(step, start):
        if not start:
            wo_wait(step, piece << step)
            if step == 2:
                wo_all.drain(lambda slots: r.wo.at[pl.ds(0, slots), pl.ds(0, piece)])
            return
        for other in range(1, count):
            slot = (me + other) % count
            remote(
                wo_rows(slot, step),
                wo_rows(slot, step),
                r.wo_sent.at[step],
                r.wo_came.at[step],
                in_plane((other_y, other_x, other_core)[step]),
            ).start()

    def first_part(c):
        part = mul(r.first_in[at(c)], r.wv1[...])
        for k in range(count):
            r.f_part[c, k] = part[:, k * cols : (k + 1) * cols].astype(BF16)
        first.open(c)

    def window(c):
        low = max(0, c * CHUNK - REACH)
        return low, (c + 1) * CHUNK - low

    def visible(c):
        low, span = window(c)
        row_index = c * CHUNK + lax.broadcasted_iota(jnp.int32, (CHUNK, span), 0)
        col_index = low + lax.broadcasted_iota(jnp.int32, (CHUNK, span), 1)
        here = r.seg_row[:, c * CHUNK : (c + 1) * CHUNK].astype(F32)
        diagonal = lax.broadcasted_iota(jnp.int32, (CHUNK, CHUNK), 0) == (
            lax.broadcasted_iota(jnp.int32, (CHUNK, CHUNK), 1)
        )
        column = jnp.sum(jnp.where(diagonal, here, 0.0), axis=1, keepdims=True)
        same = column == r.seg_row[:, low : low + span].astype(F32)
        return same & (col_index <= row_index)

    def mask_bias(c):
        span = window(c)[1]
        r.bias[:, :span] = jnp.where(visible(c), 0.0, -1e30)

    def angle_tables(c):
        position = jnp.sum(jnp.where(visible(c), 1.0, 0.0), axis=1, keepdims=True) - 1.0
        angles = position * r.rates[...]
        r.cosine[at(c)] = jnp.cos(angles)
        r.sine[at(c)] = jnp.sin(angles)

    def project(c):
        angle_tables(c)
        x = r.x[at(c)].astype(F32)
        scale = lax.rsqrt(jnp.mean(x * x, axis=-1, keepdims=True) + EPSILON)
        normed = (x * scale * r.norm_one[...]).astype(BF16)
        r.a1[at(c)] = normed
        tables = [table[at(c)] for table in (r.cosine, r.sine)]
        queries = turn(mul(normed, r.wq[...]), *tables, 1.0)
        r.q[at(c)] = (queries.astype(BF16).astype(F32) * score_scale).astype(BF16)
        r.k[at(c)] = turn(mul(normed, r.wk[...]), *tables, 1.0).astype(BF16)

    def head_lanes(head):
        return (lax.broadcasted_iota(jnp.int32, (1, cols), 1) // HD) == head

    def only(tensor, lanes):
        return jnp.where(lanes, tensor, jnp.zeros_like(tensor))

    def attend(c):
        first.total(c, r.sum_a)
        own = mul(r.a1[at(c)], r.wv[...])
        r.vm[at(c)] = (0.5 * own + 0.5 * r.sum_a[...]).astype(BF16)
        low, span = window(c)
        mask_bias(c)
        r.sum_a[...] = jnp.zeros_like(r.sum_a)

        def one(head, carry):
            lanes = head_lanes(head)
            scores = mul(only(r.q[at(c)], lanes), r.k[low : low + span], NT)
            scores = scores + r.bias[:, :span]
            largest = jnp.max(scores, axis=-1, keepdims=True)
            raised = jnp.exp(scores - largest)
            summed = jnp.sum(raised, axis=-1, keepdims=True)
            weights = (raised * (1.0 / summed)).astype(BF16)
            r.sum_a[...] += mul(weights, only(r.vm[low : low + span], lanes))
            here = lax.broadcasted_iota(jnp.int32, (1, 128), 1) == head
            r.lse[at(c)] = jnp.where(here, largest + jnp.log(summed), r.lse[at(c)])
            return carry

        lax.fori_loop(0, heads, one, 0)
        r.att[c, me] = r.sum_a[...].astype(BF16)
        heads_all.own(c, r.att.at[c, me])

    def feed(c):
        h = r.x[at(c)].astype(F32)
        for k in range(count):
            h = h + mul(r.att[c, k], r.wo[k])
        r.big[...] = h
        r.h_own[c] = r.big[pl.ds(pl.multiple_of(side * owned, owned), owned)]
        scale = lax.rsqrt(jnp.mean(h * h, axis=-1, keepdims=True) + EPSILON)
        normed = (h * scale * r.norm_two[...]).astype(BF16)
        r.a2[at(c)] = normed
        gate = mul(normed, r.wg[...], NT)
        up = mul(normed, r.wu[...], NT)
        sig = jax.nn.sigmoid(gate)
        silu = gate * sig
        hidden = (silu * up).astype(BF16)
        r.hid[at(c)] = hidden
        grad_hidden = mul(r.g[at(c)], r.wd[...], NT)
        grad_gate = (grad_hidden * up * sig * (1.0 + gate * (1.0 - sig))).astype(BF16)
        grad_up = (grad_hidden * silu).astype(BF16)
        r.dga[at(c)] = grad_gate
        r.dup[at(c)] = grad_up
        back = mul(grad_gate, r.wg[...]) + mul(grad_up, r.wu[...])
        r.b_part[c] = back.astype(BF16).reshape(count, share, width)
        back2.open(c)

    def down(c):
        part = mul(r.hid[at(c)], r.wd[...])
        r.o_part[c] = part.astype(BF16).reshape(count, share, width)

    def add_gain(which, grad):
        quarter = width // 4
        for j in range(4):
            r.gains[4 * which + j : 4 * which + j + 1] += grad[:, j * quarter : (j + 1) * quarter]

    def norm_back(values, gain, grad):
        scale = lax.rsqrt(jnp.mean(values * values, axis=-1, keepdims=True) + EPSILON)
        grad_gain = jnp.sum(grad * values * scale, axis=0, keepdims=True)
        scaled = grad * gain
        inner = jnp.mean(scaled * values, axis=-1, keepdims=True)
        return grad_gain, scale * scaled - values * scale * scale * scale * inner

    def through_two(c):
        pl.when(edge)(lambda: through_two_owned(c))

    def through_two_owned(c):
        back2.total(c, r.sum_b)
        grad_gain, grad = norm_back(r.h_own[c], r.norm_two[...], r.sum_b[...])
        add_gain(1, grad_gain)
        low = (r.g[mine(c)].astype(F32) + grad).astype(BF16)
        r.db_own[c] = low
        first.drain_one(c)
        for k in range(count):
            part = mul(low, r.wo[k], NT).astype(BF16)

            @pl.when(me == k)
            def _():
                r.do[mine(c)] = part

            @pl.when(me != k)
            def _():
                r.f_part[c, k, :owned] = part
                remote(
                    r.f_part.at[c, k, pl.ds(0, owned)],
                    r.do.at[mine(c)],
                    r.do_sent.at[0],
                    r.do_came.at[c, side],
                    on_line(k),
                ).start()

    def do_wait(c):
        for s in range(2):

            @pl.when(me != s * (count - 1))
            def _():
                slot = r.do.at[pl.ds(c * CHUNK + s * owned, owned)]
                remote(
                    slot, slot, r.do_sent.at[0], r.do_came.at[c, s], on_line(0)
                ).wait_recv()

    def attend_back(c):
        do_wait(c)
        low, span = window(c)
        mask_bias(c)
        r.sum_a[...] = jnp.zeros_like(r.sum_a)
        r.dk_sum[at(c)] = jnp.zeros((CHUNK, cols), F32)
        r.dv_sum[at(c)] = jnp.zeros((CHUNK, cols), F32)

        def one(head, carry):
            lanes = head_lanes(head)
            q_head = only(r.q[at(c)], lanes)
            do_head = only(r.do[at(c)], lanes)
            here = lax.broadcasted_iota(jnp.int32, (1, 128), 1) == head
            lse = jnp.sum(jnp.where(here, r.lse[at(c)], 0.0), axis=-1, keepdims=True)
            scores = mul(q_head, r.k[low : low + span], NT) + r.bias[:, :span]
            probs = jnp.exp(scores - lse)
            grad_probs = mul(do_head, r.vm[low : low + span], NT)
            inner = jnp.sum(probs * grad_probs, axis=-1, keepdims=True)
            grad_scores = (probs * (grad_probs - inner)).astype(BF16)
            r.sum_a[...] += mul(grad_scores, only(r.k[low : low + span], lanes))
            r.dk_sum[low : low + span] += mul(grad_scores, q_head, TN)
            r.dv_sum[low : low + span] += mul(probs.astype(BF16), do_head, TN)
            return carry

        lax.fori_loop(0, heads, one, 0)
        tables = [table[at(c)] for table in (r.cosine, r.sine)]
        r.dqkv[at(c), :cols] = turn(r.sum_a[...] * score_scale, *tables, -1.0).astype(BF16)

    def values_back(c):
        tables = [table[at(c)] for table in (r.cosine, r.sine)]
        r.dqkv[at(c), cols : 2 * cols] = turn(r.dk_sum[at(c)], *tables, -1.0).astype(BF16)
        grad_values = (0.5 * r.dv_sum[at(c)]).astype(BF16)
        r.dv_all[c, me] = grad_values
        r.dqkv[at(c), 2 * cols :] = grad_values
        values_all.own(c, r.dv_all.at[c, me])

    def keys_back(c):
        back = mul(r.dqkv[at(c), :cols], r.wq[...], NT)
        back = back + mul(r.dqkv[at(c), cols : 2 * cols], r.wk[...], NT)
        back = back + mul(r.dqkv[at(c), 2 * cols :], r.wv[...], NT)
        back2.drain_one(c)
        r.b_part[c] = back.astype(BF16).reshape(count, share, width)
        back1.open(c)

    stores = []

    def local(src, dst):
        copy = pltpu.make_async_copy(src, dst, r.store_sem.at[len(stores)])
        copy.start()
        return copy

    def own_copy(which, c, j):
        parts, dst = ((r.b_part, r.grad_input), (r.o_part, r.output))[which]
        place = pl.ds(pl.multiple_of(c * CHUNK + side * owned + j * share, share), share)
        return pltpu.make_async_copy(
            parts.at[c, side * (count // 2) + j], dst.at[place], r.own_sem.at[which]
        )

    def own_rows(which, c, parts, rows):
        for j in range(count // 2):
            parts[c, side * (count // 2) + j] = rows[j * share : (j + 1) * share]
            own_copy(which, c, j).start()

    def through_one(c):
        pl.when(edge)(lambda: through_one_owned(c))

    def through_one_owned(c):
        back1.total(c, r.sum_b)
        x = r.x[mine(c)].astype(F32)
        grad_gain, grad = norm_back(x, r.norm_one[...], r.sum_b[...])
        add_gain(0, grad_gain)
        own_rows(0, c, r.b_part, (r.db_own[c].astype(F32) + grad).astype(BF16))
        gin_all.own(c, r.b_part)

    def finish_out(c):
        pl.when(edge)(lambda: finish_out_owned(c))

    def finish_out_owned(c):
        out.total(c, r.sum_b)
        own_rows(1, c, r.o_part, (r.h_own[c] + r.sum_b[...]).astype(BF16))
        outs_all.own(c, r.o_part)

    def settle():
        for c in range(chunks):
            outs_all.settle(c)
            gin_all.settle(c)

    x_first = ((other_core, other_x, other_y), (core, along_x, along_y))
    y_first = ((other_core, other_y, other_x), (core, along_y, along_x))

    def by_cols(ref, size):
        return lambda start, n: ref.at[:, pl.ds(pl.multiple_of(start * size, size), n * size)]

    def by_rows(ref, size):
        return lambda start, n: ref.at[pl.ds(pl.multiple_of(start * size, size), n * size)]

    def keep(src, dst):
        return lambda: stores.append(local(src, dst))

    eighth = width // 8
    part = cols // 8
    plane_gate = Plane(
        *x_first,
        by_cols(r.wg, eighth),
        [r.u_in0.at[0], r.u_in1.at[0], r.u_in2.at[0]],
        r.p_sent.at[0],
        r.p_came.at[0],
        r.p_free.at[0],
        keep(r.wg, r.grad_gate),
    )
    plane_up = Plane(
        *y_first,
        by_cols(r.wu, eighth),
        [r.u_in0.at[1], r.u_in1.at[1], r.u_in2.at[1]],
        r.p_sent.at[1],
        r.p_came.at[1],
        r.p_free.at[1],
        keep(r.wu, r.grad_up),
    )
    plane_down = Plane(
        *x_first,
        by_cols(r.wd, eighth),
        [r.u_in0.at[2], r.u_in1.at[2], r.u_in2.at[2]],
        r.p_sent.at[2],
        r.p_came.at[2],
        r.p_free.at[2],
        keep(r.wd, r.grad_down),
    )
    plane_out = Plane(
        *y_first,
        by_rows(r.a2, eighth),
        [
            r.g.at[pl.ds(0, 4 * eighth)],
            r.g.at[pl.ds(4 * eighth, 2 * eighth)],
            r.g.at[pl.ds(6 * eighth, eighth)],
        ],
        r.p_sent.at[3],
        r.p_came.at[3],
        r.p_free.at[3],
        keep(r.wo.at[me], r.grad_out),
        by_rows(r.wo.at[me], part),
    )
    plane_qkv = [
        Plane(
            *(x_first if index == 1 else y_first),
            by_rows(ref, eighth),
            [
                r.f_in.at[pl.ds((7 * index) * eighth, 4 * eighth)],
                r.f_in.at[pl.ds((7 * index + 4) * eighth, 2 * eighth)],
                r.f_in.at[pl.ds((7 * index + 6) * eighth, eighth)],
            ],
            r.p_sent.at[4 + index],
            r.p_came.at[4 + index],
            r.p_free.at[4 + index],
            keep(ref, grad),
        )
        for index, (ref, grad) in enumerate(
            ((r.wq, r.grad_query), (r.wk, r.grad_key), (r.wv, r.grad_value))
        )
    ]
    plane_one = Plane(
        *x_first,
        by_cols(r.wv1, eighth),
        [r.v_in0, r.v_in1, r.v_in2],
        r.p_sent.at[7],
        r.p_came.at[7],
        r.p_free.at[7],
        keep(r.wv1, r.grad_one),
    )

    def units_grad(left, right, into):
        for start in range(0, units, 256):
            span = min(256, units - start)
            into[start : start + span] = mul(left[:, start : start + span], right[...], TN).astype(
                BF16
            )

    def out_grad():
        pl.when(edge)(out_grad_owned)

    def out_grad_owned():
        low = r.db_own[...].reshape(chunks * owned, width)
        for k in range(count):
            own = jnp.concatenate(
                [
                    r.att[c, k, pl.ds(pl.multiple_of(side * owned, owned), owned)]
                    for c in range(chunks)
                ],
                axis=0,
            )
            grad = mul(own, low, TN).astype(BF16)
            for s in range(8):
                r.a2[s * eighth + k * part : s * eighth + (k + 1) * part] = grad[
                    s * part : (s + 1) * part
                ]

    def out_next(step):
        if step < 3:
            pl.when(edge)(lambda: plane_out.next(step))
        else:
            plane_out.next(step)

    def out_piece(peer):
        slot = plane_out.start_of(3)
        return pl.ds(pl.multiple_of(slot * eighth + peer * part, part), part)

    def out_line_copy(step):
        peer = (me + step) % count
        return remote(
            r.a2.at[out_piece(peer)],
            r.z_in.at[side],
            r.z_sent.at[step],
            r.z_came.at[side],
            on_line(peer),
        )

    def out_line_send():
        @pl.when(edge)
        def _():
            plane_out.add(2)
            for step in range(1, count):
                out_line_copy(step).start()

    def out_line_sum():
        for s in range(2):

            @pl.when(me != s * (count - 1))
            def _():
                slot = r.z_in.at[s]
                remote(slot, slot, r.z_sent.at[0], r.z_came.at[s], on_line(0)).wait_recv()

        @pl.when(edge)
        def _():
            r.z_in[side] = r.a2[out_piece(me)]

        grad = r.z_in[0].astype(F32) + r.z_in[1].astype(F32)
        slot = plane_out.start_of(3)
        r.wo[me, pl.ds(pl.multiple_of(slot * part, part), part)] = grad.astype(BF16)
        plane_out.send(3)

    def values_one(c):
        grad = None
        for k in range(count):
            values = r.dv_all[c, k]
            piece = mul(values, r.wv1[:, k * cols : (k + 1) * cols], NT)
            grad = piece if grad is None else grad + piece
            piece = mul(r.first_in[at(c)], values, TN)
            if c > 0:
                piece = piece + r.big[:, k * cols : (k + 1) * cols]
            r.big[:, k * cols : (k + 1) * cols] = piece
        r.dk_sum[at(c)] = grad
        stores.append(local(r.dk_sum.at[at(c)], r.grad_first.at[at(c)]))

    def qkv_grad():
        for start in range(0, width, 256):
            grad = mul(r.a1[:, start : start + 256], r.dqkv[...], TN).astype(BF16)
            for index, into in enumerate((r.wq, r.wk, r.wv)):
                into[start : start + 256] = grad[:, index * cols : (index + 1) * cols]

    def grad_gate():
        units_grad(r.dga, r.a2, r.wg)

    def grad_up():
        units_grad(r.dup, r.a2, r.wu)

    def grad_down():
        units_grad(r.hid, r.g, r.wd)

    def qkv_next(step):
        for plane in plane_qkv:
            plane.next(step)

    def one_start():
        r.wv1[...] = r.big[...].astype(BF16)

    def gain_line_copy(step):
        return remote(
            r.gains,
            r.gain_in.at[side],
            r.gain_sent.at[2 + step],
            r.gain_came.at[side],
            on_line((me + step) % count),
        )

    def gain_copy(index):
        return remote(
            r.gain_sum.at[index],
            r.gain_in.at[2 + index],
            r.gain_sent.at[index],
            r.gain_came.at[2 + index],
            in_plane((other_core, other_x, other_y)[index]),
        )

    def gain_line():
        @pl.when(edge)
        def _():
            for step in range(1, count):
                gain_line_copy(step).start()

    def gain_plane(index):
        if index == 0:
            for s in range(2):

                @pl.when(me != s * (count - 1))
                def _():
                    slot = r.gain_in.at[s]
                    remote(
                        slot, slot, r.gain_sent.at[0], r.gain_came.at[s], on_line(0)
                    ).wait_recv()

            @pl.when(edge)
            def _():
                r.gain_in[side] = r.gains[...]

            total = r.gain_in[0] + r.gain_in[1]
        else:
            gain_copy(index - 1).wait_recv()
            total = r.gain_sum[index - 1] + r.gain_in[1 + index]
        if index < 3:
            r.gain_sum[index] = total
            gain_copy(index).start()
        else:
            for which, into in enumerate((r.gain_one, r.gain_two)):
                into[...] = jnp.concatenate(
                    [total[4 * which + j : 4 * which + j + 1] for j in range(4)], axis=1
                )

    r.gains[...] = jnp.zeros_like(r.gains)
    wo_line()
    first_part(0)
    wo_all.hop(0, 1)
    first_part(1)
    loaded(2, 3, 4, 5, 11, 13, 14)
    project(0)
    first.near(0, 0)
    wo_all.hop(0, 2)
    project(1)
    first_part(2)
    wo_all.hop(0, 3)
    first.near(0, 1)
    first.near(1, 0)
    wo_plane(0, True)
    project(2)
    first.near(1, 1)
    first.far(0)
    attend(0)
    wo_plane(0, False)
    first_part(3)
    first.far(1)
    loaded(7, 8, 9, 10, 12)
    wo_plane(1, True)
    first.near(2, 0)
    attend(1)
    first.far(2)
    first.near(2, 1)
    heads_all.hop(0, 1)
    first.near(3, 0)
    wo_plane(1, False)
    first.near(3, 1)
    wo_plane(2, True)
    heads_all.hop(0, 2)
    attend(2)
    heads_all.hop(1, 1)
    first.far(3)
    wo_plane(2, False)
    heads_all.hop(0, 3)
    feed(0)
    project(3)
    down(0)
    out.open(0)
    heads_all.hop(2, 1)
    heads_all.hop(1, 2)
    back2.near(0, 0)
    attend(3)
    heads_all.hop(2, 2)
    back2.far(0, 0)
    out.near(0, 0)
    heads_all.hop(1, 3)
    out.near(0, 1)
    feed(1)
    heads_all.hop(3, 1)
    heads_all.hop(2, 3)
    feed(2)
    back2.near(1, 0)
    down(2)
    heads_all.hop(3, 2)
    back2.near(1, 1)
    out.far(0, 0)
    back2.far(1, 0)
    back2.near(2, 0)
    back2.far(1, 1)
    back2.near(2, 1)
    down(1)
    out.far(0, 1)
    out.open(2)
    heads_all.hop(3, 3)
    back2.near(0, 1)
    feed(3)
    down(3)
    back2.far(2, 0)
    out.near(2, 0)
    out.open(1)
    back2.near(3, 0)
    back2.far(0, 1)
    grad_gate()
    out.near(2, 1)
    back2.far(2, 1)
    back2.far(3, 0)
    back2.near(3, 1)
    out.far(2, 0)
    out.near(1, 0)
    out.open(3)
    out.far(2, 1)
    through_two(0)
    back2.far(3, 1)
    out.near(3, 0)
    grad_up()
    plane_up.next(0)
    grad_down()
    through_two(1)
    through_two(2)
    out.far(1, 0)
    attend_back(0)
    plane_gate.next(0)
    through_two(3)
    out.far(3, 0)
    finish_out(0)
    out.near(1, 1)
    plane_down.next(0)
    attend_back(1)
    attend_back(2)
    out.far(1, 1)
    values_back(0)
    attend_back(3)
    values_back(2)
    values_back(1)
    plane_down.next(1)
    values_back(3)
    values_all.hop(0, 1)
    plane_up.next(1)
    plane_gate.next(1)
    values_all.hop(1, 1)
    outs_all.pass_on(0, 0)
    keys_back(1)
    values_all.hop(0, 2)
    plane_down.next(2)
    out.near(3, 1)
    finish_out(2)
    values_all.hop(3, 1)
    outs_all.pass_far(0, 0)
    keys_back(2)
    plane_up.next(2)
    out.far(3, 1)
    back1.near(1, 0)
    out_grad()
    plane_gate.next(2)
    plane_down.next(3)
    keys_back(0)
    values_all.hop(3, 2)
    back1.near(1, 1)
    values_all.hop(1, 2)
    keys_back(3)
    back1.far(1, 0)
    finish_out(1)
    back1.near(2, 0)
    outs_all.pass_on(2, 0)
    plane_gate.next(3)
    finish_out(3)
    plane_up.next(3)
    back1.near(0, 0)
    back1.far(2, 0)
    qkv_grad()
    values_all.hop(0, 3)
    qkv_next(0)
    values_all.hop(2, 1)
    back1.near(3, 0)
    back1.far(0, 0)
    back1.far(1, 1)
    back1.near(2, 1)
    back1.near(0, 1)
    qkv_next(1)
    values_all.hop(2, 2)
    outs_all.pass_on(0, 1)
    plane_gate.next(4)
    back1.far(2, 1)
    out_next(0)
    values_all.hop(3, 3)
    back1.far(3, 0)
    out_next(1)
    plane_down.next(4)
    through_one(1)
    outs_all.pass_on(3, 0)
    outs_all.pass_far(2, 0)
    back1.near(3, 1)
    outs_all.pass_on(1, 0)
    outs_all.pass_on(2, 1)
    values_all.hop(1, 3)
    back1.far(0, 1)
    through_one(2)
    back1.far(3, 1)
    values_all.hop(2, 3)
    values_one(0)
    gin_all.pass_on(1, 0)
    outs_all.pass_on(1, 1)
    plane_up.next(4)
    outs_all.pass_far(0, 1)
    outs_all.pass_far(1, 0)
    values_one(1)
    values_one(2)
    through_one(0)
    values_one(3)
    out_next(2)
    gin_all.pass_on(1, 1)
    plane_gate.next(5)
    one_start()
    through_one(3)
    outs_all.pass_far(2, 1)
    plane_one.next(0)
    plane_down.next(5)
    outs_all.pass_far(1, 1)
    outs_all.pass_on(3, 1)
    gin_all.pass_far(1, 0)
    out_line_send()
    gain_line()
    plane_one.next(1)
    outs_all.pass_far(3, 0)
    plane_up.next(5)
    gin_all.pass_on(2, 0)
    gin_all.pass_on(3, 0)
    gin_all.pass_far(1, 1)
    gin_all.pass_on(2, 1)
    qkv_next(2)
    plane_gate.next(6)
    plane_one.next(2)
    gin_all.pass_far(2, 0)
    qkv_next(3)
    gin_all.pass_on(0, 0)
    gain_plane(0)
    plane_one.next(3)
    out_line_sum()
    gin_all.pass_on(0, 1)
    outs_all.pass_far(3, 1)
    qkv_next(4)
    gin_all.pass_on(3, 1)
    gin_all.pass_far(3, 0)
    plane_one.next(4)
    gin_all.pass_far(2, 1)
    plane_down.next(6)
    out_next(4)
    gin_all.pass_far(0, 0)
    qkv_next(5)
    gin_all.pass_far(0, 1)
    gain_plane(1)
    gin_all.pass_far(3, 1)
    plane_one.next(5)
    gain_plane(2)
    plane_up.next(6)
    qkv_next(6)
    plane_one.next(6)
    gain_plane(3)
    out_next(5)
    out_next(6)
    settle()
    for copy in stores:
        copy.wait()
    for line in (back1, out, outs_all, gin_all):
        line.drain(chunks)
    heads_all.drain(lambda slots: r.att.at[:, pl.ds(0, slots)])
    values_all.drain(lambda slots: r.dv_all.at[:, pl.ds(0, slots)])
    for plane in (plane_gate, plane_up, plane_down, plane_out, plane_one, *plane_qkv):
        plane.drain()
    for index in range(3):
        gain_copy(index).wait_send()

    @pl.when(me != 0)
    def _():
        pl.when(me != count - 1)(lambda: first.drain(chunks))

    @pl.when(edge)
    def _():
        for which, dst in enumerate((r.grad_input, r.output)):
            rows = dst.at[pl.ds(0, chunks * owned)]
            pltpu.make_async_copy(rows, rows, r.own_sem.at[which]).wait()
        for step in range(1, count):
            out_line_copy(step).wait_send()
            gain_line_copy(step).wait_send()

        slots = r.f_part.at[pl.ds(0, chunks // 2), pl.ds(0, count - 1)]
        remote(slots, slots, r.do_sent.at[0], r.do_came.at[0, 0], on_line(0)).wait_send()


def fused_layer(arrays, sizes):
    count, groups, tokens, width, cols, units = sizes
    chunks = tokens // CHUNK
    share = CHUNK // count
    eighth = width // 8
    hbm = pl.BlockSpec(memory_space=pl.ANY)
    vmem = pl.BlockSpec(memory_space=pltpu.VMEM)
    ins = dict(
        block_input=hbm,
        layer_one=hbm,
        grad_output=hbm,
        norm_one_in=hbm,
        w_query=hbm,
        w_key=hbm,
        w_value=hbm,
        w_out=hbm,
        norm_two_in=hbm,
        w_gate=hbm,
        w_up=hbm,
        w_down=hbm,
        w_value_one=hbm,
        rates_in=hbm,
        seg_row_in=hbm,
    )
    outs = dict(
        output=((tokens, width), BF16, hbm),
        grad_input=((tokens, width), BF16, hbm),
        grad_first=((tokens, cols), F32, hbm),
        grad_query=((width, cols), BF16, hbm),
        grad_key=((width, cols), BF16, hbm),
        grad_value=((width, cols), BF16, hbm),
        grad_out=((cols, width), BF16, hbm),
        grad_gate=((units, width), BF16, hbm),
        grad_up=((units, width), BF16, hbm),
        grad_down=((units, width), BF16, hbm),
        grad_one=((cols, width), BF16, hbm),
        gain_one=((1, width), F32, vmem),
        gain_two=((1, width), F32, vmem),
    )
    dma = pltpu.SemaphoreType.DMA

    def low(*shape):
        return pltpu.VMEM(shape, BF16)

    def full(*shape):
        return pltpu.VMEM(shape, F32)

    slots = (chunks, count)
    scratch = dict(
        norm_one=full(1, width),
        norm_two=full(1, width),
        rates=full(1, 128),
        seg_row=pltpu.VMEM((1, tokens), jnp.int32),
        cosine=full(tokens, 128),
        sine=full(tokens, 128),
        x=low(tokens, width),
        g=low(tokens, width),
        first_in=low(tokens, cols),
        wq=low(width, cols),
        wk=low(width, cols),
        wv=low(width, cols),
        wv1=low(cols, width),
        wo=low(count, cols, width),
        wg=low(units, width),
        wu=low(units, width),
        wd=low(units, width),
        a1=low(tokens, width),
        a2=low(tokens, width),
        q=low(tokens, cols),
        k=low(tokens, cols),
        vm=low(tokens, cols),
        lse=full(tokens, 128),
        bias=full(CHUNK, CHUNK + REACH),
        sum_a=full(CHUNK, cols),
        sum_b=full(CHUNK // 2, width),
        big=full(CHUNK, width),
        att=low(*slots, CHUNK, cols),
        dv_all=low(*slots, CHUNK, cols),
        hid=low(tokens, units),
        dga=low(tokens, units),
        dup=low(tokens, units),
        h_own=full(chunks, CHUNK // 2, width),
        db_own=low(chunks, CHUNK // 2, width),
        do=low(tokens, cols),
        dqkv=low(tokens, 3 * cols),
        dk_sum=full(tokens, cols),
        dv_sum=full(tokens, cols),
        gains=full(8, width // 4),
        gain_sum=full(3, 8, width // 4),
        gain_in=full(5, 8, width // 4),
        u_in0=low(3, units, 4 * eighth),
        u_in1=low(3, units, 2 * eighth),
        u_in2=low(3, units, eighth),
        z_in=low(2, cols // 8, width),
        v_in0=low(cols, 4 * eighth),
        v_in1=low(cols, 2 * eighth),
        v_in2=low(cols, eighth),
        f_part=low(*slots, CHUNK, cols),
        f_in=low(chunks * count * CHUNK, cols),
        f_meet=low(chunks, CHUNK, cols),
        b_part=low(*slots, share, width),
        b_in=low(*slots, share, width),
        o_part=low(*slots, share, width),
        o_in=low(*slots, share, width),
        load_sem=dma((15,)),
        store_sem=dma((chunks + 8,)),
        own_sem=dma((2,)),
        wo_sent=dma((3,)),
        wo_came=dma((3,)),
        wo_line_came=dma((1, count)),
        wo_right=dma((1,)),
        wo_left=dma((1,)),
        do_sent=dma((1,)),
        do_came=dma((chunks, 2)),
        p_sent=dma((8, 6)),
        p_came=dma((8, 6)),
        p_free=pltpu.SemaphoreType.REGULAR((8, 3)),
        z_sent=dma((count,)),
        z_came=dma((2,)),
        gain_sent=dma((count + 2,)),
        gain_came=dma((5,)),
        f_sent=dma((chunks,)),
        f_came=dma(slots),
        f_met=dma((chunks,)),
        b_sent=dma((chunks,)),
        b_came=dma(slots),
        o_sent=dma((chunks,)),
        o_came=dma(slots),
        d_sent=dma((chunks,)),
        d_came=dma(slots),
        att_came=dma(slots),
        att_right=dma((1,)),
        att_left=dma((1,)),
        dv_came=dma(slots),
        dv_right=dma((1,)),
        dv_left=dma((1,)),
        out_came=dma(slots),
        out_sent=dma((chunks,)),
        gin_came=dma(slots),
        gin_sent=dma((chunks,)),
    )
    results = pl.pallas_call(
        functools.partial(layer_kernel, [*ins, *outs, *scratch], sizes),
        out_shape=[jax.ShapeDtypeStruct(item[0], item[1]) for item in outs.values()],
        in_specs=list(ins.values()),
        out_specs=[item[2] for item in outs.values()],
        scratch_shapes=list(scratch.values()),
        compiler_params=pltpu.CompilerParams(
            collective_id=0, has_side_effects=True, vmem_limit_bytes=VMEM_LIMIT
        ),
        cost_estimate=pl.CostEstimate(
            flops=2 * 13 * 10**9, bytes_accessed=40 * 2**20, transcendentals=0
        ),
    )(*arrays)
    return widen(results)


def widen(results):
    steps = 2
    *arrays, gain_one, gain_two = results
    width = gain_one.shape[1]

    def one(*refs):
        half = len(refs) // 2
        for src, dst in zip(refs[: half - 2], refs[half:-2]):
            dst[...] = src[...].astype(dst.dtype)
        for src, dst in zip(refs[half - 2 : half], refs[-2:]):
            dst[...] = src[0]

    specs = [
        pl.BlockSpec((array.shape[0] // steps, array.shape[1]), lambda i: (i, 0))
        for array in arrays
    ]
    shapes = [
        jax.ShapeDtypeStruct(array.shape, F32 if index else BF16)
        for index, array in enumerate(arrays)
    ]
    return pl.pallas_call(
        one,
        grid=(steps,),
        in_specs=specs + [pl.BlockSpec((1, width), lambda i: (0, 0))] * 2,
        out_specs=specs + [pl.BlockSpec((width,), lambda i: (0,))] * 2,
        out_shape=shapes + [jax.ShapeDtypeStruct((width,), F32)] * 2,
        compiler_params=pltpu.CompilerParams(vmem_limit_bytes=VMEM_LIMIT),
    )(*arrays, gain_one, gain_two)


def on_device(*arguments):
    (
        block_input,
        layer_one_input,
        segment_ids,
        grad_output,
        norm_one,
        w_query,
        w_key,
        w_value,
        w_out,
        norm_two,
        w_gate,
        w_up,
        w_down,
        w_value_one,
    ) = arguments
    count = lax.axis_size("mp")
    groups = lax.axis_size("dp")
    tokens, width = block_input.shape
    cols = w_query.shape[1]
    units = w_gate.shape[1]
    fits = (
        count == 4
        and groups == 8
        and tokens == 4 * CHUNK
        and cols == 256
        and width == count * cols
        and units % 64 == 0
        and units <= 704
        and segment_ids.shape[0] == 1
    )
    if not fits:
        return by_collectives(*arguments)
    half = HD // 2
    rates = np.exp(np.arange(half, dtype=np.float32) * np.float32(-math.log(10000.0) / half))
    r = fused_layer(
        (
            block_input,
            layer_one_input,
            grad_output,
            norm_one[None, :],
            w_query,
            w_key,
            w_value,
            w_out,
            norm_two[None, :],
            w_gate.T,
            w_up.T,
            w_down,
            w_value_one,
            jnp.asarray(np.tile(rates, 4)[None, :]),
            segment_ids,
        ),
        (count, groups, tokens, width, cols, units),
    )
    (
        output,
        grad_input,
        grad_first,
        grad_query,
        grad_key,
        grad_value,
        grad_out,
        grad_gate,
        grad_up,
        grad_down,
        grad_one,
        gain_one,
        gain_two,
    ) = r
    return (
        output,
        grad_input,
        grad_first,
        gain_one,
        grad_query,
        grad_key,
        grad_value,
        grad_out,
        gain_two,
        grad_gate.T,
        grad_up.T,
        grad_down,
        grad_one,
    )


def solution(mesh):
    return jax.shard_map(
        on_device,
        mesh=mesh,
        in_specs=(
            P("dp", None),
            P("dp", "mp"),
            P("dp", None),
            P("dp", None),
            P(),
            P(None, "mp"),
            P(None, "mp"),
            P(None, "mp"),
            P("mp", None),
            P(),
            P(None, "mp"),
            P(None, "mp"),
            P("mp", None),
            P("mp", None),
        ),
        out_specs=(
            P("dp", None),
            P("dp", None),
            P("dp", "mp"),
            P(),
            P(None, "mp"),
            P(None, "mp"),
            P(None, "mp"),
            P("mp", None),
            P(),
            P(None, "mp"),
            P(None, "mp"),
            P("mp", None),
            P("mp", None),
        ),
        check_vma=False,
    )
```
